32 devices in a mesh: groups: 2 (over y), img: 8 (over z, x), slab: 2 (over core).
Axes of the slice: x: 2, y: 2, z: 4, core: 2. Of those that a mesh axis runs over, the one named last changes fastest.
Arguments:
- images: bfloat16 [256, 256, 256], P(('groups', 'img')), parts along dimension 0, may hold values from -24 to 24
- class_index: int32 [256, 1], P(('groups', 'img')), parts along dimension 0, may hold values from 0 to 7
- pose_index: int32 [256], P(('groups', 'img')), parts along dimension 0, may hold values from 0 to 7
- defocus_bin: int32 [256], P(('groups', 'img')), parts along dimension 0, may hold values from 0 to 15
- defocus: float32 [16], replicated, may hold values from 1 to 6
- rows_table: bfloat16 [8, 128, 256], replicated, may hold values from -0.375 to 0.375
- cols_table: bfloat16 [8, 256, 256], P(None, None, 'slab'), may hold values from -0.375 to 0.375
- plane_weight: float32 [8, 2], replicated, may hold values from 0.25 to 1
Outputs:
- volume: float32 [128, 16, 2, 2, 256], P('img', 'groups', None, None, 'slab'), parts along dimension 1
The draws below stay inside these ranges and needn't reach their ends.
There are 2 independent parts, one for each index of `groups`. The reference program is written for one: setup_inputs(seed, part) draws one part's arguments, and reference() takes and returns one part's arrays. A program takes and returns all parts, laid end to end along the dimension named above; an argument that names none is the same for every part. Nothing has to cross between parts.
All inputs are finite; a program needn't handle non-finite values.
Results may differ from the reference program's by a relative error of at most 0.0059.
Values may be sent and summed in bfloat16 or wider, within the bound.
No kernel may reach another device: no remote copies, remote signals or barrier semaphores. Data moves between devices by JAX's collectives and lax.ppermute only.
A program may use at most 64 MiB of HBM per device.

```python
import math
import jax
import jax.numpy as jnp
from jax import lax

BOX = 256
ROWS = 128
CLASSES = 8
PLANES = 2
POSES = 8
BINS = 16
IMG_DEV = 16
IMAGES = 128


def with_ends(result, key, smallest, high):
    place = [jax.random.randint(jax.random.fold_in(key, axis), (), 0, length) for axis, length in enumerate(result.shape)]
    widest = result.shape.index(max(result.shape))
    neighbour = place[:widest] + [(place[widest] + 1) % result.shape[widest]] + place[widest + 1:]
    return result.at[tuple(place)].set(smallest).at[tuple(neighbour)].set(high)


def steps_of(rng, extent, cuts, least, high):
    gain = 1.0
    for position, shards_of in cuts:
        heights = jax.random.uniform(jax.random.fold_in(jax.random.fold_in(rng, 6), position), (shards_of,), jnp.float32, least / len(cuts), high / len(cuts))
        gain = gain * jnp.repeat(jnp.exp(heights), extent[position] // shards_of).reshape((-1,) + (1,) * (len(extent) - 1 - position))
    return gain


def different_ones(stream_key, rows, amount, top, lift):
    order = jax.random.permutation(jax.random.fold_in(stream_key, 1), amount)
    boost = order
    for power in range(3):
        boost = boost * boost // amount
    boost = boost * lift // amount
    tickets = jax.random.randint(jax.random.fold_in(stream_key, 2), (rows, amount), 0, 4096) + boost
    fixed_rows = jax.random.permutation(jax.random.fold_in(stream_key, 3), rows)[jnp.arange(amount) % rows]
    tickets = jnp.where(jnp.arange(rows)[:, None] == fixed_rows[None, :], 1 << 14, tickets)
    priority = tickets * amount + jnp.arange(amount)
    return lax.top_k(priority.astype(jnp.int32), top)[1].astype(jnp.int32)


def gaussian(own_key, shape, spread, reach, split=(), kind=jnp.bfloat16):
    result = jax.random.normal(own_key, shape, jnp.float32) * spread
    if len(split) > 0:
        result = steps_of(own_key, shape, split, -0.22, 0.18) * result
    return jnp.clip(result, min=-reach, max=reach).astype(kind)


def setup_inputs(seed: int = 0, part: int = 0) -> dict:
    arg_keys = jax.random.split(jax.random.key(seed), 9)
    part_keys = jax.random.split(jax.random.fold_in(arg_keys[8], part), 9)
    return {
        "images": gaussian(part_keys[0], (IMAGES, BOX, BOX), 4.0, 24.0, ((0, 8),)),
        "class_index": different_ones(part_keys[1], IMAGES, CLASSES, 1, 2048),
        "pose_index": with_ends(jax.random.randint(part_keys[2], (IMAGES,), 0, POSES), jax.random.fold_in(part_keys[2], 1), 0, POSES - 1).astype(jnp.int32),
        "defocus_bin": with_ends(jax.random.randint(part_keys[3], (IMAGES,), 0, BINS), jax.random.fold_in(part_keys[3], 1), 0, BINS - 1).astype(jnp.int32),
        "defocus": jnp.clip(jax.random.uniform(arg_keys[4], (BINS,), jnp.float32, 1.0, 6.0), 1.0, 6.0),
        "rows_table": gaussian(arg_keys[5], (POSES, ROWS, BOX), BOX ** -0.5, 0.375),
        "cols_table": gaussian(arg_keys[6], (POSES, BOX, BOX), BOX ** -0.5, 0.375, ((2, 2),)),
        "plane_weight": jnp.clip(jax.random.uniform(arg_keys[7], (POSES, PLANES), jnp.float32, 0.25, 1.0), 0.25, 1.0),
    }


wiener_ridge = 1.0
ctf_phase = 0.1

def dft_tables(first_row, row_count):
    freq_rows = (first_row + jnp.arange(row_count, dtype=jnp.int32))[:, None]
    positions = jnp.arange(BOX, dtype=jnp.int32)[None, :]
    phase_angle = (freq_rows * positions % BOX).astype(jnp.float32) * (2.0 * math.pi / BOX)
    factor = 1.0 / math.sqrt(BOX)
    return ((jnp.cos(phase_angle) * factor).astype(jnp.bfloat16), (jnp.sin(phase_angle) * factor).astype(jnp.bfloat16))

def signed_freq(first_row, row_count):
    index_values = first_row + jnp.arange(row_count, dtype=jnp.int32)
    return jnp.where(index_values < BOX // 2, index_values, index_values - BOX)

def ctf_field(defocus_values, first_row, row_count):
    freq_y = signed_freq(first_row, row_count).astype(jnp.float32)
    freq_x = signed_freq(0, BOX).astype(jnp.float32)
    radius_sq = (freq_y[:, None] * freq_y[:, None] + freq_x[None, :] * freq_x[None, :]) / float(BOX // 2 * (BOX // 2))
    return -jnp.sin(math.pi * defocus_values[:, None, None] * radius_sq[None] + ctf_phase)

def squared_table(weight_table):
    wide_table = weight_table.astype(jnp.float32)
    return (wide_table * wide_table).astype(jnp.bfloat16)

def reference(images, class_index, pose_index, defocus_bin, defocus, rows_table, cols_table, plane_weight):
    cos_full, sin_full = dft_tables(0, BOX)
    cos_wide = cos_full.astype(jnp.float32)
    sin_wide = sin_full.astype(jnp.float32)
    rows_wide = rows_table.astype(jnp.float32)
    rows_square = squared_table(rows_table).astype(jnp.float32)
    cols_wide = cols_table.astype(jnp.float32)
    cols_square = squared_table(cols_table).astype(jnp.float32)
    count_blocks = IMAGES // IMG_DEV
    class_ids = jnp.arange(CLASSES, dtype=jnp.int32)

    def one_block(totals, pieces):
        block_images, block_class, block_pose, block_bin = pieces
        pixels = block_images.astype(jnp.float32)
        half_real = jnp.einsum('ky,nyx->nkx', cos_wide, pixels).astype(jnp.bfloat16)
        half_imag = (-jnp.einsum('ky,nyx->nkx', sin_wide, pixels)).astype(jnp.bfloat16)
        half_real, half_imag = lax.optimization_barrier((half_real, half_imag))
        real_wide = half_real.astype(jnp.float32)
        imag_wide = half_imag.astype(jnp.float32)
        four_real = jnp.einsum('nkx,jx->nkj', real_wide, cos_wide) + jnp.einsum('nkx,jx->nkj', imag_wide, sin_wide)
        four_imag = jnp.einsum('nkx,jx->nkj', imag_wide, cos_wide) - jnp.einsum('nkx,jx->nkj', real_wide, sin_wide)
        contrast = ctf_field(defocus[block_bin], 0, BOX)
        spectra = jnp.stack([contrast * four_real, contrast * four_imag, contrast * contrast], 1).astype(jnp.bfloat16)
        spectra = lax.optimization_barrier(spectra).astype(jnp.float32)
        col_pick = cols_wide[block_pose]
        colsq_pick = cols_square[block_pose]
        mixed_pair = jnp.einsum('nkyx,nxj->nkyj', spectra[:, :2], col_pick)
        mixed_weight = jnp.einsum('nyx,nxj->nyj', spectra[:, 2], colsq_pick)
        mixed_terms = jnp.concatenate([mixed_pair, mixed_weight[:, None]], 1).astype(jnp.bfloat16)
        mixed_terms = lax.optimization_barrier(mixed_terms).astype(jnp.float32)
        row_pick = rows_wide[block_pose]
        rowsq_pick = rows_square[block_pose]
        slice_pair = jnp.einsum('nry,nkyj->nkrj', row_pick, mixed_terms[:, :2])
        slice_weight = jnp.einsum('nry,nyj->nrj', rowsq_pick, mixed_terms[:, 2])
        slices = jnp.concatenate([slice_pair, slice_weight[:, None]], 1)
        member = (block_class[:, 0][:, None] == class_ids[None, :]).astype(jnp.float32)
        coefficients = member[:, :, None] * plane_weight[block_pose][:, None, :]
        update = jnp.einsum('ncp,nkrj->rcpkj', coefficients, slices, precision=lax.Precision.HIGHEST)
        return (totals + update, None)
    pieces = (images.reshape(count_blocks, IMG_DEV, BOX, BOX), class_index.reshape(count_blocks, IMG_DEV, 1), pose_index.reshape(count_blocks, IMG_DEV), defocus_bin.reshape(count_blocks, IMG_DEV))
    start_totals = jnp.zeros((ROWS, CLASSES, PLANES, 3, BOX), jnp.float32)
    totals, unused = lax.scan(one_block, start_totals, pieces)
    return totals[:, :, :, 0:2] / (totals[:, :, :, 2:3] + wiener_ridge)
```

```python
import functools
import math

import jax
import jax.numpy as jnp
import numpy as np
from jax import lax
from jax.experimental import pallas as pl
from jax.experimental.pallas import tpu as pltpu
from jax.sharding import PartitionSpec as P

CLASSES = 8

wiener_ridge = 1.0
ctf_phase = 0.1
f32 = jnp.float32
bf16 = jnp.bfloat16


def packed_dft(box):
    half = box // 2
    k = np.concatenate([np.arange(half), [half], np.arange(1, half)])
    angle = (k[:, None] * np.arange(box)[None, :] % box) * (2.0 * math.pi / box)
    table = np.where((np.arange(box) <= half)[:, None], np.cos(angle), np.sin(angle))
    return (table / math.sqrt(box)).astype(np.float32)


def iota(shape, axis):
    return lax.broadcasted_iota(jnp.int32, shape, axis)


def dot(a, b, dims=((1,), (0,))):
    return lax.dot_general(a, b, (dims, ((), ())), preferred_element_type=f32)


def turns_sine(turns):
    return jnp.sin((turns - jnp.round(turns)) * (2.0 * math.pi))


def split_two(value):
    high = value.astype(bf16)
    return high, (value - high.astype(f32)).astype(bf16)


def fold_of(place, half):
    box = 2 * half
    return jnp.where(place <= half, place, box + half - place)


def slices_kernel(
    class_ref, pose_ref, bin_ref, defocus_ref, plane_ref,
    dft_ref, dft_t_ref, images_ref, rows_ref, cols_ref,
    out_ref,
    z_ref, rows_fold, cols_fold, ctf_left, ctf_right, spec_ref, mix_ref, totals,
):
    count, box, _ = images_ref.shape
    half = box // 2
    poses, rows, _ = rows_ref.shape
    cols = cols_ref.shape[2]
    planes = plane_ref.shape[1]

    place = iota((box, box), 0)
    other = iota((box, box), 1)
    near = (fold_of(place, half) == other).astype(f32).astype(bf16)
    far = (jnp.remainder(box - fold_of(place, half), box) == other).astype(f32).astype(bf16)

    z_ref[...] = dot(images_ref[...].reshape(count * box, box), dft_t_ref[...]).astype(bf16)
    rows_fold[...] = dot(
        rows_ref[...].reshape(poses * rows, box), near, ((1,), (1,))
    ).astype(bf16)
    for p in range(poses):
        cols_fold[p, :, :cols] = dot(near, cols_ref[p]).astype(bf16)
        cols_fold[p, :, cols:] = dot(far, cols_ref[p]).astype(bf16)

    lanes = ctf_left.shape[1]
    tall = ctf_left.shape[0]
    lane = iota((1, lanes), 1)
    sub = iota((count, box), 0)
    lane_defocus = jnp.zeros((1, lanes), f32)
    sub_defocus = jnp.zeros((count, box), f32)
    for i in range(count):
        value = defocus_ref[bin_ref[i]]
        lane_defocus = jnp.where(lane % count == i, value, lane_defocus)
        sub_defocus = jnp.where(sub == i, value, sub_defocus)
    scale = 1.0 / (2 * half * half)
    ky = jnp.minimum(iota((tall, lanes), 0), half).astype(f32)
    group = iota((tall, lanes), 1) // count
    turns = lane_defocus * (ky * ky * scale) + ctf_phase / (2.0 * math.pi)
    wave = turns_sine(turns + (group % 2).astype(f32) * 0.25)
    high, low = split_two(wave)
    ctf_left[...] = jnp.where(
        group < 4, high.astype(f32), jnp.where(group < 6, low.astype(f32), 0.0)
    ).astype(bf16)
    kx = iota((count, box), 1)
    kx = jnp.where(kx <= half, kx, kx - half).astype(f32)
    turns = sub_defocus * (kx * kx * scale)
    cos_high, cos_low = split_two(-turns_sine(turns + 0.25))
    sin_high, sin_low = split_two(-turns_sine(turns))
    zero = jnp.zeros((lanes - 6 * count, box), bf16)
    ctf_right[...] = jnp.concatenate(
        [cos_high, sin_high, cos_low, sin_low, cos_high, sin_high, zero], 0
    )

    totals[...] = jnp.zeros_like(totals)

    row_zero = iota((half, half), 0) == 0
    col_zero = iota((half, half), 1) == 0
    edge = row_zero | col_zero
    short_row = iota((16, half), 0) == 0
    short_col = iota((16, half), 1) == 0
    right_row = iota((lanes, box), 0) % count

    def one_image(i, carry):
        pose = pose_ref[i]
        chosen = jnp.where(right_row == i, ctf_right[...].astype(f32), 0.0).astype(bf16)
        contrast = dot(ctf_left[...], chosen)
        y = dot(dft_ref[...], z_ref[pl.ds(pl.multiple_of(i * box, box), box), :])
        cc, cs = y[:half, :half], y[:half, half:]
        sc, ss = y[half:, :half], y[half:, half:]
        ss_in = jnp.where(edge, 0.0, ss)
        sc_in = jnp.where(row_zero, 0.0, sc)
        cs_in = jnp.where(col_zero, 0.0, cs)
        near_ctf, far_ctf = contrast[:half, :half], contrast[:half, half:]
        spec_ref[0:half, 0:half] = (near_ctf * (cc - ss_in)).astype(bf16)
        spec_ref[0:half, half:] = (far_ctf * jnp.where(col_zero, cs, cc + ss_in)).astype(bf16)
        spec_ref[half:box, 0:half] = (-near_ctf * (sc_in + cs_in)).astype(bf16)
        spec_ref[half:box, half:] = (
            far_ctf * jnp.where(col_zero, jnp.where(row_zero, 0.0, -ss), cs_in - sc_in)
        ).astype(bf16)
        sc_top = jnp.broadcast_to(sc[0:1], (16, half))
        ss_top = jnp.broadcast_to(ss[0:1], (16, half))
        ss_top_in = jnp.where(short_col, 0.0, ss_top)
        edge_ctf = contrast[half : half + 1]
        spec_ref[box : box + 16, 0:half] = (
            edge_ctf[:, :half] * jnp.where(short_row, sc_top, -ss_top_in)
        ).astype(bf16)
        spec_ref[box : box + 16, half:] = (
            edge_ctf[:, half:]
            * jnp.where(short_row, jnp.where(short_col, ss_top, sc_top), ss_top_in)
        ).astype(bf16)
        mixed = dot(spec_ref[...], cols_fold[pose])
        top = iota((half, cols), 0) == 0
        mix_ref[0:half, 0:cols] = mixed[:half, :cols].astype(bf16)
        mix_ref[0:half, cols:] = mixed[half:box, :cols].astype(bf16)
        mix_ref[half:, 0:cols] = jnp.where(
            top, mixed[box : box + 1, :cols], mixed[:half, cols:]
        ).astype(bf16)
        mix_ref[half:, cols:] = jnp.where(
            top, mixed[box + 1 : box + 2, :cols], -mixed[half:box, cols:]
        ).astype(bf16)
        pose_rows = rows_fold[pl.ds(pl.multiple_of(pose * rows, rows), rows), :]
        piece = dot(pose_rows, mix_ref[...])
        for z in range(planes):
            slot = class_ref[i, 0] * planes + z
            totals[slot] += plane_ref[pose, z] * piece
        return carry

    lax.fori_loop(0, count, one_image, 0, unroll=True)
    owned = out_ref.shape[2]
    for d in range(out_ref.shape[0]):
        out_ref[d] = totals[:, d * owned : (d + 1) * owned, :].astype(bf16)


def own_totals(images, class_index, pose_index, defocus_bin, defocus, rows_table, cols_table, plane_weight, pieces):
    count, box, _ = images.shape
    poses, rows, _ = rows_table.shape
    cols = cols_table.shape[2]
    planes = plane_weight.shape[1]
    slots = CLASSES * planes
    owned = rows // pieces
    table = packed_dft(box)
    smem = pl.BlockSpec(memory_space=pltpu.SMEM)
    vmem = pl.BlockSpec(memory_space=pltpu.VMEM)
    lanes = 128 * (-(-6 * count // 128))
    return pl.pallas_call(
        slices_kernel,
        out_shape=jax.ShapeDtypeStruct((pieces, slots, owned, 2 * cols), bf16),
        in_specs=[smem] * 5 + [vmem] * 5,
        out_specs=vmem,
        scratch_shapes=[
            pltpu.VMEM((count * box, box), bf16),
            pltpu.VMEM((poses * rows, box), bf16),
            pltpu.VMEM((poses, box, 2 * cols), bf16),
            pltpu.VMEM((box // 2 + 16, lanes), bf16),
            pltpu.VMEM((lanes, box), bf16),
            pltpu.VMEM((box + 16, box), bf16),
            pltpu.VMEM((box, 2 * cols), bf16),
            pltpu.VMEM((slots, rows, 2 * cols), f32),
        ],
        compiler_params=pltpu.CompilerParams(vmem_limit_bytes=48 * 1024 * 1024),
        cost_estimate=pl.CostEstimate(
            flops=2 * count * box * box * 1000, bytes_accessed=6 * 1024 * 1024, transcendentals=0
        ),
    )(
        class_index, pose_index, defocus_bin, defocus, plane_weight,
        jnp.asarray(table, bf16), jnp.asarray(table.T.copy(), bf16),
        images, rows_table, cols_table,
    )


def squared_table(weight_table):
    wide_table = weight_table.astype(f32)
    return (wide_table * wide_table).astype(bf16)


def weight_totals(class_index, pose_index, defocus_bin, defocus, rows_table, cols_table, plane_weight, first_row, owned):
    box = rows_table.shape[2]
    poses = rows_table.shape[0]
    bins = defocus.shape[0]
    half = box // 2
    exact = lax.Precision.HIGHEST
    code = (class_index[:, 0] * poses + pose_index) * bins + defocus_bin
    codes = lax.all_gather(code, "img", tiled=True)
    hits = (codes[:, None] == jnp.arange(CLASSES * poses * bins, dtype=jnp.int32)).astype(f32)
    counts = jnp.sum(hits, 0).reshape(CLASSES, poses, bins)
    place = jnp.arange(box, dtype=jnp.int32)
    freq = jnp.where(place < half, place, place - box).astype(f32)
    turns = defocus[:, None] * (freq * freq)[None, :] * (1.0 / (half * half))
    turns_y = turns + ctf_phase / math.pi
    ones = jnp.ones_like(turns)
    wave_y = jnp.stack([0.5 * ones, -0.5 * turns_sine(turns_y + 0.25), 0.5 * turns_sine(turns_y)])
    wave_x = jnp.stack([ones, turns_sine(turns + 0.25), turns_sine(turns)])
    rows_own = lax.dynamic_slice_in_dim(rows_table, first_row, owned, 1)
    u = jnp.einsum("pry,mby->pmbr", squared_table(rows_own).astype(f32), wave_y, precision=exact)
    v = jnp.einsum("pxj,mbx->pmbj", squared_table(cols_table).astype(f32), wave_x, precision=exact)
    weight = counts[:, None] * plane_weight.T[None, :, :, None]
    left = weight[:, :, :, None, :, None] * u[None, None]
    return jnp.einsum("czpmbr,pmbj->rczj", left, v, precision=exact)


def body(images, class_index, pose_index, defocus_bin, defocus, rows_table, cols_table, plane_weight):
    rows = rows_table.shape[1]
    cols = cols_table.shape[2]
    planes = plane_weight.shape[1]
    members = lax.axis_size("img")
    owned = rows // members
    pieces = members if owned % 16 == 0 else 1
    totals = own_totals(
        images, class_index, pose_index, defocus_bin, defocus, rows_table, cols_table, plane_weight, pieces
    )
    slots = totals.shape[1]
    if pieces == 1:
        totals = totals.reshape(slots, members, owned, 2 * cols).transpose(1, 0, 2, 3)
    own = lax.psum_scatter(totals, "img", scatter_dimension=0, tiled=False)
    weight = weight_totals(
        class_index, pose_index, defocus_bin, defocus, rows_table, cols_table, plane_weight,
        lax.axis_index("img") * owned, owned,
    )
    own = own.astype(f32).reshape(CLASSES, planes, owned, 2, cols).transpose(2, 0, 1, 3, 4)
    return own / (weight[:, :, :, None, :] + wiener_ridge)


def solution(mesh):
    placed = (
        P(("groups", "img"), None, None),
        P(("groups", "img"), None),
        P(("groups", "img")),
        P(("groups", "img")),
        P(),
        P(),
        P(None, None, "slab"),
        P(),
    )
    return jax.shard_map(
        body,
        mesh=mesh,
        in_specs=placed,
        out_specs=P("img", "groups", None, None, "slab"),
        check_vma=False,
    )
```

```python
import functools
import math

import jax
import jax.numpy as jnp
import numpy as np
from jax import lax
from jax.experimental import pallas as pl
from jax.experimental.pallas import tpu as pltpu
from jax.sharding import PartitionSpec as P

CLASSES = 8

wiener_ridge = 1.0
ctf_phase = 0.1
f32 = jnp.float32
bf16 = jnp.bfloat16


def packed_dft(box):
    half = box // 2
    k = np.concatenate([np.arange(half), [half], np.arange(1, half)])
    angle = (k[:, None] * np.arange(box)[None, :] % box) * (2.0 * math.pi / box)
    table = np.where((np.arange(box) <= half)[:, None], np.cos(angle), np.sin(angle))
    return (table / math.sqrt(box)).astype(np.float32)


def iota(shape, axis):
    return lax.broadcasted_iota(jnp.int32, shape, axis)


def dot(a, b, dims=((1,), (0,))):
    return lax.dot_general(a, b, (dims, ((), ())), preferred_element_type=f32)


def turns_sine(turns):
    return jnp.sin((turns - jnp.round(turns)) * (2.0 * math.pi))


def split_two(value):
    high = value.astype(bf16)
    return high, (value - high.astype(f32)).astype(bf16)


def fold_of(place, half):
    box = 2 * half
    return jnp.where(place <= half, place, box + half - place)


def slices_kernel(
    class_hbm, pose_hbm, bin_hbm, defocus_hbm, plane_hbm,
    dft_hbm, dft_t_hbm, images_hbm, rows_hbm, cols_hbm,
    *refs,
):
    outs, refs = refs[:-SCRATCH], refs[-SCRATCH:]
    (
        class_ref, pose_ref, bin_ref, defocus_ref, plane_ref,
        dft_ref, dft_t_ref, images_ref, rows_ref, cols_ref, arrived,
        z_ref, rows_fold, cols_fold, ctf_left, ctf_right, spec_ref, mix_ref, totals,
    ) = refs
    count, box, _ = images_ref.shape
    half = box // 2
    poses, rows, _ = rows_ref.shape
    cols = cols_ref.shape[2]
    planes = plane_ref.shape[0]

    pairs = (
        (class_hbm, class_ref), (pose_hbm, pose_ref), (bin_hbm, bin_ref),
        (defocus_hbm, defocus_ref), (plane_hbm, plane_ref),
        (rows_hbm, rows_ref), (cols_hbm, cols_ref), (dft_t_hbm, dft_t_ref),
        (images_hbm, images_ref), (dft_hbm, dft_ref),
    )
    copies = [
        pltpu.make_async_copy(source, target, arrived.at[n])
        for n, (source, target) in enumerate(pairs)
    ]
    for copy in copies:
        copy.start()

    place = iota((box, box), 0)
    other = iota((box, box), 1)
    folded = fold_of(place, half)
    near = (folded == other).astype(f32).astype(bf16)
    far = (jnp.where(folded == 0, 0, box - folded) == other).astype(f32).astype(bf16)

    for copy in copies[:5]:
        copy.wait()
    lanes = ctf_left.shape[1]
    tall = ctf_left.shape[0]
    lane = iota((1, lanes), 1)
    sub = iota((count, box), 0)
    lane_defocus = jnp.zeros((1, lanes), f32)
    sub_defocus = jnp.zeros((count, box), f32)
    for i in range(count):
        value = defocus_ref[bin_ref[i]]
        lane_defocus = jnp.where(lane % count == i, value, lane_defocus)
        sub_defocus = jnp.where(sub == i, value, sub_defocus)
    scale = 1.0 / (2 * half * half)
    ky = jnp.minimum(iota((tall, lanes), 0), half).astype(f32)
    group = iota((tall, lanes), 1) // count
    turns = lane_defocus * (ky * ky * scale) + ctf_phase / (2.0 * math.pi)
    wave = turns_sine(turns + (group % 2).astype(f32) * 0.25)
    high, low = split_two(wave)
    ctf_left[...] = jnp.where(
        group < 4, high.astype(f32), jnp.where(group < 6, low.astype(f32), 0.0)
    ).astype(bf16)
    kx = iota((count, box), 1)
    kx = jnp.where(kx <= half, kx, kx - half).astype(f32)
    turns = sub_defocus * (kx * kx * scale)
    cos_high, cos_low = split_two(-turns_sine(turns + 0.25))
    sin_high, sin_low = split_two(-turns_sine(turns))
    zero = jnp.zeros((lanes - 6 * count, box), bf16)
    ctf_right[...] = jnp.concatenate(
        [cos_high, sin_high, cos_low, sin_low, cos_high, sin_high, zero], 0
    )
    totals[...] = jnp.zeros_like(totals)

    copies[5].wait()
    rows_fold[...] = dot(
        rows_ref[...].reshape(poses * rows, box), near, ((1,), (1,))
    ).astype(bf16)
    copies[6].wait()
    for p in range(poses):
        cols_fold[p, :, :cols] = dot(near, cols_ref[p]).astype(bf16)
        cols_fold[p, :, cols:] = dot(far, cols_ref[p]).astype(bf16)
    for copy in copies[7:]:
        copy.wait()
    z_ref[...] = dot(images_ref[...].reshape(count * box, box), dft_t_ref[...]).astype(bf16)

    row_zero = iota((half, half), 0) == 0
    col_zero = iota((half, half), 1) == 0
    edge = row_zero | col_zero
    short_row = iota((16, half), 0) == 0
    short_col = iota((16, half), 1) == 0
    right_row = iota((lanes, box), 0) % count

    def one_image(i, carry):
        pose = pose_ref[i]
        chosen = jnp.where(right_row == i, ctf_right[...].astype(f32), 0.0).astype(bf16)
        contrast = dot(ctf_left[...], chosen)
        y = dot(dft_ref[...], z_ref[pl.ds(pl.multiple_of(i * box, box), box), :])
        cc, cs = y[:half, :half], y[:half, half:]
        sc, ss = y[half:, :half], y[half:, half:]
        ss_in = jnp.where(edge, 0.0, ss)
        sc_in = jnp.where(row_zero, 0.0, sc)
        cs_in = jnp.where(col_zero, 0.0, cs)
        near_ctf, far_ctf = contrast[:half, :half], contrast[:half, half:]
        spec_ref[0:half, 0:half] = (near_ctf * (cc - ss_in)).astype(bf16)
        spec_ref[0:half, half:] = (far_ctf * jnp.where(col_zero, cs, cc + ss_in)).astype(bf16)
        spec_ref[half:box, 0:half] = (-near_ctf * (sc_in + cs_in)).astype(bf16)
        spec_ref[half:box, half:] = (
            far_ctf * jnp.where(col_zero, jnp.where(row_zero, 0.0, -ss), cs_in - sc_in)
        ).astype(bf16)
        sc_top = jnp.broadcast_to(sc[0:1], (16, half))
        ss_top = jnp.broadcast_to(ss[0:1], (16, half))
        ss_top_in = jnp.where(short_col, 0.0, ss_top)
        edge_ctf = contrast[half : half + 1]
        spec_ref[box : box + 16, 0:half] = (
            edge_ctf[:, :half] * jnp.where(short_row, sc_top, -ss_top_in)
        ).astype(bf16)
        spec_ref[box : box + 16, half:] = (
            edge_ctf[:, half:]
            * jnp.where(short_row, jnp.where(short_col, ss_top, sc_top), ss_top_in)
        ).astype(bf16)
        mixed = dot(spec_ref[...], cols_fold[pose])
        top = iota((half, cols), 0) == 0
        mix_ref[0:half, 0:cols] = mixed[:half, :cols].astype(bf16)
        mix_ref[0:half, cols:] = mixed[half:box, :cols].astype(bf16)
        mix_ref[half:, 0:cols] = jnp.where(
            top, mixed[box : box + 1, :cols], mixed[:half, cols:]
        ).astype(bf16)
        mix_ref[half:, cols:] = jnp.where(
            top, mixed[box + 1 : box + 2, :cols], -mixed[half:box, cols:]
        ).astype(bf16)
        pose_rows = rows_fold[pl.ds(pl.multiple_of(pose * rows, rows), rows), :]
        piece = dot(pose_rows, mix_ref[...])
        for z in range(planes):
            slot = class_ref[i] * planes + z
            totals[slot] += plane_ref[z, pose] * piece
        return carry

    lax.fori_loop(0, count, one_image, 0, unroll=True)

    if len(outs) == 1:
        outs[0][...] = totals[...].astype(bf16)
    else:
        turns_round = len(outs) // 2
        members = 2 * turns_round
        owned = rows // members
        me = lax.axis_index("img")
        for k in range(turns_round):
            mine = lax.rem(me + 2 * k, members)
            theirs = mine + 1 - 2 * lax.rem(me, 2)
            first = pl.multiple_of(theirs * owned, owned)
            outs[k][...] = totals[:, pl.ds(first, owned), :].astype(bf16)
            first = pl.multiple_of(mine * owned, owned)
            outs[turns_round + k][...] = totals[:, pl.ds(first, owned), :]


SCRATCH = 19


def own_totals(images, class_index, pose_index, defocus_bin, defocus, rows_table, cols_table, plane_weight, turns_round):
    count, box, _ = images.shape
    poses, rows, _ = rows_table.shape
    cols = cols_table.shape[2]
    planes = plane_weight.shape[1]
    slots = CLASSES * planes
    table = packed_dft(box)
    any_place = pl.BlockSpec(memory_space=pl.ANY)
    vmem = pl.BlockSpec(memory_space=pltpu.VMEM)
    lanes = 128 * (-(-6 * count // 128))
    if turns_round == 0:
        out_shape = [jax.ShapeDtypeStruct((slots, rows, 2 * cols), bf16)]
    else:
        piece = (slots, rows // (2 * turns_round), 2 * cols)
        out_shape = [jax.ShapeDtypeStruct(piece, bf16)] * turns_round
        out_shape += [jax.ShapeDtypeStruct(piece, f32)] * turns_round
    operands = (
        class_index[:, 0], pose_index, defocus_bin, defocus, plane_weight.T,
        jnp.asarray(table, bf16), jnp.asarray(table.T.copy(), bf16),
        images, rows_table, cols_table,
    )
    return pl.pallas_call(
        slices_kernel,
        out_shape=out_shape,
        in_specs=[any_place] * 10,
        out_specs=[vmem] * len(out_shape),
        scratch_shapes=[pltpu.SMEM(x.shape, x.dtype) for x in operands[:5]]
        + [pltpu.VMEM(x.shape, x.dtype) for x in operands[5:]]
        + [
            pltpu.SemaphoreType.DMA((10,)),
            pltpu.VMEM((count * box, box), bf16),
            pltpu.VMEM((poses * rows, box), bf16),
            pltpu.VMEM((poses, box, 2 * cols), bf16),
            pltpu.VMEM((box // 2 + 16, lanes), bf16),
            pltpu.VMEM((lanes, box), bf16),
            pltpu.VMEM((box + 16, box), bf16),
            pltpu.VMEM((box, 2 * cols), bf16),
            pltpu.VMEM((slots, rows, 2 * cols), f32),
        ],
        compiler_params=pltpu.CompilerParams(vmem_limit_bytes=VMEM_LIMIT),
        cost_estimate=pl.CostEstimate(
            flops=2 * count * box * box * 1000, bytes_accessed=6 * 1024 * 1024, transcendentals=0
        ),
    )(*operands)


VMEM_LIMIT = 56 * 1024 * 1024


def ridge_kernel(defocus_hbm, plane_hbm, rows_hbm, cols_hbm, *refs):
    codes, refs = refs[:-6], refs[-6:]
    out_ref, defocus_ref, plane_ref, rows_ref, cols_ref, arrived = refs
    poses, owned, box = rows_ref.shape
    cols = cols_ref.shape[2]
    bins = defocus_ref.shape[0]
    planes = plane_ref.shape[0]
    slots = CLASSES * planes
    half = box // 2
    first = pl.multiple_of(lax.axis_index("img") * owned, owned)
    copies = [
        pltpu.make_async_copy(defocus_hbm, defocus_ref, arrived.at[0]),
        pltpu.make_async_copy(plane_hbm, plane_ref, arrived.at[1]),
        pltpu.make_async_copy(rows_hbm.at[:, pl.ds(first, owned), :], rows_ref, arrived.at[2]),
        pltpu.make_async_copy(cols_hbm, cols_ref, arrived.at[3]),
    ]
    for copy in copies:
        copy.start()

    code = codes[0][...]
    for ref in codes[1:]:
        code = jnp.maximum(code, ref[...])
    images = code.shape[1]
    wide = 128
    kind = code // bins
    slot_row = iota((slots, images), 0) // planes
    left = (slot_row == kind // poses).astype(f32).astype(bf16)
    term = iota((poses * wide, images), 0)
    right_code = jnp.where(
        term % wide < 3 * bins, (term // wide) * bins + term % bins, poses * bins
    )
    right = (right_code == code % (poses * bins)).astype(f32).astype(bf16)
    counts = dot(left, right, ((1,), (1,)))

    copies[0].wait()
    copies[1].wait()
    share_slot = iota((slots, poses * wide), 0) % planes
    share_pose = iota((slots, poses * wide), 1) // wide
    share = jnp.zeros((slots, poses * wide), f32)
    for p in range(poses):
        for z in range(planes):
            share = jnp.where((share_slot == z) & (share_pose == p), plane_ref[z, p], share)
    counts = counts * share

    bin_row = iota((bins, box), 0)
    sub_defocus = jnp.zeros((bins, box), f32)
    for b in range(bins):
        sub_defocus = jnp.where(bin_row == b, defocus_ref[b], sub_defocus)
    freq = iota((bins, box), 1)
    freq = jnp.where(freq < half, freq, box - freq).astype(f32)
    turns_x = sub_defocus * (freq * freq * (1.0 / (half * half)))
    turns_y = turns_x + ctf_phase / math.pi
    zero = jnp.zeros((wide - 3 * bins, box), f32)
    ones = jnp.ones((bins, box), f32)
    wave_y = jnp.concatenate(
        [0.5 * ones, -0.5 * turns_sine(turns_y + 0.25), 0.5 * turns_sine(turns_y), zero], 0
    )
    wave_x = jnp.concatenate([ones, turns_sine(turns_x + 0.25), turns_sine(turns_x), zero], 0)
    y_high, y_low = split_two(wave_y)
    x_high, x_low = split_two(wave_x)
    copies[2].wait()
    copies[3].wait()
    rows_sq = rows_ref[...].reshape(poses * owned, box).astype(f32)
    rows_sq = (rows_sq * rows_sq).astype(bf16)
    u = dot(rows_sq, y_high, ((1,), (1,))) + dot(rows_sq, y_low, ((1,), (1,)))
    total = jnp.zeros((slots * owned, cols), f32)
    for p in range(poses):
        cols_sq = cols_ref[p].astype(f32)
        cols_sq = (cols_sq * cols_sq).astype(bf16)
        v_high, v_low = split_two(dot(x_high, cols_sq) + dot(x_low, cols_sq))
        scaled = counts[:, p * wide : (p + 1) * wide][:, None, :] * u[p * owned : (p + 1) * owned][None]
        scaled = scaled.reshape(slots * owned, wide)
        s_high, s_low = split_two(scaled)
        total += dot(s_high, v_high) + dot(s_low, v_high) + dot(s_high, v_low)
    out_ref[...] = (1.0 / (total + wiener_ridge)).reshape(slots, owned, cols)


def own_ridges(codes, defocus, plane_weight, rows_table, cols_table, owned):
    poses, _, box = rows_table.shape
    cols = cols_table.shape[2]
    slots = CLASSES * plane_weight.shape[1]
    any_place = pl.BlockSpec(memory_space=pl.ANY)
    vmem = pl.BlockSpec(memory_space=pltpu.VMEM)
    planes = plane_weight.T
    return pl.pallas_call(
        ridge_kernel,
        out_shape=jax.ShapeDtypeStruct((slots, owned, cols), f32),
        in_specs=[any_place] * 4 + [vmem] * len(codes),
        out_specs=vmem,
        scratch_shapes=[
            pltpu.SMEM(defocus.shape, f32),
            pltpu.SMEM(planes.shape, f32),
            pltpu.VMEM((poses, owned, box), bf16),
            pltpu.VMEM(cols_table.shape, bf16),
            pltpu.SemaphoreType.DMA((4,)),
        ],
        compiler_params=pltpu.CompilerParams(vmem_limit_bytes=16 * 1024 * 1024),
        cost_estimate=pl.CostEstimate(
            flops=2 * poses * 1000 * 128 * 256, bytes_accessed=2 * 1024 * 1024, transcendentals=0
        ),
    )(defocus, planes, rows_table, cols_table, *codes)


def finish_kernel(ridge_ref, keep_ref, *refs):
    parts, out_ref = refs[:-1], refs[-1]
    slots, owned, cols = ridge_ref.shape
    for s in range(slots):
        value = keep_ref[s]
        for part in parts:
            value = value + part[s].astype(f32)
        ridge = ridge_ref[s]
        out_ref[:, 2 * s, :] = value[:, :cols] * ridge
        out_ref[:, 2 * s + 1, :] = value[:, cols:] * ridge


def finish(ridge, keep, parts):
    slots, owned, cols = ridge.shape
    vmem = pl.BlockSpec(memory_space=pltpu.VMEM)
    return pl.pallas_call(
        finish_kernel,
        out_shape=jax.ShapeDtypeStruct((owned, 2 * slots, cols), f32),
        in_specs=[vmem] * (2 + len(parts)),
        out_specs=vmem,
        compiler_params=pltpu.CompilerParams(vmem_limit_bytes=16 * 1024 * 1024),
        cost_estimate=pl.CostEstimate(
            flops=8 * slots * owned * cols, bytes_accessed=8 * 1024 * 1024 // 4, transcendentals=0
        ),
    )(ridge, keep, *parts)


def squared_table(weight_table):
    wide_table = weight_table.astype(f32)
    return (wide_table * wide_table).astype(bf16)


def weight_totals(class_index, pose_index, defocus_bin, defocus, rows_table, cols_table, plane_weight, first_row, owned):
    box = rows_table.shape[2]
    poses = rows_table.shape[0]
    bins = defocus.shape[0]
    half = box // 2
    exact = lax.Precision.HIGHEST
    code = (class_index[:, 0] * poses + pose_index) * bins + defocus_bin
    codes = lax.all_gather(code, "img", tiled=True)
    hits = (codes[:, None] == jnp.arange(CLASSES * poses * bins, dtype=jnp.int32)).astype(f32)
    counts = jnp.sum(hits, 0).reshape(CLASSES, poses, bins)
    place = jnp.arange(box, dtype=jnp.int32)
    freq = jnp.where(place < half, place, place - box).astype(f32)
    turns = defocus[:, None] * (freq * freq)[None, :] * (1.0 / (half * half))
    turns_y = turns + ctf_phase / math.pi
    ones = jnp.ones_like(turns)
    wave_y = jnp.stack([0.5 * ones, -0.5 * turns_sine(turns_y + 0.25), 0.5 * turns_sine(turns_y)])
    wave_x = jnp.stack([ones, turns_sine(turns + 0.25), turns_sine(turns)])
    rows_own = lax.dynamic_slice_in_dim(rows_table, first_row, owned, 1)
    u = jnp.einsum("pry,mby->pmbr", squared_table(rows_own).astype(f32), wave_y, precision=exact)
    v = jnp.einsum("pxj,mbx->pmbj", squared_table(cols_table).astype(f32), wave_x, precision=exact)
    weight = counts[:, None] * plane_weight.T[None, :, :, None]
    left = weight[:, :, :, None, :, None] * u[None, None]
    return jnp.einsum("czpmbr,pmbj->rczj", left, v, precision=exact)


def by_rounds(images, class_index, pose_index, defocus_bin, defocus, rows_table, cols_table, plane_weight):
    members = lax.axis_size("img")
    rounds = members // 2
    count = images.shape[0]
    poses, rows, _ = rows_table.shape
    planes = plane_weight.shape[1]
    cols = cols_table.shape[2]
    owned = rows // members
    me = lax.axis_index("img")

    code = (class_index[:, 0] * poses + pose_index) * defocus.shape[0] + defocus_bin
    seat = jnp.arange(members * count, dtype=jnp.int32) // count
    code = jnp.where(seat == me, jnp.tile(code, members), -1)[None]
    codes = [code] + [
        lax.ppermute(code, "img", [(i, (i + k) % members) for i in range(members)])
        for k in range(1, members)
    ]
    outs = own_totals(
        images, class_index, pose_index, defocus_bin, defocus, rows_table, cols_table, plane_weight, rounds
    )
    sends, keeps = outs[:rounds], outs[rounds:]
    order = sorted(range(rounds), key=lambda k: (k == 0, -min(k, rounds - k)))
    parts = []
    for k in order:
        came = lax.ppermute(sends[k], "img", [(i, i ^ 1) for i in range(members)])
        if k == 0:
            parts.append(came)
        else:
            both = (keeps[k] + came.astype(f32)).astype(bf16)
            parts.append(lax.ppermute(both, "img", [(i, (i + 2 * k) % members) for i in range(members)]))
    ridge = own_ridges(codes, defocus, plane_weight, rows_table, cols_table, owned)
    out = finish(ridge, keeps[0], parts)
    return out.reshape(owned, CLASSES, planes, 2, cols)


def by_scatter(images, class_index, pose_index, defocus_bin, defocus, rows_table, cols_table, plane_weight):
    rows = rows_table.shape[1]
    cols = cols_table.shape[2]
    planes = plane_weight.shape[1]
    members = lax.axis_size("img")
    owned = rows // members
    (totals,) = own_totals(
        images, class_index, pose_index, defocus_bin, defocus, rows_table, cols_table, plane_weight, 0
    )
    slots = totals.shape[0]
    totals = totals.reshape(slots, members, owned, 2 * cols).transpose(1, 0, 2, 3)
    own = lax.psum_scatter(totals, "img", scatter_dimension=0, tiled=False)
    weight = weight_totals(
        class_index, pose_index, defocus_bin, defocus, rows_table, cols_table, plane_weight,
        lax.axis_index("img") * owned, owned,
    )
    own = own.astype(f32).reshape(CLASSES, planes, owned, 2, cols).transpose(2, 0, 1, 3, 4)
    return own / (weight[:, :, :, None, :] + wiener_ridge)


def body(*arrays):
    rows = arrays[5].shape[1]
    members = lax.axis_size("img")
    small = 2 <= members <= 8 and members % 2 == 0 and rows % (16 * members) == 0
    return (by_rounds if small else by_scatter)(*arrays)


def solution(mesh):
    placed = (
        P(("groups", "img"), None, None),
        P(("groups", "img"), None),
        P(("groups", "img")),
        P(("groups", "img")),
        P(),
        P(),
        P(None, None, "slab"),
        P(),
    )
    return jax.shard_map(
        body,
        mesh=mesh,
        in_specs=placed,
        out_specs=P("img", "groups", None, None, "slab"),
        check_vma=False,
    )
```

```python
import functools
import math

import jax
import jax.numpy as jnp
import numpy as np
from jax import lax
from jax.experimental import pallas as pl
from jax.experimental.pallas import tpu as pltpu
from jax.sharding import PartitionSpec as P

CLASSES = 8

wiener_ridge = 1.0
ctf_phase = 0.1
f32 = jnp.float32
bf16 = jnp.bfloat16


def packed_dft(box):
    half = box // 2
    k = np.concatenate([np.arange(half), [half], np.arange(1, half)])
    angle = (k[:, None] * np.arange(box)[None, :] % box) * (2.0 * math.pi / box)
    table = np.where((np.arange(box) <= half)[:, None], np.cos(angle), np.sin(angle))
    return (table / math.sqrt(box)).astype(np.float32)


def iota(shape, axis):
    return lax.broadcasted_iota(jnp.int32, shape, axis)


def dot(a, b, dims=((1,), (0,))):
    return lax.dot_general(a, b, (dims, ((), ())), preferred_element_type=f32)


def turns_sine(turns):
    return jnp.sin((turns - jnp.round(turns)) * (2.0 * math.pi))


def split_two(value):
    high = value.astype(bf16)
    return high, (value - high.astype(f32)).astype(bf16)


def fold_of(place, half):
    box = 2 * half
    return jnp.where(place <= half, place, box + half - place)


def slices_kernel(
    class_hbm, pose_hbm, bin_hbm, defocus_hbm, plane_hbm,
    dft_hbm, dft_t_hbm, images_hbm, rows_hbm, cols_hbm,
    *refs,
):
    outs, refs = refs[:-SCRATCH], refs[-SCRATCH:]
    (
        class_ref, pose_ref, bin_ref, defocus_ref, plane_ref,
        dft_ref, dft_t_ref, images_ref, rows_ref, cols_ref, arrived,
        z_ref, rows_fold, cols_fold, ctf_left, ctf_right, spec_ref, mix_ref, totals,
    ) = refs
    count, box, _ = images_ref.shape
    half = box // 2
    poses, rows, _ = rows_ref.shape
    cols = cols_ref.shape[2]
    planes = plane_ref.shape[0]

    pairs = (
        (class_hbm, class_ref), (pose_hbm, pose_ref), (bin_hbm, bin_ref),
        (defocus_hbm, defocus_ref), (plane_hbm, plane_ref),
        (rows_hbm, rows_ref), (cols_hbm, cols_ref), (dft_t_hbm, dft_t_ref),
        (images_hbm, images_ref), (dft_hbm, dft_ref),
    )
    copies = [
        pltpu.make_async_copy(source, target, arrived.at[n])
        for n, (source, target) in enumerate(pairs)
    ]
    for copy in copies:
        copy.start()

    place = iota((box, box), 0)
    other = iota((box, box), 1)
    folded = fold_of(place, half)
    near = (folded == other).astype(f32).astype(bf16)
    far = (jnp.where(folded == 0, 0, box - folded) == other).astype(f32).astype(bf16)

    for copy in copies[:5]:
        copy.wait()
    lanes = ctf_left.shape[1]
    tall = ctf_left.shape[0]
    lane = iota((1, lanes), 1)
    sub = iota((count, box), 0)
    lane_defocus = jnp.zeros((1, lanes), f32)
    sub_defocus = jnp.zeros((count, box), f32)
    for i in range(count):
        value = defocus_ref[bin_ref[i]]
        lane_defocus = jnp.where(lane % count == i, value, lane_defocus)
        sub_defocus = jnp.where(sub == i, value, sub_defocus)
    scale = 1.0 / (2 * half * half)
    ky = jnp.minimum(iota((tall, lanes), 0), half).astype(f32)
    group = iota((tall, lanes), 1) // count
    turns = lane_defocus * (ky * ky * scale) + ctf_phase / (2.0 * math.pi)
    wave = turns_sine(turns + (group % 2).astype(f32) * 0.25)
    high, low = split_two(wave)
    ctf_left[...] = jnp.where(
        group < 4, high.astype(f32), jnp.where(group < 6, low.astype(f32), 0.0)
    ).astype(bf16)
    kx = iota((count, box), 1)
    kx = jnp.where(kx <= half, kx, kx - half).astype(f32)
    turns = sub_defocus * (kx * kx * scale)
    cos_high, cos_low = split_two(-turns_sine(turns + 0.25))
    sin_high, sin_low = split_two(-turns_sine(turns))
    zero = jnp.zeros((lanes - 6 * count, box), bf16)
    ctf_right[...] = jnp.concatenate(
        [cos_high, sin_high, cos_low, sin_low, cos_high, sin_high, zero], 0
    )
    totals[...] = jnp.zeros_like(totals)
    if len(outs) > 1:
        bins = defocus_ref.shape[0]
        count_row = iota((16, 2 * cols), 0)
        count_lane = iota((16, 2 * cols), 1)
        counts = jnp.zeros((16, 2 * cols), f32)
        for i in range(count):
            hit = (count_row == class_ref[i]) & (count_lane == pose_ref[i] * bins + bin_ref[i])
            counts = counts + jnp.where(hit, 1.0, 0.0)
        totals[planes * CLASSES] = jnp.tile(counts, (rows // 16, 1))

    copies[5].wait()
    rows_fold[...] = dot(
        rows_ref[...].reshape(poses * rows, box), near, ((1,), (1,))
    ).astype(bf16)
    copies[6].wait()
    for p in range(poses):
        cols_fold[p, :, :cols] = dot(near, cols_ref[p]).astype(bf16)
        cols_fold[p, :, cols:] = dot(far, cols_ref[p]).astype(bf16)
    for copy in copies[7:]:
        copy.wait()
    z_ref[...] = dot(images_ref[...].reshape(count * box, box), dft_t_ref[...]).astype(bf16)

    row_zero = iota((half, half), 0) == 0
    col_zero = iota((half, half), 1) == 0
    edge = row_zero | col_zero
    short_row = iota((16, half), 0) == 0
    short_col = iota((16, half), 1) == 0
    right_row = iota((lanes, box), 0) % count

    def one_image(i, carry):
        pose = pose_ref[i]
        chosen = jnp.where(right_row == i, ctf_right[...].astype(f32), 0.0).astype(bf16)
        contrast = dot(ctf_left[...], chosen)
        y = dot(dft_ref[...], z_ref[pl.ds(pl.multiple_of(i * box, box), box), :])
        cc, cs = y[:half, :half], y[:half, half:]
        sc, ss = y[half:, :half], y[half:, half:]
        ss_in = jnp.where(edge, 0.0, ss)
        sc_in = jnp.where(row_zero, 0.0, sc)
        cs_in = jnp.where(col_zero, 0.0, cs)
        near_ctf, far_ctf = contrast[:half, :half], contrast[:half, half:]
        spec_ref[0:half, 0:half] = (near_ctf * (cc - ss_in)).astype(bf16)
        spec_ref[0:half, half:] = (far_ctf * jnp.where(col_zero, cs, cc + ss_in)).astype(bf16)
        spec_ref[half:box, 0:half] = (-near_ctf * (sc_in + cs_in)).astype(bf16)
        spec_ref[half:box, half:] = (
            far_ctf * jnp.where(col_zero, jnp.where(row_zero, 0.0, -ss), cs_in - sc_in)
        ).astype(bf16)
        sc_top = jnp.broadcast_to(sc[0:1], (16, half))
        ss_top = jnp.broadcast_to(ss[0:1], (16, half))
        ss_top_in = jnp.where(short_col, 0.0, ss_top)
        edge_ctf = contrast[half : half + 1]
        spec_ref[box : box + 16, 0:half] = (
            edge_ctf[:, :half] * jnp.where(short_row, sc_top, -ss_top_in)
        ).astype(bf16)
        spec_ref[box : box + 16, half:] = (
            edge_ctf[:, half:]
            * jnp.where(short_row, jnp.where(short_col, ss_top, sc_top), ss_top_in)
        ).astype(bf16)
        mixed = dot(spec_ref[...], cols_fold[pose])
        top = iota((half, cols), 0) == 0
        mix_ref[0:half, 0:cols] = mixed[:half, :cols].astype(bf16)
        mix_ref[0:half, cols:] = mixed[half:box, :cols].astype(bf16)
        mix_ref[half:, 0:cols] = jnp.where(
            top, mixed[box : box + 1, :cols], mixed[:half, cols:]
        ).astype(bf16)
        mix_ref[half:, cols:] = jnp.where(
            top, mixed[box + 1 : box + 2, :cols], -mixed[half:box, cols:]
        ).astype(bf16)
        pose_rows = rows_fold[pl.ds(pl.multiple_of(pose * rows, rows), rows), :]
        piece = dot(pose_rows, mix_ref[...])
        for z in range(planes):
            slot = z * CLASSES + class_ref[i]
            totals[slot] += plane_ref[z, pose] * piece
        return carry

    lax.fori_loop(0, count, one_image, 0, unroll=True)

    if len(outs) == 1:
        outs[0][...] = totals[...].astype(bf16)
    else:
        turns_round = len(outs) // 2
        members = 2 * turns_round
        owned = rows // members
        me = lax.axis_index("img")
        for k in range(turns_round):
            mine = lax.rem(me + 2 * k, members)
            theirs = mine + 1 - 2 * lax.rem(me, 2)
            first = pl.multiple_of(theirs * owned, owned)
            outs[k][...] = totals[:, pl.ds(first, owned), :].astype(bf16)
            first = pl.multiple_of(mine * owned, owned)
            outs[turns_round + k][...] = totals[:, pl.ds(first, owned), :]


SCRATCH = 19


def own_totals(images, class_index, pose_index, defocus_bin, defocus, rows_table, cols_table, plane_weight, turns_round):
    count, box, _ = images.shape
    poses, rows, _ = rows_table.shape
    cols = cols_table.shape[2]
    planes = plane_weight.shape[1]
    slots = CLASSES * planes
    table = packed_dft(box)
    any_place = pl.BlockSpec(memory_space=pl.ANY)
    vmem = pl.BlockSpec(memory_space=pltpu.VMEM)
    lanes = 128 * (-(-6 * count // 128))
    if turns_round == 0:
        out_shape = [jax.ShapeDtypeStruct((slots, rows, 2 * cols), bf16)]
    else:
        slots += 1
        piece = (slots, rows // (2 * turns_round), 2 * cols)
        out_shape = [jax.ShapeDtypeStruct(piece, bf16)] * turns_round
        out_shape += [jax.ShapeDtypeStruct(piece, f32)] * turns_round
    operands = (
        class_index[:, 0], pose_index, defocus_bin, defocus, plane_weight.T,
        jnp.asarray(table, bf16), jnp.asarray(table.T.copy(), bf16),
        images, rows_table, cols_table,
    )
    return pl.pallas_call(
        slices_kernel,
        out_shape=out_shape,
        in_specs=[any_place] * 10,
        out_specs=[vmem] * len(out_shape),
        scratch_shapes=[pltpu.SMEM(x.shape, x.dtype) for x in operands[:5]]
        + [pltpu.VMEM(x.shape, x.dtype) for x in operands[5:]]
        + [
            pltpu.SemaphoreType.DMA((10,)),
            pltpu.VMEM((count * box, box), bf16),
            pltpu.VMEM((poses * rows, box), bf16),
            pltpu.VMEM((poses, box, 2 * cols), bf16),
            pltpu.VMEM((box // 2 + 16, lanes), bf16),
            pltpu.VMEM((lanes, box), bf16),
            pltpu.VMEM((box + 16, box), bf16),
            pltpu.VMEM((box, 2 * cols), bf16),
            pltpu.VMEM((slots, rows, 2 * cols), f32),
        ],
        compiler_params=pltpu.CompilerParams(vmem_limit_bytes=VMEM_LIMIT),
        cost_estimate=pl.CostEstimate(
            flops=2 * count * box * box * 1000, bytes_accessed=6 * 1024 * 1024, transcendentals=0
        ),
    )(*operands)


VMEM_LIMIT = 56 * 1024 * 1024


def ridge_kernel(defocus_hbm, plane_hbm, rows_hbm, cols_hbm, high_ref, low_ref, share_ref, *refs):
    defocus_ref, plane_ref, rows_ref, cols_ref, arrived = refs
    poses, owned, box = rows_ref.shape
    cols = cols_ref.shape[2]
    bins = defocus_ref.shape[0]
    planes = plane_ref.shape[0]
    half = box // 2
    first = pl.multiple_of(lax.axis_index("img") * owned, owned)
    copies = [
        pltpu.make_async_copy(defocus_hbm, defocus_ref, arrived.at[0]),
        pltpu.make_async_copy(plane_hbm, plane_ref, arrived.at[1]),
        pltpu.make_async_copy(rows_hbm.at[:, pl.ds(first, owned), :], rows_ref, arrived.at[2]),
        pltpu.make_async_copy(cols_hbm, cols_ref, arrived.at[3]),
    ]
    for copy in copies:
        copy.start()
    for copy in copies:
        copy.wait()
    share_plane = iota((planes * CLASSES, poses * bins), 0) // CLASSES
    share_pose = iota((planes * CLASSES, poses * bins), 1) // bins
    share = jnp.zeros((planes * CLASSES, poses * bins), f32)
    for p in range(poses):
        for z in range(planes):
            share = jnp.where((share_plane == z) & (share_pose == p), plane_ref[z, p], share)
    share_ref[...] = share

    bin_row = iota((bins, box), 0)
    sub_defocus = jnp.zeros((bins, box), f32)
    for b in range(bins):
        sub_defocus = jnp.where(bin_row == b, defocus_ref[b], sub_defocus)
    freq = iota((bins, box), 1)
    freq = jnp.where(freq < half, freq, box - freq).astype(f32)
    turns_x = sub_defocus * (freq * freq * (1.0 / (half * half)))
    turns_y = turns_x + ctf_phase / math.pi
    ones = jnp.ones((bins, box), f32)
    wave_y = jnp.concatenate(
        [0.5 * ones, -0.5 * turns_sine(turns_y + 0.25), 0.5 * turns_sine(turns_y)], 0
    )
    wave_x = jnp.concatenate([ones, turns_sine(turns_x + 0.25), turns_sine(turns_x)], 0)
    y_high, y_low = split_two(wave_y)
    x_high, x_low = split_two(wave_x)
    rows_sq = rows_ref[...].reshape(poses * owned, box).astype(f32)
    rows_sq = (rows_sq * rows_sq).astype(bf16)
    u = dot(y_high, rows_sq, ((1,), (1,))) + dot(y_low, rows_sq, ((1,), (1,)))
    for p in range(poses):
        cols_sq = cols_ref[p].astype(f32)
        cols_sq = (cols_sq * cols_sq).astype(bf16)
        v = dot(x_high, cols_sq) + dot(x_low, cols_sq)
        for r in range(owned):
            column = u[:, p * owned + r : p * owned + r + 1]
            product = v * column
            weight = product[:bins] + product[bins : 2 * bins] + product[2 * bins :]
            high, low = split_two(weight)
            high_ref[p * bins : (p + 1) * bins, r * cols : (r + 1) * cols] = high
            low_ref[p * bins : (p + 1) * bins, r * cols : (r + 1) * cols] = low


def own_ridges(defocus, plane_weight, rows_table, cols_table, owned):
    poses, _, box = rows_table.shape
    cols = cols_table.shape[2]
    bins = defocus.shape[0]
    any_place = pl.BlockSpec(memory_space=pl.ANY)
    vmem = pl.BlockSpec(memory_space=pltpu.VMEM)
    planes = plane_weight.T
    table = jax.ShapeDtypeStruct((poses * bins, owned * cols), bf16)
    return pl.pallas_call(
        ridge_kernel,
        out_shape=[table, table, jax.ShapeDtypeStruct((planes.shape[0] * CLASSES, poses * bins), f32)],
        in_specs=[any_place] * 4,
        out_specs=[vmem] * 3,
        scratch_shapes=[
            pltpu.SMEM(defocus.shape, f32),
            pltpu.SMEM(planes.shape, f32),
            pltpu.VMEM((poses, owned, box), bf16),
            pltpu.VMEM(cols_table.shape, bf16),
            pltpu.SemaphoreType.DMA((4,)),
        ],
        compiler_params=pltpu.CompilerParams(vmem_limit_bytes=16 * 1024 * 1024),
        cost_estimate=pl.CostEstimate(
            flops=2 * poses * 1000 * 128 * 256, bytes_accessed=2 * 1024 * 1024, transcendentals=0
        ),
    )(defocus, planes, rows_table, cols_table)


def finish_kernel(high_ref, low_ref, share_ref, *refs):
    parts, out_ref, ridge_ref = refs[:-2], refs[-2], refs[-1]
    slots, pairs = share_ref.shape
    owned, _, cols = ridge_ref.shape
    planes = slots // CLASSES

    def summed(s):
        value = parts[0][s].astype(f32)
        for part in parts[1:]:
            value = value + part[s].astype(f32)
        return value

    counts = summed(slots)[:CLASSES, :pairs]
    scaled = jnp.concatenate([counts] * planes, 0) * share_ref[...]
    c_high, c_low = split_two(scaled)
    weight = (
        dot(c_high, high_ref[...]) + dot(c_low, high_ref[...]) + dot(c_high, low_ref[...])
    )
    ridge = 1.0 / (weight + wiener_ridge)
    for r in range(owned):
        ridge_ref[r] = ridge[:, r * cols : (r + 1) * cols]
    for s in range(slots):
        value = summed(s)
        factor = ridge_ref[:, s, :]
        place = (s % CLASSES) * planes + s // CLASSES
        out_ref[:, 2 * place, :] = value[:, :cols] * factor
        out_ref[:, 2 * place + 1, :] = value[:, cols:] * factor


def finish(tables, parts):
    slots = tables[2].shape[0]
    _, owned, wide = parts[0].shape
    cols = wide // 2
    vmem = pl.BlockSpec(memory_space=pltpu.VMEM)
    return pl.pallas_call(
        finish_kernel,
        out_shape=jax.ShapeDtypeStruct((owned, 2 * slots, cols), f32),
        in_specs=[vmem] * (3 + len(parts)),
        out_specs=vmem,
        scratch_shapes=[pltpu.VMEM((owned, slots, cols), f32)],
        compiler_params=pltpu.CompilerParams(vmem_limit_bytes=16 * 1024 * 1024),
        cost_estimate=pl.CostEstimate(
            flops=8 * slots * owned * cols, bytes_accessed=8 * 1024 * 1024 // 4, transcendentals=0
        ),
    )(*tables, *parts)


def squared_table(weight_table):
    wide_table = weight_table.astype(f32)
    return (wide_table * wide_table).astype(bf16)


def weight_totals(class_index, pose_index, defocus_bin, defocus, rows_table, cols_table, plane_weight, first_row, owned):
    box = rows_table.shape[2]
    poses = rows_table.shape[0]
    bins = defocus.shape[0]
    half = box // 2
    exact = lax.Precision.HIGHEST
    code = (class_index[:, 0] * poses + pose_index) * bins + defocus_bin
    codes = lax.all_gather(code, "img", tiled=True)
    hits = (codes[:, None] == jnp.arange(CLASSES * poses * bins, dtype=jnp.int32)).astype(f32)
    counts = jnp.sum(hits, 0).reshape(CLASSES, poses, bins)
    place = jnp.arange(box, dtype=jnp.int32)
    freq = jnp.where(place < half, place, place - box).astype(f32)
    turns = defocus[:, None] * (freq * freq)[None, :] * (1.0 / (half * half))
    turns_y = turns + ctf_phase / math.pi
    ones = jnp.ones_like(turns)
    wave_y = jnp.stack([0.5 * ones, -0.5 * turns_sine(turns_y + 0.25), 0.5 * turns_sine(turns_y)])
    wave_x = jnp.stack([ones, turns_sine(turns + 0.25), turns_sine(turns)])
    rows_own = lax.dynamic_slice_in_dim(rows_table, first_row, owned, 1)
    u = jnp.einsum("pry,mby->pmbr", squared_table(rows_own).astype(f32), wave_y, precision=exact)
    v = jnp.einsum("pxj,mbx->pmbj", squared_table(cols_table).astype(f32), wave_x, precision=exact)
    weight = counts[:, None] * plane_weight.T[None, :, :, None]
    left = weight[:, :, :, None, :, None] * u[None, None]
    return jnp.einsum("czpmbr,pmbj->rczj", left, v, precision=exact)


def by_rounds(images, class_index, pose_index, defocus_bin, defocus, rows_table, cols_table, plane_weight):
    members = lax.axis_size("img")
    rounds = members // 2
    rows = rows_table.shape[1]
    planes = plane_weight.shape[1]
    cols = cols_table.shape[2]
    owned = rows // members
    outs = own_totals(
        images, class_index, pose_index, defocus_bin, defocus, rows_table, cols_table, plane_weight, rounds
    )
    sends, keeps = outs[:rounds], outs[rounds:]
    order = sorted(range(rounds), key=lambda k: (k == 0, -min(k, rounds - k)))
    parts = [keeps[0]]
    for k in order:
        came = lax.ppermute(sends[k], "img", [(i, i ^ 1) for i in range(members)])
        if k == 0:
            parts.append(came)
        else:
            both = (keeps[k] + came.astype(f32)).astype(bf16)
            parts.append(lax.ppermute(both, "img", [(i, (i + 2 * k) % members) for i in range(members)]))
    tables = own_ridges(defocus, plane_weight, rows_table, cols_table, owned)
    out = finish(tables, parts)
    return out.reshape(owned, CLASSES, planes, 2, cols)


def by_scatter(images, class_index, pose_index, defocus_bin, defocus, rows_table, cols_table, plane_weight):
    rows = rows_table.shape[1]
    cols = cols_table.shape[2]
    planes = plane_weight.shape[1]
    members = lax.axis_size("img")
    owned = rows // members
    (totals,) = own_totals(
        images, class_index, pose_index, defocus_bin, defocus, rows_table, cols_table, plane_weight, 0
    )
    slots = totals.shape[0]
    totals = totals.reshape(slots, members, owned, 2 * cols).transpose(1, 0, 2, 3)
    own = lax.psum_scatter(totals, "img", scatter_dimension=0, tiled=False)
    weight = weight_totals(
        class_index, pose_index, defocus_bin, defocus, rows_table, cols_table, plane_weight,
        lax.axis_index("img") * owned, owned,
    )
    own = own.astype(f32).reshape(planes, CLASSES, owned, 2, cols).transpose(2, 1, 0, 3, 4)
    return own / (weight[:, :, :, None, :] + wiener_ridge)


def body(*arrays):
    rows = arrays[5].shape[1]
    members = lax.axis_size("img")
    images = members * arrays[0].shape[0]
    small = members % 2 == 0 and images <= 256 and rows % (16 * members) == 0
    return (by_rounds if small else by_scatter)(*arrays)


def solution(mesh):
    placed = (
        P(("groups", "img"), None, None),
        P(("groups", "img"), None),
        P(("groups", "img")),
        P(("groups", "img")),
        P(),
        P(),
        P(None, None, "slab"),
        P(),
    )
    return jax.shard_map(
        body,
        mesh=mesh,
        in_specs=placed,
        out_specs=P("img", "groups", None, None, "slab"),
        check_vma=False,
    )
```

```python
import functools
import math

import jax
import jax.numpy as jnp
import numpy as np
from jax import lax
from jax.experimental import pallas as pl
from jax.experimental.pallas import tpu as pltpu
from jax.sharding import PartitionSpec as P

CLASSES = 8

wiener_ridge = 1.0
ctf_phase = 0.1
f32 = jnp.float32
bf16 = jnp.bfloat16


def packed_dft(box, sine_sign):
    half = box // 2
    k = np.concatenate([np.arange(half), [half], np.arange(1, half)])
    angle = (k[:, None] * np.arange(box)[None, :] % box) * (2.0 * math.pi / box)
    table = np.where((np.arange(box) <= half)[:, None], np.cos(angle), sine_sign * np.sin(angle))
    return (table / math.sqrt(box)).astype(np.float32)


def iota(shape, axis):
    return lax.broadcasted_iota(jnp.int32, shape, axis)


def dot(a, b, dims=((1,), (0,))):
    return lax.dot_general(a, b, (dims, ((), ())), preferred_element_type=f32)


def turns_sine(turns):
    return jnp.sin((turns - jnp.round(turns)) * (2.0 * math.pi))


def split_two(value):
    high = value.astype(bf16)
    return high, (value - high.astype(f32)).astype(bf16)


def fold_of(place, half):
    box = 2 * half
    return jnp.where(place <= half, place, box + half - place)


def slices_kernel(
    class_hbm, pose_hbm, bin_hbm, defocus_hbm, plane_hbm,
    dft_hbm, dft_t_hbm, images_hbm, rows_hbm, cols_hbm,
    *refs,
):
    outs, refs = refs[:-SCRATCH], refs[-SCRATCH:]
    (
        class_ref, pose_ref, bin_ref, defocus_ref, plane_ref,
        dft_ref, dft_t_ref, images_ref, rows_ref, cols_ref, arrived,
        rows_fold, cols_fold, wave_y, cos_x, sin_x, spec_ref, mix_ref, totals,
    ) = refs
    count, box, _ = images_ref.shape
    half = box // 2
    poses, rows, _ = rows_ref.shape
    cols = cols_ref.shape[2]
    planes = plane_ref.shape[0]

    pairs = (
        (class_hbm, class_ref), (pose_hbm, pose_ref), (bin_hbm, bin_ref),
        (defocus_hbm, defocus_ref), (plane_hbm, plane_ref),
        (rows_hbm, rows_ref), (cols_hbm, cols_ref), (dft_t_hbm, dft_t_ref),
        (images_hbm, images_ref), (dft_hbm, dft_ref),
    )
    copies = [
        pltpu.make_async_copy(source, target, arrived.at[n])
        for n, (source, target) in enumerate(pairs)
    ]
    for copy in copies:
        copy.start()

    place = iota((box, box), 0)
    other = iota((box, box), 1)
    folded = fold_of(place, half)
    near = (folded == other).astype(f32).astype(bf16)
    far = (jnp.where(folded == 0, 0, box - folded) == other).astype(f32).astype(bf16)

    for copy in copies[:5]:
        copy.wait()
    tall, lanes = wave_y.shape
    lane = iota((1, lanes), 1)
    sub = iota((count, box), 0)
    lane_defocus = jnp.zeros((1, lanes), f32)
    sub_defocus = jnp.zeros((count, box), f32)
    for i in range(count):
        value = defocus_ref[bin_ref[i]]
        lane_defocus = jnp.where(lane % count == i, value, lane_defocus)
        sub_defocus = jnp.where(sub == i, value, sub_defocus)
    scale = 1.0 / (2 * half * half)
    ky = iota((tall, lanes), 0).astype(f32)
    quarter = jnp.where(lane < count, 0.0, 0.25) + ctf_phase / (2.0 * math.pi)
    wave_y[...] = turns_sine(lane_defocus * (ky * ky * scale) + quarter)
    kx = iota((count, box), 1)
    kx = jnp.where(kx <= half, kx, kx - half).astype(f32)
    turns = sub_defocus * (kx * kx * scale)
    cos_x[...] = -turns_sine(turns + 0.25)
    sin_x[...] = -turns_sine(turns)
    totals[...] = jnp.zeros_like(totals)
    if len(outs) > 1:
        bins = defocus_ref.shape[0]
        count_row = iota((16, 2 * cols), 0)
        count_lane = iota((16, 2 * cols), 1)
        counts = jnp.zeros((16, 2 * cols), f32)
        for i in range(count):
            hit = (count_row == class_ref[i]) & (count_lane == pose_ref[i] * bins + bin_ref[i])
            counts = counts + jnp.where(hit, 1.0, 0.0)
        totals[planes * CLASSES] = jnp.tile(counts, (rows // 16, 1))

    copies[5].wait()
    rows_fold[...] = dot(
        rows_ref[...].reshape(poses * rows, box), near, ((1,), (1,))
    ).astype(bf16)
    copies[6].wait()
    for p in range(0, poses, 2):
        two = jnp.concatenate([cols_ref[p], cols_ref[p + 1]], 1)
        near_two = dot(near, two).astype(bf16)
        far_two = dot(far, two).astype(bf16)
        cols_fold[p] = jnp.concatenate([near_two[:, :cols], far_two[:, :cols]], 1)
        cols_fold[p + 1] = jnp.concatenate([near_two[:, cols:], far_two[:, cols:]], 1)
    for copy in copies[7:]:
        copy.wait()

    tile = 8
    tile_row = iota((tile, half), 0) == 0
    tile_col = iota((tile, half), 1) == 0
    col_zero = iota((half, half), 1) == 0
    short_row = iota((16, half), 0) == 0
    short_col = iota((16, half), 1) == 0

    def without_row(value):
        return jnp.concatenate([jnp.where(tile_row, 0.0, value[:tile]), value[tile:]], 0)

    def transform(i):
        z = dot(images_ref[i], dft_t_ref[...]).astype(bf16)
        y = dot(dft_ref[...], z)
        sin_col = jnp.broadcast_to(wave_y[:, i : i + 1], (tall, half))
        cos_col = jnp.broadcast_to(wave_y[:, count + i : count + i + 1], (tall, half))
        near_ctf = sin_col * cos_x[i : i + 1, :half] + cos_col * sin_x[i : i + 1, :half]
        far_ctf = sin_col * cos_x[i : i + 1, half:] + cos_col * sin_x[i : i + 1, half:]
        cc, cs = y[:half, :half], y[:half, half:]
        sc, ss = y[half:, :half], y[half:, half:]
        ss_row = without_row(ss)
        ss_in = jnp.where(col_zero, 0.0, ss_row)
        sc_in = without_row(sc)
        cs_in = jnp.where(col_zero, 0.0, cs)
        near_y, far_y = near_ctf[:half], far_ctf[:half]
        spec = spec_ref.at[i % SLOTS]
        spec[0:half, 0:half] = (near_y * (cc + ss_in)).astype(bf16)
        spec[0:half, half:] = (far_y * jnp.where(col_zero, cs, cc - ss_in)).astype(bf16)
        spec[half:box, 0:half] = (near_y * (sc_in - cs_in)).astype(bf16)
        spec[half:box, half:] = (far_y * jnp.where(col_zero, ss_row, sc_in + cs_in)).astype(bf16)
        sc_top = jnp.broadcast_to(sc[0:1], (16, half))
        ss_top = jnp.broadcast_to(ss[0:1], (16, half))
        ss_top_in = jnp.where(short_col, 0.0, ss_top)
        spec[box : box + 16, 0:half] = (
            near_ctf[half : half + 1] * jnp.where(short_row, sc_top, -ss_top_in)
        ).astype(bf16)
        spec[box : box + 16, half:] = (
            far_ctf[half : half + 1]
            * jnp.where(short_row, jnp.where(short_col, ss_top, sc_top), ss_top_in)
        ).astype(bf16)

    def mix(i):
        mixed = dot(spec_ref[i % SLOTS], cols_fold[pose_ref[i]])
        out = mix_ref.at[i % SLOTS]
        out[0:half, 0:cols] = mixed[:half, :cols].astype(bf16)
        out[0:half, cols:] = mixed[half:box, :cols].astype(bf16)
        top = iota((16, cols), 0) == 0
        real, imag = mixed[:half, cols:], -mixed[half:box, cols:]
        out[half : half + 16, 0:cols] = jnp.where(
            top, mixed[box : box + 1, :cols], real[:16]
        ).astype(bf16)
        out[half : half + 16, cols:] = jnp.where(
            top, mixed[box + 1 : box + 2, :cols], imag[:16]
        ).astype(bf16)
        out[half + 16 :, 0:cols] = real[16:].astype(bf16)
        out[half + 16 :, cols:] = imag[16:].astype(bf16)

    def insert(i):
        pose = pose_ref[i]
        pose_rows = rows_fold[pl.ds(pl.multiple_of(pose * rows, rows), rows), :]
        piece = dot(pose_rows, mix_ref[i % SLOTS])
        for z in range(planes):
            slot = z * CLASSES + class_ref[i]
            totals[slot] += plane_ref[z, pose] * piece

    for step in range(count + 2):
        if step >= 2:
            insert(step - 2)
        if 1 <= step <= count:
            mix(step - 1)
        if step < count:
            transform(step)

    if len(outs) == 1:
        outs[0][...] = totals[...].astype(bf16)
    else:
        turns_round = len(outs) // 2
        members = 2 * turns_round
        owned = rows // members
        me = lax.axis_index("img")
        for k in range(turns_round):
            mine = lax.rem(me + 2 * k, members)
            theirs = mine + 1 - 2 * lax.rem(me, 2)
            first = pl.multiple_of(theirs * owned, owned)
            outs[k][...] = totals[:, pl.ds(first, owned), :].astype(bf16)
            first = pl.multiple_of(mine * owned, owned)
            outs[turns_round + k][...] = totals[:, pl.ds(first, owned), :]


SCRATCH = 19
SLOTS = 3


def own_totals(images, class_index, pose_index, defocus_bin, defocus, rows_table, cols_table, plane_weight, turns_round):
    count, box, _ = images.shape
    poses, rows, _ = rows_table.shape
    cols = cols_table.shape[2]
    planes = plane_weight.shape[1]
    slots = CLASSES * planes
    table_y, table_x = packed_dft(box, -1.0), packed_dft(box, 1.0)
    any_place = pl.BlockSpec(memory_space=pl.ANY)
    vmem = pl.BlockSpec(memory_space=pltpu.VMEM)
    lanes = 128 * (-(-2 * count // 128))
    if turns_round == 0:
        out_shape = [jax.ShapeDtypeStruct((slots, rows, 2 * cols), bf16)]
    else:
        slots += 1
        piece = (slots, rows // (2 * turns_round), 2 * cols)
        out_shape = [jax.ShapeDtypeStruct(piece, bf16)] * turns_round
        out_shape += [jax.ShapeDtypeStruct(piece, f32)] * turns_round
    operands = (
        class_index[:, 0], pose_index, defocus_bin, defocus, plane_weight.T,
        jnp.asarray(table_y, bf16), jnp.asarray(table_x.T.copy(), bf16),
        images, rows_table, cols_table,
    )
    return pl.pallas_call(
        slices_kernel,
        out_shape=out_shape,
        in_specs=[any_place] * 10,
        out_specs=[vmem] * len(out_shape),
        scratch_shapes=[pltpu.SMEM(x.shape, x.dtype) for x in operands[:5]]
        + [pltpu.VMEM(x.shape, x.dtype) for x in operands[5:]]
        + [
            pltpu.SemaphoreType.DMA((10,)),
            pltpu.VMEM((poses * rows, box), bf16),
            pltpu.VMEM((poses, box, 2 * cols), bf16),
            pltpu.VMEM((box // 2 + 8, lanes), f32),
            pltpu.VMEM((count, box), f32),
            pltpu.VMEM((count, box), f32),
            pltpu.VMEM((SLOTS, box + 16, box), bf16),
            pltpu.VMEM((SLOTS, box, 2 * cols), bf16),
            pltpu.VMEM((slots, rows, 2 * cols), f32),
        ],
        compiler_params=pltpu.CompilerParams(vmem_limit_bytes=VMEM_LIMIT),
        cost_estimate=pl.CostEstimate(
            flops=2 * count * box * box * 1000, bytes_accessed=6 * 1024 * 1024, transcendentals=0
        ),
    )(*operands)


VMEM_LIMIT = 56 * 1024 * 1024


def ridge_kernel(defocus_hbm, plane_hbm, rows_hbm, cols_hbm, high_ref, low_ref, share_ref, *refs):
    defocus_ref, plane_ref, rows_ref, cols_ref, arrived = refs
    poses, owned, box = rows_ref.shape
    cols = cols_ref.shape[2]
    bins = defocus_ref.shape[0]
    planes = plane_ref.shape[0]
    half = box // 2
    first = pl.multiple_of(lax.axis_index("img") * owned, owned)
    copies = [
        pltpu.make_async_copy(defocus_hbm, defocus_ref, arrived.at[0]),
        pltpu.make_async_copy(plane_hbm, plane_ref, arrived.at[1]),
        pltpu.make_async_copy(rows_hbm.at[:, pl.ds(first, owned), :], rows_ref, arrived.at[2]),
        pltpu.make_async_copy(cols_hbm, cols_ref, arrived.at[3]),
    ]
    for copy in copies:
        copy.start()
    for copy in copies:
        copy.wait()
    share_plane = iota((planes * CLASSES, poses * bins), 0) // CLASSES
    share_pose = iota((planes * CLASSES, poses * bins), 1) // bins
    share = jnp.zeros((planes * CLASSES, poses * bins), f32)
    for p in range(poses):
        for z in range(planes):
            share = jnp.where((share_plane == z) & (share_pose == p), plane_ref[z, p], share)
    share_ref[...] = share

    bin_row = iota((bins, box), 0)
    sub_defocus = jnp.zeros((bins, box), f32)
    for b in range(bins):
        sub_defocus = jnp.where(bin_row == b, defocus_ref[b], sub_defocus)
    freq = iota((bins, box), 1)
    freq = jnp.where(freq < half, freq, box - freq).astype(f32)
    turns_x = sub_defocus * (freq * freq * (1.0 / (half * half)))
    turns_y = turns_x + ctf_phase / math.pi
    ones = jnp.ones((bins, box), f32)
    wave_y = jnp.concatenate(
        [0.5 * ones, -0.5 * turns_sine(turns_y + 0.25), 0.5 * turns_sine(turns_y)], 0
    )
    wave_x = jnp.concatenate([ones, turns_sine(turns_x + 0.25), turns_sine(turns_x)], 0)
    y_high, y_low = split_two(wave_y)
    x_high, x_low = split_two(wave_x)
    rows_sq = rows_ref[...].reshape(poses * owned, box).astype(f32)
    rows_sq = (rows_sq * rows_sq).astype(bf16)
    u = dot(y_high, rows_sq, ((1,), (1,))) + dot(y_low, rows_sq, ((1,), (1,)))
    for p in range(poses):
        cols_sq = cols_ref[p].astype(f32)
        cols_sq = (cols_sq * cols_sq).astype(bf16)
        v = dot(x_high, cols_sq) + dot(x_low, cols_sq)
        for r in range(owned):
            column = u[:, p * owned + r : p * owned + r + 1]
            product = v * column
            weight = product[:bins] + product[bins : 2 * bins] + product[2 * bins :]
            high, low = split_two(weight)
            high_ref[p * bins : (p + 1) * bins, r * cols : (r + 1) * cols] = high
            low_ref[p * bins : (p + 1) * bins, r * cols : (r + 1) * cols] = low


def own_ridges(defocus, plane_weight, rows_table, cols_table, owned):
    poses, _, box = rows_table.shape
    cols = cols_table.shape[2]
    bins = defocus.shape[0]
    any_place = pl.BlockSpec(memory_space=pl.ANY)
    vmem = pl.BlockSpec(memory_space=pltpu.VMEM)
    planes = plane_weight.T
    table = jax.ShapeDtypeStruct((poses * bins, owned * cols), bf16)
    return pl.pallas_call(
        ridge_kernel,
        out_shape=[table, table, jax.ShapeDtypeStruct((planes.shape[0] * CLASSES, poses * bins), f32)],
        in_specs=[any_place] * 4,
        out_specs=[vmem] * 3,
        scratch_shapes=[
            pltpu.SMEM(defocus.shape, f32),
            pltpu.SMEM(planes.shape, f32),
            pltpu.VMEM((poses, owned, box), bf16),
            pltpu.VMEM(cols_table.shape, bf16),
            pltpu.SemaphoreType.DMA((4,)),
        ],
        compiler_params=pltpu.CompilerParams(vmem_limit_bytes=16 * 1024 * 1024),
        cost_estimate=pl.CostEstimate(
            flops=2 * poses * 1000 * 128 * 256, bytes_accessed=2 * 1024 * 1024, transcendentals=0
        ),
    )(defocus, planes, rows_table, cols_table)


def finish_kernel(high_ref, low_ref, share_ref, *refs):
    parts, out_ref, ridge_ref = refs[:-2], refs[-2], refs[-1]
    slots, pairs = share_ref.shape
    owned, _, cols = ridge_ref.shape
    planes = slots // CLASSES

    def summed(s):
        value = parts[0][s].astype(f32)
        for part in parts[1:]:
            value = value + part[s].astype(f32)
        return value

    counts = summed(slots)[:CLASSES, :pairs]
    scaled = jnp.concatenate([counts] * planes, 0) * share_ref[...]
    c_high, c_low = split_two(scaled)
    weight = (
        dot(c_high, high_ref[...]) + dot(c_low, high_ref[...]) + dot(c_high, low_ref[...])
    )
    ridge = 1.0 / (weight + wiener_ridge)
    for r in range(owned):
        ridge_ref[r] = ridge[:, r * cols : (r + 1) * cols]
    for s in range(slots):
        value = summed(s)
        factor = ridge_ref[:, s, :]
        place = (s % CLASSES) * planes + s // CLASSES
        out_ref[:, 2 * place, :] = value[:, :cols] * factor
        out_ref[:, 2 * place + 1, :] = value[:, cols:] * factor


def finish(tables, parts):
    slots = tables[2].shape[0]
    _, owned, wide = parts[0].shape
    cols = wide // 2
    vmem = pl.BlockSpec(memory_space=pltpu.VMEM)
    return pl.pallas_call(
        finish_kernel,
        out_shape=jax.ShapeDtypeStruct((owned, 2 * slots, cols), f32),
        in_specs=[vmem] * (3 + len(parts)),
        out_specs=vmem,
        scratch_shapes=[pltpu.VMEM((owned, slots, cols), f32)],
        compiler_params=pltpu.CompilerParams(vmem_limit_bytes=16 * 1024 * 1024),
        cost_estimate=pl.CostEstimate(
            flops=8 * slots * owned * cols, bytes_accessed=8 * 1024 * 1024 // 4, transcendentals=0
        ),
    )(*tables, *parts)


def squared_table(weight_table):
    wide_table = weight_table.astype(f32)
    return (wide_table * wide_table).astype(bf16)


def weight_totals(class_index, pose_index, defocus_bin, defocus, rows_table, cols_table, plane_weight, first_row, owned):
    box = rows_table.shape[2]
    poses = rows_table.shape[0]
    bins = defocus.shape[0]
    half = box // 2
    exact = lax.Precision.HIGHEST
    code = (class_index[:, 0] * poses + pose_index) * bins + defocus_bin
    codes = lax.all_gather(code, "img", tiled=True)
    hits = (codes[:, None] == jnp.arange(CLASSES * poses * bins, dtype=jnp.int32)).astype(f32)
    counts = jnp.sum(hits, 0).reshape(CLASSES, poses, bins)
    place = jnp.arange(box, dtype=jnp.int32)
    freq = jnp.where(place < half, place, place - box).astype(f32)
    turns = defocus[:, None] * (freq * freq)[None, :] * (1.0 / (half * half))
    turns_y = turns + ctf_phase / math.pi
    ones = jnp.ones_like(turns)
    wave_y = jnp.stack([0.5 * ones, -0.5 * turns_sine(turns_y + 0.25), 0.5 * turns_sine(turns_y)])
    wave_x = jnp.stack([ones, turns_sine(turns + 0.25), turns_sine(turns)])
    rows_own = lax.dynamic_slice_in_dim(rows_table, first_row, owned, 1)
    u = jnp.einsum("pry,mby->pmbr", squared_table(rows_own).astype(f32), wave_y, precision=exact)
    v = jnp.einsum("pxj,mbx->pmbj", squared_table(cols_table).astype(f32), wave_x, precision=exact)
    weight = counts[:, None] * plane_weight.T[None, :, :, None]
    left = weight[:, :, :, None, :, None] * u[None, None]
    return jnp.einsum("czpmbr,pmbj->rczj", left, v, precision=exact)


def by_rounds(images, class_index, pose_index, defocus_bin, defocus, rows_table, cols_table, plane_weight):
    members = lax.axis_size("img")
    rounds = members // 2
    rows = rows_table.shape[1]
    planes = plane_weight.shape[1]
    cols = cols_table.shape[2]
    owned = rows // members
    outs = own_totals(
        images, class_index, pose_index, defocus_bin, defocus, rows_table, cols_table, plane_weight, rounds
    )
    sends, keeps = outs[:rounds], outs[rounds:]
    order = sorted(range(rounds), key=lambda k: (k == 0, -min(k, rounds - k)))
    parts = [keeps[0]]
    for k in order:
        came = lax.ppermute(sends[k], "img", [(i, i ^ 1) for i in range(members)])
        if k == 0:
            parts.append(came)
        else:
            both = (keeps[k] + came.astype(f32)).astype(bf16)
            parts.append(lax.ppermute(both, "img", [(i, (i + 2 * k) % members) for i in range(members)]))
    tables = own_ridges(defocus, plane_weight, rows_table, cols_table, owned)
    out = finish(tables, parts)
    return out.reshape(owned, CLASSES, planes, 2, cols)


def by_scatter(images, class_index, pose_index, defocus_bin, defocus, rows_table, cols_table, plane_weight):
    rows = rows_table.shape[1]
    cols = cols_table.shape[2]
    planes = plane_weight.shape[1]
    members = lax.axis_size("img")
    owned = rows // members
    (totals,) = own_totals(
        images, class_index, pose_index, defocus_bin, defocus, rows_table, cols_table, plane_weight, 0
    )
    slots = totals.shape[0]
    totals = totals.reshape(slots, members, owned, 2 * cols).transpose(1, 0, 2, 3)
    own = lax.psum_scatter(totals, "img", scatter_dimension=0, tiled=False)
    weight = weight_totals(
        class_index, pose_index, defocus_bin, defocus, rows_table, cols_table, plane_weight,
        lax.axis_index("img") * owned, owned,
    )
    own = own.astype(f32).reshape(planes, CLASSES, owned, 2, cols).transpose(2, 1, 0, 3, 4)
    return own / (weight[:, :, :, None, :] + wiener_ridge)


def body(*arrays):
    rows = arrays[5].shape[1]
    members = lax.axis_size("img")
    images = members * arrays[0].shape[0]
    small = members % 2 == 0 and images <= 256 and rows % (16 * members) == 0
    return (by_rounds if small else by_scatter)(*arrays)


def solution(mesh):
    placed = (
        P(("groups", "img"), None, None),
        P(("groups", "img"), None),
        P(("groups", "img")),
        P(("groups", "img")),
        P(),
        P(),
        P(None, None, "slab"),
        P(),
    )
    return jax.shard_map(
        body,
        mesh=mesh,
        in_specs=placed,
        out_specs=P("img", "groups", None, None, "slab"),
        check_vma=False,
    )
```

```python
import functools
import math

import jax
import jax.numpy as jnp
import numpy as np
from jax import lax
from jax.experimental import pallas as pl
from jax.experimental.pallas import tpu as pltpu
from jax.sharding import PartitionSpec as P

CLASSES = 8

wiener_ridge = 1.0
ctf_phase = 0.1
f32 = jnp.float32
bf16 = jnp.bfloat16


def packed_dft(box, sine_sign):
    half = box // 2
    k = np.concatenate([np.arange(half), [half], np.arange(1, half)])
    angle = (k[:, None] * np.arange(box)[None, :] % box) * (2.0 * math.pi / box)
    table = np.where((np.arange(box) <= half)[:, None], np.cos(angle), sine_sign * np.sin(angle))
    return (table / math.sqrt(box)).astype(np.float32)


def iota(shape, axis):
    return lax.broadcasted_iota(jnp.int32, shape, axis)


def dot(a, b, dims=((1,), (0,))):
    return lax.dot_general(a, b, (dims, ((), ())), preferred_element_type=f32)


def turns_sine(turns):
    return jnp.sin((turns - jnp.round(turns)) * (2.0 * math.pi))


def split_two(value):
    high = value.astype(bf16)
    return high, (value - high.astype(f32)).astype(bf16)


def fold_of(place, half):
    box = 2 * half
    return jnp.where(place <= half, place, box + half - place)


def slices_kernel(
    class_hbm, pose_hbm, bin_hbm, defocus_hbm, plane_hbm,
    dft_hbm, dft_t_hbm, images_hbm, rows_hbm, cols_hbm,
    *refs,
):
    outs, refs = refs[:-SCRATCH], refs[-SCRATCH:]
    (
        class_ref, pose_ref, bin_ref, defocus_ref, plane_ref,
        dft_ref, dft_t_ref, images_ref, rows_ref, cols_ref, arrived,
        rows_fold, cols_fold, wave_y, cos_x, sin_x, spec_ref, mix_ref, totals,
    ) = refs
    count, box, _ = images_ref.shape
    half = box // 2
    poses, rows, _ = rows_ref.shape
    cols = cols_ref.shape[2]
    planes = plane_ref.shape[0]

    pairs = (
        (class_hbm, class_ref), (pose_hbm, pose_ref), (bin_hbm, bin_ref),
        (defocus_hbm, defocus_ref), (plane_hbm, plane_ref),
        (rows_hbm, rows_ref), (cols_hbm, cols_ref), (dft_t_hbm, dft_t_ref),
        (images_hbm, images_ref), (dft_hbm, dft_ref),
    )
    copies = [
        pltpu.make_async_copy(source, target, arrived.at[n])
        for n, (source, target) in enumerate(pairs)
    ]
    for copy in copies:
        copy.start()

    place = iota((box, box), 0)
    other = iota((box, box), 1)
    folded = fold_of(place, half)
    near = (folded == other).astype(f32).astype(bf16)
    far = (jnp.where(folded == 0, 0, box - folded) == other).astype(f32).astype(bf16)

    for copy in copies[:5]:
        copy.wait()
    tall, lanes = wave_y.shape
    lane = iota((1, lanes), 1)
    sub = iota((count, box), 0)
    lane_defocus = jnp.zeros((1, lanes), f32)
    sub_defocus = jnp.zeros((count, box), f32)
    for i in range(count):
        value = defocus_ref[bin_ref[i]]
        lane_defocus = jnp.where(lane % count == i, value, lane_defocus)
        sub_defocus = jnp.where(sub == i, value, sub_defocus)
    scale = 1.0 / (2 * half * half)
    ky = iota((tall, lanes), 0).astype(f32)
    quarter = jnp.where(lane < count, 0.0, 0.25) + ctf_phase / (2.0 * math.pi)
    wave_y[...] = turns_sine(lane_defocus * (ky * ky * scale) + quarter)
    kx = iota((count, box), 1)
    kx = jnp.where(kx <= half, kx, kx - half).astype(f32)
    turns = sub_defocus * (kx * kx * scale)
    cos_x[...] = -turns_sine(turns + 0.25)
    sin_x[...] = -turns_sine(turns)
    totals[...] = jnp.zeros_like(totals)
    if len(outs) > 1:
        bins = defocus_ref.shape[0]
        count_row = iota((16, 2 * cols), 0)
        count_lane = iota((16, 2 * cols), 1)
        counts = jnp.zeros((16, 2 * cols), f32)
        for i in range(count):
            hit = (count_row == class_ref[i]) & (count_lane == pose_ref[i] * bins + bin_ref[i])
            counts = counts + jnp.where(hit, 1.0, 0.0)
        totals[planes * CLASSES] = jnp.tile(counts, (rows // 16, 1))

    copies[5].wait()
    rows_fold[...] = dot(
        rows_ref[...].reshape(poses * rows, box), near, ((1,), (1,))
    ).astype(bf16)
    copies[6].wait()
    for p in range(0, poses, 2):
        two = jnp.concatenate([cols_ref[p], cols_ref[p + 1]], 1)
        near_two = dot(near, two).astype(bf16)
        far_two = dot(far, two).astype(bf16)
        cols_fold[p] = jnp.concatenate([near_two[:, :cols], far_two[:, :cols]], 1)
        cols_fold[p + 1] = jnp.concatenate([near_two[:, cols:], far_two[:, cols:]], 1)
    for copy in copies[7:]:
        copy.wait()

    tile = 8
    tile_row = iota((tile, half), 0) == 0
    tile_col = iota((tile, half), 1) == 0
    col_zero = iota((half, half), 1) == 0
    short_row = iota((16, half), 0) == 0
    short_col = iota((16, half), 1) == 0

    def without_row(value):
        return jnp.concatenate([jnp.where(tile_row, 0.0, value[:tile]), value[tile:]], 0)

    def transform(i):
        z = dot(images_ref[i], dft_t_ref[...]).astype(bf16)
        y = dot(dft_ref[...], z)
        sin_col = jnp.broadcast_to(wave_y[:, i : i + 1], (tall, half))
        cos_col = jnp.broadcast_to(wave_y[:, count + i : count + i + 1], (tall, half))
        near_ctf = sin_col * cos_x[i : i + 1, :half] + cos_col * sin_x[i : i + 1, :half]
        far_ctf = sin_col * cos_x[i : i + 1, half:] + cos_col * sin_x[i : i + 1, half:]
        cc, cs = y[:half, :half], y[:half, half:]
        sc, ss = y[half:, :half], y[half:, half:]
        ss_row = without_row(ss)
        ss_in = jnp.where(col_zero, 0.0, ss_row)
        sc_in = without_row(sc)
        cs_in = jnp.where(col_zero, 0.0, cs)
        near_y, far_y = near_ctf[:half], far_ctf[:half]
        spec = spec_ref.at[i % SLOTS]
        spec[0:half, 0:half] = (near_y * (cc + ss_in)).astype(bf16)
        spec[0:half, half:] = (far_y * jnp.where(col_zero, cs, cc - ss_in)).astype(bf16)
        spec[half:box, 0:half] = (near_y * (sc_in - cs_in)).astype(bf16)
        spec[half:box, half:] = (far_y * jnp.where(col_zero, ss_row, sc_in + cs_in)).astype(bf16)
        sc_top = jnp.broadcast_to(sc[0:1], (16, half))
        ss_top = jnp.broadcast_to(ss[0:1], (16, half))
        ss_top_in = jnp.where(short_col, 0.0, ss_top)
        spec[box : box + 16, 0:half] = (
            near_ctf[half : half + 1] * jnp.where(short_row, sc_top, -ss_top_in)
        ).astype(bf16)
        spec[box : box + 16, half:] = (
            far_ctf[half : half + 1]
            * jnp.where(short_row, jnp.where(short_col, ss_top, sc_top), ss_top_in)
        ).astype(bf16)

    def mix(i):
        mixed = dot(spec_ref[i % SLOTS], cols_fold[pose_ref[i]])
        out = mix_ref.at[i % SLOTS]
        out[0:half, 0:cols] = mixed[:half, :cols].astype(bf16)
        out[0:half, cols:] = mixed[half:box, :cols].astype(bf16)
        top = iota((16, cols), 0) == 0
        real, imag = mixed[:half, cols:], -mixed[half:box, cols:]
        out[half : half + 16, 0:cols] = jnp.where(
            top, mixed[box : box + 1, :cols], real[:16]
        ).astype(bf16)
        out[half : half + 16, cols:] = jnp.where(
            top, mixed[box + 1 : box + 2, :cols], imag[:16]
        ).astype(bf16)
        out[half + 16 :, 0:cols] = real[16:].astype(bf16)
        out[half + 16 :, cols:] = imag[16:].astype(bf16)

    def insert(i):
        pose = pose_ref[i]
        pose_rows = rows_fold[pl.ds(pl.multiple_of(pose * rows, rows), rows), :]
        piece = dot(pose_rows, mix_ref[i % SLOTS])
        for z in range(planes):
            slot = z * CLASSES + class_ref[i]
            totals[slot] += plane_ref[z, pose] * piece

    for step in range(count + 2):
        if step >= 2:
            insert(step - 2)
        if 1 <= step <= count:
            mix(step - 1)
        if step < count:
            transform(step)

    if len(outs) == 1:
        outs[0][...] = totals[...].astype(bf16)
        return
    x_send, x_keep, z_keep = outs[:3]
    z_sends = outs[3:]
    rounds, x_slots, owned, _ = x_keep.shape
    me = lax.axis_index("img")
    side = lax.rem(me, 2)
    for k in range(rounds):
        base = lax.rem(me - side + 2 * k, 2 * rounds)
        mine = pl.ds(pl.multiple_of((base + side) * owned, owned), owned)
        theirs = pl.ds(pl.multiple_of((base + 1 - side) * owned, owned), owned)
        x_keep[k] = totals[-x_slots:, mine, :]
        x_send[k] = totals[-x_slots:, theirs, :].astype(bf16)
        if k == 0:
            z_keep[0] = totals[:-x_slots, mine, :]
            z_keep[1] = totals[:-x_slots, theirs, :]
        else:
            z_sends[k - 1][0] = totals[:-x_slots, mine, :].astype(bf16)
            z_sends[k - 1][1] = totals[:-x_slots, theirs, :].astype(bf16)


SCRATCH = 19
SLOTS = 3
Z_SLOTS = 5


def own_totals(images, class_index, pose_index, defocus_bin, defocus, rows_table, cols_table, plane_weight, turns_round):
    count, box, _ = images.shape
    poses, rows, _ = rows_table.shape
    cols = cols_table.shape[2]
    planes = plane_weight.shape[1]
    slots = CLASSES * planes
    table_y, table_x = packed_dft(box, -1.0), packed_dft(box, 1.0)
    any_place = pl.BlockSpec(memory_space=pl.ANY)
    vmem = pl.BlockSpec(memory_space=pltpu.VMEM)
    lanes = 128 * (-(-2 * count // 128))
    if turns_round == 0:
        out_shape = [jax.ShapeDtypeStruct((slots, rows, 2 * cols), bf16)]
    else:
        slots += 1
        x_piece = (turns_round, slots - Z_SLOTS, rows // (2 * turns_round), 2 * cols)
        z_piece = (2, Z_SLOTS, rows // (2 * turns_round), 2 * cols)
        out_shape = [pltpu.VMEM(x_piece, bf16), pltpu.VMEM(x_piece, f32), pltpu.VMEM(z_piece, f32)]
        out_shape += [pltpu.VMEM(z_piece, bf16)] * (turns_round - 1)
    operands = (
        class_index[:, 0], pose_index, defocus_bin, defocus, plane_weight.T,
        jnp.asarray(table_y, bf16), jnp.asarray(table_x.T.copy(), bf16),
        images, rows_table, cols_table,
    )
    return pl.pallas_call(
        slices_kernel,
        out_shape=out_shape,
        in_specs=[any_place] * 10,
        out_specs=[vmem] * len(out_shape),
        scratch_shapes=[pltpu.SMEM(x.shape, x.dtype) for x in operands[:5]]
        + [pltpu.VMEM(x.shape, x.dtype) for x in operands[5:]]
        + [
            pltpu.SemaphoreType.DMA((10,)),
            pltpu.VMEM((poses * rows, box), bf16),
            pltpu.VMEM((poses, box, 2 * cols), bf16),
            pltpu.VMEM((box // 2 + 8, lanes), f32),
            pltpu.VMEM((count, box), f32),
            pltpu.VMEM((count, box), f32),
            pltpu.VMEM((SLOTS, box + 16, box), bf16),
            pltpu.VMEM((SLOTS, box, 2 * cols), bf16),
            pltpu.VMEM((slots, rows, 2 * cols), f32),
        ],
        compiler_params=pltpu.CompilerParams(vmem_limit_bytes=VMEM_LIMIT),
        cost_estimate=pl.CostEstimate(
            flops=2 * count * box * box * 1000, bytes_accessed=6 * 1024 * 1024, transcendentals=0
        ),
    )(*operands)


VMEM_LIMIT = 56 * 1024 * 1024


def ridge_kernel(defocus_hbm, plane_hbm, rows_hbm, cols_hbm, high_ref, low_ref, share_ref, *refs):
    defocus_ref, plane_ref, rows_ref, cols_ref, arrived = refs
    poses, owned, box = rows_ref.shape
    cols = cols_ref.shape[2]
    bins = defocus_ref.shape[0]
    planes = plane_ref.shape[0]
    half = box // 2
    first = pl.multiple_of(lax.axis_index("img") * owned, owned)
    copies = [
        pltpu.make_async_copy(defocus_hbm, defocus_ref, arrived.at[0]),
        pltpu.make_async_copy(plane_hbm, plane_ref, arrived.at[1]),
        pltpu.make_async_copy(rows_hbm.at[:, pl.ds(first, owned), :], rows_ref, arrived.at[2]),
        pltpu.make_async_copy(cols_hbm, cols_ref, arrived.at[3]),
    ]
    for copy in copies:
        copy.start()
    for copy in copies:
        copy.wait()
    share_plane = iota((planes * CLASSES, poses * bins), 0) // CLASSES
    share_pose = iota((planes * CLASSES, poses * bins), 1) // bins
    share = jnp.zeros((planes * CLASSES, poses * bins), f32)
    for p in range(poses):
        for z in range(planes):
            share = jnp.where((share_plane == z) & (share_pose == p), plane_ref[z, p], share)
    share_ref[...] = share

    bin_row = iota((bins, box), 0)
    sub_defocus = jnp.zeros((bins, box), f32)
    for b in range(bins):
        sub_defocus = jnp.where(bin_row == b, defocus_ref[b], sub_defocus)
    freq = iota((bins, box), 1)
    freq = jnp.where(freq < half, freq, box - freq).astype(f32)
    turns_x = sub_defocus * (freq * freq * (1.0 / (half * half)))
    turns_y = turns_x + ctf_phase / math.pi
    ones = jnp.ones((bins, box), f32)
    wave_y = jnp.concatenate(
        [0.5 * ones, -0.5 * turns_sine(turns_y + 0.25), 0.5 * turns_sine(turns_y)], 0
    )
    wave_x = jnp.concatenate([ones, turns_sine(turns_x + 0.25), turns_sine(turns_x)], 0)
    y_high, y_low = split_two(wave_y)
    x_high, x_low = split_two(wave_x)
    rows_sq = rows_ref[...].reshape(poses * owned, box).astype(f32)
    rows_sq = (rows_sq * rows_sq).astype(bf16)
    u = dot(y_high, rows_sq, ((1,), (1,))) + dot(y_low, rows_sq, ((1,), (1,)))
    for p in range(poses):
        cols_sq = cols_ref[p].astype(f32)
        cols_sq = (cols_sq * cols_sq).astype(bf16)
        v = dot(x_high, cols_sq) + dot(x_low, cols_sq)
        for r in range(owned):
            column = u[:, p * owned + r : p * owned + r + 1]
            product = v * column
            weight = product[:bins] + product[bins : 2 * bins] + product[2 * bins :]
            high, low = split_two(weight)
            high_ref[p * bins : (p + 1) * bins, r * cols : (r + 1) * cols] = high
            low_ref[p * bins : (p + 1) * bins, r * cols : (r + 1) * cols] = low


def own_ridges(defocus, plane_weight, rows_table, cols_table, owned):
    poses, _, box = rows_table.shape
    cols = cols_table.shape[2]
    bins = defocus.shape[0]
    any_place = pl.BlockSpec(memory_space=pl.ANY)
    vmem = pl.BlockSpec(memory_space=pltpu.VMEM)
    planes = plane_weight.T
    table = jax.ShapeDtypeStruct((poses * bins, owned * cols), bf16)
    return pl.pallas_call(
        ridge_kernel,
        out_shape=[table, table, jax.ShapeDtypeStruct((planes.shape[0] * CLASSES, poses * bins), f32)],
        in_specs=[any_place] * 4,
        out_specs=[vmem] * 3,
        scratch_shapes=[
            pltpu.SMEM(defocus.shape, f32),
            pltpu.SMEM(planes.shape, f32),
            pltpu.VMEM((poses, owned, box), bf16),
            pltpu.VMEM(cols_table.shape, bf16),
            pltpu.SemaphoreType.DMA((4,)),
        ],
        compiler_params=pltpu.CompilerParams(vmem_limit_bytes=16 * 1024 * 1024),
        cost_estimate=pl.CostEstimate(
            flops=2 * poses * 1000 * 128 * 256, bytes_accessed=2 * 1024 * 1024, transcendentals=0
        ),
    )(defocus, planes, rows_table, cols_table)


def middle_kernel(x_keep, z_keep, x_came, *refs):
    rounds = x_keep.shape[0]
    z_came, outs = refs[: rounds - 1], refs[rounds - 1 :]
    x_own, z_own, z_send = outs[:3]
    x_own[...] = x_keep[0] + x_came[0].astype(f32)
    for k in range(1, rounds):
        outs[2 + k][...] = (x_keep[k] + x_came[k].astype(f32)).astype(bf16)
    for side in range(2):
        value = z_keep[side]
        for came in z_came:
            value = value + came[side].astype(f32)
        if side == 0:
            z_own[...] = value
        else:
            z_send[...] = value.astype(bf16)


def middle(x_keep, z_keep, x_came, z_came):
    rounds, x_slots, owned, wide = x_keep.shape
    vmem = pl.BlockSpec(memory_space=pltpu.VMEM)
    x_piece, z_piece = x_keep.shape[1:], z_keep.shape[1:]
    out_shape = [pltpu.VMEM(x_piece, f32), pltpu.VMEM(z_piece, f32), pltpu.VMEM(z_piece, bf16)]
    out_shape += [pltpu.VMEM(x_piece, bf16)] * (rounds - 1)
    return pl.pallas_call(
        middle_kernel,
        out_shape=out_shape,
        in_specs=[vmem] * (3 + len(z_came)),
        out_specs=[vmem] * len(out_shape),
        compiler_params=pltpu.CompilerParams(vmem_limit_bytes=16 * 1024 * 1024),
        cost_estimate=pl.CostEstimate(flops=1000000, bytes_accessed=4 * 1024 * 1024, transcendentals=0),
    )(x_keep, z_keep, x_came, *z_came)


def finish_kernel(high_ref, low_ref, share_ref, x_own, z_own, z_came, *refs):
    x_came, out_ref, ridge_ref = refs[:-2], refs[-2], refs[-1]
    slots, pairs = share_ref.shape
    owned, _, cols = ridge_ref.shape
    planes = slots // CLASSES
    first = z_own.shape[0]

    def summed(s):
        if s < first:
            return z_own[s] + z_came[s].astype(f32)
        value = x_own[s - first]
        for part in x_came:
            value = value + part[s - first].astype(f32)
        return value

    counts = summed(slots)[:CLASSES, :pairs]
    scaled = jnp.concatenate([counts] * planes, 0) * share_ref[...]
    c_high, c_low = split_two(scaled)
    weight = (
        dot(c_high, high_ref[...]) + dot(c_low, high_ref[...]) + dot(c_high, low_ref[...])
    )
    ridge = 1.0 / (weight + wiener_ridge)
    for r in range(owned):
        ridge_ref[r] = ridge[:, r * cols : (r + 1) * cols]
    for s in range(slots):
        value = summed(s)
        factor = ridge_ref[:, s, :]
        place = (s % CLASSES) * planes + s // CLASSES
        out_ref[:, 2 * place, :] = value[:, :cols] * factor
        out_ref[:, 2 * place + 1, :] = value[:, cols:] * factor


def finish(tables, x_own, z_own, z_came, x_came):
    slots = tables[2].shape[0]
    _, owned, wide = x_own.shape
    cols = wide // 2
    vmem = pl.BlockSpec(memory_space=pltpu.VMEM)
    return pl.pallas_call(
        finish_kernel,
        out_shape=jax.ShapeDtypeStruct((owned, 2 * slots, cols), f32),
        in_specs=[vmem] * (6 + len(x_came)),
        out_specs=vmem,
        scratch_shapes=[pltpu.VMEM((owned, slots, cols), f32)],
        compiler_params=pltpu.CompilerParams(vmem_limit_bytes=16 * 1024 * 1024),
        cost_estimate=pl.CostEstimate(
            flops=8 * slots * owned * cols, bytes_accessed=8 * 1024 * 1024 // 4, transcendentals=0
        ),
    )(*tables, x_own, z_own, z_came, *x_came)


def squared_table(weight_table):
    wide_table = weight_table.astype(f32)
    return (wide_table * wide_table).astype(bf16)


def weight_totals(class_index, pose_index, defocus_bin, defocus, rows_table, cols_table, plane_weight, first_row, owned):
    box = rows_table.shape[2]
    poses = rows_table.shape[0]
    bins = defocus.shape[0]
    half = box // 2
    exact = lax.Precision.HIGHEST
    code = (class_index[:, 0] * poses + pose_index) * bins + defocus_bin
    codes = lax.all_gather(code, "img", tiled=True)
    hits = (codes[:, None] == jnp.arange(CLASSES * poses * bins, dtype=jnp.int32)).astype(f32)
    counts = jnp.sum(hits, 0).reshape(CLASSES, poses, bins)
    place = jnp.arange(box, dtype=jnp.int32)
    freq = jnp.where(place < half, place, place - box).astype(f32)
    turns = defocus[:, None] * (freq * freq)[None, :] * (1.0 / (half * half))
    turns_y = turns + ctf_phase / math.pi
    ones = jnp.ones_like(turns)
    wave_y = jnp.stack([0.5 * ones, -0.5 * turns_sine(turns_y + 0.25), 0.5 * turns_sine(turns_y)])
    wave_x = jnp.stack([ones, turns_sine(turns + 0.25), turns_sine(turns)])
    rows_own = lax.dynamic_slice_in_dim(rows_table, first_row, owned, 1)
    u = jnp.einsum("pry,mby->pmbr", squared_table(rows_own).astype(f32), wave_y, precision=exact)
    v = jnp.einsum("pxj,mbx->pmbj", squared_table(cols_table).astype(f32), wave_x, precision=exact)
    weight = counts[:, None] * plane_weight.T[None, :, :, None]
    left = weight[:, :, :, None, :, None] * u[None, None]
    return jnp.einsum("czpmbr,pmbj->rczj", left, v, precision=exact)


def by_rounds(images, class_index, pose_index, defocus_bin, defocus, rows_table, cols_table, plane_weight):
    members = lax.axis_size("img")
    rounds = members // 2
    rows = rows_table.shape[1]
    planes = plane_weight.shape[1]
    cols = cols_table.shape[2]
    owned = rows // members
    outs = own_totals(
        images, class_index, pose_index, defocus_bin, defocus, rows_table, cols_table, plane_weight, rounds
    )
    x_send, x_keep, z_keep = outs[:3]
    z_sends = dict(zip(range(1, rounds), outs[3:]))

    def along_x(value):
        return lax.ppermute(value, "img", [(i, i ^ 1) for i in range(members)])

    def along_z(value, k):
        return lax.ppermute(value, "img", [(i, (i + 2 * k) % members) for i in range(members)])

    order = sorted(range(1, rounds), key=lambda k: -min(k, rounds - k))
    x_came = along_x(x_send)
    z_came = [along_z(z_sends[k], k) for k in order]
    x_own, z_own, z_send, *x_sends = middle(x_keep, z_keep, x_came, z_came)
    x_came = [along_z(x_sends[k - 1], k) for k in order]
    z_came = along_x(z_send)
    tables = own_ridges(defocus, plane_weight, rows_table, cols_table, owned)
    out = finish(tables, x_own, z_own, z_came, x_came)
    return out.reshape(owned, CLASSES, planes, 2, cols)


def by_scatter(images, class_index, pose_index, defocus_bin, defocus, rows_table, cols_table, plane_weight):
    rows = rows_table.shape[1]
    cols = cols_table.shape[2]
    planes = plane_weight.shape[1]
    members = lax.axis_size("img")
    owned = rows // members
    (totals,) = own_totals(
        images, class_index, pose_index, defocus_bin, defocus, rows_table, cols_table, plane_weight, 0
    )
    slots = totals.shape[0]
    totals = totals.reshape(slots, members, owned, 2 * cols).transpose(1, 0, 2, 3)
    own = lax.psum_scatter(totals, "img", scatter_dimension=0, tiled=False)
    weight = weight_totals(
        class_index, pose_index, defocus_bin, defocus, rows_table, cols_table, plane_weight,
        lax.axis_index("img") * owned, owned,
    )
    own = own.astype(f32).reshape(planes, CLASSES, owned, 2, cols).transpose(2, 1, 0, 3, 4)
    return own / (weight[:, :, :, None, :] + wiener_ridge)


def body(*arrays):
    rows = arrays[5].shape[1]
    members = lax.axis_size("img")
    images = members * arrays[0].shape[0]
    small = members % 2 == 0 and images <= 256 and rows % (16 * members) == 0
    return (by_rounds if small else by_scatter)(*arrays)


def solution(mesh):
    placed = (
        P(("groups", "img"), None, None),
        P(("groups", "img"), None),
        P(("groups", "img")),
        P(("groups", "img")),
        P(),
        P(),
        P(None, None, "slab"),
        P(),
    )
    return jax.shard_map(
        body,
        mesh=mesh,
        in_specs=placed,
        out_specs=P("img", "groups", None, None, "slab"),
        check_vma=False,
    )
```

```python
import functools
import math

import jax
import jax.numpy as jnp
import numpy as np
from jax import lax
from jax.experimental import pallas as pl
from jax.experimental.pallas import tpu as pltpu
from jax.sharding import PartitionSpec as P

CLASSES = 8

wiener_ridge = 1.0
ctf_phase = 0.1
f32 = jnp.float32
bf16 = jnp.bfloat16


def packed_dft(box, sine_sign):
    half = box // 2
    k = np.concatenate([np.arange(half), [half], np.arange(1, half)])
    angle = (k[:, None] * np.arange(box)[None, :] % box) * (2.0 * math.pi / box)
    table = np.where((np.arange(box) <= half)[:, None], np.cos(angle), sine_sign * np.sin(angle))
    return (table / math.sqrt(box)).astype(np.float32)


def iota(shape, axis):
    return lax.broadcasted_iota(jnp.int32, shape, axis)


def dot(a, b, dims=((1,), (0,))):
    return lax.dot_general(a, b, (dims, ((), ())), preferred_element_type=f32)


def turns_sine(turns):
    return jnp.sin((turns - jnp.round(turns)) * (2.0 * math.pi))


def split_two(value):
    high = value.astype(bf16)
    return high, (value - high.astype(f32)).astype(bf16)


def fold_of(place, half):
    box = 2 * half
    return jnp.where(place <= half, place, box + half - place)


def slices_kernel(
    class_hbm, pose_hbm, bin_hbm, defocus_hbm, plane_hbm,
    dft_hbm, dft_t_hbm, images_hbm, rows_hbm, cols_hbm,
    *refs,
):
    outs, refs = refs[:-SCRATCH], refs[-SCRATCH:]
    (
        class_ref, pose_ref, bin_ref, defocus_ref, plane_ref,
        dft_ref, dft_t_ref, images_ref, rows_ref, cols_ref, arrived,
        rows_fold, cols_fold, wave_y, cos_x, sin_x, spec_ref, mix_ref, totals,
    ) = refs
    count, box, _ = images_ref.shape
    half = box // 2
    poses, rows, _ = rows_ref.shape
    cols = cols_ref.shape[2]
    planes = plane_ref.shape[0]

    pairs = (
        (class_hbm, class_ref), (pose_hbm, pose_ref), (bin_hbm, bin_ref),
        (defocus_hbm, defocus_ref), (plane_hbm, plane_ref),
        (rows_hbm, rows_ref), (cols_hbm, cols_ref), (dft_t_hbm, dft_t_ref),
        (images_hbm, images_ref), (dft_hbm, dft_ref),
    )
    copies = [
        pltpu.make_async_copy(source, target, arrived.at[n])
        for n, (source, target) in enumerate(pairs)
    ]
    for copy in copies:
        copy.start()

    place = iota((box, box), 0)
    other = iota((box, box), 1)
    folded = fold_of(place, half)
    near = (folded == other).astype(f32).astype(bf16)
    far = (jnp.where(folded == 0, 0, box - folded) == other).astype(f32).astype(bf16)

    for copy in copies[:5]:
        copy.wait()
    tall, lanes = wave_y.shape
    lane = iota((1, lanes), 1)
    sub = iota((count, box), 0)
    lane_defocus = jnp.zeros((1, lanes), f32)
    sub_defocus = jnp.zeros((count, box), f32)
    for i in range(count):
        value = defocus_ref[bin_ref[i]]
        lane_defocus = jnp.where(lane % count == i, value, lane_defocus)
        sub_defocus = jnp.where(sub == i, value, sub_defocus)
    scale = 1.0 / (2 * half * half)
    ky = iota((tall, lanes), 0).astype(f32)
    quarter = jnp.where(lane < count, 0.0, 0.25) + ctf_phase / (2.0 * math.pi)
    wave_y[...] = turns_sine(lane_defocus * (ky * ky * scale) + quarter)
    kx = iota((count, box), 1)
    kx = jnp.where(kx <= half, kx, kx - half).astype(f32)
    turns = sub_defocus * (kx * kx * scale)
    cos_x[...] = -turns_sine(turns + 0.25)
    sin_x[...] = -turns_sine(turns)
    totals[...] = jnp.zeros_like(totals)
    if len(outs) > 1:
        bins = defocus_ref.shape[0]
        count_row = iota((16, 2 * cols), 0)
        count_lane = iota((16, 2 * cols), 1)
        counts = jnp.zeros((16, 2 * cols), f32)
        for i in range(count):
            hit = (count_row == class_ref[i]) & (count_lane == pose_ref[i] * bins + bin_ref[i])
            counts = counts + jnp.where(hit, 1.0, 0.0)
        totals[planes * CLASSES] = jnp.tile(counts, (rows // 16, 1))

    copies[5].wait()
    rows_fold[...] = dot(
        rows_ref[...].reshape(poses * rows, box), near, ((1,), (1,))
    ).astype(bf16)
    copies[6].wait()
    for p in range(0, poses, 2):
        two = jnp.concatenate([cols_ref[p], cols_ref[p + 1]], 1)
        near_two = dot(near, two).astype(bf16)
        far_two = dot(far, two).astype(bf16)
        cols_fold[p] = jnp.concatenate([near_two[:, :cols], far_two[:, :cols]], 1)
        cols_fold[p + 1] = jnp.concatenate([near_two[:, cols:], far_two[:, cols:]], 1)
    for copy in copies[7:]:
        copy.wait()

    tile = 8
    tile_row = iota((tile, half), 0) == 0
    tile_col = iota((tile, half), 1) == 0
    col_zero = iota((half, half), 1) == 0
    short_row = iota((16, half), 0) == 0
    short_col = iota((16, half), 1) == 0

    def without_row(value):
        return jnp.concatenate([jnp.where(tile_row, 0.0, value[:tile]), value[tile:]], 0)

    def transform(i):
        z = dot(images_ref[i], dft_t_ref[...]).astype(bf16)
        y = dot(dft_ref[...], z)
        sin_col = jnp.broadcast_to(wave_y[:, i : i + 1], (tall, half))
        cos_col = jnp.broadcast_to(wave_y[:, count + i : count + i + 1], (tall, half))
        near_ctf = sin_col * cos_x[i : i + 1, :half] + cos_col * sin_x[i : i + 1, :half]
        far_ctf = sin_col * cos_x[i : i + 1, half:] + cos_col * sin_x[i : i + 1, half:]
        cc, cs = y[:half, :half], y[:half, half:]
        sc, ss = y[half:, :half], y[half:, half:]
        ss_row = without_row(ss)
        ss_in = jnp.where(col_zero, 0.0, ss_row)
        sc_in = without_row(sc)
        cs_in = jnp.where(col_zero, 0.0, cs)
        near_y, far_y = near_ctf[:half], far_ctf[:half]
        spec = spec_ref.at[i % SLOTS]
        spec[0:half, 0:half] = (near_y * (cc + ss_in)).astype(bf16)
        spec[0:half, half:] = (far_y * jnp.where(col_zero, cs, cc - ss_in)).astype(bf16)
        spec[half:box, 0:half] = (near_y * (sc_in - cs_in)).astype(bf16)
        spec[half:box, half:] = (far_y * jnp.where(col_zero, ss_row, sc_in + cs_in)).astype(bf16)
        sc_top = jnp.broadcast_to(sc[0:1], (16, half))
        ss_top = jnp.broadcast_to(ss[0:1], (16, half))
        ss_top_in = jnp.where(short_col, 0.0, ss_top)
        spec[box : box + 16, 0:half] = (
            near_ctf[half : half + 1] * jnp.where(short_row, sc_top, -ss_top_in)
        ).astype(bf16)
        spec[box : box + 16, half:] = (
            far_ctf[half : half + 1]
            * jnp.where(short_row, jnp.where(short_col, ss_top, sc_top), ss_top_in)
        ).astype(bf16)

    def mix(i):
        mixed = dot(spec_ref[i % SLOTS], cols_fold[pose_ref[i]])
        out = mix_ref.at[i % SLOTS]
        out[0:half, 0:cols] = mixed[:half, :cols].astype(bf16)
        out[0:half, cols:] = mixed[half:box, :cols].astype(bf16)
        top = iota((16, cols), 0) == 0
        real, imag = mixed[:half, cols:], -mixed[half:box, cols:]
        out[half : half + 16, 0:cols] = jnp.where(
            top, mixed[box : box + 1, :cols], real[:16]
        ).astype(bf16)
        out[half : half + 16, cols:] = jnp.where(
            top, mixed[box + 1 : box + 2, :cols], imag[:16]
        ).astype(bf16)
        out[half + 16 :, 0:cols] = real[16:].astype(bf16)
        out[half + 16 :, cols:] = imag[16:].astype(bf16)

    def insert(i):
        pose = pose_ref[i]
        pose_rows = rows_fold[pl.ds(pl.multiple_of(pose * rows, rows), rows), :]
        piece = dot(pose_rows, mix_ref[i % SLOTS])
        for z in range(planes):
            slot = z * CLASSES + class_ref[i]
            totals[slot] += plane_ref[z, pose] * piece

    for step in range(count + 2):
        if step >= 2:
            insert(step - 2)
        if 1 <= step <= count:
            mix(step - 1)
        if step < count:
            transform(step)

    if len(outs) == 1:
        outs[0][...] = totals[...].astype(bf16)
        return
    x_send, x_keep, z_keep = outs[:3]
    z_sends = outs[3:]
    rounds, x_slots, owned, _ = x_keep.shape
    me = lax.axis_index("img")
    side = lax.rem(me, 2)
    for k in range(rounds):
        base = lax.rem(me - side + 2 * k, 2 * rounds)
        mine = pl.ds(pl.multiple_of((base + side) * owned, owned), owned)
        theirs = pl.ds(pl.multiple_of((base + 1 - side) * owned, owned), owned)
        x_keep[k] = totals[-x_slots:, mine, :]
        x_send[k] = totals[-x_slots:, theirs, :].astype(bf16)
        if k == 0:
            z_keep[0] = totals[:-x_slots, mine, :]
            z_keep[1] = totals[:-x_slots, theirs, :]
        else:
            z_sends[k - 1][0] = totals[:-x_slots, mine, :].astype(bf16)
            z_sends[k - 1][1] = totals[:-x_slots, theirs, :].astype(bf16)


SCRATCH = 19
SLOTS = 3
Z_SLOTS = 5


def own_totals(images, class_index, pose_index, defocus_bin, defocus, rows_table, cols_table, plane_weight, turns_round):
    count, box, _ = images.shape
    poses, rows, _ = rows_table.shape
    cols = cols_table.shape[2]
    planes = plane_weight.shape[1]
    slots = CLASSES * planes
    table_y, table_x = packed_dft(box, -1.0), packed_dft(box, 1.0)
    any_place = pl.BlockSpec(memory_space=pl.ANY)
    vmem = pl.BlockSpec(memory_space=pltpu.VMEM)
    lanes = 128 * (-(-2 * count // 128))
    if turns_round == 0:
        out_shape = [jax.ShapeDtypeStruct((slots, rows, 2 * cols), bf16)]
    else:
        slots += 1
        x_piece = (turns_round, slots - Z_SLOTS, rows // (2 * turns_round), 2 * cols)
        z_piece = (2, Z_SLOTS, rows // (2 * turns_round), 2 * cols)
        out_shape = [pltpu.VMEM(x_piece, bf16), pltpu.VMEM(x_piece, f32), pltpu.VMEM(z_piece, f32)]
        out_shape += [pltpu.VMEM(z_piece, bf16)] * (turns_round - 1)
    operands = (
        class_index[:, 0], pose_index, defocus_bin, defocus, plane_weight.T,
        jnp.asarray(table_y, bf16), jnp.asarray(table_x.T.copy(), bf16),
        images, rows_table, cols_table,
    )
    return pl.pallas_call(
        slices_kernel,
        out_shape=out_shape,
        in_specs=[any_place] * 10,
        out_specs=[vmem] * len(out_shape),
        scratch_shapes=[pltpu.SMEM(x.shape, x.dtype) for x in operands[:5]]
        + [pltpu.VMEM(x.shape, x.dtype) for x in operands[5:]]
        + [
            pltpu.SemaphoreType.DMA((10,)),
            pltpu.VMEM((poses * rows, box), bf16),
            pltpu.VMEM((poses, box, 2 * cols), bf16),
            pltpu.VMEM((box // 2 + 8, lanes), f32),
            pltpu.VMEM((count, box), f32),
            pltpu.VMEM((count, box), f32),
            pltpu.VMEM((SLOTS, box + 16, box), bf16),
            pltpu.VMEM((SLOTS, box, 2 * cols), bf16),
            pltpu.VMEM((slots, rows, 2 * cols), f32),
        ],
        compiler_params=pltpu.CompilerParams(vmem_limit_bytes=VMEM_LIMIT),
        cost_estimate=pl.CostEstimate(
            flops=2 * count * box * box * 1000, bytes_accessed=6 * 1024 * 1024, transcendentals=0
        ),
    )(*operands)


VMEM_LIMIT = 56 * 1024 * 1024


def ridge_kernel(defocus_hbm, plane_hbm, rows_hbm, cols_hbm, high_ref, low_ref, share_ref, *refs):
    defocus_ref, plane_ref, rows_ref, cols_ref, arrived = refs
    poses, owned, box = rows_ref.shape
    cols = cols_ref.shape[2]
    bins = defocus_ref.shape[0]
    planes = plane_ref.shape[0]
    half = box // 2
    first = pl.multiple_of(lax.axis_index("img") * owned, owned)
    copies = [
        pltpu.make_async_copy(defocus_hbm, defocus_ref, arrived.at[0]),
        pltpu.make_async_copy(plane_hbm, plane_ref, arrived.at[1]),
        pltpu.make_async_copy(rows_hbm.at[:, pl.ds(first, owned), :], rows_ref, arrived.at[2]),
        pltpu.make_async_copy(cols_hbm, cols_ref, arrived.at[3]),
    ]
    for copy in copies:
        copy.start()
    for copy in copies:
        copy.wait()
    share_plane = iota((planes * CLASSES, poses * bins), 0) // CLASSES
    share_pose = iota((planes * CLASSES, poses * bins), 1) // bins
    share = jnp.zeros((planes * CLASSES, poses * bins), f32)
    for p in range(poses):
        for z in range(planes):
            share = jnp.where((share_plane == z) & (share_pose == p), plane_ref[z, p], share)
    share_ref[...] = share

    bin_row = iota((bins, box), 0)
    sub_defocus = jnp.zeros((bins, box), f32)
    for b in range(bins):
        sub_defocus = jnp.where(bin_row == b, defocus_ref[b], sub_defocus)
    freq = iota((bins, box), 1)
    freq = jnp.where(freq < half, freq, box - freq).astype(f32)
    turns_x = sub_defocus * (freq * freq * (1.0 / (half * half)))
    turns_y = turns_x + ctf_phase / math.pi
    ones = jnp.ones((bins, box), f32)
    wave_y = jnp.concatenate(
        [0.5 * ones, -0.5 * turns_sine(turns_y + 0.25), 0.5 * turns_sine(turns_y)], 0
    )
    wave_x = jnp.concatenate([ones, turns_sine(turns_x + 0.25), turns_sine(turns_x)], 0)
    y_high, y_low = split_two(wave_y)
    x_high, x_low = split_two(wave_x)
    rows_sq = rows_ref[...].reshape(poses * owned, box).astype(f32)
    rows_sq = (rows_sq * rows_sq).astype(bf16)
    u = dot(y_high, rows_sq, ((1,), (1,))) + dot(y_low, rows_sq, ((1,), (1,)))
    for p in range(poses):
        cols_sq = cols_ref[p].astype(f32)
        cols_sq = (cols_sq * cols_sq).astype(bf16)
        v = dot(x_high, cols_sq) + dot(x_low, cols_sq)
        for r in range(owned):
            column = u[:, p * owned + r : p * owned + r + 1]
            product = v * column
            weight = product[:bins] + product[bins : 2 * bins] + product[2 * bins :]
            high, low = split_two(weight)
            high_ref[p * bins : (p + 1) * bins, r * cols : (r + 1) * cols] = high
            low_ref[p * bins : (p + 1) * bins, r * cols : (r + 1) * cols] = low


def own_ridges(defocus, plane_weight, rows_table, cols_table, owned):
    poses, _, box = rows_table.shape
    cols = cols_table.shape[2]
    bins = defocus.shape[0]
    any_place = pl.BlockSpec(memory_space=pl.ANY)
    vmem = pl.BlockSpec(memory_space=pltpu.VMEM)
    planes = plane_weight.T
    table = jax.ShapeDtypeStruct((poses * bins, owned * cols), bf16)
    return pl.pallas_call(
        ridge_kernel,
        out_shape=[table, table, jax.ShapeDtypeStruct((planes.shape[0] * CLASSES, poses * bins), f32)],
        in_specs=[any_place] * 4,
        out_specs=[vmem] * 3,
        scratch_shapes=[
            pltpu.SMEM(defocus.shape, f32),
            pltpu.SMEM(planes.shape, f32),
            pltpu.VMEM((poses, owned, box), bf16),
            pltpu.VMEM(cols_table.shape, bf16),
            pltpu.SemaphoreType.DMA((4,)),
        ],
        compiler_params=pltpu.CompilerParams(vmem_limit_bytes=16 * 1024 * 1024),
        cost_estimate=pl.CostEstimate(
            flops=2 * poses * 1000 * 128 * 256, bytes_accessed=2 * 1024 * 1024, transcendentals=0
        ),
    )(defocus, planes, rows_table, cols_table)


def middle_kernel(x_keep, z_keep, x_came, *refs):
    rounds = x_keep.shape[0]
    z_came, outs = refs[: rounds - 1], refs[rounds - 1 :]
    x_own, z_own, z_send = outs[:3]
    x_own[...] = x_keep[0] + x_came[0].astype(f32)
    for k in range(1, rounds):
        outs[2 + k][...] = (x_keep[k] + x_came[k].astype(f32)).astype(bf16)
    for side in range(2):
        value = z_keep[side]
        for came in z_came:
            value = value + came[side].astype(f32)
        if side == 0:
            z_own[...] = value
        else:
            z_send[...] = value.astype(bf16)


def middle(x_keep, z_keep, x_came, z_came):
    rounds, x_slots, owned, wide = x_keep.shape
    vmem = pl.BlockSpec(memory_space=pltpu.VMEM)
    x_piece, z_piece = x_keep.shape[1:], z_keep.shape[1:]
    out_shape = [pltpu.VMEM(x_piece, f32), pltpu.VMEM(z_piece, f32), pltpu.VMEM(z_piece, bf16)]
    out_shape += [pltpu.VMEM(x_piece, bf16)] * (rounds - 1)
    return pl.pallas_call(
        middle_kernel,
        out_shape=out_shape,
        in_specs=[vmem] * (3 + len(z_came)),
        out_specs=[vmem] * len(out_shape),
        compiler_params=pltpu.CompilerParams(vmem_limit_bytes=16 * 1024 * 1024),
        cost_estimate=pl.CostEstimate(flops=1000000, bytes_accessed=4 * 1024 * 1024, transcendentals=0),
    )(x_keep, z_keep, x_came, *z_came)


def finish_kernel(high_ref, low_ref, share_ref, x_own, z_own, z_came, *refs):
    x_came, out_ref, ridge_ref = refs[:-2], refs[-2], refs[-1]
    slots, pairs = share_ref.shape
    owned, _, cols = ridge_ref.shape
    planes = slots // CLASSES
    first = z_own.shape[0]

    def summed(s):
        if s < first:
            return z_own[s] + z_came[s].astype(f32)
        value = x_own[s - first]
        for part in x_came:
            value = value + part[s - first].astype(f32)
        return value

    counts = summed(slots)[:CLASSES, :pairs]
    scaled = jnp.concatenate([counts] * planes, 0) * share_ref[...]
    c_high, c_low = split_two(scaled)
    weight = (
        dot(c_high, high_ref[...]) + dot(c_low, high_ref[...]) + dot(c_high, low_ref[...])
    )
    ridge = 1.0 / (weight + wiener_ridge)
    for r in range(owned):
        ridge_ref[r] = ridge[:, r * cols : (r + 1) * cols]
    for s in range(slots):
        value = summed(s)
        factor = ridge_ref[:, s, :]
        place = (s % CLASSES) * planes + s // CLASSES
        out_ref[:, 2 * place, :] = value[:, :cols] * factor
        out_ref[:, 2 * place + 1, :] = value[:, cols:] * factor


def finish(tables, x_own, z_own, z_came, x_came):
    slots = tables[2].shape[0]
    _, owned, wide = x_own.shape
    cols = wide // 2
    vmem = pl.BlockSpec(memory_space=pltpu.VMEM)
    return pl.pallas_call(
        finish_kernel,
        out_shape=jax.ShapeDtypeStruct((owned, 2 * slots, cols), f32),
        in_specs=[vmem] * (6 + len(x_came)),
        out_specs=vmem,
        scratch_shapes=[pltpu.VMEM((owned, slots, cols), f32)],
        compiler_params=pltpu.CompilerParams(vmem_limit_bytes=16 * 1024 * 1024),
        cost_estimate=pl.CostEstimate(
            flops=8 * slots * owned * cols, bytes_accessed=8 * 1024 * 1024 // 4, transcendentals=0
        ),
    )(*tables, x_own, z_own, z_came, *x_came)


def squared_table(weight_table):
    wide_table = weight_table.astype(f32)
    return (wide_table * wide_table).astype(bf16)


def weight_totals(class_index, pose_index, defocus_bin, defocus, rows_table, cols_table, plane_weight, first_row, owned):
    box = rows_table.shape[2]
    poses = rows_table.shape[0]
    bins = defocus.shape[0]
    half = box // 2
    exact = lax.Precision.HIGHEST
    code = (class_index[:, 0] * poses + pose_index) * bins + defocus_bin
    codes = lax.all_gather(code, "img", tiled=True)
    hits = (codes[:, None] == jnp.arange(CLASSES * poses * bins, dtype=jnp.int32)).astype(f32)
    counts = jnp.sum(hits, 0).reshape(CLASSES, poses, bins)
    place = jnp.arange(box, dtype=jnp.int32)
    freq = jnp.where(place < half, place, place - box).astype(f32)
    turns = defocus[:, None] * (freq * freq)[None, :] * (1.0 / (half * half))
    turns_y = turns + ctf_phase / math.pi
    ones = jnp.ones_like(turns)
    wave_y = jnp.stack([0.5 * ones, -0.5 * turns_sine(turns_y + 0.25), 0.5 * turns_sine(turns_y)])
    wave_x = jnp.stack([ones, turns_sine(turns + 0.25), turns_sine(turns)])
    rows_own = lax.dynamic_slice_in_dim(rows_table, first_row, owned, 1)
    u = jnp.einsum("pry,mby->pmbr", squared_table(rows_own).astype(f32), wave_y, precision=exact)
    v = jnp.einsum("pxj,mbx->pmbj", squared_table(cols_table).astype(f32), wave_x, precision=exact)
    weight = counts[:, None] * plane_weight.T[None, :, :, None]
    left = weight[:, :, :, None, :, None] * u[None, None]
    return jnp.einsum("czpmbr,pmbj->rczj", left, v, precision=exact)


def by_rounds(images, class_index, pose_index, defocus_bin, defocus, rows_table, cols_table, plane_weight):
    members = lax.axis_size("img")
    rounds = members // 2
    rows = rows_table.shape[1]
    planes = plane_weight.shape[1]
    cols = cols_table.shape[2]
    owned = rows // members
    outs = own_totals(
        images, class_index, pose_index, defocus_bin, defocus, rows_table, cols_table, plane_weight, rounds
    )
    x_send, x_keep, z_keep = outs[:3]
    z_sends = dict(zip(range(1, rounds), outs[3:]))

    def along_x(value):
        return lax.ppermute(value, "img", [(i, i ^ 1) for i in range(members)])

    def along_z(value, k):
        return lax.ppermute(value, "img", [(i, (i + 2 * k) % members) for i in range(members)])

    order = sorted(range(1, rounds), key=lambda k: -min(k, rounds - k))
    x_came = along_x(x_send)
    z_came = [along_z(z_sends[k], k) for k in order]
    tables = own_ridges(defocus, plane_weight, rows_table, cols_table, owned)
    x_keep, tables = lax.optimization_barrier((x_keep, tables))
    x_own, z_own, z_send, *x_sends = middle(x_keep, z_keep, x_came, z_came)
    x_came = [along_z(x_sends[k - 1], k) for k in order]
    z_came = along_x(z_send)
    out = finish(tables, x_own, z_own, z_came, x_came)
    return out.reshape(owned, CLASSES, planes, 2, cols)


def by_scatter(images, class_index, pose_index, defocus_bin, defocus, rows_table, cols_table, plane_weight):
    rows = rows_table.shape[1]
    cols = cols_table.shape[2]
    planes = plane_weight.shape[1]
    members = lax.axis_size("img")
    owned = rows // members
    (totals,) = own_totals(
        images, class_index, pose_index, defocus_bin, defocus, rows_table, cols_table, plane_weight, 0
    )
    slots = totals.shape[0]
    totals = totals.reshape(slots, members, owned, 2 * cols).transpose(1, 0, 2, 3)
    own = lax.psum_scatter(totals, "img", scatter_dimension=0, tiled=False)
    weight = weight_totals(
        class_index, pose_index, defocus_bin, defocus, rows_table, cols_table, plane_weight,
        lax.axis_index("img") * owned, owned,
    )
    own = own.astype(f32).reshape(planes, CLASSES, owned, 2, cols).transpose(2, 1, 0, 3, 4)
    return own / (weight[:, :, :, None, :] + wiener_ridge)


def body(*arrays):
    rows = arrays[5].shape[1]
    members = lax.axis_size("img")
    images = members * arrays[0].shape[0]
    small = members % 2 == 0 and images <= 256 and rows % (16 * members) == 0
    return (by_rounds if small else by_scatter)(*arrays)


def solution(mesh):
    placed = (
        P(("groups", "img"), None, None),
        P(("groups", "img"), None),
        P(("groups", "img")),
        P(("groups", "img")),
        P(),
        P(),
        P(None, None, "slab"),
        P(),
    )
    return jax.shard_map(
        body,
        mesh=mesh,
        in_specs=placed,
        out_specs=P("img", "groups", None, None, "slab"),
        check_vma=False,
    )
```

```python
import functools
import math

import jax
import jax.numpy as jnp
import numpy as np
from jax import lax
from jax.experimental import pallas as pl
from jax.experimental.pallas import tpu as pltpu
from jax.sharding import PartitionSpec as P

CLASSES = 8

wiener_ridge = 1.0
ctf_phase = 0.1
f32 = jnp.float32
bf16 = jnp.bfloat16


def packed_dft(box, sine_sign):
    half = box // 2
    k = np.concatenate([np.arange(half), [half], np.arange(1, half)])
    angle = (k[:, None] * np.arange(box)[None, :] % box) * (2.0 * math.pi / box)
    table = np.where((np.arange(box) <= half)[:, None], np.cos(angle), sine_sign * np.sin(angle))
    return (table / math.sqrt(box)).astype(np.float32)


def iota(shape, axis):
    return lax.broadcasted_iota(jnp.int32, shape, axis)


def dot(a, b, dims=((1,), (0,))):
    return lax.dot_general(a, b, (dims, ((), ())), preferred_element_type=f32)


def turns_sine(turns):
    return jnp.sin((turns - jnp.round(turns)) * (2.0 * math.pi))


def split_two(value):
    high = value.astype(bf16)
    return high, (value - high.astype(f32)).astype(bf16)


def fold_of(place, half):
    box = 2 * half
    return jnp.where(place <= half, place, box + half - place)


def slices_kernel(
    class_hbm, pose_hbm, bin_hbm, defocus_hbm, plane_hbm,
    dft_hbm, dft_t_hbm, images_hbm, rows_hbm, cols_hbm,
    *refs,
):
    outs, refs = refs[:-SCRATCH], refs[-SCRATCH:]
    (
        class_ref, pose_ref, bin_ref, defocus_ref, plane_ref,
        dft_ref, dft_t_ref, images_ref, rows_ref, cols_ref, arrived,
        rows_fold, cols_fold, wave_y, cos_x, sin_x, spec_ref, mix_ref, totals,
    ) = refs
    count, box, _ = images_ref.shape
    half = box // 2
    poses, rows, _ = rows_ref.shape
    cols = cols_ref.shape[2]
    planes = plane_ref.shape[0]

    pairs = (
        (class_hbm, class_ref), (pose_hbm, pose_ref), (bin_hbm, bin_ref),
        (defocus_hbm, defocus_ref), (plane_hbm, plane_ref),
        (rows_hbm, rows_ref), (cols_hbm, cols_ref), (dft_t_hbm, dft_t_ref),
        (images_hbm, images_ref), (dft_hbm, dft_ref),
    )
    copies = [
        pltpu.make_async_copy(source, target, arrived.at[n])
        for n, (source, target) in enumerate(pairs)
    ]
    for copy in copies:
        copy.start()

    place = iota((box, box), 0)
    other = iota((box, box), 1)
    folded = fold_of(place, half)
    near = (folded == other).astype(f32).astype(bf16)
    far = (jnp.where(folded == 0, 0, box - folded) == other).astype(f32).astype(bf16)

    for copy in copies[:5]:
        copy.wait()
    tall, lanes = wave_y.shape
    lane = iota((1, lanes), 1)
    sub = iota((count, box), 0)
    lane_defocus = jnp.zeros((1, lanes), f32)
    sub_defocus = jnp.zeros((count, box), f32)
    for i in range(count):
        value = defocus_ref[bin_ref[i]]
        lane_defocus = jnp.where(lane % count == i, value, lane_defocus)
        sub_defocus = jnp.where(sub == i, value, sub_defocus)
    scale = 1.0 / (2 * half * half)
    ky = iota((tall, lanes), 0).astype(f32)
    quarter = jnp.where(lane < count, 0.0, 0.25) + ctf_phase / (2.0 * math.pi)
    wave_y[...] = turns_sine(lane_defocus * (ky * ky * scale) + quarter)
    kx = iota((count, box), 1)
    kx = jnp.where(kx <= half, kx, kx - half).astype(f32)
    turns = sub_defocus * (kx * kx * scale)
    cos_x[...] = -turns_sine(turns + 0.25)
    sin_x[...] = -turns_sine(turns)
    totals[...] = jnp.zeros_like(totals)
    if len(outs) > 1:
        bins = defocus_ref.shape[0]
        count_row = iota((16, 2 * cols), 0)
        count_lane = iota((16, 2 * cols), 1)
        counts = jnp.zeros((16, 2 * cols), f32)
        for i in range(count):
            hit = (count_row == class_ref[i]) & (count_lane == pose_ref[i] * bins + bin_ref[i])
            counts = counts + jnp.where(hit, 1.0, 0.0)
        totals[planes * CLASSES] = jnp.tile(counts, (rows // 16, 1))

    copies[5].wait()
    rows_fold[...] = dot(
        rows_ref[...].reshape(poses * rows, box), near, ((1,), (1,))
    ).astype(bf16)
    copies[6].wait()
    for p in range(0, poses, 2):
        two = jnp.concatenate([cols_ref[p], cols_ref[p + 1]], 1)
        near_two = dot(near, two).astype(bf16)
        far_two = dot(far, two).astype(bf16)
        cols_fold[p] = jnp.concatenate([near_two[:, :cols], far_two[:, :cols]], 1)
        cols_fold[p + 1] = jnp.concatenate([near_two[:, cols:], far_two[:, cols:]], 1)
    for copy in copies[7:]:
        copy.wait()

    tile = 8
    tile_row = iota((tile, half), 0) == 0
    tile_col = iota((tile, half), 1) == 0
    col_zero = iota((half, half), 1) == 0
    short_row = iota((16, half), 0) == 0
    short_col = iota((16, half), 1) == 0

    def without_row(value):
        return jnp.concatenate([jnp.where(tile_row, 0.0, value[:tile]), value[tile:]], 0)

    def transform(i):
        z = dot(images_ref[i], dft_t_ref[...]).astype(bf16)
        y = dot(dft_ref[...], z)
        sin_col = jnp.broadcast_to(wave_y[:, i : i + 1], (tall, half))
        cos_col = jnp.broadcast_to(wave_y[:, count + i : count + i + 1], (tall, half))
        near_ctf = sin_col * cos_x[i : i + 1, :half] + cos_col * sin_x[i : i + 1, :half]
        far_ctf = sin_col * cos_x[i : i + 1, half:] + cos_col * sin_x[i : i + 1, half:]
        cc, cs = y[:half, :half], y[:half, half:]
        sc, ss = y[half:, :half], y[half:, half:]
        ss_row = without_row(ss)
        ss_in = jnp.where(col_zero, 0.0, ss_row)
        sc_in = without_row(sc)
        cs_in = jnp.where(col_zero, 0.0, cs)
        near_y, far_y = near_ctf[:half], far_ctf[:half]
        spec = spec_ref.at[i % SLOTS]
        spec[0:half, 0:half] = (near_y * (cc + ss_in)).astype(bf16)
        spec[0:half, half:] = (far_y * jnp.where(col_zero, cs, cc - ss_in)).astype(bf16)
        spec[half:box, 0:half] = (near_y * (sc_in - cs_in)).astype(bf16)
        spec[half:box, half:] = (far_y * jnp.where(col_zero, ss_row, sc_in + cs_in)).astype(bf16)
        sc_top = jnp.broadcast_to(sc[0:1], (16, half))
        ss_top = jnp.broadcast_to(ss[0:1], (16, half))
        ss_top_in = jnp.where(short_col, 0.0, ss_top)
        spec[box : box + 16, 0:half] = (
            near_ctf[half : half + 1] * jnp.where(short_row, sc_top, -ss_top_in)
        ).astype(bf16)
        spec[box : box + 16, half:] = (
            far_ctf[half : half + 1]
            * jnp.where(short_row, jnp.where(short_col, ss_top, sc_top), ss_top_in)
        ).astype(bf16)

    def mix(i):
        mixed = dot(spec_ref[i % SLOTS], cols_fold[pose_ref[i]])
        out = mix_ref.at[i % SLOTS]
        out[0:half, 0:cols] = mixed[:half, :cols].astype(bf16)
        out[0:half, cols:] = mixed[half:box, :cols].astype(bf16)
        top = iota((16, cols), 0) == 0
        real, imag = mixed[:half, cols:], -mixed[half:box, cols:]
        out[half : half + 16, 0:cols] = jnp.where(
            top, mixed[box : box + 1, :cols], real[:16]
        ).astype(bf16)
        out[half : half + 16, cols:] = jnp.where(
            top, mixed[box + 1 : box + 2, :cols], imag[:16]
        ).astype(bf16)
        out[half + 16 :, 0:cols] = real[16:].astype(bf16)
        out[half + 16 :, cols:] = imag[16:].astype(bf16)

    def insert(i):
        pose = pose_ref[i]
        pose_rows = rows_fold[pl.ds(pl.multiple_of(pose * rows, rows), rows), :]
        piece = dot(pose_rows, mix_ref[i % SLOTS])
        for z in range(planes):
            slot = z * CLASSES + class_ref[i]
            totals[slot] += plane_ref[z, pose] * piece

    for step in range(count + 2):
        if step >= 2:
            insert(step - 2)
        if 1 <= step <= count:
            mix(step - 1)
        if step < count:
            transform(step)

    if len(outs) == 1:
        outs[0][...] = totals[...].astype(bf16)
        return
    x_send, x_keep, z_keep, z_send = outs
    rounds, x_slots, owned, _ = x_keep.shape
    me = lax.axis_index("img")
    side = lax.rem(me, 2)
    for k in range(rounds):
        base = lax.rem(me - side + 2 * k, 2 * rounds)
        mine = pl.ds(pl.multiple_of((base + side) * owned, owned), owned)
        theirs = pl.ds(pl.multiple_of((base + 1 - side) * owned, owned), owned)
        x_keep[k] = totals[-x_slots:, mine, :]
        x_send[k] = totals[-x_slots:, theirs, :].astype(bf16)
        layer = lax.div(base, 2)
        if k == 0:
            z_keep[0] = totals[:-x_slots, mine, :]
            z_keep[1] = totals[:-x_slots, theirs, :]
            z_send[layer] = jnp.zeros_like(z_send[0])
        else:
            z_send[layer, 0] = totals[:-x_slots, mine, :].astype(bf16)
            z_send[layer, 1] = totals[:-x_slots, theirs, :].astype(bf16)


SCRATCH = 19
SLOTS = 3
Z_SLOTS = 5


def own_totals(images, class_index, pose_index, defocus_bin, defocus, rows_table, cols_table, plane_weight, turns_round):
    count, box, _ = images.shape
    poses, rows, _ = rows_table.shape
    cols = cols_table.shape[2]
    planes = plane_weight.shape[1]
    slots = CLASSES * planes
    table_y, table_x = packed_dft(box, -1.0), packed_dft(box, 1.0)
    any_place = pl.BlockSpec(memory_space=pl.ANY)
    vmem = pl.BlockSpec(memory_space=pltpu.VMEM)
    lanes = 128 * (-(-2 * count // 128))
    if turns_round == 0:
        out_shape = [jax.ShapeDtypeStruct((slots, rows, 2 * cols), bf16)]
    else:
        slots += 1
        x_piece = (turns_round, slots - Z_SLOTS, rows // (2 * turns_round), 2 * cols)
        z_piece = (2, Z_SLOTS, rows // (2 * turns_round), 2 * cols)
        out_shape = [pltpu.VMEM(x_piece, bf16), pltpu.VMEM(x_piece, f32), pltpu.VMEM(z_piece, f32)]
        out_shape += [pltpu.VMEM((turns_round,) + z_piece, bf16)]
    operands = (
        class_index[:, 0], pose_index, defocus_bin, defocus, plane_weight.T,
        jnp.asarray(table_y, bf16), jnp.asarray(table_x.T.copy(), bf16),
        images, rows_table, cols_table,
    )
    return pl.pallas_call(
        slices_kernel,
        out_shape=out_shape,
        in_specs=[any_place] * 10,
        out_specs=[vmem] * len(out_shape),
        scratch_shapes=[pltpu.SMEM(x.shape, x.dtype) for x in operands[:5]]
        + [pltpu.VMEM(x.shape, x.dtype) for x in operands[5:]]
        + [
            pltpu.SemaphoreType.DMA((10,)),
            pltpu.VMEM((poses * rows, box), bf16),
            pltpu.VMEM((poses, box, 2 * cols), bf16),
            pltpu.VMEM((box // 2 + 8, lanes), f32),
            pltpu.VMEM((count, box), f32),
            pltpu.VMEM((count, box), f32),
            pltpu.VMEM((SLOTS, box + 16, box), bf16),
            pltpu.VMEM((SLOTS, box, 2 * cols), bf16),
            pltpu.VMEM((slots, rows, 2 * cols), f32),
        ],
        compiler_params=pltpu.CompilerParams(vmem_limit_bytes=VMEM_LIMIT),
        cost_estimate=pl.CostEstimate(
            flops=2 * count * box * box * 1000, bytes_accessed=6 * 1024 * 1024, transcendentals=0
        ),
    )(*operands)


VMEM_LIMIT = 56 * 1024 * 1024


def ridge_kernel(defocus_hbm, plane_hbm, rows_hbm, cols_hbm, high_ref, low_ref, share_ref, *refs):
    defocus_ref, plane_ref, rows_ref, cols_ref, arrived = refs
    poses, owned, box = rows_ref.shape
    cols = cols_ref.shape[2]
    bins = defocus_ref.shape[0]
    planes = plane_ref.shape[0]
    half = box // 2
    first = pl.multiple_of(lax.axis_index("img") * owned, owned)
    copies = [
        pltpu.make_async_copy(defocus_hbm, defocus_ref, arrived.at[0]),
        pltpu.make_async_copy(plane_hbm, plane_ref, arrived.at[1]),
        pltpu.make_async_copy(rows_hbm.at[:, pl.ds(first, owned), :], rows_ref, arrived.at[2]),
        pltpu.make_async_copy(cols_hbm, cols_ref, arrived.at[3]),
    ]
    for copy in copies:
        copy.start()
    for copy in copies:
        copy.wait()
    share_plane = iota((planes * CLASSES, poses * bins), 0) // CLASSES
    share_pose = iota((planes * CLASSES, poses * bins), 1) // bins
    share = jnp.zeros((planes * CLASSES, poses * bins), f32)
    for p in range(poses):
        for z in range(planes):
            share = jnp.where((share_plane == z) & (share_pose == p), plane_ref[z, p], share)
    share_ref[...] = share

    bin_row = iota((bins, box), 0)
    sub_defocus = jnp.zeros((bins, box), f32)
    for b in range(bins):
        sub_defocus = jnp.where(bin_row == b, defocus_ref[b], sub_defocus)
    freq = iota((bins, box), 1)
    freq = jnp.where(freq < half, freq, box - freq).astype(f32)
    turns_x = sub_defocus * (freq * freq * (1.0 / (half * half)))
    turns_y = turns_x + ctf_phase / math.pi
    ones = jnp.ones((bins, box), f32)
    wave_y = jnp.concatenate(
        [0.5 * ones, -0.5 * turns_sine(turns_y + 0.25), 0.5 * turns_sine(turns_y)], 0
    )
    wave_x = jnp.concatenate([ones, turns_sine(turns_x + 0.25), turns_sine(turns_x)], 0)
    y_high, y_low = split_two(wave_y)
    x_high, x_low = split_two(wave_x)
    rows_sq = rows_ref[...].reshape(poses * owned, box).astype(f32)
    rows_sq = (rows_sq * rows_sq).astype(bf16)
    u = dot(y_high, rows_sq, ((1,), (1,))) + dot(y_low, rows_sq, ((1,), (1,)))
    for p in range(poses):
        cols_sq = cols_ref[p].astype(f32)
        cols_sq = (cols_sq * cols_sq).astype(bf16)
        v = dot(x_high, cols_sq) + dot(x_low, cols_sq)
        for r in range(owned):
            column = u[:, p * owned + r : p * owned + r + 1]
            product = v * column
            weight = product[:bins] + product[bins : 2 * bins] + product[2 * bins :]
            high, low = split_two(weight)
            high_ref[p * bins : (p + 1) * bins, r * cols : (r + 1) * cols] = high
            low_ref[p * bins : (p + 1) * bins, r * cols : (r + 1) * cols] = low


def own_ridges(defocus, plane_weight, rows_table, cols_table, owned):
    poses, _, box = rows_table.shape
    cols = cols_table.shape[2]
    bins = defocus.shape[0]
    any_place = pl.BlockSpec(memory_space=pl.ANY)
    vmem = pl.BlockSpec(memory_space=pltpu.VMEM)
    planes = plane_weight.T
    table = jax.ShapeDtypeStruct((poses * bins, owned * cols), bf16)
    return pl.pallas_call(
        ridge_kernel,
        out_shape=[table, table, jax.ShapeDtypeStruct((planes.shape[0] * CLASSES, poses * bins), f32)],
        in_specs=[any_place] * 4,
        out_specs=[vmem] * 3,
        scratch_shapes=[
            pltpu.SMEM(defocus.shape, f32),
            pltpu.SMEM(planes.shape, f32),
            pltpu.VMEM((poses, owned, box), bf16),
            pltpu.VMEM(cols_table.shape, bf16),
            pltpu.SemaphoreType.DMA((4,)),
        ],
        compiler_params=pltpu.CompilerParams(vmem_limit_bytes=16 * 1024 * 1024),
        cost_estimate=pl.CostEstimate(
            flops=2 * poses * 1000 * 128 * 256, bytes_accessed=2 * 1024 * 1024, transcendentals=0
        ),
    )(defocus, planes, rows_table, cols_table)


def middle_kernel(x_keep, z_keep, x_came, z_came, x_own, z_own, z_send, x_send):
    rounds = x_keep.shape[0]
    layer = lax.div(lax.axis_index("img"), 2)
    x_own[...] = x_keep[0] + x_came[0].astype(f32)
    x_send[layer] = jnp.zeros_like(x_send[0])
    for k in range(1, rounds):
        x_send[lax.rem(layer + k, rounds)] = (x_keep[k] + x_came[k].astype(f32)).astype(bf16)
    for side in range(2):
        value = z_keep[side]
        for k in range(rounds):
            value = value + z_came[k, side].astype(f32)
        if side == 0:
            z_own[...] = value
        else:
            z_send[...] = value.astype(bf16)


def middle(x_keep, z_keep, x_came, z_came):
    vmem = pl.BlockSpec(memory_space=pltpu.VMEM)
    x_piece, z_piece = x_keep.shape[1:], z_keep.shape[1:]
    out_shape = [pltpu.VMEM(x_piece, f32), pltpu.VMEM(z_piece, f32), pltpu.VMEM(z_piece, bf16)]
    out_shape += [pltpu.VMEM(x_keep.shape, bf16)]
    return pl.pallas_call(
        middle_kernel,
        out_shape=out_shape,
        in_specs=[vmem] * 4,
        out_specs=[vmem] * 4,
        compiler_params=pltpu.CompilerParams(vmem_limit_bytes=16 * 1024 * 1024),
        cost_estimate=pl.CostEstimate(flops=1000000, bytes_accessed=4 * 1024 * 1024, transcendentals=0),
    )(x_keep, z_keep, x_came, z_came)


def finish_kernel(high_ref, low_ref, share_ref, x_own, z_own, z_came, x_came, out_ref, ridge_ref):
    slots, pairs = share_ref.shape
    owned, _, cols = ridge_ref.shape
    planes = slots // CLASSES
    first = z_own.shape[0]

    def summed(s):
        if s < first:
            return z_own[s] + z_came[s].astype(f32)
        value = x_own[s - first]
        for k in range(x_came.shape[0]):
            value = value + x_came[k, s - first].astype(f32)
        return value

    counts = summed(slots)[:CLASSES, :pairs]
    scaled = jnp.concatenate([counts] * planes, 0) * share_ref[...]
    c_high, c_low = split_two(scaled)
    weight = (
        dot(c_high, high_ref[...]) + dot(c_low, high_ref[...]) + dot(c_high, low_ref[...])
    )
    ridge = 1.0 / (weight + wiener_ridge)
    for r in range(owned):
        ridge_ref[r] = ridge[:, r * cols : (r + 1) * cols]
    for s in range(slots):
        value = summed(s)
        factor = ridge_ref[:, s, :]
        place = (s % CLASSES) * planes + s // CLASSES
        out_ref[:, 2 * place, :] = value[:, :cols] * factor
        out_ref[:, 2 * place + 1, :] = value[:, cols:] * factor


def finish(tables, x_own, z_own, z_came, x_came):
    slots = tables[2].shape[0]
    _, owned, wide = x_own.shape
    cols = wide // 2
    vmem = pl.BlockSpec(memory_space=pltpu.VMEM)
    return pl.pallas_call(
        finish_kernel,
        out_shape=jax.ShapeDtypeStruct((owned, 2 * slots, cols), f32),
        in_specs=[vmem] * 7,
        out_specs=vmem,
        scratch_shapes=[pltpu.VMEM((owned, slots, cols), f32)],
        compiler_params=pltpu.CompilerParams(vmem_limit_bytes=16 * 1024 * 1024),
        cost_estimate=pl.CostEstimate(
            flops=8 * slots * owned * cols, bytes_accessed=8 * 1024 * 1024 // 4, transcendentals=0
        ),
    )(*tables, x_own, z_own, z_came, x_came)


def squared_table(weight_table):
    wide_table = weight_table.astype(f32)
    return (wide_table * wide_table).astype(bf16)


def weight_totals(class_index, pose_index, defocus_bin, defocus, rows_table, cols_table, plane_weight, first_row, owned):
    box = rows_table.shape[2]
    poses = rows_table.shape[0]
    bins = defocus.shape[0]
    half = box // 2
    exact = lax.Precision.HIGHEST
    code = (class_index[:, 0] * poses + pose_index) * bins + defocus_bin
    codes = lax.all_gather(code, "img", tiled=True)
    hits = (codes[:, None] == jnp.arange(CLASSES * poses * bins, dtype=jnp.int32)).astype(f32)
    counts = jnp.sum(hits, 0).reshape(CLASSES, poses, bins)
    place = jnp.arange(box, dtype=jnp.int32)
    freq = jnp.where(place < half, place, place - box).astype(f32)
    turns = defocus[:, None] * (freq * freq)[None, :] * (1.0 / (half * half))
    turns_y = turns + ctf_phase / math.pi
    ones = jnp.ones_like(turns)
    wave_y = jnp.stack([0.5 * ones, -0.5 * turns_sine(turns_y + 0.25), 0.5 * turns_sine(turns_y)])
    wave_x = jnp.stack([ones, turns_sine(turns + 0.25), turns_sine(turns)])
    rows_own = lax.dynamic_slice_in_dim(rows_table, first_row, owned, 1)
    u = jnp.einsum("pry,mby->pmbr", squared_table(rows_own).astype(f32), wave_y, precision=exact)
    v = jnp.einsum("pxj,mbx->pmbj", squared_table(cols_table).astype(f32), wave_x, precision=exact)
    weight = counts[:, None] * plane_weight.T[None, :, :, None]
    left = weight[:, :, :, None, :, None] * u[None, None]
    return jnp.einsum("czpmbr,pmbj->rczj", left, v, precision=exact)


def by_rounds(images, class_index, pose_index, defocus_bin, defocus, rows_table, cols_table, plane_weight):
    members = lax.axis_size("img")
    rounds = members // 2
    rows = rows_table.shape[1]
    planes = plane_weight.shape[1]
    cols = cols_table.shape[2]
    owned = rows // members
    outs = own_totals(
        images, class_index, pose_index, defocus_bin, defocus, rows_table, cols_table, plane_weight, rounds
    )
    x_send, x_keep, z_keep, z_send = outs
    lines = [[2 * i + side for i in range(rounds)] for side in range(2)]

    def along_x(value):
        return lax.ppermute(value, "img", [(i, i ^ 1) for i in range(members)])

    def along_z(value):
        return lax.all_to_all(value, "img", 0, 0, axis_index_groups=lines, tiled=True)

    x_came = along_x(x_send)
    z_came = along_z(z_send)
    tables = own_ridges(defocus, plane_weight, rows_table, cols_table, owned)
    x_keep, tables = lax.optimization_barrier((x_keep, tables))
    x_own, z_own, z_send, x_send = middle(x_keep, z_keep, x_came, z_came)
    z_came = along_x(z_send)
    x_came = along_z(x_send)
    out = finish(tables, x_own, z_own, z_came, x_came)
    return out.reshape(owned, CLASSES, planes, 2, cols)


def by_scatter(images, class_index, pose_index, defocus_bin, defocus, rows_table, cols_table, plane_weight):
    rows = rows_table.shape[1]
    cols = cols_table.shape[2]
    planes = plane_weight.shape[1]
    members = lax.axis_size("img")
    owned = rows // members
    (totals,) = own_totals(
        images, class_index, pose_index, defocus_bin, defocus, rows_table, cols_table, plane_weight, 0
    )
    slots = totals.shape[0]
    totals = totals.reshape(slots, members, owned, 2 * cols).transpose(1, 0, 2, 3)
    own = lax.psum_scatter(totals, "img", scatter_dimension=0, tiled=False)
    weight = weight_totals(
        class_index, pose_index, defocus_bin, defocus, rows_table, cols_table, plane_weight,
        lax.axis_index("img") * owned, owned,
    )
    own = own.astype(f32).reshape(planes, CLASSES, owned, 2, cols).transpose(2, 1, 0, 3, 4)
    return own / (weight[:, :, :, None, :] + wiener_ridge)


def body(*arrays):
    rows = arrays[5].shape[1]
    members = lax.axis_size("img")
    images = members * arrays[0].shape[0]
    small = members % 2 == 0 and images <= 256 and rows % (16 * members) == 0
    return (by_rounds if small else by_scatter)(*arrays)


def solution(mesh):
    placed = (
        P(("groups", "img"), None, None),
        P(("groups", "img"), None),
        P(("groups", "img")),
        P(("groups", "img")),
        P(),
        P(),
        P(None, None, "slab"),
        P(),
    )
    return jax.shard_map(
        body,
        mesh=mesh,
        in_specs=placed,
        out_specs=P("img", "groups", None, None, "slab"),
        check_vma=False,
    )
```

```python
import functools
import math

import jax
import jax.numpy as jnp
import numpy as np
from jax import lax
from jax.experimental import pallas as pl
from jax.experimental.pallas import tpu as pltpu
from jax.sharding import PartitionSpec as P

CLASSES = 8

wiener_ridge = 1.0
ctf_phase = 0.1
f32 = jnp.float32
bf16 = jnp.bfloat16


def packed_dft(box, sine_sign):
    half = box // 2
    k = np.concatenate([np.arange(half), [half], np.arange(1, half)])
    angle = (k[:, None] * np.arange(box)[None, :] % box) * (2.0 * math.pi / box)
    table = np.where((np.arange(box) <= half)[:, None], np.cos(angle), sine_sign * np.sin(angle))
    return (table / math.sqrt(box)).astype(np.float32)


def iota(shape, axis):
    return lax.broadcasted_iota(jnp.int32, shape, axis)


def dot(a, b, dims=((1,), (0,))):
    return lax.dot_general(a, b, (dims, ((), ())), preferred_element_type=f32)


def turns_sine(turns):
    return jnp.sin((turns - jnp.round(turns)) * (2.0 * math.pi))


def split_two(value):
    high = value.astype(bf16)
    return high, (value - high.astype(f32)).astype(bf16)


def fold_of(place, half):
    box = 2 * half
    return jnp.where(place <= half, place, box + half - place)


def slices_kernel(
    class_hbm, pose_hbm, bin_hbm, defocus_hbm, plane_hbm,
    dft_hbm, dft_t_hbm, images_hbm, rows_hbm, cols_hbm,
    *refs,
):
    outs, refs = refs[:-SCRATCH], refs[-SCRATCH:]
    (
        class_ref, pose_ref, bin_ref, defocus_ref, plane_ref,
        dft_ref, dft_t_ref, images_ref, rows_ref, cols_ref, arrived,
        rows_fold, cols_fold, wave_y, cos_x, sin_x, spec_ref, mix_ref, totals,
    ) = refs
    count, box, _ = images_ref.shape
    half = box // 2
    poses, rows, _ = rows_ref.shape
    cols = cols_ref.shape[2]
    planes = plane_ref.shape[0]

    pairs = (
        (class_hbm, class_ref), (pose_hbm, pose_ref), (bin_hbm, bin_ref),
        (defocus_hbm, defocus_ref), (plane_hbm, plane_ref),
        (rows_hbm, rows_ref), (cols_hbm, cols_ref), (dft_t_hbm, dft_t_ref),
        (images_hbm, images_ref), (dft_hbm, dft_ref),
    )
    copies = [
        pltpu.make_async_copy(source, target, arrived.at[n])
        for n, (source, target) in enumerate(pairs)
    ]
    for copy in copies:
        copy.start()

    place = iota((box, box), 0)
    other = iota((box, box), 1)
    folded = fold_of(place, half)
    near = (folded == other).astype(f32).astype(bf16)
    far = (jnp.where(folded == 0, 0, box - folded) == other).astype(f32).astype(bf16)

    for copy in copies[:5]:
        copy.wait()
    tall, lanes = wave_y.shape
    lane = iota((1, lanes), 1)
    sub = iota((count, box), 0)
    lane_defocus = jnp.zeros((1, lanes), f32)
    sub_defocus = jnp.zeros((count, box), f32)
    for i in range(count):
        value = defocus_ref[bin_ref[i]]
        lane_defocus = jnp.where(lane % count == i, value, lane_defocus)
        sub_defocus = jnp.where(sub == i, value, sub_defocus)
    scale = 1.0 / (2 * half * half)
    ky = iota((tall, lanes), 0).astype(f32)
    quarter = jnp.where(lane < count, 0.0, 0.25) + ctf_phase / (2.0 * math.pi)
    wave_y[...] = turns_sine(lane_defocus * (ky * ky * scale) + quarter)
    kx = iota((count, box), 1)
    kx = jnp.where(kx <= half, kx, kx - half).astype(f32)
    turns = sub_defocus * (kx * kx * scale)
    cos_x[...] = -turns_sine(turns + 0.25)
    sin_x[...] = -turns_sine(turns)
    totals[...] = jnp.zeros_like(totals)
    if len(outs) > 1:
        bins = defocus_ref.shape[0]
        count_row = iota((16, 2 * cols), 0)
        count_lane = iota((16, 2 * cols), 1)
        counts = jnp.zeros((16, 2 * cols), f32)
        for i in range(count):
            hit = (count_row == class_ref[i]) & (count_lane == pose_ref[i] * bins + bin_ref[i])
            counts = counts + jnp.where(hit, 1.0, 0.0)
        totals[planes * CLASSES] = jnp.tile(counts, (rows // 16, 1))

    copies[5].wait()
    rows_fold[...] = dot(
        rows_ref[...].reshape(poses * rows, box), near, ((1,), (1,))
    ).astype(bf16)
    copies[6].wait()
    for p in range(0, poses, 2):
        two = jnp.concatenate([cols_ref[p], cols_ref[p + 1]], 1)
        near_two = dot(near, two).astype(bf16)
        far_two = dot(far, two).astype(bf16)
        cols_fold[p] = jnp.concatenate([near_two[:, :cols], far_two[:, :cols]], 1)
        cols_fold[p + 1] = jnp.concatenate([near_two[:, cols:], far_two[:, cols:]], 1)
    for copy in copies[7:]:
        copy.wait()

    tile = 8
    tile_row = iota((tile, half), 0) == 0
    tile_col = iota((tile, half), 1) == 0
    col_zero = iota((half, half), 1) == 0
    short_row = iota((16, half), 0) == 0
    short_col = iota((16, half), 1) == 0

    def without_row(value):
        return jnp.concatenate([jnp.where(tile_row, 0.0, value[:tile]), value[tile:]], 0)

    def transform(i):
        z = dot(images_ref[i], dft_t_ref[...]).astype(bf16)
        y = dot(dft_ref[...], z)
        sin_col = jnp.broadcast_to(wave_y[:, i : i + 1], (tall, half))
        cos_col = jnp.broadcast_to(wave_y[:, count + i : count + i + 1], (tall, half))
        near_ctf = sin_col * cos_x[i : i + 1, :half] + cos_col * sin_x[i : i + 1, :half]
        far_ctf = sin_col * cos_x[i : i + 1, half:] + cos_col * sin_x[i : i + 1, half:]
        cc, cs = y[:half, :half], y[:half, half:]
        sc, ss = y[half:, :half], y[half:, half:]
        ss_row = without_row(ss)
        ss_in = jnp.where(col_zero, 0.0, ss_row)
        sc_in = without_row(sc)
        cs_in = jnp.where(col_zero, 0.0, cs)
        near_y, far_y = near_ctf[:half], far_ctf[:half]
        spec = spec_ref.at[i % SLOTS]
        spec[0:half, 0:half] = (near_y * (cc + ss_in)).astype(bf16)
        spec[0:half, half:] = (far_y * jnp.where(col_zero, cs, cc - ss_in)).astype(bf16)
        spec[half:box, 0:half] = (near_y * (sc_in - cs_in)).astype(bf16)
        spec[half:box, half:] = (far_y * jnp.where(col_zero, ss_row, sc_in + cs_in)).astype(bf16)
        sc_top = jnp.broadcast_to(sc[0:1], (16, half))
        ss_top = jnp.broadcast_to(ss[0:1], (16, half))
        ss_top_in = jnp.where(short_col, 0.0, ss_top)
        spec[box : box + 16, 0:half] = (
            near_ctf[half : half + 1] * jnp.where(short_row, sc_top, -ss_top_in)
        ).astype(bf16)
        spec[box : box + 16, half:] = (
            far_ctf[half : half + 1]
            * jnp.where(short_row, jnp.where(short_col, ss_top, sc_top), ss_top_in)
        ).astype(bf16)

    def mix(i):
        mixed = dot(spec_ref[i % SLOTS], cols_fold[pose_ref[i]])
        out = mix_ref.at[i % SLOTS]
        out[0:half, 0:cols] = mixed[:half, :cols].astype(bf16)
        out[0:half, cols:] = mixed[half:box, :cols].astype(bf16)
        top = iota((16, cols), 0) == 0
        real, imag = mixed[:half, cols:], -mixed[half:box, cols:]
        out[half : half + 16, 0:cols] = jnp.where(
            top, mixed[box : box + 1, :cols], real[:16]
        ).astype(bf16)
        out[half : half + 16, cols:] = jnp.where(
            top, mixed[box + 1 : box + 2, :cols], imag[:16]
        ).astype(bf16)
        out[half + 16 :, 0:cols] = real[16:].astype(bf16)
        out[half + 16 :, cols:] = imag[16:].astype(bf16)

    def insert(i):
        pose = pose_ref[i]
        pose_rows = rows_fold[pl.ds(pl.multiple_of(pose * rows, rows), rows), :]
        piece = dot(pose_rows, mix_ref[i % SLOTS])
        for z in range(planes):
            slot = z * CLASSES + class_ref[i]
            totals[slot] += plane_ref[z, pose] * piece

    for step in range(count + 2):
        if step >= 2:
            insert(step - 2)
        if 1 <= step <= count:
            mix(step - 1)
        if step < count:
            transform(step)

    if len(outs) == 1:
        outs[0][...] = totals[...].astype(bf16)
        return
    send, keep = outs
    half_members, _, owned, _ = keep.shape
    steps = half_members.bit_length()
    me = lax.axis_index("img")
    odd = lax.rem(lax.axis_index("slab"), 2) if steps > 1 else 0
    masks = [1 << n for n in range(steps)]
    if steps > 1:
        masks[:2] = [1 + odd, 2 - odd]
    for q in range(half_members):
        other = me
        for n in range(1, steps):
            if (q >> (steps - 1 - n)) & 1:
                other = other ^ masks[n]
        for out, whose in ((keep, other), (send, other ^ masks[0])):
            first = pl.multiple_of(whose * owned, owned)
            out[q] = totals[:, pl.ds(first, owned), :].astype(out.dtype)


SCRATCH = 19
SLOTS = 3


def own_totals(images, class_index, pose_index, defocus_bin, defocus, rows_table, cols_table, plane_weight, members):
    count, box, _ = images.shape
    poses, rows, _ = rows_table.shape
    cols = cols_table.shape[2]
    planes = plane_weight.shape[1]
    slots = CLASSES * planes
    table_y, table_x = packed_dft(box, -1.0), packed_dft(box, 1.0)
    any_place = pl.BlockSpec(memory_space=pl.ANY)
    vmem = pl.BlockSpec(memory_space=pltpu.VMEM)
    lanes = 128 * (-(-2 * count // 128))
    if members == 1:
        out_shape = [jax.ShapeDtypeStruct((slots, rows, 2 * cols), bf16)]
    else:
        slots += 1
        piece = (members // 2, slots, rows // members, 2 * cols)
        out_shape = [pltpu.VMEM(piece, bf16), pltpu.VMEM(piece, f32)]
    operands = (
        class_index[:, 0], pose_index, defocus_bin, defocus, plane_weight.T,
        jnp.asarray(table_y, bf16), jnp.asarray(table_x.T.copy(), bf16),
        images, rows_table, cols_table,
    )
    return pl.pallas_call(
        slices_kernel,
        out_shape=out_shape,
        in_specs=[any_place] * 10,
        out_specs=[vmem] * len(out_shape),
        scratch_shapes=[pltpu.SMEM(x.shape, x.dtype) for x in operands[:5]]
        + [pltpu.VMEM(x.shape, x.dtype) for x in operands[5:]]
        + [
            pltpu.SemaphoreType.DMA((10,)),
            pltpu.VMEM((poses * rows, box), bf16),
            pltpu.VMEM((poses, box, 2 * cols), bf16),
            pltpu.VMEM((box // 2 + 8, lanes), f32),
            pltpu.VMEM((count, box), f32),
            pltpu.VMEM((count, box), f32),
            pltpu.VMEM((SLOTS, box + 16, box), bf16),
            pltpu.VMEM((SLOTS, box, 2 * cols), bf16),
            pltpu.VMEM((slots, rows, 2 * cols), f32),
        ],
        compiler_params=pltpu.CompilerParams(vmem_limit_bytes=VMEM_LIMIT),
        cost_estimate=pl.CostEstimate(
            flops=2 * count * box * box * 1000, bytes_accessed=6 * 1024 * 1024, transcendentals=0
        ),
    )(*operands)


VMEM_LIMIT = 56 * 1024 * 1024


def ridge_kernel(defocus_hbm, plane_hbm, rows_hbm, cols_hbm, high_ref, low_ref, share_ref, *refs):
    defocus_ref, plane_ref, rows_ref, cols_ref, arrived = refs
    poses, owned, box = rows_ref.shape
    cols = cols_ref.shape[2]
    bins = defocus_ref.shape[0]
    planes = plane_ref.shape[0]
    half = box // 2
    first = pl.multiple_of(lax.axis_index("img") * owned, owned)
    copies = [
        pltpu.make_async_copy(defocus_hbm, defocus_ref, arrived.at[0]),
        pltpu.make_async_copy(plane_hbm, plane_ref, arrived.at[1]),
        pltpu.make_async_copy(rows_hbm.at[:, pl.ds(first, owned), :], rows_ref, arrived.at[2]),
        pltpu.make_async_copy(cols_hbm, cols_ref, arrived.at[3]),
    ]
    for copy in copies:
        copy.start()
    for copy in copies:
        copy.wait()
    share_plane = iota((planes * CLASSES, poses * bins), 0) // CLASSES
    share_pose = iota((planes * CLASSES, poses * bins), 1) // bins
    share = jnp.zeros((planes * CLASSES, poses * bins), f32)
    for p in range(poses):
        for z in range(planes):
            share = jnp.where((share_plane == z) & (share_pose == p), plane_ref[z, p], share)
    share_ref[...] = share

    bin_row = iota((bins, box), 0)
    sub_defocus = jnp.zeros((bins, box), f32)
    for b in range(bins):
        sub_defocus = jnp.where(bin_row == b, defocus_ref[b], sub_defocus)
    freq = iota((bins, box), 1)
    freq = jnp.where(freq < half, freq, box - freq).astype(f32)
    turns_x = sub_defocus * (freq * freq * (1.0 / (half * half)))
    turns_y = turns_x + ctf_phase / math.pi
    ones = jnp.ones((bins, box), f32)
    wave_y = jnp.concatenate(
        [0.5 * ones, -0.5 * turns_sine(turns_y + 0.25), 0.5 * turns_sine(turns_y)], 0
    )
    wave_x = jnp.concatenate([ones, turns_sine(turns_x + 0.25), turns_sine(turns_x)], 0)
    y_high, y_low = split_two(wave_y)
    x_high, x_low = split_two(wave_x)
    rows_sq = rows_ref[...].reshape(poses * owned, box).astype(f32)
    rows_sq = (rows_sq * rows_sq).astype(bf16)
    u = dot(y_high, rows_sq, ((1,), (1,))) + dot(y_low, rows_sq, ((1,), (1,)))
    for p in range(poses):
        cols_sq = cols_ref[p].astype(f32)
        cols_sq = (cols_sq * cols_sq).astype(bf16)
        v = dot(x_high, cols_sq) + dot(x_low, cols_sq)
        for r in range(owned):
            column = u[:, p * owned + r : p * owned + r + 1]
            product = v * column
            weight = product[:bins] + product[bins : 2 * bins] + product[2 * bins :]
            high, low = split_two(weight)
            high_ref[p * bins : (p + 1) * bins, r * cols : (r + 1) * cols] = high
            low_ref[p * bins : (p + 1) * bins, r * cols : (r + 1) * cols] = low


def own_ridges(defocus, plane_weight, rows_table, cols_table, owned):
    poses, _, box = rows_table.shape
    cols = cols_table.shape[2]
    bins = defocus.shape[0]
    any_place = pl.BlockSpec(memory_space=pl.ANY)
    vmem = pl.BlockSpec(memory_space=pltpu.VMEM)
    planes = plane_weight.T
    table = jax.ShapeDtypeStruct((poses * bins, owned * cols), bf16)
    return pl.pallas_call(
        ridge_kernel,
        out_shape=[table, table, jax.ShapeDtypeStruct((planes.shape[0] * CLASSES, poses * bins), f32)],
        in_specs=[any_place] * 4,
        out_specs=[vmem] * 3,
        scratch_shapes=[
            pltpu.SMEM(defocus.shape, f32),
            pltpu.SMEM(planes.shape, f32),
            pltpu.VMEM((poses, owned, box), bf16),
            pltpu.VMEM(cols_table.shape, bf16),
            pltpu.SemaphoreType.DMA((4,)),
        ],
        compiler_params=pltpu.CompilerParams(vmem_limit_bytes=16 * 1024 * 1024),
        cost_estimate=pl.CostEstimate(
            flops=2 * poses * 1000 * 128 * 256, bytes_accessed=2 * 1024 * 1024, transcendentals=0
        ),
    )(defocus, planes, rows_table, cols_table)


def middle_kernel(keep, came, send, kept):
    half = send.shape[0]
    kept[...] = keep[:half] + came[:half].astype(f32)
    send[...] = (keep[half:] + came[half:].astype(f32)).astype(bf16)


def middle(keep, came):
    vmem = pl.BlockSpec(memory_space=pltpu.VMEM)
    piece = (keep.shape[0] // 2,) + keep.shape[1:]
    return pl.pallas_call(
        middle_kernel,
        out_shape=[pltpu.VMEM(piece, bf16), pltpu.VMEM(piece, f32)],
        in_specs=[vmem] * 2,
        out_specs=[vmem] * 2,
        compiler_params=pltpu.CompilerParams(vmem_limit_bytes=16 * 1024 * 1024),
        cost_estimate=pl.CostEstimate(flops=1000000, bytes_accessed=4 * 1024 * 1024, transcendentals=0),
    )(keep, came)


def finish_kernel(high_ref, low_ref, share_ref, keep, came, out_ref, ridge_ref):
    slots, pairs = share_ref.shape
    owned, _, cols = ridge_ref.shape
    planes = slots // CLASSES

    def summed(s):
        return keep[0, s] + came[0, s].astype(f32)

    counts = summed(slots)[:CLASSES, :pairs]
    scaled = jnp.concatenate([counts] * planes, 0) * share_ref[...]
    c_high, c_low = split_two(scaled)
    weight = (
        dot(c_high, high_ref[...]) + dot(c_low, high_ref[...]) + dot(c_high, low_ref[...])
    )
    ridge = 1.0 / (weight + wiener_ridge)
    for r in range(owned):
        ridge_ref[r] = ridge[:, r * cols : (r + 1) * cols]
    for s in range(slots):
        value = summed(s)
        factor = ridge_ref[:, s, :]
        place = (s % CLASSES) * planes + s // CLASSES
        out_ref[:, 2 * place, :] = value[:, :cols] * factor
        out_ref[:, 2 * place + 1, :] = value[:, cols:] * factor


def finish(tables, keep, came):
    slots = tables[2].shape[0]
    _, _, owned, wide = keep.shape
    cols = wide // 2
    vmem = pl.BlockSpec(memory_space=pltpu.VMEM)
    return pl.pallas_call(
        finish_kernel,
        out_shape=jax.ShapeDtypeStruct((owned, 2 * slots, cols), f32),
        in_specs=[vmem] * 5,
        out_specs=vmem,
        scratch_shapes=[pltpu.VMEM((owned, slots, cols), f32)],
        compiler_params=pltpu.CompilerParams(vmem_limit_bytes=16 * 1024 * 1024),
        cost_estimate=pl.CostEstimate(
            flops=8 * slots * owned * cols, bytes_accessed=8 * 1024 * 1024 // 4, transcendentals=0
        ),
    )(*tables, keep, came)


def squared_table(weight_table):
    wide_table = weight_table.astype(f32)
    return (wide_table * wide_table).astype(bf16)


def weight_totals(class_index, pose_index, defocus_bin, defocus, rows_table, cols_table, plane_weight, first_row, owned):
    box = rows_table.shape[2]
    poses = rows_table.shape[0]
    bins = defocus.shape[0]
    half = box // 2
    exact = lax.Precision.HIGHEST
    code = (class_index[:, 0] * poses + pose_index) * bins + defocus_bin
    codes = lax.all_gather(code, "img", tiled=True)
    hits = (codes[:, None] == jnp.arange(CLASSES * poses * bins, dtype=jnp.int32)).astype(f32)
    counts = jnp.sum(hits, 0).reshape(CLASSES, poses, bins)
    place = jnp.arange(box, dtype=jnp.int32)
    freq = jnp.where(place < half, place, place - box).astype(f32)
    turns = defocus[:, None] * (freq * freq)[None, :] * (1.0 / (half * half))
    turns_y = turns + ctf_phase / math.pi
    ones = jnp.ones_like(turns)
    wave_y = jnp.stack([0.5 * ones, -0.5 * turns_sine(turns_y + 0.25), 0.5 * turns_sine(turns_y)])
    wave_x = jnp.stack([ones, turns_sine(turns + 0.25), turns_sine(turns)])
    rows_own = lax.dynamic_slice_in_dim(rows_table, first_row, owned, 1)
    u = jnp.einsum("pry,mby->pmbr", squared_table(rows_own).astype(f32), wave_y, precision=exact)
    v = jnp.einsum("pxj,mbx->pmbj", squared_table(cols_table).astype(f32), wave_x, precision=exact)
    weight = counts[:, None] * plane_weight.T[None, :, :, None]
    left = weight[:, :, :, None, :, None] * u[None, None]
    return jnp.einsum("czpmbr,pmbj->rczj", left, v, precision=exact)


def by_halves(images, class_index, pose_index, defocus_bin, defocus, rows_table, cols_table, plane_weight):
    members = lax.axis_size("img")
    cores = lax.axis_size("slab")
    rows = rows_table.shape[1]
    planes = plane_weight.shape[1]
    cols = cols_table.shape[2]
    owned = rows // members
    steps = members.bit_length() - 1
    send, keep = own_totals(
        images, class_index, pose_index, defocus_bin, defocus, rows_table, cols_table, plane_weight, members
    )
    tables = own_ridges(defocus, plane_weight, rows_table, cols_table, owned)

    def exchange(value, step):
        pairs = []
        for i in range(members):
            for c in range(cores):
                axis = step ^ (c % 2) if steps > 1 and step < 2 else step
                pairs.append((i * cores + c, (i ^ (1 << axis)) * cores + c))
        return lax.ppermute(value, ("img", "slab"), pairs)

    came = exchange(send, 0)
    for step in range(1, steps):
        if step == 1:
            keep, tables = lax.optimization_barrier((keep, tables))
        send, keep = middle(keep, came)
        came = exchange(send, step)
    out = finish(tables, keep, came)
    return out.reshape(owned, CLASSES, planes, 2, cols)


def by_scatter(images, class_index, pose_index, defocus_bin, defocus, rows_table, cols_table, plane_weight):
    rows = rows_table.shape[1]
    cols = cols_table.shape[2]
    planes = plane_weight.shape[1]
    members = lax.axis_size("img")
    owned = rows // members
    (totals,) = own_totals(
        images, class_index, pose_index, defocus_bin, defocus, rows_table, cols_table, plane_weight, 1
    )
    slots = totals.shape[0]
    totals = totals.reshape(slots, members, owned, 2 * cols).transpose(1, 0, 2, 3)
    own = lax.psum_scatter(totals, "img", scatter_dimension=0, tiled=False)
    weight = weight_totals(
        class_index, pose_index, defocus_bin, defocus, rows_table, cols_table, plane_weight,
        lax.axis_index("img") * owned, owned,
    )
    own = own.astype(f32).reshape(planes, CLASSES, owned, 2, cols).transpose(2, 1, 0, 3, 4)
    return own / (weight[:, :, :, None, :] + wiener_ridge)


def body(*arrays):
    rows = arrays[5].shape[1]
    members = lax.axis_size("img")
    images = members * arrays[0].shape[0]
    small = members > 1 and members & (members - 1) == 0 and images <= 256 and rows % (16 * members) == 0
    return (by_halves if small else by_scatter)(*arrays)


def solution(mesh):
    placed = (
        P(("groups", "img"), None, None),
        P(("groups", "img"), None),
        P(("groups", "img")),
        P(("groups", "img")),
        P(),
        P(),
        P(None, None, "slab"),
        P(),
    )
    return jax.shard_map(
        body,
        mesh=mesh,
        in_specs=placed,
        out_specs=P("img", "groups", None, None, "slab"),
        check_vma=False,
    )
```

```python
import functools
import math

import jax
import jax.numpy as jnp
import numpy as np
from jax import lax
from jax.experimental import pallas as pl
from jax.experimental.pallas import tpu as pltpu
from jax.sharding import PartitionSpec as P

CLASSES = 8

wiener_ridge = 1.0
ctf_phase = 0.1
f32 = jnp.float32
bf16 = jnp.bfloat16


def packed_dft(box, sine_sign):
    half = box // 2
    k = np.concatenate([np.arange(half), [half], np.arange(1, half)])
    angle = (k[:, None] * np.arange(box)[None, :] % box) * (2.0 * math.pi / box)
    table = np.where((np.arange(box) <= half)[:, None], np.cos(angle), sine_sign * np.sin(angle))
    return (table / math.sqrt(box)).astype(np.float32)


def iota(shape, axis):
    return lax.broadcasted_iota(jnp.int32, shape, axis)


def dot(a, b, dims=((1,), (0,))):
    return lax.dot_general(a, b, (dims, ((), ())), preferred_element_type=f32)


def turns_sine(turns):
    return jnp.sin((turns - jnp.round(turns)) * (2.0 * math.pi))


def split_two(value):
    high = value.astype(bf16)
    return high, (value - high.astype(f32)).astype(bf16)


def fold_of(place, half):
    box = 2 * half
    return jnp.where(place <= half, place, box + half - place)


def slices_kernel(
    class_hbm, pose_hbm, bin_hbm, defocus_hbm, plane_hbm,
    dft_hbm, dft_t_hbm, images_hbm, rows_hbm, cols_hbm,
    *refs,
):
    outs, refs = refs[:-SCRATCH], refs[-SCRATCH:]
    (
        class_ref, pose_ref, bin_ref, defocus_ref, plane_ref,
        dft_ref, dft_t_ref, images_ref, rows_ref, cols_ref, arrived,
        rows_fold, cols_fold, wave_y, cos_x, sin_x, spec_ref, mix_ref, totals,
    ) = refs
    count, box, _ = images_ref.shape
    half = box // 2
    poses, rows, _ = rows_ref.shape
    cols = cols_ref.shape[2]
    planes = plane_ref.shape[0]

    pairs = (
        (class_hbm, class_ref), (pose_hbm, pose_ref), (bin_hbm, bin_ref),
        (defocus_hbm, defocus_ref), (plane_hbm, plane_ref),
        (rows_hbm, rows_ref), (cols_hbm, cols_ref), (dft_t_hbm, dft_t_ref),
        (images_hbm, images_ref), (dft_hbm, dft_ref),
    )
    copies = [
        pltpu.make_async_copy(source, target, arrived.at[n])
        for n, (source, target) in enumerate(pairs)
    ]
    for copy in copies:
        copy.start()

    place = iota((box, box), 0)
    other = iota((box, box), 1)
    folded = fold_of(place, half)
    near = (folded == other).astype(f32).astype(bf16)
    far = (jnp.where(folded == 0, 0, box - folded) == other).astype(f32).astype(bf16)

    for copy in copies[:5]:
        copy.wait()
    tall, lanes = wave_y.shape
    lane = iota((1, lanes), 1)
    sub = iota((count, box), 0)
    lane_defocus = jnp.zeros((1, lanes), f32)
    sub_defocus = jnp.zeros((count, box), f32)
    for i in range(count):
        value = defocus_ref[bin_ref[i]]
        lane_defocus = jnp.where(lane % count == i, value, lane_defocus)
        sub_defocus = jnp.where(sub == i, value, sub_defocus)
    scale = 1.0 / (2 * half * half)
    ky = iota((tall, lanes), 0).astype(f32)
    quarter = jnp.where(lane < count, 0.0, 0.25) + ctf_phase / (2.0 * math.pi)
    wave_y[...] = turns_sine(lane_defocus * (ky * ky * scale) + quarter)
    kx = iota((count, box), 1)
    kx = jnp.where(kx <= half, kx, kx - half).astype(f32)
    turns = sub_defocus * (kx * kx * scale)
    cos_x[...] = -turns_sine(turns + 0.25)
    sin_x[...] = -turns_sine(turns)
    totals[...] = jnp.zeros_like(totals)
    if len(outs) > 1:
        bins = defocus_ref.shape[0]
        count_row = iota((16, 2 * cols), 0)
        count_lane = iota((16, 2 * cols), 1)
        counts = jnp.zeros((16, 2 * cols), f32)
        for i in range(count):
            hit = (count_row == class_ref[i]) & (count_lane == pose_ref[i] * bins + bin_ref[i])
            counts = counts + jnp.where(hit, 1.0, 0.0)
        totals[planes * CLASSES] = jnp.tile(counts, (rows // 16, 1))

    copies[5].wait()
    rows_fold[...] = dot(
        rows_ref[...].reshape(poses * rows, box), near, ((1,), (1,))
    ).astype(bf16)
    copies[6].wait()
    for p in range(0, poses, 2):
        two = jnp.concatenate([cols_ref[p], cols_ref[p + 1]], 1)
        near_two = dot(near, two).astype(bf16)
        far_two = dot(far, two).astype(bf16)
        cols_fold[p] = jnp.concatenate([near_two[:, :cols], far_two[:, :cols]], 1)
        cols_fold[p + 1] = jnp.concatenate([near_two[:, cols:], far_two[:, cols:]], 1)
    for copy in copies[7:]:
        copy.wait()

    tile = 8
    tile_row = iota((tile, half), 0) == 0
    tile_col = iota((tile, half), 1) == 0
    col_zero = iota((half, half), 1) == 0
    short_row = iota((16, half), 0) == 0
    short_col = iota((16, half), 1) == 0

    def without_row(value):
        return jnp.concatenate([jnp.where(tile_row, 0.0, value[:tile]), value[tile:]], 0)

    def transform(i):
        z = dot(images_ref[i], dft_t_ref[...]).astype(bf16)
        y = dot(dft_ref[...], z)
        sin_col = jnp.broadcast_to(wave_y[:, i : i + 1], (tall, half))
        cos_col = jnp.broadcast_to(wave_y[:, count + i : count + i + 1], (tall, half))
        near_ctf = sin_col * cos_x[i : i + 1, :half] + cos_col * sin_x[i : i + 1, :half]
        far_ctf = sin_col * cos_x[i : i + 1, half:] + cos_col * sin_x[i : i + 1, half:]
        cc, cs = y[:half, :half], y[:half, half:]
        sc, ss = y[half:, :half], y[half:, half:]
        ss_row = without_row(ss)
        ss_in = jnp.where(col_zero, 0.0, ss_row)
        sc_in = without_row(sc)
        cs_in = jnp.where(col_zero, 0.0, cs)
        near_y, far_y = near_ctf[:half], far_ctf[:half]
        spec = spec_ref.at[i % SLOTS]
        spec[0:half, 0:half] = (near_y * (cc + ss_in)).astype(bf16)
        spec[0:half, half:] = (far_y * jnp.where(col_zero, cs, cc - ss_in)).astype(bf16)
        spec[half:box, 0:half] = (near_y * (sc_in - cs_in)).astype(bf16)
        spec[half:box, half:] = (far_y * jnp.where(col_zero, ss_row, sc_in + cs_in)).astype(bf16)
        sc_top = jnp.broadcast_to(sc[0:1], (16, half))
        ss_top = jnp.broadcast_to(ss[0:1], (16, half))
        ss_top_in = jnp.where(short_col, 0.0, ss_top)
        spec[box : box + 16, 0:half] = (
            near_ctf[half : half + 1] * jnp.where(short_row, sc_top, -ss_top_in)
        ).astype(bf16)
        spec[box : box + 16, half:] = (
            far_ctf[half : half + 1]
            * jnp.where(short_row, jnp.where(short_col, ss_top, sc_top), ss_top_in)
        ).astype(bf16)

    def mix(i):
        mixed = dot(spec_ref[i % SLOTS], cols_fold[pose_ref[i]])
        out = mix_ref.at[i % SLOTS]
        out[0:half, 0:cols] = mixed[:half, :cols].astype(bf16)
        out[0:half, cols:] = mixed[half:box, :cols].astype(bf16)
        top = iota((16, cols), 0) == 0
        real, imag = mixed[:half, cols:], -mixed[half:box, cols:]
        out[half : half + 16, 0:cols] = jnp.where(
            top, mixed[box : box + 1, :cols], real[:16]
        ).astype(bf16)
        out[half : half + 16, cols:] = jnp.where(
            top, mixed[box + 1 : box + 2, :cols], imag[:16]
        ).astype(bf16)
        out[half + 16 :, 0:cols] = real[16:].astype(bf16)
        out[half + 16 :, cols:] = imag[16:].astype(bf16)

    def insert(i):
        pose = pose_ref[i]
        pose_rows = rows_fold[pl.ds(pl.multiple_of(pose * rows, rows), rows), :]
        piece = dot(pose_rows, mix_ref[i % SLOTS])
        for z in range(planes):
            slot = z * CLASSES + class_ref[i]
            totals[slot] += plane_ref[z, pose] * piece

    for step in range(count + 2):
        if step >= 2:
            insert(step - 2)
        if 1 <= step <= count:
            mix(step - 1)
        if step < count:
            transform(step)

    if len(outs) == 1:
        outs[0][...] = totals[...].astype(bf16)
        return
    half_members, _, owned, _ = outs[0].shape
    steps = half_members.bit_length()
    me = lax.axis_index("img")
    routes = [[0, 1] + list(range(2, steps)), [1, 0] + list(range(2, steps))]
    base = 0
    for route, send, keep in zip(routes, outs[::2], outs[1::2]):
        part = slice(base, base + keep.shape[1])
        base += keep.shape[1]
        for q in range(half_members):
            other = me
            for n in range(1, steps):
                if (q >> (steps - 1 - n)) & 1:
                    other = other ^ (1 << route[n])
            for out, whose in ((keep, other), (send, other ^ (1 << route[0]))):
                first = pl.multiple_of(whose * owned, owned)
                out[q] = totals[part, pl.ds(first, owned), :].astype(out.dtype)


SCRATCH = 19
SLOTS = 3


def own_totals(images, class_index, pose_index, defocus_bin, defocus, rows_table, cols_table, plane_weight, members):
    count, box, _ = images.shape
    poses, rows, _ = rows_table.shape
    cols = cols_table.shape[2]
    planes = plane_weight.shape[1]
    slots = CLASSES * planes
    table_y, table_x = packed_dft(box, -1.0), packed_dft(box, 1.0)
    any_place = pl.BlockSpec(memory_space=pl.ANY)
    vmem = pl.BlockSpec(memory_space=pltpu.VMEM)
    lanes = 128 * (-(-2 * count // 128))
    if members == 1:
        out_shape = [jax.ShapeDtypeStruct((slots, rows, 2 * cols), bf16)]
    else:
        slots += 1
        out_shape = []
        for part in (slots // 2, slots - slots // 2):
            piece = (members // 2, part, rows // members, 2 * cols)
            out_shape += [pltpu.VMEM(piece, bf16), pltpu.VMEM(piece, f32)]
    operands = (
        class_index[:, 0], pose_index, defocus_bin, defocus, plane_weight.T,
        jnp.asarray(table_y, bf16), jnp.asarray(table_x.T.copy(), bf16),
        images, rows_table, cols_table,
    )
    return pl.pallas_call(
        slices_kernel,
        out_shape=out_shape,
        in_specs=[any_place] * 10,
        out_specs=[vmem] * len(out_shape),
        scratch_shapes=[pltpu.SMEM(x.shape, x.dtype) for x in operands[:5]]
        + [pltpu.VMEM(x.shape, x.dtype) for x in operands[5:]]
        + [
            pltpu.SemaphoreType.DMA((10,)),
            pltpu.VMEM((poses * rows, box), bf16),
            pltpu.VMEM((poses, box, 2 * cols), bf16),
            pltpu.VMEM((box // 2 + 8, lanes), f32),
            pltpu.VMEM((count, box), f32),
            pltpu.VMEM((count, box), f32),
            pltpu.VMEM((SLOTS, box + 16, box), bf16),
            pltpu.VMEM((SLOTS, box, 2 * cols), bf16),
            pltpu.VMEM((slots, rows, 2 * cols), f32),
        ],
        compiler_params=pltpu.CompilerParams(vmem_limit_bytes=VMEM_LIMIT),
        cost_estimate=pl.CostEstimate(
            flops=2 * count * box * box * 1000, bytes_accessed=6 * 1024 * 1024, transcendentals=0
        ),
    )(*operands)


VMEM_LIMIT = 56 * 1024 * 1024


def ridge_kernel(defocus_hbm, plane_hbm, rows_hbm, cols_hbm, high_ref, low_ref, share_ref, *refs):
    defocus_ref, plane_ref, rows_ref, cols_ref, arrived = refs
    poses, owned, box = rows_ref.shape
    cols = cols_ref.shape[2]
    bins = defocus_ref.shape[0]
    planes = plane_ref.shape[0]
    half = box // 2
    first = pl.multiple_of(lax.axis_index("img") * owned, owned)
    copies = [
        pltpu.make_async_copy(defocus_hbm, defocus_ref, arrived.at[0]),
        pltpu.make_async_copy(plane_hbm, plane_ref, arrived.at[1]),
        pltpu.make_async_copy(rows_hbm.at[:, pl.ds(first, owned), :], rows_ref, arrived.at[2]),
        pltpu.make_async_copy(cols_hbm, cols_ref, arrived.at[3]),
    ]
    for copy in copies:
        copy.start()
    for copy in copies:
        copy.wait()
    share_plane = iota((planes * CLASSES, poses * bins), 0) // CLASSES
    share_pose = iota((planes * CLASSES, poses * bins), 1) // bins
    share = jnp.zeros((planes * CLASSES, poses * bins), f32)
    for p in range(poses):
        for z in range(planes):
            share = jnp.where((share_plane == z) & (share_pose == p), plane_ref[z, p], share)
    share_ref[...] = share

    bin_row = iota((bins, box), 0)
    sub_defocus = jnp.zeros((bins, box), f32)
    for b in range(bins):
        sub_defocus = jnp.where(bin_row == b, defocus_ref[b], sub_defocus)
    freq = iota((bins, box), 1)
    freq = jnp.where(freq < half, freq, box - freq).astype(f32)
    turns_x = sub_defocus * (freq * freq * (1.0 / (half * half)))
    turns_y = turns_x + ctf_phase / math.pi
    ones = jnp.ones((bins, box), f32)
    wave_y = jnp.concatenate(
        [0.5 * ones, -0.5 * turns_sine(turns_y + 0.25), 0.5 * turns_sine(turns_y)], 0
    )
    wave_x = jnp.concatenate([ones, turns_sine(turns_x + 0.25), turns_sine(turns_x)], 0)
    y_high, y_low = split_two(wave_y)
    x_high, x_low = split_two(wave_x)
    rows_sq = rows_ref[...].reshape(poses * owned, box).astype(f32)
    rows_sq = (rows_sq * rows_sq).astype(bf16)
    u = dot(y_high, rows_sq, ((1,), (1,))) + dot(y_low, rows_sq, ((1,), (1,)))
    for p in range(poses):
        cols_sq = cols_ref[p].astype(f32)
        cols_sq = (cols_sq * cols_sq).astype(bf16)
        v = dot(x_high, cols_sq) + dot(x_low, cols_sq)
        for r in range(owned):
            column = u[:, p * owned + r : p * owned + r + 1]
            product = v * column
            weight = product[:bins] + product[bins : 2 * bins] + product[2 * bins :]
            high, low = split_two(weight)
            high_ref[p * bins : (p + 1) * bins, r * cols : (r + 1) * cols] = high
            low_ref[p * bins : (p + 1) * bins, r * cols : (r + 1) * cols] = low


def own_ridges(defocus, plane_weight, rows_table, cols_table, owned):
    poses, _, box = rows_table.shape
    cols = cols_table.shape[2]
    bins = defocus.shape[0]
    any_place = pl.BlockSpec(memory_space=pl.ANY)
    vmem = pl.BlockSpec(memory_space=pltpu.VMEM)
    planes = plane_weight.T
    table = jax.ShapeDtypeStruct((poses * bins, owned * cols), bf16)
    return pl.pallas_call(
        ridge_kernel,
        out_shape=[table, table, jax.ShapeDtypeStruct((planes.shape[0] * CLASSES, poses * bins), f32)],
        in_specs=[any_place] * 4,
        out_specs=[vmem] * 3,
        scratch_shapes=[
            pltpu.SMEM(defocus.shape, f32),
            pltpu.SMEM(planes.shape, f32),
            pltpu.VMEM((poses, owned, box), bf16),
            pltpu.VMEM(cols_table.shape, bf16),
            pltpu.SemaphoreType.DMA((4,)),
        ],
        compiler_params=pltpu.CompilerParams(vmem_limit_bytes=16 * 1024 * 1024),
        cost_estimate=pl.CostEstimate(
            flops=2 * poses * 1000 * 128 * 256, bytes_accessed=2 * 1024 * 1024, transcendentals=0
        ),
    )(defocus, planes, rows_table, cols_table)


def middle_kernel(ways, *refs):
    pairs, outs = refs[: 2 * ways], refs[2 * ways :]
    base = 0
    for n in range(ways):
        keep, came = pairs[2 * n], pairs[2 * n + 1]
        half, part = keep.shape[0] // 2, keep.shape[1]
        if len(outs) == 2:
            send, kept = (out.at[:, base : base + part] for out in outs)
            base += part
        else:
            send, kept = outs[2 * n], outs[2 * n + 1]
        kept[...] = keep[:half] + came[:half].astype(f32)
        send[...] = (keep[half:] + came[half:].astype(f32)).astype(bf16)


def middle(arrays, merge):
    vmem = pl.BlockSpec(memory_space=pltpu.VMEM)
    keeps = arrays[::2]
    pieces = [(keep.shape[0] // 2,) + keep.shape[1:] for keep in keeps]
    if merge:
        pieces = [(pieces[0][0], sum(piece[1] for piece in pieces)) + pieces[0][2:]]
    out_shape = []
    for piece in pieces:
        out_shape += [pltpu.VMEM(piece, bf16), pltpu.VMEM(piece, f32)]
    return pl.pallas_call(
        functools.partial(middle_kernel, len(keeps)),
        out_shape=out_shape,
        in_specs=[vmem] * len(arrays),
        out_specs=[vmem] * len(out_shape),
        compiler_params=pltpu.CompilerParams(vmem_limit_bytes=16 * 1024 * 1024),
        cost_estimate=pl.CostEstimate(flops=1000000, bytes_accessed=4 * 1024 * 1024, transcendentals=0),
    )(*arrays)


def finish_kernel(high_ref, low_ref, share_ref, keep, came, out_ref, ridge_ref):
    slots, pairs = share_ref.shape
    owned, _, cols = ridge_ref.shape
    planes = slots // CLASSES

    def summed(s):
        return keep[0, s] + came[0, s].astype(f32)

    counts = summed(slots)[:CLASSES, :pairs]
    scaled = jnp.concatenate([counts] * planes, 0) * share_ref[...]
    c_high, c_low = split_two(scaled)
    weight = (
        dot(c_high, high_ref[...]) + dot(c_low, high_ref[...]) + dot(c_high, low_ref[...])
    )
    ridge = 1.0 / (weight + wiener_ridge)
    for r in range(owned):
        ridge_ref[r] = ridge[:, r * cols : (r + 1) * cols]
    for s in range(slots):
        value = summed(s)
        factor = ridge_ref[:, s, :]
        place = (s % CLASSES) * planes + s // CLASSES
        out_ref[:, 2 * place, :] = value[:, :cols] * factor
        out_ref[:, 2 * place + 1, :] = value[:, cols:] * factor


def finish(tables, keep, came):
    slots = tables[2].shape[0]
    _, _, owned, wide = keep.shape
    cols = wide // 2
    vmem = pl.BlockSpec(memory_space=pltpu.VMEM)
    return pl.pallas_call(
        finish_kernel,
        out_shape=jax.ShapeDtypeStruct((owned, 2 * slots, cols), f32),
        in_specs=[vmem] * 5,
        out_specs=vmem,
        scratch_shapes=[pltpu.VMEM((owned, slots, cols), f32)],
        compiler_params=pltpu.CompilerParams(vmem_limit_bytes=16 * 1024 * 1024),
        cost_estimate=pl.CostEstimate(
            flops=8 * slots * owned * cols, bytes_accessed=8 * 1024 * 1024 // 4, transcendentals=0
        ),
    )(*tables, keep, came)


def squared_table(weight_table):
    wide_table = weight_table.astype(f32)
    return (wide_table * wide_table).astype(bf16)


def weight_totals(class_index, pose_index, defocus_bin, defocus, rows_table, cols_table, plane_weight, first_row, owned):
    box = rows_table.shape[2]
    poses = rows_table.shape[0]
    bins = defocus.shape[0]
    half = box // 2
    exact = lax.Precision.HIGHEST
    code = (class_index[:, 0] * poses + pose_index) * bins + defocus_bin
    codes = lax.all_gather(code, "img", tiled=True)
    hits = (codes[:, None] == jnp.arange(CLASSES * poses * bins, dtype=jnp.int32)).astype(f32)
    counts = jnp.sum(hits, 0).reshape(CLASSES, poses, bins)
    place = jnp.arange(box, dtype=jnp.int32)
    freq = jnp.where(place < half, place, place - box).astype(f32)
    turns = defocus[:, None] * (freq * freq)[None, :] * (1.0 / (half * half))
    turns_y = turns + ctf_phase / math.pi
    ones = jnp.ones_like(turns)
    wave_y = jnp.stack([0.5 * ones, -0.5 * turns_sine(turns_y + 0.25), 0.5 * turns_sine(turns_y)])
    wave_x = jnp.stack([ones, turns_sine(turns + 0.25), turns_sine(turns)])
    rows_own = lax.dynamic_slice_in_dim(rows_table, first_row, owned, 1)
    u = jnp.einsum("pry,mby->pmbr", squared_table(rows_own).astype(f32), wave_y, precision=exact)
    v = jnp.einsum("pxj,mbx->pmbj", squared_table(cols_table).astype(f32), wave_x, precision=exact)
    weight = counts[:, None] * plane_weight.T[None, :, :, None]
    left = weight[:, :, :, None, :, None] * u[None, None]
    return jnp.einsum("czpmbr,pmbj->rczj", left, v, precision=exact)


def by_halves(images, class_index, pose_index, defocus_bin, defocus, rows_table, cols_table, plane_weight):
    members = lax.axis_size("img")
    rows = rows_table.shape[1]
    planes = plane_weight.shape[1]
    cols = cols_table.shape[2]
    owned = rows // members
    steps = members.bit_length() - 1
    x_send, x_keep, z_send, z_keep = own_totals(
        images, class_index, pose_index, defocus_bin, defocus, rows_table, cols_table, plane_weight, members
    )
    tables = own_ridges(defocus, plane_weight, rows_table, cols_table, owned)

    def exchange(value, axis):
        return lax.ppermute(value, "img", [(i, i ^ (1 << axis)) for i in range(members)])

    x_came, z_came = exchange(x_send, 0), exchange(z_send, 1)
    x_keep, tables = lax.optimization_barrier((x_keep, tables))
    x_send, x_keep, z_send, z_keep = middle((x_keep, x_came, z_keep, z_came), False)
    x_came, z_came = exchange(x_send, 1), exchange(z_send, 0)
    send, keep = middle((x_keep, x_came, z_keep, z_came), True)
    came = exchange(send, 2)
    for step in range(3, steps):
        send, keep = middle((keep, came), False)
        came = exchange(send, step)
    out = finish(tables, keep, came)
    return out.reshape(owned, CLASSES, planes, 2, cols)


def by_scatter(images, class_index, pose_index, defocus_bin, defocus, rows_table, cols_table, plane_weight):
    rows = rows_table.shape[1]
    cols = cols_table.shape[2]
    planes = plane_weight.shape[1]
    members = lax.axis_size("img")
    owned = rows // members
    (totals,) = own_totals(
        images, class_index, pose_index, defocus_bin, defocus, rows_table, cols_table, plane_weight, 1
    )
    slots = totals.shape[0]
    totals = totals.reshape(slots, members, owned, 2 * cols).transpose(1, 0, 2, 3)
    own = lax.psum_scatter(totals, "img", scatter_dimension=0, tiled=False)
    weight = weight_totals(
        class_index, pose_index, defocus_bin, defocus, rows_table, cols_table, plane_weight,
        lax.axis_index("img") * owned, owned,
    )
    own = own.astype(f32).reshape(planes, CLASSES, owned, 2, cols).transpose(2, 1, 0, 3, 4)
    return own / (weight[:, :, :, None, :] + wiener_ridge)


def body(*arrays):
    rows = arrays[5].shape[1]
    members = lax.axis_size("img")
    images = members * arrays[0].shape[0]
    small = members >= 8 and members & (members - 1) == 0 and images <= 256 and rows % (16 * members) == 0
    return (by_halves if small else by_scatter)(*arrays)


def solution(mesh):
    placed = (
        P(("groups", "img"), None, None),
        P(("groups", "img"), None),
        P(("groups", "img")),
        P(("groups", "img")),
        P(),
        P(),
        P(None, None, "slab"),
        P(),
    )
    return jax.shard_map(
        body,
        mesh=mesh,
        in_specs=placed,
        out_specs=P("img", "groups", None, None, "slab"),
        check_vma=False,
    )
```

```python
import functools
import math

import jax
import jax.numpy as jnp
import numpy as np
from jax import lax
from jax.experimental import pallas as pl
from jax.experimental.pallas import tpu as pltpu
from jax.sharding import PartitionSpec as P

CLASSES = 8

wiener_ridge = 1.0
ctf_phase = 0.1
f32 = jnp.float32
bf16 = jnp.bfloat16


def packed_dft(box, sine_sign):
    half = box // 2
    k = np.concatenate([np.arange(half), [half], np.arange(1, half)])
    angle = (k[:, None] * np.arange(box)[None, :] % box) * (2.0 * math.pi / box)
    table = np.where((np.arange(box) <= half)[:, None], np.cos(angle), sine_sign * np.sin(angle))
    return (table / math.sqrt(box)).astype(np.float32)


def iota(shape, axis):
    return lax.broadcasted_iota(jnp.int32, shape, axis)


def dot(a, b, dims=((1,), (0,))):
    return lax.dot_general(a, b, (dims, ((), ())), preferred_element_type=f32)


def turns_sine(turns):
    return jnp.sin((turns - jnp.round(turns)) * (2.0 * math.pi))


def split_two(value):
    high = value.astype(bf16)
    return high, (value - high.astype(f32)).astype(bf16)


def fold_of(place, half):
    box = 2 * half
    return jnp.where(place <= half, place, box + half - place)


def slices_kernel(
    class_hbm, pose_hbm, bin_hbm, defocus_hbm, plane_hbm,
    dft_hbm, dft_t_hbm, images_hbm, rows_hbm, cols_hbm,
    *refs,
):
    outs, refs = refs[:-SCRATCH], refs[-SCRATCH:]
    (
        class_ref, pose_ref, bin_ref, defocus_ref, plane_ref,
        dft_ref, dft_t_ref, images_ref, rows_ref, cols_ref, arrived,
        rows_fold, cols_fold, wave_y, cos_x, sin_x, half_ref, spec_ref, mix_ref, totals,
    ) = refs
    count, box, _ = images_ref.shape
    half = box // 2
    poses, rows, _ = rows_ref.shape
    cols = cols_ref.shape[2]
    planes = plane_ref.shape[0]

    pairs = (
        (class_hbm, class_ref), (pose_hbm, pose_ref), (bin_hbm, bin_ref),
        (defocus_hbm, defocus_ref), (plane_hbm, plane_ref),
        (dft_t_hbm, dft_t_ref), (images_hbm.at[0:GROUP], images_ref.at[0:GROUP]),
        (dft_hbm, dft_ref), (cols_hbm, cols_ref), (rows_hbm, rows_ref),
    ) + tuple(
        (images_hbm.at[i : i + GROUP], images_ref.at[i : i + GROUP])
        for i in range(GROUP, count, GROUP)
    )
    copies = [
        pltpu.make_async_copy(source, target, arrived.at[n])
        for n, (source, target) in enumerate(pairs)
    ]
    for copy in copies:
        copy.start()

    place = iota((box, box), 0)
    other = iota((box, box), 1)
    folded = fold_of(place, half)
    near = (folded == other).astype(f32).astype(bf16)
    far = (jnp.where(folded == 0, 0, box - folded) == other).astype(f32).astype(bf16)

    for copy in copies[:5]:
        copy.wait()
    tall, lanes = wave_y.shape
    lane = iota((1, lanes), 1)
    sub = iota((count, box), 0)
    lane_defocus = jnp.zeros((1, lanes), f32)
    sub_defocus = jnp.zeros((count, box), f32)
    for i in range(count):
        value = defocus_ref[bin_ref[i]]
        lane_defocus = jnp.where(lane % count == i, value, lane_defocus)
        sub_defocus = jnp.where(sub == i, value, sub_defocus)
    scale = 1.0 / (2 * half * half)
    ky = iota((tall, lanes), 0).astype(f32)
    quarter = jnp.where(lane < count, 0.0, 0.25) + ctf_phase / (2.0 * math.pi)
    wave_y[...] = turns_sine(lane_defocus * (ky * ky * scale) + quarter)
    kx = iota((count, box), 1)
    kx = jnp.where(kx <= half, kx, kx - half).astype(f32)
    turns = sub_defocus * (kx * kx * scale)
    cos_x[...] = -turns_sine(turns + 0.25)
    sin_x[...] = -turns_sine(turns)
    totals[...] = jnp.zeros_like(totals)
    if len(outs) > 1:
        bins = defocus_ref.shape[0]
        count_row = iota((16, 2 * cols), 0)
        count_lane = iota((16, 2 * cols), 1)
        counts = jnp.zeros((16, 2 * cols), f32)
        for i in range(count):
            hit = (count_row == class_ref[i]) & (count_lane == pose_ref[i] * bins + bin_ref[i])
            counts = counts + jnp.where(hit, 1.0, 0.0)
        totals[planes * CLASSES] = jnp.tile(counts, (rows // 16, 1))

    tile = 8
    tile_row = iota((tile, half), 0) == 0
    tile_col = iota((tile, half), 1) == 0
    col_zero = iota((half, half), 1) == 0
    short_row = iota((16, half), 0) == 0
    short_col = iota((16, half), 1) == 0

    def without_row(value):
        return jnp.concatenate([jnp.where(tile_row, 0.0, value[:tile]), value[tile:]], 0)

    def along_columns(i):
        if i % GROUP == 0:
            copies[6 if i == 0 else 9 + i // GROUP].wait()
        half_ref[i % SLOTS] = dot(images_ref[i], dft_t_ref[...]).astype(bf16)

    def along_rows(i):
        y = dot(dft_ref[...], half_ref[i % SLOTS])
        sin_col = jnp.broadcast_to(wave_y[:, i : i + 1], (tall, half))
        cos_col = jnp.broadcast_to(wave_y[:, count + i : count + i + 1], (tall, half))
        near_ctf = sin_col * cos_x[i : i + 1, :half] + cos_col * sin_x[i : i + 1, :half]
        far_ctf = sin_col * cos_x[i : i + 1, half:] + cos_col * sin_x[i : i + 1, half:]
        cc, cs = y[:half, :half], y[:half, half:]
        sc, ss = y[half:, :half], y[half:, half:]
        ss_row = without_row(ss)
        ss_in = jnp.where(col_zero, 0.0, ss_row)
        sc_in = without_row(sc)
        cs_in = jnp.where(col_zero, 0.0, cs)
        near_y, far_y = near_ctf[:half], far_ctf[:half]
        spec = spec_ref.at[i % SLOTS]
        spec[0:half, 0:half] = (near_y * (cc + ss_in)).astype(bf16)
        spec[0:half, half:] = (far_y * jnp.where(col_zero, cs, cc - ss_in)).astype(bf16)
        spec[half:box, 0:half] = (near_y * (sc_in - cs_in)).astype(bf16)
        spec[half:box, half:] = (far_y * jnp.where(col_zero, ss_row, sc_in + cs_in)).astype(bf16)
        sc_top = jnp.broadcast_to(sc[0:1], (16, half))
        ss_top = jnp.broadcast_to(ss[0:1], (16, half))
        ss_top_in = jnp.where(short_col, 0.0, ss_top)
        spec[box : box + 16, 0:half] = (
            near_ctf[half : half + 1] * jnp.where(short_row, sc_top, -ss_top_in)
        ).astype(bf16)
        spec[box : box + 16, half:] = (
            far_ctf[half : half + 1]
            * jnp.where(short_row, jnp.where(short_col, ss_top, sc_top), ss_top_in)
        ).astype(bf16)

    def mix(i):
        mixed = dot(spec_ref[i % SLOTS], cols_fold[pose_ref[i]])
        out = mix_ref.at[i % SLOTS]
        out[0:half, 0:cols] = mixed[:half, :cols].astype(bf16)
        out[0:half, cols:] = mixed[half:box, :cols].astype(bf16)
        top = iota((16, cols), 0) == 0
        real, imag = mixed[:half, cols:], -mixed[half:box, cols:]
        out[half : half + 16, 0:cols] = jnp.where(
            top, mixed[box : box + 1, :cols], real[:16]
        ).astype(bf16)
        out[half : half + 16, cols:] = jnp.where(
            top, mixed[box + 1 : box + 2, :cols], imag[:16]
        ).astype(bf16)
        out[half + 16 :, 0:cols] = real[16:].astype(bf16)
        out[half + 16 :, cols:] = imag[16:].astype(bf16)

    def insert(i):
        pose = pose_ref[i]
        pose_rows = rows_fold[pl.ds(pl.multiple_of(pose * rows, rows), rows), :]
        piece = dot(pose_rows, mix_ref[i % SLOTS])
        for z in range(planes):
            slot = z * CLASSES + class_ref[i]
            totals[slot] += plane_ref[z, pose] * piece

    copies[5].wait()
    along_columns(0)
    copies[7].wait()
    copies[8].wait()
    for p in range(0, poses, 2):
        two = jnp.concatenate([cols_ref[p], cols_ref[p + 1]], 1)
        near_two = dot(near, two).astype(bf16)
        far_two = dot(far, two).astype(bf16)
        cols_fold[p] = jnp.concatenate([near_two[:, :cols], far_two[:, :cols]], 1)
        cols_fold[p + 1] = jnp.concatenate([near_two[:, cols:], far_two[:, cols:]], 1)
    along_columns(1)
    along_rows(0)
    copies[9].wait()
    rows_fold[...] = dot(
        rows_ref[...].reshape(poses * rows, box), near, ((1,), (1,))
    ).astype(bf16)
    for step in range(2, count + 3):
        if step >= 3:
            insert(step - 3)
        if step - 2 < count:
            mix(step - 2)
        if step - 1 < count:
            along_rows(step - 1)
        if step < count:
            along_columns(step)

    if len(outs) == 1:
        outs[0][...] = totals[...].astype(bf16)
        return
    x_send, x_keep, z_keep = outs[:3]
    z_sends = outs[3:]
    rounds, x_slots, owned, _ = x_keep.shape
    me = lax.axis_index("img")
    for k in range(rounds):
        mine = pl.ds(pl.multiple_of((me ^ (2 * k)) * owned, owned), owned)
        theirs = pl.ds(pl.multiple_of((me ^ (2 * k + 1)) * owned, owned), owned)
        x_keep[k] = totals[-x_slots:, mine, :]
        x_send[k] = totals[-x_slots:, theirs, :].astype(bf16)
        z_out = z_keep if k == 0 else z_sends[k - 1]
        z_out[0] = totals[:-x_slots, mine, :].astype(z_out.dtype)
        z_out[1] = totals[:-x_slots, theirs, :].astype(z_out.dtype)


SCRATCH = 20
SLOTS = 3
GROUP = 4
Z_SLOTS = 5


def own_totals(images, class_index, pose_index, defocus_bin, defocus, rows_table, cols_table, plane_weight, turns_round):
    count, box, _ = images.shape
    poses, rows, _ = rows_table.shape
    cols = cols_table.shape[2]
    planes = plane_weight.shape[1]
    slots = CLASSES * planes
    table_y, table_x = packed_dft(box, -1.0), packed_dft(box, 1.0)
    any_place = pl.BlockSpec(memory_space=pl.ANY)
    vmem = pl.BlockSpec(memory_space=pltpu.VMEM)
    lanes = 128 * (-(-2 * count // 128))
    if turns_round == 0:
        out_shape = [jax.ShapeDtypeStruct((slots, rows, 2 * cols), bf16)]
    else:
        slots += 1
        x_piece = (turns_round, slots - Z_SLOTS, rows // (2 * turns_round), 2 * cols)
        z_piece = (2, Z_SLOTS, rows // (2 * turns_round), 2 * cols)
        out_shape = [pltpu.VMEM(x_piece, bf16), pltpu.VMEM(x_piece, f32), pltpu.VMEM(z_piece, f32)]
        out_shape += [pltpu.VMEM(z_piece, bf16)] * (turns_round - 1)
    operands = (
        class_index[:, 0], pose_index, defocus_bin, defocus, plane_weight.T,
        jnp.asarray(table_y, bf16), jnp.asarray(table_x.T.copy(), bf16),
        images, rows_table, cols_table,
    )
    return pl.pallas_call(
        slices_kernel,
        out_shape=out_shape,
        in_specs=[any_place] * 10,
        out_specs=[vmem] * len(out_shape),
        scratch_shapes=[pltpu.SMEM(x.shape, x.dtype) for x in operands[:5]]
        + [pltpu.VMEM(x.shape, x.dtype) for x in operands[5:]]
        + [
            pltpu.SemaphoreType.DMA((9 + count // GROUP,)),
            pltpu.VMEM((poses * rows, box), bf16),
            pltpu.VMEM((poses, box, 2 * cols), bf16),
            pltpu.VMEM((box // 2 + 8, lanes), f32),
            pltpu.VMEM((count, box), f32),
            pltpu.VMEM((count, box), f32),
            pltpu.VMEM((SLOTS, box, box), bf16),
            pltpu.VMEM((SLOTS, box + 16, box), bf16),
            pltpu.VMEM((SLOTS, box, 2 * cols), bf16),
            pltpu.VMEM((slots, rows, 2 * cols), f32),
        ],
        compiler_params=pltpu.CompilerParams(vmem_limit_bytes=VMEM_LIMIT),
        cost_estimate=pl.CostEstimate(
            flops=2 * count * box * box * 1000, bytes_accessed=6 * 1024 * 1024, transcendentals=0
        ),
    )(*operands)


VMEM_LIMIT = 56 * 1024 * 1024


def ridge_kernel(defocus_hbm, plane_hbm, rows_hbm, cols_hbm, high_ref, low_ref, share_ref, *refs):
    defocus_ref, plane_ref, rows_ref, cols_ref, arrived = refs
    poses, owned, box = rows_ref.shape
    cols = cols_ref.shape[2]
    bins = defocus_ref.shape[0]
    planes = plane_ref.shape[0]
    half = box // 2
    first = pl.multiple_of(lax.axis_index("img") * owned, owned)
    copies = [
        pltpu.make_async_copy(defocus_hbm, defocus_ref, arrived.at[0]),
        pltpu.make_async_copy(plane_hbm, plane_ref, arrived.at[1]),
        pltpu.make_async_copy(rows_hbm.at[:, pl.ds(first, owned), :], rows_ref, arrived.at[2]),
        pltpu.make_async_copy(cols_hbm, cols_ref, arrived.at[3]),
    ]
    for copy in copies:
        copy.start()
    for copy in copies:
        copy.wait()
    share_plane = iota((planes * CLASSES, poses * bins), 0) // CLASSES
    share_pose = iota((planes * CLASSES, poses * bins), 1) // bins
    share = jnp.zeros((planes * CLASSES, poses * bins), f32)
    for p in range(poses):
        for z in range(planes):
            share = jnp.where((share_plane == z) & (share_pose == p), plane_ref[z, p], share)
    share_ref[...] = share

    bin_row = iota((bins, box), 0)
    sub_defocus = jnp.zeros((bins, box), f32)
    for b in range(bins):
        sub_defocus = jnp.where(bin_row == b, defocus_ref[b], sub_defocus)
    freq = iota((bins, box), 1)
    freq = jnp.where(freq < half, freq, box - freq).astype(f32)
    turns_x = sub_defocus * (freq * freq * (1.0 / (half * half)))
    turns_y = turns_x + ctf_phase / math.pi
    ones = jnp.ones((bins, box), f32)
    wave_y = jnp.concatenate(
        [0.5 * ones, -0.5 * turns_sine(turns_y + 0.25), 0.5 * turns_sine(turns_y)], 0
    )
    wave_x = jnp.concatenate([ones, turns_sine(turns_x + 0.25), turns_sine(turns_x)], 0)
    y_high, y_low = split_two(wave_y)
    x_high, x_low = split_two(wave_x)
    rows_sq = rows_ref[...].reshape(poses * owned, box).astype(f32)
    rows_sq = (rows_sq * rows_sq).astype(bf16)
    u = dot(y_high, rows_sq, ((1,), (1,))) + dot(y_low, rows_sq, ((1,), (1,)))
    for p in range(poses):
        cols_sq = cols_ref[p].astype(f32)
        cols_sq = (cols_sq * cols_sq).astype(bf16)
        v = dot(x_high, cols_sq) + dot(x_low, cols_sq)
        for r in range(owned):
            column = u[:, p * owned + r : p * owned + r + 1]
            product = v * column
            weight = product[:bins] + product[bins : 2 * bins] + product[2 * bins :]
            high, low = split_two(weight)
            high_ref[p * bins : (p + 1) * bins, r * cols : (r + 1) * cols] = high
            low_ref[p * bins : (p + 1) * bins, r * cols : (r + 1) * cols] = low


def own_ridges(defocus, plane_weight, rows_table, cols_table, owned):
    poses, _, box = rows_table.shape
    cols = cols_table.shape[2]
    bins = defocus.shape[0]
    any_place = pl.BlockSpec(memory_space=pl.ANY)
    vmem = pl.BlockSpec(memory_space=pltpu.VMEM)
    planes = plane_weight.T
    table = jax.ShapeDtypeStruct((poses * bins, owned * cols), bf16)
    return pl.pallas_call(
        ridge_kernel,
        out_shape=[table, table, jax.ShapeDtypeStruct((planes.shape[0] * CLASSES, poses * bins), f32)],
        in_specs=[any_place] * 4,
        out_specs=[vmem] * 3,
        scratch_shapes=[
            pltpu.SMEM(defocus.shape, f32),
            pltpu.SMEM(planes.shape, f32),
            pltpu.VMEM((poses, owned, box), bf16),
            pltpu.VMEM(cols_table.shape, bf16),
            pltpu.SemaphoreType.DMA((4,)),
        ],
        compiler_params=pltpu.CompilerParams(vmem_limit_bytes=16 * 1024 * 1024),
        cost_estimate=pl.CostEstimate(
            flops=2 * poses * 1000 * 128 * 256, bytes_accessed=2 * 1024 * 1024, transcendentals=0
        ),
    )(defocus, planes, rows_table, cols_table)


def middle_kernel(x_keep, z_keep, x_came, *refs):
    rounds = x_keep.shape[0]
    z_came, outs = refs[: rounds - 1], refs[rounds - 1 :]
    x_own, z_own, z_send = outs[:3]
    x_own[...] = x_keep[0] + x_came[0].astype(f32)
    for k in range(1, rounds):
        outs[2 + k][...] = (x_keep[k] + x_came[k].astype(f32)).astype(bf16)
    for side in range(2):
        value = z_keep[side]
        for came in z_came:
            value = value + came[side].astype(f32)
        if side == 0:
            z_own[...] = value
        else:
            z_send[...] = value.astype(bf16)


def middle(x_keep, z_keep, x_came, z_came):
    rounds, x_slots, owned, wide = x_keep.shape
    vmem = pl.BlockSpec(memory_space=pltpu.VMEM)
    x_piece, z_piece = x_keep.shape[1:], z_keep.shape[1:]
    out_shape = [pltpu.VMEM(x_piece, f32), pltpu.VMEM(z_piece, f32), pltpu.VMEM(z_piece, bf16)]
    out_shape += [pltpu.VMEM(x_piece, bf16)] * (rounds - 1)
    return pl.pallas_call(
        middle_kernel,
        out_shape=out_shape,
        in_specs=[vmem] * (3 + len(z_came)),
        out_specs=[vmem] * len(out_shape),
        compiler_params=pltpu.CompilerParams(vmem_limit_bytes=16 * 1024 * 1024),
        cost_estimate=pl.CostEstimate(flops=1000000, bytes_accessed=4 * 1024 * 1024, transcendentals=0),
    )(x_keep, z_keep, x_came, *z_came)


def finish_kernel(high_ref, low_ref, share_ref, x_own, z_own, z_came, *refs):
    x_came, out_ref, ridge_ref = refs[:-2], refs[-2], refs[-1]
    slots, pairs = share_ref.shape
    owned, _, cols = ridge_ref.shape
    planes = slots // CLASSES
    first = z_own.shape[0]

    def summed(s):
        if s < first:
            return z_own[s] + z_came[s].astype(f32)
        value = x_own[s - first]
        for part in x_came:
            value = value + part[s - first].astype(f32)
        return value

    counts = summed(slots)[:CLASSES, :pairs]
    scaled = jnp.concatenate([counts] * planes, 0) * share_ref[...]
    c_high, c_low = split_two(scaled)
    weight = (
        dot(c_high, high_ref[...]) + dot(c_low, high_ref[...]) + dot(c_high, low_ref[...])
    )
    ridge = 1.0 / (weight + wiener_ridge)
    for r in range(owned):
        ridge_ref[r] = ridge[:, r * cols : (r + 1) * cols]
    for s in range(slots):
        value = summed(s)
        factor = ridge_ref[:, s, :]
        place = (s % CLASSES) * planes + s // CLASSES
        out_ref[:, 2 * place, :] = value[:, :cols] * factor
        out_ref[:, 2 * place + 1, :] = value[:, cols:] * factor


def finish(tables, x_own, z_own, z_came, x_came):
    slots = tables[2].shape[0]
    _, owned, wide = x_own.shape
    cols = wide // 2
    vmem = pl.BlockSpec(memory_space=pltpu.VMEM)
    return pl.pallas_call(
        finish_kernel,
        out_shape=jax.ShapeDtypeStruct((owned, 2 * slots, cols), f32),
        in_specs=[vmem] * (6 + len(x_came)),
        out_specs=vmem,
        scratch_shapes=[pltpu.VMEM((owned, slots, cols), f32)],
        compiler_params=pltpu.CompilerParams(vmem_limit_bytes=16 * 1024 * 1024),
        cost_estimate=pl.CostEstimate(
            flops=8 * slots * owned * cols, bytes_accessed=8 * 1024 * 1024 // 4, transcendentals=0
        ),
    )(*tables, x_own, z_own, z_came, *x_came)


def squared_table(weight_table):
    wide_table = weight_table.astype(f32)
    return (wide_table * wide_table).astype(bf16)


def weight_totals(class_index, pose_index, defocus_bin, defocus, rows_table, cols_table, plane_weight, first_row, owned):
    box = rows_table.shape[2]
    poses = rows_table.shape[0]
    bins = defocus.shape[0]
    half = box // 2
    exact = lax.Precision.HIGHEST
    code = (class_index[:, 0] * poses + pose_index) * bins + defocus_bin
    codes = lax.all_gather(code, "img", tiled=True)
    hits = (codes[:, None] == jnp.arange(CLASSES * poses * bins, dtype=jnp.int32)).astype(f32)
    counts = jnp.sum(hits, 0).reshape(CLASSES, poses, bins)
    place = jnp.arange(box, dtype=jnp.int32)
    freq = jnp.where(place < half, place, place - box).astype(f32)
    turns = defocus[:, None] * (freq * freq)[None, :] * (1.0 / (half * half))
    turns_y = turns + ctf_phase / math.pi
    ones = jnp.ones_like(turns)
    wave_y = jnp.stack([0.5 * ones, -0.5 * turns_sine(turns_y + 0.25), 0.5 * turns_sine(turns_y)])
    wave_x = jnp.stack([ones, turns_sine(turns + 0.25), turns_sine(turns)])
    rows_own = lax.dynamic_slice_in_dim(rows_table, first_row, owned, 1)
    u = jnp.einsum("pry,mby->pmbr", squared_table(rows_own).astype(f32), wave_y, precision=exact)
    v = jnp.einsum("pxj,mbx->pmbj", squared_table(cols_table).astype(f32), wave_x, precision=exact)
    weight = counts[:, None] * plane_weight.T[None, :, :, None]
    left = weight[:, :, :, None, :, None] * u[None, None]
    return jnp.einsum("czpmbr,pmbj->rczj", left, v, precision=exact)


def by_rounds(images, class_index, pose_index, defocus_bin, defocus, rows_table, cols_table, plane_weight):
    members = lax.axis_size("img")
    rounds = members // 2
    rows = rows_table.shape[1]
    planes = plane_weight.shape[1]
    cols = cols_table.shape[2]
    owned = rows // members
    outs = own_totals(
        images, class_index, pose_index, defocus_bin, defocus, rows_table, cols_table, plane_weight, rounds
    )
    x_send, x_keep, z_keep = outs[:3]
    z_sends = dict(zip(range(1, rounds), outs[3:]))

    def along_x(value):
        return lax.ppermute(value, "img", [(i, i ^ 1) for i in range(members)])

    def along_z(value, k):
        return lax.ppermute(value, "img", [(i, i ^ (2 * k)) for i in range(members)])

    order = [2, 3, 1] if rounds == 4 else list(range(1, rounds))
    x_came = along_x(x_send)
    z_came = [along_z(z_sends[k], k) for k in order]
    tables = own_ridges(defocus, plane_weight, rows_table, cols_table, owned)
    x_keep, tables = lax.optimization_barrier((x_keep, tables))
    x_own, z_own, z_send, *x_sends = middle(x_keep, z_keep, x_came, z_came)
    x_came = [along_z(x_sends[k - 1], k) for k in order]
    z_came = along_x(z_send)
    out = finish(tables, x_own, z_own, z_came, x_came)
    return out.reshape(owned, CLASSES, planes, 2, cols)


def by_scatter(images, class_index, pose_index, defocus_bin, defocus, rows_table, cols_table, plane_weight):
    rows = rows_table.shape[1]
    cols = cols_table.shape[2]
    planes = plane_weight.shape[1]
    members = lax.axis_size("img")
    owned = rows // members
    (totals,) = own_totals(
        images, class_index, pose_index, defocus_bin, defocus, rows_table, cols_table, plane_weight, 0
    )
    slots = totals.shape[0]
    totals = totals.reshape(slots, members, owned, 2 * cols).transpose(1, 0, 2, 3)
    own = lax.psum_scatter(totals, "img", scatter_dimension=0, tiled=False)
    weight = weight_totals(
        class_index, pose_index, defocus_bin, defocus, rows_table, cols_table, plane_weight,
        lax.axis_index("img") * owned, owned,
    )
    own = own.astype(f32).reshape(planes, CLASSES, owned, 2, cols).transpose(2, 1, 0, 3, 4)
    return own / (weight[:, :, :, None, :] + wiener_ridge)


def body(*arrays):
    rows = arrays[5].shape[1]
    members = lax.axis_size("img")
    images = members * arrays[0].shape[0]
    small = members > 1 and members & (members - 1) == 0 and images <= 256 and rows % (16 * members) == 0
    return (by_rounds if small else by_scatter)(*arrays)


def solution(mesh):
    placed = (
        P(("groups", "img"), None, None),
        P(("groups", "img"), None),
        P(("groups", "img")),
        P(("groups", "img")),
        P(),
        P(),
        P(None, None, "slab"),
        P(),
    )
    return jax.shard_map(
        body,
        mesh=mesh,
        in_specs=placed,
        out_specs=P("img", "groups", None, None, "slab"),
        check_vma=False,
    )
```

```python
import functools
import math

import jax
import jax.numpy as jnp
import numpy as np
from jax import lax
from jax.experimental import pallas as pl
from jax.experimental.pallas import tpu as pltpu
from jax.sharding import PartitionSpec as P

CLASSES = 8

wiener_ridge = 1.0
ctf_phase = 0.1
f32 = jnp.float32
bf16 = jnp.bfloat16


def packed_dft(box, sine_sign):
    half = box // 2
    k = np.concatenate([np.arange(half), [half], np.arange(1, half)])
    angle = (k[:, None] * np.arange(box)[None, :] % box) * (2.0 * math.pi / box)
    table = np.where((np.arange(box) <= half)[:, None], np.cos(angle), sine_sign * np.sin(angle))
    return (table / math.sqrt(box)).astype(np.float32)


def iota(shape, axis):
    return lax.broadcasted_iota(jnp.int32, shape, axis)


def dot(a, b, dims=((1,), (0,))):
    return lax.dot_general(a, b, (dims, ((), ())), preferred_element_type=f32)


def turns_sine(turns):
    return jnp.sin((turns - jnp.round(turns)) * (2.0 * math.pi))


def split_two(value):
    high = value.astype(bf16)
    return high, (value - high.astype(f32)).astype(bf16)


def fold_of(place, half):
    box = 2 * half
    return jnp.where(place <= half, place, box + half - place)


def slices_kernel(
    class_hbm, pose_hbm, bin_hbm, defocus_hbm, plane_hbm,
    dft_hbm, dft_t_hbm, images_hbm, rows_hbm, cols_hbm,
    *refs,
):
    outs, refs = refs[:-SCRATCH], refs[-SCRATCH:]
    (
        class_ref, pose_ref, bin_ref, defocus_ref, plane_ref,
        dft_ref, dft_t_ref, images_ref, rows_ref, cols_ref, arrived,
        rows_fold, cols_fold, wave_y, cos_x, sin_x, half_ref, spec_ref, mix_ref, totals,
    ) = refs
    count, box, _ = images_ref.shape
    half = box // 2
    poses, rows, _ = rows_ref.shape
    cols = cols_ref.shape[2]
    planes = plane_ref.shape[0]

    pairs = (
        (class_hbm, class_ref), (pose_hbm, pose_ref), (bin_hbm, bin_ref),
        (defocus_hbm, defocus_ref), (plane_hbm, plane_ref),
        (dft_hbm, dft_ref), (images_hbm.at[0:GROUP], images_ref.at[0:GROUP]),
        (dft_t_hbm, dft_t_ref), (cols_hbm, cols_ref), (rows_hbm, rows_ref),
    ) + tuple(
        (images_hbm.at[i : i + GROUP], images_ref.at[i : i + GROUP])
        for i in range(GROUP, count, GROUP)
    )
    copies = [
        pltpu.make_async_copy(source, target, arrived.at[n])
        for n, (source, target) in enumerate(pairs)
    ]
    for copy in copies:
        copy.start()

    place = iota((box, box), 0)
    other = iota((box, box), 1)
    folded = fold_of(place, half)
    near = (folded == other).astype(f32).astype(bf16)
    far = (jnp.where(folded == 0, 0, box - folded) == other).astype(f32).astype(bf16)

    for copy in copies[:5]:
        copy.wait()
    tall, lanes = wave_y.shape
    lane = iota((1, lanes), 1)
    sub = iota((count, box), 0)
    lane_defocus = jnp.zeros((1, lanes), f32)
    sub_defocus = jnp.zeros((count, box), f32)
    for i in range(count):
        value = defocus_ref[bin_ref[i]]
        lane_defocus = jnp.where(lane % count == i, value, lane_defocus)
        sub_defocus = jnp.where(sub == i, value, sub_defocus)
    scale = 1.0 / (2 * half * half)
    ky = iota((tall, lanes), 0).astype(f32)
    quarter = jnp.where(lane < count, 0.0, 0.25) + ctf_phase / (2.0 * math.pi)
    wave_y[...] = turns_sine(lane_defocus * (ky * ky * scale) + quarter)
    kx = iota((count, box), 1)
    kx = jnp.where(kx <= half, kx, kx - half).astype(f32)
    turns = sub_defocus * (kx * kx * scale)
    cos_x[...] = -turns_sine(turns + 0.25)
    sin_x[...] = -turns_sine(turns)
    totals[...] = jnp.zeros_like(totals)
    if len(outs) > 1:
        bins = defocus_ref.shape[0]
        count_row = iota((16, 2 * cols), 0)
        count_lane = iota((16, 2 * cols), 1)
        counts = jnp.zeros((16, 2 * cols), f32)
        for i in range(count):
            hit = (count_row == class_ref[i]) & (count_lane == pose_ref[i] * bins + bin_ref[i])
            counts = counts + jnp.where(hit, 1.0, 0.0)
        totals[planes * CLASSES] = jnp.tile(counts, (rows // 16, 1))

    tile = 8
    tile_row = iota((tile, half), 0) == 0
    tile_col = iota((tile, half), 1) == 0
    col_zero = iota((half, half), 1) == 0
    short_row = iota((16, half), 0) == 0
    short_col = iota((16, half), 1) == 0

    def without_row(value):
        return jnp.concatenate([jnp.where(tile_row, 0.0, value[:tile]), value[tile:]], 0)

    def along_rows(i):
        if i % GROUP == 0:
            copies[6 if i == 0 else 9 + i // GROUP].wait()
        half_ref[i % SLOTS] = dot(dft_ref[...], images_ref[i]).astype(bf16)

    def along_columns(i):
        y = dot(half_ref[i % SLOTS], dft_t_ref[...])
        sin_col = jnp.broadcast_to(wave_y[:, i : i + 1], (tall, half))
        cos_col = jnp.broadcast_to(wave_y[:, count + i : count + i + 1], (tall, half))
        near_ctf = sin_col * cos_x[i : i + 1, :half] + cos_col * sin_x[i : i + 1, :half]
        far_ctf = sin_col * cos_x[i : i + 1, half:] + cos_col * sin_x[i : i + 1, half:]
        cc, cs = y[:half, :half], y[:half, half:]
        sc, ss = y[half:, :half], y[half:, half:]
        ss_row = without_row(ss)
        ss_in = jnp.where(col_zero, 0.0, ss_row)
        sc_in = without_row(sc)
        cs_in = jnp.where(col_zero, 0.0, cs)
        near_y, far_y = near_ctf[:half], far_ctf[:half]
        spec = spec_ref.at[i % SLOTS]
        spec[0:half, 0:half] = (near_y * (cc + ss_in)).astype(bf16)
        spec[0:half, half:] = (far_y * jnp.where(col_zero, cs, cc - ss_in)).astype(bf16)
        spec[half:box, 0:half] = (near_y * (sc_in - cs_in)).astype(bf16)
        spec[half:box, half:] = (far_y * jnp.where(col_zero, ss_row, sc_in + cs_in)).astype(bf16)
        sc_top = jnp.broadcast_to(sc[0:1], (16, half))
        ss_top = jnp.broadcast_to(ss[0:1], (16, half))
        ss_top_in = jnp.where(short_col, 0.0, ss_top)
        spec[box : box + 16, 0:half] = (
            near_ctf[half : half + 1] * jnp.where(short_row, sc_top, -ss_top_in)
        ).astype(bf16)
        spec[box : box + 16, half:] = (
            far_ctf[half : half + 1]
            * jnp.where(short_row, jnp.where(short_col, ss_top, sc_top), ss_top_in)
        ).astype(bf16)

    def mix(i):
        mixed = dot(spec_ref[i % SLOTS], cols_fold[pose_ref[i]])
        out = mix_ref.at[i % SLOTS]
        out[0:half, 0:cols] = mixed[:half, :cols].astype(bf16)
        out[0:half, cols:] = mixed[half:box, :cols].astype(bf16)
        top = iota((16, cols), 0) == 0
        real, imag = mixed[:half, cols:], -mixed[half:box, cols:]
        out[half : half + 16, 0:cols] = jnp.where(
            top, mixed[box : box + 1, :cols], real[:16]
        ).astype(bf16)
        out[half : half + 16, cols:] = jnp.where(
            top, mixed[box + 1 : box + 2, :cols], imag[:16]
        ).astype(bf16)
        out[half + 16 :, 0:cols] = real[16:].astype(bf16)
        out[half + 16 :, cols:] = imag[16:].astype(bf16)

    def insert(i):
        pose = pose_ref[i]
        pose_rows = rows_fold[pl.ds(pl.multiple_of(pose * rows, rows), rows), :]
        piece = dot(pose_rows, mix_ref[i % SLOTS])
        for z in range(planes):
            slot = z * CLASSES + class_ref[i]
            totals[slot] += plane_ref[z, pose] * piece

    copies[5].wait()
    along_rows(0)
    copies[7].wait()
    copies[8].wait()
    for p in range(0, poses, 2):
        two = jnp.concatenate([cols_ref[p], cols_ref[p + 1]], 1)
        near_two = dot(near, two).astype(bf16)
        far_two = dot(far, two).astype(bf16)
        cols_fold[p] = jnp.concatenate([near_two[:, :cols], far_two[:, :cols]], 1)
        cols_fold[p + 1] = jnp.concatenate([near_two[:, cols:], far_two[:, cols:]], 1)
    along_rows(1)
    along_columns(0)
    copies[9].wait()
    rows_fold[...] = dot(
        rows_ref[...].reshape(poses * rows, box), near, ((1,), (1,))
    ).astype(bf16)
    for step in range(2, count + 3):
        if step >= 3:
            insert(step - 3)
        if step - 2 < count:
            mix(step - 2)
        if step - 1 < count:
            along_columns(step - 1)
        if step < count:
            along_rows(step)

    if len(outs) == 1:
        outs[0][...] = totals[...].astype(bf16)
        return
    x_send, x_keep, z_keep = outs[:3]
    z_sends = outs[3:]
    rounds, x_slots, owned, _ = x_keep.shape
    me = lax.axis_index("img")
    for k in range(rounds):
        mine = pl.ds(pl.multiple_of((me ^ (2 * k)) * owned, owned), owned)
        theirs = pl.ds(pl.multiple_of((me ^ (2 * k + 1)) * owned, owned), owned)
        x_keep[k] = totals[-x_slots:, mine, :]
        x_send[k] = totals[-x_slots:, theirs, :].astype(bf16)
        z_out = z_keep if k == 0 else z_sends[k - 1]
        z_out[0] = totals[:-x_slots, mine, :].astype(z_out.dtype)
        z_out[1] = totals[:-x_slots, theirs, :].astype(z_out.dtype)


SCRATCH = 20
SLOTS = 3
GROUP = 4
Z_SLOTS = 6


def own_totals(images, class_index, pose_index, defocus_bin, defocus, rows_table, cols_table, plane_weight, turns_round):
    count, box, _ = images.shape
    poses, rows, _ = rows_table.shape
    cols = cols_table.shape[2]
    planes = plane_weight.shape[1]
    slots = CLASSES * planes
    table_y, table_x = packed_dft(box, -1.0), packed_dft(box, 1.0)
    any_place = pl.BlockSpec(memory_space=pl.ANY)
    vmem = pl.BlockSpec(memory_space=pltpu.VMEM)
    lanes = 128 * (-(-2 * count // 128))
    if turns_round == 0:
        out_shape = [jax.ShapeDtypeStruct((slots, rows, 2 * cols), bf16)]
    else:
        slots += 1
        x_piece = (turns_round, slots - Z_SLOTS, rows // (2 * turns_round), 2 * cols)
        z_piece = (2, Z_SLOTS, rows // (2 * turns_round), 2 * cols)
        out_shape = [pltpu.VMEM(x_piece, bf16), pltpu.VMEM(x_piece, f32), pltpu.VMEM(z_piece, f32)]
        out_shape += [pltpu.VMEM(z_piece, bf16)] * (turns_round - 1)
    operands = (
        class_index[:, 0], pose_index, defocus_bin, defocus, plane_weight.T,
        jnp.asarray(table_y, bf16), jnp.asarray(table_x.T.copy(), bf16),
        images, rows_table, cols_table,
    )
    return pl.pallas_call(
        slices_kernel,
        out_shape=out_shape,
        in_specs=[any_place] * 10,
        out_specs=[vmem] * len(out_shape),
        scratch_shapes=[pltpu.SMEM(x.shape, x.dtype) for x in operands[:5]]
        + [pltpu.VMEM(x.shape, x.dtype) for x in operands[5:]]
        + [
            pltpu.SemaphoreType.DMA((9 + count // GROUP,)),
            pltpu.VMEM((poses * rows, box), bf16),
            pltpu.VMEM((poses, box, 2 * cols), bf16),
            pltpu.VMEM((box // 2 + 8, lanes), f32),
            pltpu.VMEM((count, box), f32),
            pltpu.VMEM((count, box), f32),
            pltpu.VMEM((SLOTS, box, box), bf16),
            pltpu.VMEM((SLOTS, box + 16, box), bf16),
            pltpu.VMEM((SLOTS, box, 2 * cols), bf16),
            pltpu.VMEM((slots, rows, 2 * cols), f32),
        ],
        compiler_params=pltpu.CompilerParams(vmem_limit_bytes=VMEM_LIMIT),
        cost_estimate=pl.CostEstimate(
            flops=2 * count * box * box * 1000, bytes_accessed=6 * 1024 * 1024, transcendentals=0
        ),
    )(*operands)


VMEM_LIMIT = 56 * 1024 * 1024


def ridge_kernel(defocus_hbm, plane_hbm, rows_hbm, cols_hbm, high_ref, low_ref, share_ref, *refs):
    defocus_ref, plane_ref, rows_ref, cols_ref, arrived = refs
    poses, owned, box = rows_ref.shape
    cols = cols_ref.shape[2]
    bins = defocus_ref.shape[0]
    planes = plane_ref.shape[0]
    half = box // 2
    first = pl.multiple_of(lax.axis_index("img") * owned, owned)
    copies = [
        pltpu.make_async_copy(defocus_hbm, defocus_ref, arrived.at[0]),
        pltpu.make_async_copy(plane_hbm, plane_ref, arrived.at[1]),
        pltpu.make_async_copy(rows_hbm.at[:, pl.ds(first, owned), :], rows_ref, arrived.at[2]),
        pltpu.make_async_copy(cols_hbm, cols_ref, arrived.at[3]),
    ]
    for copy in copies:
        copy.start()
    for copy in copies:
        copy.wait()
    share_plane = iota((planes * CLASSES, poses * bins), 0) // CLASSES
    share_pose = iota((planes * CLASSES, poses * bins), 1) // bins
    share = jnp.zeros((planes * CLASSES, poses * bins), f32)
    for p in range(poses):
        for z in range(planes):
            share = jnp.where((share_plane == z) & (share_pose == p), plane_ref[z, p], share)
    share_ref[...] = share

    bin_row = iota((bins, box), 0)
    sub_defocus = jnp.zeros((bins, box), f32)
    for b in range(bins):
        sub_defocus = jnp.where(bin_row == b, defocus_ref[b], sub_defocus)
    freq = iota((bins, box), 1)
    freq = jnp.where(freq < half, freq, box - freq).astype(f32)
    turns_x = sub_defocus * (freq * freq * (1.0 / (half * half)))
    turns_y = turns_x + ctf_phase / math.pi
    ones = jnp.ones((bins, box), f32)
    wave_y = jnp.concatenate(
        [0.5 * ones, -0.5 * turns_sine(turns_y + 0.25), 0.5 * turns_sine(turns_y)], 0
    )
    wave_x = jnp.concatenate([ones, turns_sine(turns_x + 0.25), turns_sine(turns_x)], 0)
    y_high, y_low = split_two(wave_y)
    x_high, x_low = split_two(wave_x)
    rows_sq = rows_ref[...].reshape(poses * owned, box).astype(f32)
    rows_sq = (rows_sq * rows_sq).astype(bf16)
    u = dot(y_high, rows_sq, ((1,), (1,))) + dot(y_low, rows_sq, ((1,), (1,)))
    for p in range(poses):
        cols_sq = cols_ref[p].astype(f32)
        cols_sq = (cols_sq * cols_sq).astype(bf16)
        v = dot(x_high, cols_sq) + dot(x_low, cols_sq)
        for r in range(owned):
            column = u[:, p * owned + r : p * owned + r + 1]
            product = v * column
            weight = product[:bins] + product[bins : 2 * bins] + product[2 * bins :]
            high, low = split_two(weight)
            high_ref[p * bins : (p + 1) * bins, r * cols : (r + 1) * cols] = high
            low_ref[p * bins : (p + 1) * bins, r * cols : (r + 1) * cols] = low


def own_ridges(defocus, plane_weight, rows_table, cols_table, owned):
    poses, _, box = rows_table.shape
    cols = cols_table.shape[2]
    bins = defocus.shape[0]
    any_place = pl.BlockSpec(memory_space=pl.ANY)
    vmem = pl.BlockSpec(memory_space=pltpu.VMEM)
    planes = plane_weight.T
    table = jax.ShapeDtypeStruct((poses * bins, owned * cols), bf16)
    return pl.pallas_call(
        ridge_kernel,
        out_shape=[table, table, jax.ShapeDtypeStruct((planes.shape[0] * CLASSES, poses * bins), f32)],
        in_specs=[any_place] * 4,
        out_specs=[vmem] * 3,
        scratch_shapes=[
            pltpu.SMEM(defocus.shape, f32),
            pltpu.SMEM(planes.shape, f32),
            pltpu.VMEM((poses, owned, box), bf16),
            pltpu.VMEM(cols_table.shape, bf16),
            pltpu.SemaphoreType.DMA((4,)),
        ],
        compiler_params=pltpu.CompilerParams(vmem_limit_bytes=16 * 1024 * 1024),
        cost_estimate=pl.CostEstimate(
            flops=2 * poses * 1000 * 128 * 256, bytes_accessed=2 * 1024 * 1024, transcendentals=0
        ),
    )(defocus, planes, rows_table, cols_table)


def middle_kernel(x_keep, z_keep, x_came, *refs):
    rounds = x_keep.shape[0]
    z_came, outs = refs[: rounds - 1], refs[rounds - 1 :]
    x_own, z_own, z_send = outs[:3]
    x_own[...] = x_keep[0] + x_came[0].astype(f32)
    for k in range(1, rounds):
        outs[2 + k][...] = (x_keep[k] + x_came[k].astype(f32)).astype(bf16)
    for side in range(2):
        value = z_keep[side]
        for came in z_came:
            value = value + came[side].astype(f32)
        if side == 0:
            z_own[...] = value
        else:
            z_send[...] = value.astype(bf16)


def middle(x_keep, z_keep, x_came, z_came):
    rounds, x_slots, owned, wide = x_keep.shape
    vmem = pl.BlockSpec(memory_space=pltpu.VMEM)
    x_piece, z_piece = x_keep.shape[1:], z_keep.shape[1:]
    out_shape = [pltpu.VMEM(x_piece, f32), pltpu.VMEM(z_piece, f32), pltpu.VMEM(z_piece, bf16)]
    out_shape += [pltpu.VMEM(x_piece, bf16)] * (rounds - 1)
    return pl.pallas_call(
        middle_kernel,
        out_shape=out_shape,
        in_specs=[vmem] * (3 + len(z_came)),
        out_specs=[vmem] * len(out_shape),
        compiler_params=pltpu.CompilerParams(vmem_limit_bytes=16 * 1024 * 1024),
        cost_estimate=pl.CostEstimate(flops=1000000, bytes_accessed=4 * 1024 * 1024, transcendentals=0),
    )(x_keep, z_keep, x_came, *z_came)


def finish_kernel(high_ref, low_ref, share_ref, x_own, z_own, z_came, *refs):
    x_came, out_ref, ridge_ref = refs[:-2], refs[-2], refs[-1]
    slots, pairs = share_ref.shape
    owned, _, cols = ridge_ref.shape
    planes = slots // CLASSES
    first = z_own.shape[0]

    def summed(s):
        if s < first:
            return z_own[s] + z_came[s].astype(f32)
        value = x_own[s - first]
        for part in x_came:
            value = value + part[s - first].astype(f32)
        return value

    counts = summed(slots)[:CLASSES, :pairs]
    scaled = jnp.concatenate([counts] * planes, 0) * share_ref[...]
    c_high, c_low = split_two(scaled)
    weight = (
        dot(c_high, high_ref[...]) + dot(c_low, high_ref[...]) + dot(c_high, low_ref[...])
    )
    ridge = 1.0 / (weight + wiener_ridge)
    for r in range(owned):
        ridge_ref[r] = ridge[:, r * cols : (r + 1) * cols]
    for s in range(slots):
        value = summed(s)
        factor = ridge_ref[:, s, :]
        place = (s % CLASSES) * planes + s // CLASSES
        out_ref[:, 2 * place, :] = value[:, :cols] * factor
        out_ref[:, 2 * place + 1, :] = value[:, cols:] * factor


def finish(tables, x_own, z_own, z_came, x_came):
    slots = tables[2].shape[0]
    _, owned, wide = x_own.shape
    cols = wide // 2
    vmem = pl.BlockSpec(memory_space=pltpu.VMEM)
    return pl.pallas_call(
        finish_kernel,
        out_shape=jax.ShapeDtypeStruct((owned, 2 * slots, cols), f32),
        in_specs=[vmem] * (6 + len(x_came)),
        out_specs=vmem,
        scratch_shapes=[pltpu.VMEM((owned, slots, cols), f32)],
        compiler_params=pltpu.CompilerParams(vmem_limit_bytes=16 * 1024 * 1024),
        cost_estimate=pl.CostEstimate(
            flops=8 * slots * owned * cols, bytes_accessed=8 * 1024 * 1024 // 4, transcendentals=0
        ),
    )(*tables, x_own, z_own, z_came, *x_came)


def squared_table(weight_table):
    wide_table = weight_table.astype(f32)
    return (wide_table * wide_table).astype(bf16)


def weight_totals(class_index, pose_index, defocus_bin, defocus, rows_table, cols_table, plane_weight, first_row, owned):
    box = rows_table.shape[2]
    poses = rows_table.shape[0]
    bins = defocus.shape[0]
    half = box // 2
    exact = lax.Precision.HIGHEST
    code = (class_index[:, 0] * poses + pose_index) * bins + defocus_bin
    codes = lax.all_gather(code, "img", tiled=True)
    hits = (codes[:, None] == jnp.arange(CLASSES * poses * bins, dtype=jnp.int32)).astype(f32)
    counts = jnp.sum(hits, 0).reshape(CLASSES, poses, bins)
    place = jnp.arange(box, dtype=jnp.int32)
    freq = jnp.where(place < half, place, place - box).astype(f32)
    turns = defocus[:, None] * (freq * freq)[None, :] * (1.0 / (half * half))
    turns_y = turns + ctf_phase / math.pi
    ones = jnp.ones_like(turns)
    wave_y = jnp.stack([0.5 * ones, -0.5 * turns_sine(turns_y + 0.25), 0.5 * turns_sine(turns_y)])
    wave_x = jnp.stack([ones, turns_sine(turns + 0.25), turns_sine(turns)])
    rows_own = lax.dynamic_slice_in_dim(rows_table, first_row, owned, 1)
    u = jnp.einsum("pry,mby->pmbr", squared_table(rows_own).astype(f32), wave_y, precision=exact)
    v = jnp.einsum("pxj,mbx->pmbj", squared_table(cols_table).astype(f32), wave_x, precision=exact)
    weight = counts[:, None] * plane_weight.T[None, :, :, None]
    left = weight[:, :, :, None, :, None] * u[None, None]
    return jnp.einsum("czpmbr,pmbj->rczj", left, v, precision=exact)


def by_rounds(images, class_index, pose_index, defocus_bin, defocus, rows_table, cols_table, plane_weight):
    members = lax.axis_size("img")
    rounds = members // 2
    rows = rows_table.shape[1]
    planes = plane_weight.shape[1]
    cols = cols_table.shape[2]
    owned = rows // members
    outs = own_totals(
        images, class_index, pose_index, defocus_bin, defocus, rows_table, cols_table, plane_weight, rounds
    )
    x_send, x_keep, z_keep = outs[:3]
    z_sends = dict(zip(range(1, rounds), outs[3:]))

    def along_x(value):
        return lax.ppermute(value, "img", [(i, i ^ 1) for i in range(members)])

    def along_z(value, k):
        return lax.ppermute(value, "img", [(i, i ^ (2 * k)) for i in range(members)])

    order = [2, 3, 1] if rounds == 4 else list(range(1, rounds))
    z_came = [along_z(z_sends[order[0]], order[0])]
    x_came = along_x(x_send)
    z_came += [along_z(z_sends[k], k) for k in order[1:]]
    tables = own_ridges(defocus, plane_weight, rows_table, cols_table, owned)
    x_keep, tables = lax.optimization_barrier((x_keep, tables))
    x_own, z_own, z_send, *x_sends = middle(x_keep, z_keep, x_came, z_came)
    x_came = [along_z(x_sends[k - 1], k) for k in order]
    z_came = along_x(z_send)
    out = finish(tables, x_own, z_own, z_came, x_came)
    return out.reshape(owned, CLASSES, planes, 2, cols)


def by_scatter(images, class_index, pose_index, defocus_bin, defocus, rows_table, cols_table, plane_weight):
    rows = rows_table.shape[1]
    cols = cols_table.shape[2]
    planes = plane_weight.shape[1]
    members = lax.axis_size("img")
    owned = rows // members
    (totals,) = own_totals(
        images, class_index, pose_index, defocus_bin, defocus, rows_table, cols_table, plane_weight, 0
    )
    slots = totals.shape[0]
    totals = totals.reshape(slots, members, owned, 2 * cols).transpose(1, 0, 2, 3)
    own = lax.psum_scatter(totals, "img", scatter_dimension=0, tiled=False)
    weight = weight_totals(
        class_index, pose_index, defocus_bin, defocus, rows_table, cols_table, plane_weight,
        lax.axis_index("img") * owned, owned,
    )
    own = own.astype(f32).reshape(planes, CLASSES, owned, 2, cols).transpose(2, 1, 0, 3, 4)
    return own / (weight[:, :, :, None, :] + wiener_ridge)


def body(*arrays):
    rows = arrays[5].shape[1]
    members = lax.axis_size("img")
    images = members * arrays[0].shape[0]
    small = members > 1 and members & (members - 1) == 0 and images <= 256 and rows % (16 * members) == 0
    return (by_rounds if small else by_scatter)(*arrays)


def solution(mesh):
    placed = (
        P(("groups", "img"), None, None),
        P(("groups", "img"), None),
        P(("groups", "img")),
        P(("groups", "img")),
        P(),
        P(),
        P(None, None, "slab"),
        P(),
    )
    return jax.shard_map(
        body,
        mesh=mesh,
        in_specs=placed,
        out_specs=P("img", "groups", None, None, "slab"),
        check_vma=False,
    )
```

```python
import functools
import math

import jax
import jax.numpy as jnp
import numpy as np
from jax import lax
from jax.experimental import pallas as pl
from jax.experimental.pallas import tpu as pltpu
from jax.sharding import PartitionSpec as P

CLASSES = 8

wiener_ridge = 1.0
ctf_phase = 0.1
f32 = jnp.float32
bf16 = jnp.bfloat16


def packed_dft(box, sine_sign):
    half = box // 2
    k = np.concatenate([np.arange(half), [half], np.arange(1, half)])
    angle = (k[:, None] * np.arange(box)[None, :] % box) * (2.0 * math.pi / box)
    table = np.where((np.arange(box) <= half)[:, None], np.cos(angle), sine_sign * np.sin(angle))
    return (table / math.sqrt(box)).astype(np.float32)


def iota(shape, axis):
    return lax.broadcasted_iota(jnp.int32, shape, axis)


def dot(a, b, dims=((1,), (0,))):
    return lax.dot_general(a, b, (dims, ((), ())), preferred_element_type=f32)


def turns_sine(turns):
    return jnp.sin((turns - jnp.round(turns)) * (2.0 * math.pi))


def split_two(value):
    high = value.astype(bf16)
    return high, (value - high.astype(f32)).astype(bf16)


def fold_of(place, half):
    box = 2 * half
    return jnp.where(place <= half, place, box + half - place)


def slices_kernel(
    class_hbm, pose_hbm, bin_hbm, defocus_hbm, plane_hbm,
    dft_hbm, dft_t_hbm, images_hbm, rows_hbm, cols_hbm,
    *refs,
):
    outs, refs = refs[:-SCRATCH], refs[-SCRATCH:]
    (
        class_ref, pose_ref, bin_ref, defocus_ref, plane_ref,
        dft_ref, dft_t_ref, images_ref, rows_ref, cols_ref, arrived,
        rows_fold, cols_fold, wave_y, cos_x, sin_x, half_ref, spec_ref, mix_ref, totals,
    ) = refs
    count, box, _ = images_ref.shape
    half = box // 2
    poses, rows, _ = rows_ref.shape
    cols = cols_ref.shape[2]
    planes = plane_ref.shape[0]

    pairs = (
        (class_hbm, class_ref), (pose_hbm, pose_ref), (bin_hbm, bin_ref),
        (defocus_hbm, defocus_ref), (plane_hbm, plane_ref),
        (dft_hbm, dft_ref), (images_hbm.at[0:GROUP], images_ref.at[0:GROUP]),
        (dft_t_hbm, dft_t_ref), (cols_hbm, cols_ref), (rows_hbm, rows_ref),
    ) + tuple(
        (images_hbm.at[i : i + GROUP], images_ref.at[i : i + GROUP])
        for i in range(GROUP, count, GROUP)
    )
    copies = [
        pltpu.make_async_copy(source, target, arrived.at[n])
        for n, (source, target) in enumerate(pairs)
    ]
    for copy in copies:
        copy.start()

    place = iota((box, box), 0)
    other = iota((box, box), 1)
    folded = fold_of(place, half)
    near = (folded == other).astype(f32).astype(bf16)
    far = (jnp.where(folded == 0, 0, box - folded) == other).astype(f32).astype(bf16)

    for copy in copies[:5]:
        copy.wait()
    tall, lanes = wave_y.shape
    lane = iota((1, lanes), 1)
    sub = iota((count, box), 0)
    lane_defocus = jnp.zeros((1, lanes), f32)
    sub_defocus = jnp.zeros((count, box), f32)
    for i in range(count):
        value = defocus_ref[bin_ref[i]]
        lane_defocus = jnp.where(lane % count == i, value, lane_defocus)
        sub_defocus = jnp.where(sub == i, value, sub_defocus)
    scale = 1.0 / (2 * half * half)
    ky = iota((tall, lanes), 0).astype(f32)
    quarter = jnp.where(lane < count, 0.0, 0.25) + ctf_phase / (2.0 * math.pi)
    wave_y[...] = turns_sine(lane_defocus * (ky * ky * scale) + quarter)
    kx = iota((count, box), 1)
    kx = jnp.where(kx <= half, kx, kx - half).astype(f32)
    turns = sub_defocus * (kx * kx * scale)
    cos_x[...] = -turns_sine(turns + 0.25)
    sin_x[...] = -turns_sine(turns)
    totals[...] = jnp.zeros_like(totals)
    if len(outs) > 1:
        bins = defocus_ref.shape[0]
        count_row = iota((16, 2 * cols), 0)
        count_lane = iota((16, 2 * cols), 1)
        counts = jnp.zeros((16, 2 * cols), f32)
        for i in range(count):
            hit = (count_row == class_ref[i]) & (count_lane == pose_ref[i] * bins + bin_ref[i])
            counts = counts + jnp.where(hit, 1.0, 0.0)
        totals[planes * CLASSES] = jnp.tile(counts, (rows // 16, 1))

    tile = 8
    tile_row = iota((tile, half), 0) == 0
    tile_col = iota((tile, half), 1) == 0
    col_zero = iota((half, half), 1) == 0
    short_row = iota((16, half), 0) == 0
    short_col = iota((16, half), 1) == 0

    def without_row(value):
        return jnp.concatenate([jnp.where(tile_row, 0.0, value[:tile]), value[tile:]], 0)

    def along_rows(i):
        if i % GROUP == 0:
            copies[6 if i == 0 else 9 + i // GROUP].wait()
        half_ref[i % SLOTS] = dot(dft_ref[...], images_ref[i]).astype(bf16)

    def along_columns(i):
        y = dot(half_ref[i % SLOTS], dft_t_ref[...])
        sin_col = jnp.broadcast_to(wave_y[:, i : i + 1], (tall, half))
        cos_col = jnp.broadcast_to(wave_y[:, count + i : count + i + 1], (tall, half))
        near_ctf = sin_col * cos_x[i : i + 1, :half] + cos_col * sin_x[i : i + 1, :half]
        far_ctf = sin_col * cos_x[i : i + 1, half:] + cos_col * sin_x[i : i + 1, half:]
        cc, cs = y[:half, :half], y[:half, half:]
        sc, ss = y[half:, :half], y[half:, half:]
        ss_row = without_row(ss)
        ss_in = jnp.where(col_zero, 0.0, ss_row)
        sc_in = without_row(sc)
        cs_in = jnp.where(col_zero, 0.0, cs)
        near_y, far_y = near_ctf[:half], far_ctf[:half]
        spec = spec_ref.at[i % SLOTS]
        spec[0:half, 0:half] = (near_y * (cc + ss_in)).astype(bf16)
        spec[0:half, half:] = (far_y * jnp.where(col_zero, cs, cc - ss_in)).astype(bf16)
        spec[half:box, 0:half] = (near_y * (sc_in - cs_in)).astype(bf16)
        spec[half:box, half:] = (far_y * jnp.where(col_zero, ss_row, sc_in + cs_in)).astype(bf16)
        sc_top = jnp.broadcast_to(sc[0:1], (16, half))
        ss_top = jnp.broadcast_to(ss[0:1], (16, half))
        ss_top_in = jnp.where(short_col, 0.0, ss_top)
        spec[box : box + 16, 0:half] = (
            near_ctf[half : half + 1] * jnp.where(short_row, sc_top, -ss_top_in)
        ).astype(bf16)
        spec[box : box + 16, half:] = (
            far_ctf[half : half + 1]
            * jnp.where(short_row, jnp.where(short_col, ss_top, sc_top), ss_top_in)
        ).astype(bf16)

    def mix(i):
        mixed = dot(spec_ref[i % SLOTS], cols_fold[pose_ref[i]])
        out = mix_ref.at[i % SLOTS]
        out[0:half, 0:cols] = mixed[:half, :cols].astype(bf16)
        out[0:half, cols:] = mixed[half:box, :cols].astype(bf16)
        top = iota((16, cols), 0) == 0
        real, imag = mixed[:half, cols:], -mixed[half:box, cols:]
        out[half : half + 16, 0:cols] = jnp.where(
            top, mixed[box : box + 1, :cols], real[:16]
        ).astype(bf16)
        out[half : half + 16, cols:] = jnp.where(
            top, mixed[box + 1 : box + 2, :cols], imag[:16]
        ).astype(bf16)
        out[half + 16 :, 0:cols] = real[16:].astype(bf16)
        out[half + 16 :, cols:] = imag[16:].astype(bf16)

    def insert(i):
        pose = pose_ref[i]
        pose_rows = rows_fold[pl.ds(pl.multiple_of(pose * rows, rows), rows), :]
        piece = dot(pose_rows, mix_ref[i % SLOTS])
        for z in range(planes):
            slot = z * CLASSES + class_ref[i]
            totals[slot] += plane_ref[z, pose] * piece

    copies[5].wait()
    along_rows(0)
    copies[7].wait()
    copies[8].wait()
    for p in range(0, poses, 2):
        two = jnp.concatenate([cols_ref[p], cols_ref[p + 1]], 1)
        near_two = dot(near, two).astype(bf16)
        far_two = dot(far, two).astype(bf16)
        cols_fold[p] = jnp.concatenate([near_two[:, :cols], far_two[:, :cols]], 1)
        cols_fold[p + 1] = jnp.concatenate([near_two[:, cols:], far_two[:, cols:]], 1)
    along_rows(1)
    along_columns(0)
    copies[9].wait()
    rows_fold[...] = dot(
        rows_ref[...].reshape(poses * rows, box), near, ((1,), (1,))
    ).astype(bf16)
    for step in range(2, count + 3):
        if step >= 3:
            insert(step - 3)
        if step - 2 < count:
            mix(step - 2)
        if step - 1 < count:
            along_columns(step - 1)
        if step < count:
            along_rows(step)

    if len(outs) == 1:
        outs[0][...] = totals[...].astype(bf16)
        return
    far_send, far_keep, near_send, near_keep, z_keep = outs[:5]
    z_sends = outs[5:]
    _, x_slots, owned, _ = near_keep.shape
    rounds = len(z_sends) + 1
    me = lax.axis_index("img")
    near = near_keep.shape[0]
    for k in range(rounds):
        mine = pl.ds(pl.multiple_of((me ^ (2 * k)) * owned, owned), owned)
        theirs = pl.ds(pl.multiple_of((me ^ (2 * k + 1)) * owned, owned), owned)
        keep, send, n = (near_keep, near_send, k) if k < near else (far_keep, far_send, k - near)
        keep[n] = totals[-x_slots:, mine, :]
        send[n] = totals[-x_slots:, theirs, :].astype(bf16)
        z_out = z_keep if k == 0 else z_sends[k - 1]
        z_out[0] = totals[:-x_slots, mine, :].astype(z_out.dtype)
        z_out[1] = totals[:-x_slots, theirs, :].astype(z_out.dtype)


SCRATCH = 20
SLOTS = 3
GROUP = 4
Z_SLOTS = 3


def own_totals(images, class_index, pose_index, defocus_bin, defocus, rows_table, cols_table, plane_weight, turns_round):
    count, box, _ = images.shape
    poses, rows, _ = rows_table.shape
    cols = cols_table.shape[2]
    planes = plane_weight.shape[1]
    slots = CLASSES * planes
    table_y, table_x = packed_dft(box, -1.0), packed_dft(box, 1.0)
    any_place = pl.BlockSpec(memory_space=pl.ANY)
    vmem = pl.BlockSpec(memory_space=pltpu.VMEM)
    lanes = 128 * (-(-2 * count // 128))
    if turns_round == 0:
        out_shape = [jax.ShapeDtypeStruct((slots, rows, 2 * cols), bf16)]
    else:
        slots += 1
        owned = rows // (2 * turns_round)
        x_piece = (turns_round // 2, slots - Z_SLOTS, owned, 2 * cols)
        z_piece = (2, Z_SLOTS, owned, 2 * cols)
        out_shape = [pltpu.VMEM(x_piece, bf16), pltpu.VMEM(x_piece, f32)] * 2
        out_shape += [pltpu.VMEM(z_piece, f32)]
        out_shape += [pltpu.VMEM(z_piece, bf16)] * (turns_round - 1)
    operands = (
        class_index[:, 0], pose_index, defocus_bin, defocus, plane_weight.T,
        jnp.asarray(table_y, bf16), jnp.asarray(table_x.T.copy(), bf16),
        images, rows_table, cols_table,
    )
    return pl.pallas_call(
        slices_kernel,
        out_shape=out_shape,
        in_specs=[any_place] * 10,
        out_specs=[vmem] * len(out_shape),
        scratch_shapes=[pltpu.SMEM(x.shape, x.dtype) for x in operands[:5]]
        + [pltpu.VMEM(x.shape, x.dtype) for x in operands[5:]]
        + [
            pltpu.SemaphoreType.DMA((9 + count // GROUP,)),
            pltpu.VMEM((poses * rows, box), bf16),
            pltpu.VMEM((poses, box, 2 * cols), bf16),
            pltpu.VMEM((box // 2 + 8, lanes), f32),
            pltpu.VMEM((count, box), f32),
            pltpu.VMEM((count, box), f32),
            pltpu.VMEM((SLOTS, box, box), bf16),
            pltpu.VMEM((SLOTS, box + 16, box), bf16),
            pltpu.VMEM((SLOTS, box, 2 * cols), bf16),
            pltpu.VMEM((slots, rows, 2 * cols), f32),
        ],
        compiler_params=pltpu.CompilerParams(vmem_limit_bytes=VMEM_LIMIT),
        cost_estimate=pl.CostEstimate(
            flops=2 * count * box * box * 1000, bytes_accessed=6 * 1024 * 1024, transcendentals=0
        ),
    )(*operands)


VMEM_LIMIT = 56 * 1024 * 1024


def ridge_kernel(defocus_hbm, plane_hbm, rows_hbm, cols_hbm, high_ref, low_ref, share_ref, *refs):
    defocus_ref, plane_ref, rows_ref, cols_ref, arrived = refs
    poses, owned, box = rows_ref.shape
    cols = cols_ref.shape[2]
    bins = defocus_ref.shape[0]
    planes = plane_ref.shape[0]
    half = box // 2
    first = pl.multiple_of(lax.axis_index("img") * owned, owned)
    copies = [
        pltpu.make_async_copy(defocus_hbm, defocus_ref, arrived.at[0]),
        pltpu.make_async_copy(plane_hbm, plane_ref, arrived.at[1]),
        pltpu.make_async_copy(rows_hbm.at[:, pl.ds(first, owned), :], rows_ref, arrived.at[2]),
        pltpu.make_async_copy(cols_hbm, cols_ref, arrived.at[3]),
    ]
    for copy in copies:
        copy.start()
    for copy in copies:
        copy.wait()
    share_plane = iota((planes * CLASSES, poses * bins), 0) // CLASSES
    share_pose = iota((planes * CLASSES, poses * bins), 1) // bins
    share = jnp.zeros((planes * CLASSES, poses * bins), f32)
    for p in range(poses):
        for z in range(planes):
            share = jnp.where((share_plane == z) & (share_pose == p), plane_ref[z, p], share)
    share_ref[...] = share

    bin_row = iota((bins, box), 0)
    sub_defocus = jnp.zeros((bins, box), f32)
    for b in range(bins):
        sub_defocus = jnp.where(bin_row == b, defocus_ref[b], sub_defocus)
    freq = iota((bins, box), 1)
    freq = jnp.where(freq < half, freq, box - freq).astype(f32)
    turns_x = sub_defocus * (freq * freq * (1.0 / (half * half)))
    turns_y = turns_x + ctf_phase / math.pi
    ones = jnp.ones((bins, box), f32)
    wave_y = jnp.concatenate(
        [0.5 * ones, -0.5 * turns_sine(turns_y + 0.25), 0.5 * turns_sine(turns_y)], 0
    )
    wave_x = jnp.concatenate([ones, turns_sine(turns_x + 0.25), turns_sine(turns_x)], 0)
    y_high, y_low = split_two(wave_y)
    x_high, x_low = split_two(wave_x)
    rows_sq = rows_ref[...].reshape(poses * owned, box).astype(f32)
    rows_sq = (rows_sq * rows_sq).astype(bf16)
    u = dot(y_high, rows_sq, ((1,), (1,))) + dot(y_low, rows_sq, ((1,), (1,)))
    for p in range(poses):
        cols_sq = cols_ref[p].astype(f32)
        cols_sq = (cols_sq * cols_sq).astype(bf16)
        v = dot(x_high, cols_sq) + dot(x_low, cols_sq)
        for r in range(owned):
            column = u[:, p * owned + r : p * owned + r + 1]
            product = v * column
            weight = product[:bins] + product[bins : 2 * bins] + product[2 * bins :]
            high, low = split_two(weight)
            high_ref[p * bins : (p + 1) * bins, r * cols : (r + 1) * cols] = high
            low_ref[p * bins : (p + 1) * bins, r * cols : (r + 1) * cols] = low


def own_ridges(defocus, plane_weight, rows_table, cols_table, owned):
    poses, _, box = rows_table.shape
    cols = cols_table.shape[2]
    bins = defocus.shape[0]
    any_place = pl.BlockSpec(memory_space=pl.ANY)
    vmem = pl.BlockSpec(memory_space=pltpu.VMEM)
    planes = plane_weight.T
    table = jax.ShapeDtypeStruct((poses * bins, owned * cols), bf16)
    return pl.pallas_call(
        ridge_kernel,
        out_shape=[table, table, jax.ShapeDtypeStruct((planes.shape[0] * CLASSES, poses * bins), f32)],
        in_specs=[any_place] * 4,
        out_specs=[vmem] * 3,
        scratch_shapes=[
            pltpu.SMEM(defocus.shape, f32),
            pltpu.SMEM(planes.shape, f32),
            pltpu.VMEM((poses, owned, box), bf16),
            pltpu.VMEM(cols_table.shape, bf16),
            pltpu.SemaphoreType.DMA((4,)),
        ],
        compiler_params=pltpu.CompilerParams(vmem_limit_bytes=16 * 1024 * 1024),
        cost_estimate=pl.CostEstimate(
            flops=1000, bytes_accessed=1000, transcendentals=0
        ),
    )(defocus, planes, rows_table, cols_table)


def call_in_vmem(kernel, arrays, out_shape):
    vmem = pl.BlockSpec(memory_space=pltpu.VMEM)
    return pl.pallas_call(
        kernel,
        out_shape=out_shape,
        in_specs=[vmem] * len(arrays),
        out_specs=[vmem] * len(out_shape),
        compiler_params=pltpu.CompilerParams(vmem_limit_bytes=16 * 1024 * 1024),
        cost_estimate=pl.CostEstimate(flops=1000, bytes_accessed=1000, transcendentals=0),
    )(*arrays)


def fold_kernel(far_keep, far_came, near_send, z_keep, *refs):
    rounds = near_send.shape[0] + far_keep.shape[0]
    z_came, refs = refs[: rounds - 1], refs[rounds - 1 :]
    z_own, x_send, far_sends = refs[0], refs[1], refs[2:]
    for k, send in enumerate(far_sends):
        send[...] = (far_keep[k] + far_came[k].astype(f32)).astype(bf16)
    near, x_slots = near_send.shape[:2]
    for k in range(near):
        x_send[k * x_slots : (k + 1) * x_slots] = near_send[k]
    for side in range(2):
        value = z_keep[side]
        for came in z_came:
            value = value + came[side].astype(f32)
        if side == 0:
            z_own[...] = value
        else:
            x_send[near * x_slots :] = value.astype(bf16)


def fold_phase(far_keep, far_came, near_send, z_keep, z_came):
    far, x_slots = far_keep.shape[:2]
    z_slots = z_keep.shape[1]
    tail = far_keep.shape[2:]
    out_shape = [
        pltpu.VMEM((z_slots,) + tail, f32),
        pltpu.VMEM((near_send.shape[0] * x_slots + z_slots,) + tail, bf16),
    ]
    out_shape += [pltpu.VMEM((x_slots,) + tail, bf16)] * far
    return call_in_vmem(fold_kernel, (far_keep, far_came, near_send, z_keep, *z_came), out_shape)


def near_kernel(keep, came, own, *sends):
    near, x_slots = keep.shape[:2]
    for k, out in enumerate((own,) + sends):
        part = came[k * x_slots : (k + 1) * x_slots].astype(f32)
        out[...] = (keep[k] + part).astype(out.dtype)


def near_phase(keep, came):
    piece = keep.shape[1:]
    out_shape = [pltpu.VMEM(piece, f32)] + [pltpu.VMEM(piece, bf16)] * (keep.shape[0] - 1)
    return call_in_vmem(near_kernel, (keep, came), out_shape)


def finish_kernel(high_ref, low_ref, share_ref, x_own, z_own, z_came, *refs):
    x_came, out_ref, ridge_ref = refs[:-2], refs[-2], refs[-1]
    slots, pairs = share_ref.shape
    owned, _, cols = ridge_ref.shape
    planes = slots // CLASSES
    first = z_own.shape[0]

    def summed(s):
        if s < first:
            return z_own[s] + z_came[z_came.shape[0] - first + s].astype(f32)
        value = x_own[s - first]
        for part in x_came:
            value = value + part[s - first].astype(f32)
        return value

    counts = summed(slots)[:CLASSES, :pairs]
    scaled = jnp.concatenate([counts] * planes, 0) * share_ref[...]
    c_high, c_low = split_two(scaled)
    weight = (
        dot(c_high, high_ref[...]) + dot(c_low, high_ref[...]) + dot(c_high, low_ref[...])
    )
    ridge = 1.0 / (weight + wiener_ridge)
    for r in range(owned):
        ridge_ref[r] = ridge[:, r * cols : (r + 1) * cols]
    for s in range(slots):
        value = summed(s)
        factor = ridge_ref[:, s, :]
        place = (s % CLASSES) * planes + s // CLASSES
        out_ref[:, 2 * place, :] = value[:, :cols] * factor
        out_ref[:, 2 * place + 1, :] = value[:, cols:] * factor


def finish(tables, x_own, z_own, z_came, x_came):
    slots = tables[2].shape[0]
    _, owned, wide = x_own.shape
    cols = wide // 2
    vmem = pl.BlockSpec(memory_space=pltpu.VMEM)
    return pl.pallas_call(
        finish_kernel,
        out_shape=jax.ShapeDtypeStruct((owned, 2 * slots, cols), f32),
        in_specs=[vmem] * (6 + len(x_came)),
        out_specs=vmem,
        scratch_shapes=[pltpu.VMEM((owned, slots, cols), f32)],
        compiler_params=pltpu.CompilerParams(vmem_limit_bytes=16 * 1024 * 1024),
        cost_estimate=pl.CostEstimate(
            flops=8 * slots * owned * cols, bytes_accessed=8 * 1024 * 1024 // 4, transcendentals=0
        ),
    )(*tables, x_own, z_own, z_came, *x_came)


def squared_table(weight_table):
    wide_table = weight_table.astype(f32)
    return (wide_table * wide_table).astype(bf16)


def weight_totals(class_index, pose_index, defocus_bin, defocus, rows_table, cols_table, plane_weight, first_row, owned):
    box = rows_table.shape[2]
    poses = rows_table.shape[0]
    bins = defocus.shape[0]
    half = box // 2
    exact = lax.Precision.HIGHEST
    code = (class_index[:, 0] * poses + pose_index) * bins + defocus_bin
    codes = lax.all_gather(code, "img", tiled=True)
    hits = (codes[:, None] == jnp.arange(CLASSES * poses * bins, dtype=jnp.int32)).astype(f32)
    counts = jnp.sum(hits, 0).reshape(CLASSES, poses, bins)
    place = jnp.arange(box, dtype=jnp.int32)
    freq = jnp.where(place < half, place, place - box).astype(f32)
    turns = defocus[:, None] * (freq * freq)[None, :] * (1.0 / (half * half))
    turns_y = turns + ctf_phase / math.pi
    ones = jnp.ones_like(turns)
    wave_y = jnp.stack([0.5 * ones, -0.5 * turns_sine(turns_y + 0.25), 0.5 * turns_sine(turns_y)])
    wave_x = jnp.stack([ones, turns_sine(turns + 0.25), turns_sine(turns)])
    rows_own = lax.dynamic_slice_in_dim(rows_table, first_row, owned, 1)
    u = jnp.einsum("pry,mby->pmbr", squared_table(rows_own).astype(f32), wave_y, precision=exact)
    v = jnp.einsum("pxj,mbx->pmbj", squared_table(cols_table).astype(f32), wave_x, precision=exact)
    weight = counts[:, None] * plane_weight.T[None, :, :, None]
    left = weight[:, :, :, None, :, None] * u[None, None]
    return jnp.einsum("czpmbr,pmbj->rczj", left, v, precision=exact)


def by_rounds(images, class_index, pose_index, defocus_bin, defocus, rows_table, cols_table, plane_weight):
    members = lax.axis_size("img")
    rounds = members // 2
    rows = rows_table.shape[1]
    planes = plane_weight.shape[1]
    cols = cols_table.shape[2]
    owned = rows // members
    outs = own_totals(
        images, class_index, pose_index, defocus_bin, defocus, rows_table, cols_table, plane_weight, rounds
    )
    far_send, far_keep, near_send, near_keep, z_keep = outs[:5]
    z_sends = outs[5:]
    near = near_keep.shape[0]

    def along_x(value):
        return lax.ppermute(value, "img", [(i, i ^ 1) for i in range(members)])

    def along_z(value, k):
        return lax.ppermute(value, "img", [(i, i ^ (2 * k)) for i in range(members)])

    far_ks, near_ks = range(near, rounds), range(1, near)
    far_came = along_x(far_send)
    z_came = [along_z(z_sends[k - 1], k) for k in (*far_ks, *near_ks)]
    tables = own_ridges(defocus, plane_weight, rows_table, cols_table, owned)
    far_keep, tables = lax.optimization_barrier((far_keep, tables))
    z_own, x_send, *x_sends = fold_phase(far_keep, far_came, near_send, z_keep, z_came)
    z_came = along_x(x_send)
    x_came = [along_z(send, k) for send, k in zip(x_sends, far_ks)]
    x_own, *x_sends = near_phase(near_keep, z_came)
    x_came += [along_z(send, k) for send, k in zip(x_sends, near_ks)]
    out = finish(tables, x_own, z_own, z_came, x_came)
    return out.reshape(owned, CLASSES, planes, 2, cols)


def by_scatter(images, class_index, pose_index, defocus_bin, defocus, rows_table, cols_table, plane_weight):
    rows = rows_table.shape[1]
    cols = cols_table.shape[2]
    planes = plane_weight.shape[1]
    members = lax.axis_size("img")
    owned = rows // members
    (totals,) = own_totals(
        images, class_index, pose_index, defocus_bin, defocus, rows_table, cols_table, plane_weight, 0
    )
    slots = totals.shape[0]
    totals = totals.reshape(slots, members, owned, 2 * cols).transpose(1, 0, 2, 3)
    own = lax.psum_scatter(totals, "img", scatter_dimension=0, tiled=False)
    weight = weight_totals(
        class_index, pose_index, defocus_bin, defocus, rows_table, cols_table, plane_weight,
        lax.axis_index("img") * owned, owned,
    )
    own = own.astype(f32).reshape(planes, CLASSES, owned, 2, cols).transpose(2, 1, 0, 3, 4)
    return own / (weight[:, :, :, None, :] + wiener_ridge)


def body(*arrays):
    rows = arrays[5].shape[1]
    members = lax.axis_size("img")
    images = members * arrays[0].shape[0]
    small = members >= 4 and members & (members - 1) == 0 and images <= 256 and rows % (16 * members) == 0
    return (by_rounds if small else by_scatter)(*arrays)


def solution(mesh):
    placed = (
        P(("groups", "img"), None, None),
        P(("groups", "img"), None),
        P(("groups", "img")),
        P(("groups", "img")),
        P(),
        P(),
        P(None, None, "slab"),
        P(),
    )
    return jax.shard_map(
        body,
        mesh=mesh,
        in_specs=placed,
        out_specs=P("img", "groups", None, None, "slab"),
        check_vma=False,
    )
```

```python
import functools
import math

import jax
import jax.numpy as jnp
import numpy as np
from jax import lax
from jax.experimental import pallas as pl
from jax.experimental.pallas import tpu as pltpu
from jax.sharding import PartitionSpec as P

CLASSES = 8

wiener_ridge = 1.0
ctf_phase = 0.1
f32 = jnp.float32
bf16 = jnp.bfloat16


def packed_dft(box, sine_sign):
    half = box // 2
    k = np.concatenate([np.arange(half), [half], np.arange(1, half)])
    angle = (k[:, None] * np.arange(box)[None, :] % box) * (2.0 * math.pi / box)
    table = np.where((np.arange(box) <= half)[:, None], np.cos(angle), sine_sign * np.sin(angle))
    return (table / math.sqrt(box)).astype(np.float32)


def iota(shape, axis):
    return lax.broadcasted_iota(jnp.int32, shape, axis)


def dot(a, b, dims=((1,), (0,))):
    return lax.dot_general(a, b, (dims, ((), ())), preferred_element_type=f32)


def turns_sine(turns):
    return jnp.sin((turns - jnp.round(turns)) * (2.0 * math.pi))


def split_two(value):
    high = value.astype(bf16)
    return high, (value - high.astype(f32)).astype(bf16)


def fold_of(place, half):
    box = 2 * half
    return jnp.where(place <= half, place, box + half - place)


def slices_kernel(
    class_hbm, pose_hbm, bin_hbm, defocus_hbm, plane_hbm,
    dft_hbm, dft_t_hbm, images_hbm, rows_hbm, cols_hbm,
    *refs,
):
    outs, refs = refs[:-SCRATCH], refs[-SCRATCH:]
    (
        class_ref, pose_ref, bin_ref, defocus_ref, plane_ref,
        dft_ref, dft_t_ref, images_ref, rows_ref, cols_ref, arrived,
        rows_fold, cols_fold, wave_y, cos_x, sin_x, half_ref, spec_ref, mix_ref, totals,
    ) = refs
    count, box, _ = images_ref.shape
    half = box // 2
    poses, rows, _ = rows_ref.shape
    cols = cols_ref.shape[2]
    planes = plane_ref.shape[0]

    pairs = (
        (class_hbm, class_ref), (pose_hbm, pose_ref), (bin_hbm, bin_ref),
        (defocus_hbm, defocus_ref), (plane_hbm, plane_ref),
        (dft_hbm, dft_ref), (images_hbm.at[0:GROUP], images_ref.at[0:GROUP]),
        (dft_t_hbm, dft_t_ref), (cols_hbm, cols_ref), (rows_hbm, rows_ref),
    ) + tuple(
        (images_hbm.at[i : i + GROUP], images_ref.at[i : i + GROUP])
        for i in range(GROUP, count, GROUP)
    )
    copies = [
        pltpu.make_async_copy(source, target, arrived.at[n])
        for n, (source, target) in enumerate(pairs)
    ]
    for copy in copies:
        copy.start()

    place = iota((box, box), 0)
    other = iota((box, box), 1)
    folded = fold_of(place, half)
    near = (folded == other).astype(f32).astype(bf16)
    far = (jnp.where(folded == 0, 0, box - folded) == other).astype(f32).astype(bf16)

    for copy in copies[:5]:
        copy.wait()
    tall, lanes = wave_y.shape
    lane = iota((1, lanes), 1)
    sub = iota((count, box), 0)
    lane_defocus = jnp.zeros((1, lanes), f32)
    sub_defocus = jnp.zeros((count, box), f32)
    for i in range(count):
        value = defocus_ref[bin_ref[i]]
        lane_defocus = jnp.where(lane % count == i, value, lane_defocus)
        sub_defocus = jnp.where(sub == i, value, sub_defocus)
    scale = 1.0 / (2 * half * half)
    ky = iota((tall, lanes), 0).astype(f32)
    quarter = jnp.where(lane < count, 0.0, 0.25) + ctf_phase / (2.0 * math.pi)
    wave_y[...] = turns_sine(lane_defocus * (ky * ky * scale) + quarter)
    kx = iota((count, box), 1)
    kx = jnp.where(kx <= half, kx, kx - half).astype(f32)
    turns = sub_defocus * (kx * kx * scale)
    cos_x[...] = -turns_sine(turns + 0.25)
    sin_x[...] = -turns_sine(turns)
    totals[...] = jnp.zeros_like(totals)
    if len(outs) > 1:
        bins = defocus_ref.shape[0]
        count_row = iota((16, 2 * cols), 0)
        count_lane = iota((16, 2 * cols), 1)
        counts = jnp.zeros((16, 2 * cols), f32)
        for i in range(count):
            hit = (count_row == class_ref[i]) & (count_lane == pose_ref[i] * bins + bin_ref[i])
            counts = counts + jnp.where(hit, 1.0, 0.0)
        totals[planes * CLASSES] = jnp.tile(counts, (rows // 16, 1))

    tile = 8
    tile_row = iota((tile, half), 0) == 0
    tile_col = iota((tile, half), 1) == 0
    col_zero = iota((half, half), 1) == 0
    short_row = iota((16, half), 0) == 0
    short_col = iota((16, half), 1) == 0

    def without_row(value):
        return jnp.concatenate([jnp.where(tile_row, 0.0, value[:tile]), value[tile:]], 0)

    def along_rows(i):
        if i % GROUP == 0:
            copies[6 if i == 0 else 9 + i // GROUP].wait()
        half_ref[i % SLOTS] = dot(dft_ref[...], images_ref[i]).astype(bf16)

    def along_columns(i):
        y = dot(half_ref[i % SLOTS], dft_t_ref[...])
        sin_col = jnp.broadcast_to(wave_y[:, i : i + 1], (tall, half))
        cos_col = jnp.broadcast_to(wave_y[:, count + i : count + i + 1], (tall, half))
        near_ctf = sin_col * cos_x[i : i + 1, :half] + cos_col * sin_x[i : i + 1, :half]
        far_ctf = sin_col * cos_x[i : i + 1, half:] + cos_col * sin_x[i : i + 1, half:]
        cc, cs = y[:half, :half], y[:half, half:]
        sc, ss = y[half:, :half], y[half:, half:]
        ss_row = without_row(ss)
        ss_in = jnp.where(col_zero, 0.0, ss_row)
        sc_in = without_row(sc)
        cs_in = jnp.where(col_zero, 0.0, cs)
        near_y, far_y = near_ctf[:half], far_ctf[:half]
        spec = spec_ref.at[i % SLOTS]
        spec[0:half, 0:half] = (near_y * (cc + ss_in)).astype(bf16)
        spec[0:half, half:] = (far_y * jnp.where(col_zero, cs, cc - ss_in)).astype(bf16)
        spec[half:box, 0:half] = (near_y * (sc_in - cs_in)).astype(bf16)
        spec[half:box, half:] = (far_y * jnp.where(col_zero, ss_row, sc_in + cs_in)).astype(bf16)
        sc_top = jnp.broadcast_to(sc[0:1], (16, half))
        ss_top = jnp.broadcast_to(ss[0:1], (16, half))
        ss_top_in = jnp.where(short_col, 0.0, ss_top)
        spec[box : box + 16, 0:half] = (
            near_ctf[half : half + 1] * jnp.where(short_row, sc_top, -ss_top_in)
        ).astype(bf16)
        spec[box : box + 16, half:] = (
            far_ctf[half : half + 1]
            * jnp.where(short_row, jnp.where(short_col, ss_top, sc_top), ss_top_in)
        ).astype(bf16)

    def mix(i):
        mixed = dot(spec_ref[i % SLOTS], cols_fold[pose_ref[i]])
        out = mix_ref.at[i % SLOTS]
        out[0:half, 0:cols] = mixed[:half, :cols].astype(bf16)
        out[0:half, cols:] = mixed[half:box, :cols].astype(bf16)
        top = iota((16, cols), 0) == 0
        real, imag = mixed[:half, cols:], -mixed[half:box, cols:]
        out[half : half + 16, 0:cols] = jnp.where(
            top, mixed[box : box + 1, :cols], real[:16]
        ).astype(bf16)
        out[half : half + 16, cols:] = jnp.where(
            top, mixed[box + 1 : box + 2, :cols], imag[:16]
        ).astype(bf16)
        out[half + 16 :, 0:cols] = real[16:].astype(bf16)
        out[half + 16 :, cols:] = imag[16:].astype(bf16)

    def insert(i):
        pose = pose_ref[i]
        pose_rows = rows_fold[pl.ds(pl.multiple_of(pose * rows, rows), rows), :]
        piece = dot(pose_rows, mix_ref[i % SLOTS])
        for z in range(planes):
            slot = z * CLASSES + class_ref[i]
            totals[slot] += plane_ref[z, pose] * piece

    copies[5].wait()
    along_rows(0)
    copies[7].wait()
    copies[8].wait()
    for p in range(0, poses, 2):
        two = jnp.concatenate([cols_ref[p], cols_ref[p + 1]], 1)
        near_two = dot(near, two).astype(bf16)
        far_two = dot(far, two).astype(bf16)
        cols_fold[p] = jnp.concatenate([near_two[:, :cols], far_two[:, :cols]], 1)
        cols_fold[p + 1] = jnp.concatenate([near_two[:, cols:], far_two[:, cols:]], 1)
    along_rows(1)
    along_columns(0)
    copies[9].wait()
    rows_fold[...] = dot(
        rows_ref[...].reshape(poses * rows, box), near, ((1,), (1,))
    ).astype(bf16)
    for step in range(2, count + 3):
        if step >= 3:
            insert(step - 3)
        if step - 2 < count:
            mix(step - 2)
        if step - 1 < count:
            along_columns(step - 1)
        if step < count:
            along_rows(step)

    if len(outs) == 1:
        outs[0][...] = totals[...].astype(bf16)
        return
    far_send, far_keep, near_send, near_keep, z_send, z_keep = outs
    _, x_slots, owned, _ = near_keep.shape
    me = lax.axis_index("img")

    def rows_of(flip):
        return pl.ds(pl.multiple_of((me ^ flip) * owned, owned), owned)

    for n in range(2):
        near_send[n] = totals[-x_slots:, rows_of(2 * n + 1), :].astype(bf16)
        near_keep[n] = totals[-x_slots:, rows_of(2 * n), :]
        far_send[n] = totals[-x_slots:, rows_of(2 * n + 5), :].astype(bf16)
        far_keep[n] = totals[-x_slots:, rows_of(2 * n + 4), :]
    for n in range(4):
        z_send[n] = totals[:-x_slots, rows_of(n + 4), :].astype(bf16)
        z_keep[n] = totals[:-x_slots, rows_of(n), :]


SCRATCH = 20
SLOTS = 3
GROUP = 4
Z_SLOTS = 3


def own_totals(images, class_index, pose_index, defocus_bin, defocus, rows_table, cols_table, plane_weight, members):
    count, box, _ = images.shape
    poses, rows, _ = rows_table.shape
    cols = cols_table.shape[2]
    planes = plane_weight.shape[1]
    slots = CLASSES * planes
    table_y, table_x = packed_dft(box, -1.0), packed_dft(box, 1.0)
    any_place = pl.BlockSpec(memory_space=pl.ANY)
    vmem = pl.BlockSpec(memory_space=pltpu.VMEM)
    lanes = 128 * (-(-2 * count // 128))
    if members == 1:
        out_shape = [jax.ShapeDtypeStruct((slots, rows, 2 * cols), bf16)]
    else:
        slots += 1
        x_piece = (2, slots - Z_SLOTS, rows // members, 2 * cols)
        z_piece = (4, Z_SLOTS, rows // members, 2 * cols)
        out_shape = []
        for piece in (x_piece, x_piece, z_piece):
            out_shape += [pltpu.VMEM(piece, bf16), pltpu.VMEM(piece, f32)]
    operands = (
        class_index[:, 0], pose_index, defocus_bin, defocus, plane_weight.T,
        jnp.asarray(table_y, bf16), jnp.asarray(table_x.T.copy(), bf16),
        images, rows_table, cols_table,
    )
    return pl.pallas_call(
        slices_kernel,
        out_shape=out_shape,
        in_specs=[any_place] * 10,
        out_specs=[vmem] * len(out_shape),
        scratch_shapes=[pltpu.SMEM(x.shape, x.dtype) for x in operands[:5]]
        + [pltpu.VMEM(x.shape, x.dtype) for x in operands[5:]]
        + [
            pltpu.SemaphoreType.DMA((9 + count // GROUP,)),
            pltpu.VMEM((poses * rows, box), bf16),
            pltpu.VMEM((poses, box, 2 * cols), bf16),
            pltpu.VMEM((box // 2 + 8, lanes), f32),
            pltpu.VMEM((count, box), f32),
            pltpu.VMEM((count, box), f32),
            pltpu.VMEM((SLOTS, box, box), bf16),
            pltpu.VMEM((SLOTS, box + 16, box), bf16),
            pltpu.VMEM((SLOTS, box, 2 * cols), bf16),
            pltpu.VMEM((slots, rows, 2 * cols), f32),
        ],
        compiler_params=pltpu.CompilerParams(vmem_limit_bytes=VMEM_LIMIT),
        cost_estimate=pl.CostEstimate(
            flops=2 * count * box * box * 1000, bytes_accessed=6 * 1024 * 1024, transcendentals=0
        ),
    )(*operands)


VMEM_LIMIT = 56 * 1024 * 1024


def ridge_kernel(defocus_hbm, plane_hbm, rows_hbm, cols_hbm, high_ref, low_ref, share_ref, *refs):
    defocus_ref, plane_ref, rows_ref, cols_ref, arrived = refs
    poses, owned, box = rows_ref.shape
    cols = cols_ref.shape[2]
    bins = defocus_ref.shape[0]
    planes = plane_ref.shape[0]
    half = box // 2
    first = pl.multiple_of(lax.axis_index("img") * owned, owned)
    copies = [
        pltpu.make_async_copy(defocus_hbm, defocus_ref, arrived.at[0]),
        pltpu.make_async_copy(plane_hbm, plane_ref, arrived.at[1]),
        pltpu.make_async_copy(rows_hbm.at[:, pl.ds(first, owned), :], rows_ref, arrived.at[2]),
        pltpu.make_async_copy(cols_hbm, cols_ref, arrived.at[3]),
    ]
    for copy in copies:
        copy.start()
    for copy in copies:
        copy.wait()
    share_plane = iota((planes * CLASSES, poses * bins), 0) // CLASSES
    share_pose = iota((planes * CLASSES, poses * bins), 1) // bins
    share = jnp.zeros((planes * CLASSES, poses * bins), f32)
    for p in range(poses):
        for z in range(planes):
            share = jnp.where((share_plane == z) & (share_pose == p), plane_ref[z, p], share)
    share_ref[...] = share

    bin_row = iota((bins, box), 0)
    sub_defocus = jnp.zeros((bins, box), f32)
    for b in range(bins):
        sub_defocus = jnp.where(bin_row == b, defocus_ref[b], sub_defocus)
    freq = iota((bins, box), 1)
    freq = jnp.where(freq < half, freq, box - freq).astype(f32)
    turns_x = sub_defocus * (freq * freq * (1.0 / (half * half)))
    turns_y = turns_x + ctf_phase / math.pi
    ones = jnp.ones((bins, box), f32)
    wave_y = jnp.concatenate(
        [0.5 * ones, -0.5 * turns_sine(turns_y + 0.25), 0.5 * turns_sine(turns_y)], 0
    )
    wave_x = jnp.concatenate([ones, turns_sine(turns_x + 0.25), turns_sine(turns_x)], 0)
    y_high, y_low = split_two(wave_y)
    x_high, x_low = split_two(wave_x)
    rows_sq = rows_ref[...].reshape(poses * owned, box).astype(f32)
    rows_sq = (rows_sq * rows_sq).astype(bf16)
    u = dot(y_high, rows_sq, ((1,), (1,))) + dot(y_low, rows_sq, ((1,), (1,)))
    for p in range(poses):
        cols_sq = cols_ref[p].astype(f32)
        cols_sq = (cols_sq * cols_sq).astype(bf16)
        v = dot(x_high, cols_sq) + dot(x_low, cols_sq)
        for r in range(owned):
            column = u[:, p * owned + r : p * owned + r + 1]
            product = v * column
            weight = product[:bins] + product[bins : 2 * bins] + product[2 * bins :]
            high, low = split_two(weight)
            high_ref[p * bins : (p + 1) * bins, r * cols : (r + 1) * cols] = high
            low_ref[p * bins : (p + 1) * bins, r * cols : (r + 1) * cols] = low


def own_ridges(defocus, plane_weight, rows_table, cols_table, owned):
    poses, _, box = rows_table.shape
    cols = cols_table.shape[2]
    bins = defocus.shape[0]
    any_place = pl.BlockSpec(memory_space=pl.ANY)
    vmem = pl.BlockSpec(memory_space=pltpu.VMEM)
    planes = plane_weight.T
    table = jax.ShapeDtypeStruct((poses * bins, owned * cols), bf16)
    return pl.pallas_call(
        ridge_kernel,
        out_shape=[table, table, jax.ShapeDtypeStruct((planes.shape[0] * CLASSES, poses * bins), f32)],
        in_specs=[any_place] * 4,
        out_specs=[vmem] * 3,
        scratch_shapes=[
            pltpu.SMEM(defocus.shape, f32),
            pltpu.SMEM(planes.shape, f32),
            pltpu.VMEM((poses, owned, box), bf16),
            pltpu.VMEM(cols_table.shape, bf16),
            pltpu.SemaphoreType.DMA((4,)),
        ],
        compiler_params=pltpu.CompilerParams(vmem_limit_bytes=16 * 1024 * 1024),
        cost_estimate=pl.CostEstimate(
            flops=1000, bytes_accessed=1000, transcendentals=0
        ),
    )(defocus, planes, rows_table, cols_table)


def call_in_vmem(kernel, arrays, out_shape, weight=1000):
    vmem = pl.BlockSpec(memory_space=pltpu.VMEM)
    return pl.pallas_call(
        kernel,
        out_shape=out_shape,
        in_specs=[vmem] * len(arrays),
        out_specs=[vmem] * len(out_shape),
        compiler_params=pltpu.CompilerParams(vmem_limit_bytes=16 * 1024 * 1024),
        cost_estimate=pl.CostEstimate(flops=weight, bytes_accessed=weight, transcendentals=0),
    )(*arrays)


def fold_kernel(far_keep, far_came, near_send, z_keep, z_came, far_a, far_b, x_send, z_kept):
    for n, send in enumerate((far_a, far_b)):
        send[...] = (far_keep[n] + far_came[n].astype(f32)).astype(bf16)
    x_slots, z_slots = near_send.shape[1], z_keep.shape[1]
    for n in range(2):
        z_kept[n] = z_keep[2 * n] + z_came[2 * n].astype(f32)
        x_send[n * x_slots : (n + 1) * x_slots] = near_send[n]
        first = 2 * x_slots + n * z_slots
        x_send[first : first + z_slots] = (
            z_keep[2 * n + 1] + z_came[2 * n + 1].astype(f32)
        ).astype(bf16)


def fold_phase(far_keep, far_came, near_send, z_keep, z_came):
    x_slots, z_slots = near_send.shape[1], z_keep.shape[1]
    tail = far_keep.shape[2:]
    out_shape = [pltpu.VMEM((x_slots,) + tail, bf16)] * 2
    out_shape += [
        pltpu.VMEM((2 * x_slots + 2 * z_slots,) + tail, bf16),
        pltpu.VMEM((2, z_slots) + tail, f32),
    ]
    return call_in_vmem(fold_kernel, (far_keep, far_came, near_send, z_keep, z_came), out_shape)


def near_kernel(near_keep, z_kept, came, own, send):
    x_slots, z_slots = near_keep.shape[1], z_kept.shape[1]
    for n, out in enumerate((own, send)):
        first = 2 * x_slots + n * z_slots
        part = z_kept[n] + came[first : first + z_slots].astype(f32)
        out[:z_slots] = part.astype(out.dtype)
        part = near_keep[n] + came[n * x_slots : (n + 1) * x_slots].astype(f32)
        out[z_slots:] = part.astype(out.dtype)


def near_phase(near_keep, z_kept, came):
    piece = (near_keep.shape[1] + z_kept.shape[1],) + near_keep.shape[2:]
    out_shape = [pltpu.VMEM(piece, f32), pltpu.VMEM(piece, bf16)]
    return call_in_vmem(near_kernel, (near_keep, z_kept, came), out_shape)


def far_kernel(own, far_a, far_b, out):
    first = own.shape[0] - far_a.shape[0]
    out[:first] = own[:first]
    out[first:] = own[first:] + far_a[...].astype(f32) + far_b[...].astype(f32)


def far_phase(own, far_a, far_b):
    return call_in_vmem(far_kernel, (own, far_a, far_b), [pltpu.VMEM(own.shape, f32)], FAR_WEIGHT)[0]


FAR_WEIGHT = 1024 * 1024 * 1024


def finish_kernel(high_ref, low_ref, share_ref, own, near_came, out_ref, ridge_ref):
    slots, pairs = share_ref.shape
    owned, _, cols = ridge_ref.shape
    planes = slots // CLASSES

    def summed(s):
        return own[s] + near_came[s].astype(f32)

    counts = summed(slots)[:CLASSES, :pairs]
    scaled = jnp.concatenate([counts] * planes, 0) * share_ref[...]
    c_high, c_low = split_two(scaled)
    weight = (
        dot(c_high, high_ref[...]) + dot(c_low, high_ref[...]) + dot(c_high, low_ref[...])
    )
    ridge = 1.0 / (weight + wiener_ridge)
    for r in range(owned):
        ridge_ref[r] = ridge[:, r * cols : (r + 1) * cols]
    for s in range(slots):
        value = summed(s)
        factor = ridge_ref[:, s, :]
        place = (s % CLASSES) * planes + s // CLASSES
        out_ref[:, 2 * place, :] = value[:, :cols] * factor
        out_ref[:, 2 * place + 1, :] = value[:, cols:] * factor


def finish(tables, own, near_came):
    slots = tables[2].shape[0]
    _, owned, wide = own.shape
    cols = wide // 2
    vmem = pl.BlockSpec(memory_space=pltpu.VMEM)
    return pl.pallas_call(
        finish_kernel,
        out_shape=jax.ShapeDtypeStruct((owned, 2 * slots, cols), f32),
        in_specs=[vmem] * 5,
        out_specs=vmem,
        scratch_shapes=[pltpu.VMEM((owned, slots, cols), f32)],
        compiler_params=pltpu.CompilerParams(vmem_limit_bytes=16 * 1024 * 1024),
        cost_estimate=pl.CostEstimate(
            flops=8 * slots * owned * cols, bytes_accessed=8 * 1024 * 1024 // 4, transcendentals=0
        ),
    )(*tables, own, near_came)


def squared_table(weight_table):
    wide_table = weight_table.astype(f32)
    return (wide_table * wide_table).astype(bf16)


def weight_totals(class_index, pose_index, defocus_bin, defocus, rows_table, cols_table, plane_weight, first_row, owned):
    box = rows_table.shape[2]
    poses = rows_table.shape[0]
    bins = defocus.shape[0]
    half = box // 2
    exact = lax.Precision.HIGHEST
    code = (class_index[:, 0] * poses + pose_index) * bins + defocus_bin
    codes = lax.all_gather(code, "img", tiled=True)
    hits = (codes[:, None] == jnp.arange(CLASSES * poses * bins, dtype=jnp.int32)).astype(f32)
    counts = jnp.sum(hits, 0).reshape(CLASSES, poses, bins)
    place = jnp.arange(box, dtype=jnp.int32)
    freq = jnp.where(place < half, place, place - box).astype(f32)
    turns = defocus[:, None] * (freq * freq)[None, :] * (1.0 / (half * half))
    turns_y = turns + ctf_phase / math.pi
    ones = jnp.ones_like(turns)
    wave_y = jnp.stack([0.5 * ones, -0.5 * turns_sine(turns_y + 0.25), 0.5 * turns_sine(turns_y)])
    wave_x = jnp.stack([ones, turns_sine(turns + 0.25), turns_sine(turns)])
    rows_own = lax.dynamic_slice_in_dim(rows_table, first_row, owned, 1)
    u = jnp.einsum("pry,mby->pmbr", squared_table(rows_own).astype(f32), wave_y, precision=exact)
    v = jnp.einsum("pxj,mbx->pmbj", squared_table(cols_table).astype(f32), wave_x, precision=exact)
    weight = counts[:, None] * plane_weight.T[None, :, :, None]
    left = weight[:, :, :, None, :, None] * u[None, None]
    return jnp.einsum("czpmbr,pmbj->rczj", left, v, precision=exact)


def by_pairs(images, class_index, pose_index, defocus_bin, defocus, rows_table, cols_table, plane_weight):
    members = lax.axis_size("img")
    rows = rows_table.shape[1]
    planes = plane_weight.shape[1]
    cols = cols_table.shape[2]
    owned = rows // members

    def exchange(value, flip):
        return lax.ppermute(value, "img", [(i, i ^ flip) for i in range(members)])

    far_send, far_keep, near_send, near_keep, z_send, z_keep = own_totals(
        images, class_index, pose_index, defocus_bin, defocus, rows_table, cols_table, plane_weight, members
    )
    far_came = exchange(far_send, 1)
    z_came = exchange(z_send, 4)
    tables = own_ridges(defocus, plane_weight, rows_table, cols_table, owned)
    far_keep, tables = lax.optimization_barrier((far_keep, tables))
    far_a, far_b, x_send, z_kept = fold_phase(far_keep, far_came, near_send, z_keep, z_came)
    far_a = exchange(far_a, 4)
    x_came = exchange(x_send, 1)
    far_b = exchange(far_b, 6)
    own, near_send = near_phase(near_keep, z_kept, x_came)
    near_came = exchange(near_send, 2)
    own = far_phase(own, far_a, far_b)
    out = finish(tables, own, near_came)
    return out.reshape(owned, CLASSES, planes, 2, cols)


def by_scatter(images, class_index, pose_index, defocus_bin, defocus, rows_table, cols_table, plane_weight):
    rows = rows_table.shape[1]
    cols = cols_table.shape[2]
    planes = plane_weight.shape[1]
    members = lax.axis_size("img")
    owned = rows // members
    (totals,) = own_totals(
        images, class_index, pose_index, defocus_bin, defocus, rows_table, cols_table, plane_weight, 1
    )
    slots = totals.shape[0]
    totals = totals.reshape(slots, members, owned, 2 * cols).transpose(1, 0, 2, 3)
    own = lax.psum_scatter(totals, "img", scatter_dimension=0, tiled=False)
    weight = weight_totals(
        class_index, pose_index, defocus_bin, defocus, rows_table, cols_table, plane_weight,
        lax.axis_index("img") * owned, owned,
    )
    own = own.astype(f32).reshape(planes, CLASSES, owned, 2, cols).transpose(2, 1, 0, 3, 4)
    return own / (weight[:, :, :, None, :] + wiener_ridge)


def body(*arrays):
    rows = arrays[5].shape[1]
    members = lax.axis_size("img")
    images = members * arrays[0].shape[0]
    paired = members == 8 and images <= 256 and rows % (16 * members) == 0
    return (by_pairs if paired else by_scatter)(*arrays)


def solution(mesh):
    placed = (
        P(("groups", "img"), None, None),
        P(("groups", "img"), None),
        P(("groups", "img")),
        P(("groups", "img")),
        P(),
        P(),
        P(None, None, "slab"),
        P(),
    )
    return jax.shard_map(
        body,
        mesh=mesh,
        in_specs=placed,
        out_specs=P("img", "groups", None, None, "slab"),
        check_vma=False,
    )
```

```python
import functools
import math

import jax
import jax.numpy as jnp
import numpy as np
from jax import lax
from jax.experimental import pallas as pl
from jax.experimental.pallas import tpu as pltpu
from jax.sharding import PartitionSpec as P

CLASSES = 8

wiener_ridge = 1.0
ctf_phase = 0.1
f32 = jnp.float32
bf16 = jnp.bfloat16


def packed_dft(box, sine_sign):
    half = box // 2
    k = np.concatenate([np.arange(half), [half], np.arange(1, half)])
    angle = (k[:, None] * np.arange(box)[None, :] % box) * (2.0 * math.pi / box)
    table = np.where((np.arange(box) <= half)[:, None], np.cos(angle), sine_sign * np.sin(angle))
    return (table / math.sqrt(box)).astype(np.float32)


def iota(shape, axis):
    return lax.broadcasted_iota(jnp.int32, shape, axis)


def dot(a, b, dims=((1,), (0,))):
    return lax.dot_general(a, b, (dims, ((), ())), preferred_element_type=f32)


def turns_sine(turns):
    return jnp.sin((turns - jnp.round(turns)) * (2.0 * math.pi))


def split_two(value):
    high = value.astype(bf16)
    return high, (value - high.astype(f32)).astype(bf16)


def fold_of(place, half):
    box = 2 * half
    return jnp.where(place <= half, place, box + half - place)


def slices_kernel(
    class_hbm, pose_hbm, bin_hbm, defocus_hbm, plane_hbm,
    dft_hbm, dft_t_hbm, images_hbm, rows_hbm, cols_hbm,
    *refs,
):
    outs, refs = refs[:-SCRATCH], refs[-SCRATCH:]
    (
        class_ref, pose_ref, bin_ref, defocus_ref, plane_ref,
        dft_ref, dft_t_ref, images_ref, rows_ref, cols_ref, arrived,
        rows_fold, cols_fold, wave_y, cos_x, sin_x, half_ref, spec_ref, mix_ref, totals,
    ) = refs
    count, box, _ = images_ref.shape
    half = box // 2
    poses, rows, _ = rows_ref.shape
    cols = cols_ref.shape[2]
    planes = plane_ref.shape[0]

    pairs = (
        (class_hbm, class_ref), (pose_hbm, pose_ref), (bin_hbm, bin_ref),
        (defocus_hbm, defocus_ref), (plane_hbm, plane_ref),
        (dft_hbm, dft_ref), (images_hbm.at[0:GROUP], images_ref.at[0:GROUP]),
        (dft_t_hbm, dft_t_ref), (cols_hbm, cols_ref), (rows_hbm, rows_ref),
    ) + tuple(
        (images_hbm.at[i : i + GROUP], images_ref.at[i : i + GROUP])
        for i in range(GROUP, count, GROUP)
    )
    copies = [
        pltpu.make_async_copy(source, target, arrived.at[n])
        for n, (source, target) in enumerate(pairs)
    ]
    for copy in copies:
        copy.start()

    place = iota((box, box), 0)
    other = iota((box, box), 1)
    folded = fold_of(place, half)
    near = (folded == other).astype(f32).astype(bf16)
    far = (jnp.where(folded == 0, 0, box - folded) == other).astype(f32).astype(bf16)

    for copy in copies[:5]:
        copy.wait()
    tall, lanes = wave_y.shape
    lane = iota((1, lanes), 1)
    sub = iota((count, box), 0)
    lane_defocus = jnp.zeros((1, lanes), f32)
    sub_defocus = jnp.zeros((count, box), f32)
    for i in range(count):
        value = defocus_ref[bin_ref[i]]
        lane_defocus = jnp.where(lane % count == i, value, lane_defocus)
        sub_defocus = jnp.where(sub == i, value, sub_defocus)
    scale = 1.0 / (2 * half * half)
    ky = iota((tall, lanes), 0).astype(f32)
    quarter = jnp.where(lane < count, 0.0, 0.25) + ctf_phase / (2.0 * math.pi)
    wave_y[...] = turns_sine(lane_defocus * (ky * ky * scale) + quarter)
    kx = iota((count, box), 1)
    kx = jnp.where(kx <= half, kx, kx - half).astype(f32)
    turns = sub_defocus * (kx * kx * scale)
    cos_x[...] = -turns_sine(turns + 0.25)
    sin_x[...] = -turns_sine(turns)
    totals[...] = jnp.zeros_like(totals)
    leading = 1 if len(outs) > 1 else 0
    if len(outs) > 1:
        bins = defocus_ref.shape[0]
        count_row = iota((16, 2 * cols), 0)
        count_lane = iota((16, 2 * cols), 1)
        counts = jnp.zeros((16, 2 * cols), f32)
        for i in range(count):
            hit = (count_row == class_ref[i]) & (count_lane == pose_ref[i] * bins + bin_ref[i])
            counts = counts + jnp.where(hit, 1.0, 0.0)
        totals[0] = jnp.tile(counts, (rows // 16, 1))

    tile = 8
    tile_row = iota((tile, half), 0) == 0
    tile_col = iota((tile, half), 1) == 0
    col_zero = iota((half, half), 1) == 0
    short_row = iota((16, half), 0) == 0
    short_col = iota((16, half), 1) == 0

    def without_row(value):
        return jnp.concatenate([jnp.where(tile_row, 0.0, value[:tile]), value[tile:]], 0)

    def along_rows(i):
        if i % GROUP == 0:
            copies[6 if i == 0 else 9 + i // GROUP].wait()
        two = jnp.concatenate([images_ref[i], images_ref[i + 1]], 1)
        product = dot(dft_ref[...], two).astype(bf16)
        for n in range(2):
            half_ref[i // 2 % 2, n * box : (n + 1) * box] = product[:, n * box : (n + 1) * box]

    def along_columns(i):
        product = dot(half_ref[i // 2 % 2], dft_t_ref[...])
        for n in range(2):
            weigh(i + n, product[n * box : (n + 1) * box])

    def weigh(i, y):
        sin_col = jnp.broadcast_to(wave_y[:, i : i + 1], (tall, half))
        cos_col = jnp.broadcast_to(wave_y[:, count + i : count + i + 1], (tall, half))
        near_ctf = sin_col * cos_x[i : i + 1, :half] + cos_col * sin_x[i : i + 1, :half]
        far_ctf = sin_col * cos_x[i : i + 1, half:] + cos_col * sin_x[i : i + 1, half:]
        cc, cs = y[:half, :half], y[:half, half:]
        sc, ss = y[half:, :half], y[half:, half:]
        ss_row = without_row(ss)
        ss_in = jnp.where(col_zero, 0.0, ss_row)
        sc_in = without_row(sc)
        cs_in = jnp.where(col_zero, 0.0, cs)
        near_y, far_y = near_ctf[:half], far_ctf[:half]
        spec = spec_ref.at[i % SLOTS]
        spec[0:half, 0:half] = (near_y * (cc + ss_in)).astype(bf16)
        spec[0:half, half:] = (far_y * jnp.where(col_zero, cs, cc - ss_in)).astype(bf16)
        spec[half:box, 0:half] = (near_y * (sc_in - cs_in)).astype(bf16)
        spec[half:box, half:] = (far_y * jnp.where(col_zero, ss_row, sc_in + cs_in)).astype(bf16)
        sc_top = jnp.broadcast_to(sc[0:1], (16, half))
        ss_top = jnp.broadcast_to(ss[0:1], (16, half))
        ss_top_in = jnp.where(short_col, 0.0, ss_top)
        spec[box : box + 16, 0:half] = (
            near_ctf[half : half + 1] * jnp.where(short_row, sc_top, -ss_top_in)
        ).astype(bf16)
        spec[box : box + 16, half:] = (
            far_ctf[half : half + 1]
            * jnp.where(short_row, jnp.where(short_col, ss_top, sc_top), ss_top_in)
        ).astype(bf16)

    def mix(i):
        mixed = dot(spec_ref[i % SLOTS], cols_fold[pose_ref[i]])
        out = mix_ref.at[i % SLOTS]
        out[0:half, 0:cols] = mixed[:half, :cols].astype(bf16)
        out[0:half, cols:] = mixed[half:box, :cols].astype(bf16)
        top = iota((16, cols), 0) == 0
        real, imag = mixed[:half, cols:], -mixed[half:box, cols:]
        out[half : half + 16, 0:cols] = jnp.where(
            top, mixed[box : box + 1, :cols], real[:16]
        ).astype(bf16)
        out[half : half + 16, cols:] = jnp.where(
            top, mixed[box + 1 : box + 2, :cols], imag[:16]
        ).astype(bf16)
        out[half + 16 :, 0:cols] = real[16:].astype(bf16)
        out[half + 16 :, cols:] = imag[16:].astype(bf16)

    def insert(i):
        pose = pose_ref[i]
        pose_rows = rows_fold[pl.ds(pl.multiple_of(pose * rows, rows), rows), :]
        piece = dot(pose_rows, mix_ref[i % SLOTS])
        for z in range(planes):
            slot = leading + z * CLASSES + class_ref[i]
            totals[slot] += plane_ref[z, pose] * piece

    copies[5].wait()
    along_rows(0)
    copies[7].wait()
    copies[8].wait()
    for p in range(0, poses, 2):
        two = jnp.concatenate([cols_ref[p], cols_ref[p + 1]], 1)
        near_two = dot(near, two).astype(bf16)
        far_two = dot(far, two).astype(bf16)
        cols_fold[p] = jnp.concatenate([near_two[:, :cols], far_two[:, :cols]], 1)
        cols_fold[p + 1] = jnp.concatenate([near_two[:, cols:], far_two[:, cols:]], 1)
    along_rows(2)
    along_columns(0)
    copies[9].wait()
    rows_fold[...] = dot(
        rows_ref[...].reshape(poses * rows, box), near, ((1,), (1,))
    ).astype(bf16)
    for step in range(4, count + 6, 2):
        for n in range(2):
            if step >= 6:
                insert(step - 6 + n)
        for n in range(2):
            if step - 4 < count:
                mix(step - 4 + n)
        if step - 2 < count:
            along_columns(step - 2)
        if step < count:
            along_rows(step)

    if len(outs) == 1:
        outs[0][...] = totals[...].astype(bf16)
        return
    far_send, far_keep, near_send, near_keep, z_keep = outs[:5]
    z_sends = outs[5:]
    _, x_slots, owned, _ = near_keep.shape
    rounds = len(z_sends) + 1
    me = lax.axis_index("img")
    near = near_keep.shape[0]
    for k in range(rounds):
        mine = pl.ds(pl.multiple_of((me ^ (2 * k)) * owned, owned), owned)
        theirs = pl.ds(pl.multiple_of((me ^ (2 * k + 1)) * owned, owned), owned)
        keep, send, n = (near_keep, near_send, k) if k < near else (far_keep, far_send, k - near)
        keep[n] = totals[-x_slots:, mine, :]
        send[n] = totals[-x_slots:, theirs, :].astype(bf16)
        z_out = z_keep if k == 0 else z_sends[k - 1]
        z_out[0] = totals[:-x_slots, mine, :].astype(z_out.dtype)
        z_out[1] = totals[:-x_slots, theirs, :].astype(z_out.dtype)


SCRATCH = 20
SLOTS = 4
GROUP = 4
Z_SLOTS = 3


def own_totals(images, class_index, pose_index, defocus_bin, defocus, rows_table, cols_table, plane_weight, turns_round):
    count, box, _ = images.shape
    poses, rows, _ = rows_table.shape
    cols = cols_table.shape[2]
    planes = plane_weight.shape[1]
    slots = CLASSES * planes
    table_y, table_x = packed_dft(box, -1.0), packed_dft(box, 1.0)
    any_place = pl.BlockSpec(memory_space=pl.ANY)
    vmem = pl.BlockSpec(memory_space=pltpu.VMEM)
    lanes = 128 * (-(-2 * count // 128))
    if turns_round == 0:
        out_shape = [jax.ShapeDtypeStruct((slots, rows, 2 * cols), bf16)]
    else:
        slots += 1
        owned = rows // (2 * turns_round)
        x_piece = (turns_round // 2, slots - Z_SLOTS, owned, 2 * cols)
        z_piece = (2, Z_SLOTS, owned, 2 * cols)
        out_shape = [pltpu.VMEM(x_piece, bf16), pltpu.VMEM(x_piece, f32)] * 2
        out_shape += [pltpu.VMEM(z_piece, f32)]
        out_shape += [pltpu.VMEM(z_piece, bf16)] * (turns_round - 1)
    operands = (
        class_index[:, 0], pose_index, defocus_bin, defocus, plane_weight.T,
        jnp.asarray(table_y, bf16), jnp.asarray(table_x.T.copy(), bf16),
        images, rows_table, cols_table,
    )
    return pl.pallas_call(
        slices_kernel,
        out_shape=out_shape,
        in_specs=[any_place] * 10,
        out_specs=[vmem] * len(out_shape),
        scratch_shapes=[pltpu.SMEM(x.shape, x.dtype) for x in operands[:5]]
        + [pltpu.VMEM(x.shape, x.dtype) for x in operands[5:]]
        + [
            pltpu.SemaphoreType.DMA((9 + count // GROUP,)),
            pltpu.VMEM((poses * rows, box), bf16),
            pltpu.VMEM((poses, box, 2 * cols), bf16),
            pltpu.VMEM((box // 2 + 8, lanes), f32),
            pltpu.VMEM((count, box), f32),
            pltpu.VMEM((count, box), f32),
            pltpu.VMEM((2, 2 * box, box), bf16),
            pltpu.VMEM((SLOTS, box + 16, box), bf16),
            pltpu.VMEM((SLOTS, box, 2 * cols), bf16),
            pltpu.VMEM((slots, rows, 2 * cols), f32),
        ],
        compiler_params=pltpu.CompilerParams(vmem_limit_bytes=VMEM_LIMIT),
        cost_estimate=pl.CostEstimate(
            flops=2 * count * box * box * 1000, bytes_accessed=6 * 1024 * 1024, transcendentals=0
        ),
    )(*operands)


VMEM_LIMIT = 56 * 1024 * 1024


def ridge_kernel(defocus_hbm, plane_hbm, rows_hbm, cols_hbm, high_ref, low_ref, share_ref, *refs):
    defocus_ref, plane_ref, rows_ref, cols_ref, arrived = refs
    poses, owned, box = rows_ref.shape
    cols = cols_ref.shape[2]
    bins = defocus_ref.shape[0]
    planes = plane_ref.shape[0]
    half = box // 2
    first = pl.multiple_of(lax.axis_index("img") * owned, owned)
    copies = [
        pltpu.make_async_copy(defocus_hbm, defocus_ref, arrived.at[0]),
        pltpu.make_async_copy(plane_hbm, plane_ref, arrived.at[1]),
        pltpu.make_async_copy(rows_hbm.at[:, pl.ds(first, owned), :], rows_ref, arrived.at[2]),
        pltpu.make_async_copy(cols_hbm, cols_ref, arrived.at[3]),
    ]
    for copy in copies:
        copy.start()
    for copy in copies:
        copy.wait()
    share_plane = iota((planes * CLASSES, poses * bins), 0) // CLASSES
    share_pose = iota((planes * CLASSES, poses * bins), 1) // bins
    share = jnp.zeros((planes * CLASSES, poses * bins), f32)
    for p in range(poses):
        for z in range(planes):
            share = jnp.where((share_plane == z) & (share_pose == p), plane_ref[z, p], share)
    share_ref[...] = share

    bin_row = iota((bins, box), 0)
    sub_defocus = jnp.zeros((bins, box), f32)
    for b in range(bins):
        sub_defocus = jnp.where(bin_row == b, defocus_ref[b], sub_defocus)
    freq = iota((bins, box), 1)
    freq = jnp.where(freq < half, freq, box - freq).astype(f32)
    turns_x = sub_defocus * (freq * freq * (1.0 / (half * half)))
    turns_y = turns_x + ctf_phase / math.pi
    ones = jnp.ones((bins, box), f32)
    wave_y = jnp.concatenate(
        [0.5 * ones, -0.5 * turns_sine(turns_y + 0.25), 0.5 * turns_sine(turns_y)], 0
    )
    wave_x = jnp.concatenate([ones, turns_sine(turns_x + 0.25), turns_sine(turns_x)], 0)
    y_high, y_low = split_two(wave_y)
    x_high, x_low = split_two(wave_x)
    rows_sq = rows_ref[...].reshape(poses * owned, box).astype(f32)
    rows_sq = (rows_sq * rows_sq).astype(bf16)
    u = dot(y_high, rows_sq, ((1,), (1,))) + dot(y_low, rows_sq, ((1,), (1,)))
    for p in range(poses):
        cols_sq = cols_ref[p].astype(f32)
        cols_sq = (cols_sq * cols_sq).astype(bf16)
        v = dot(x_high, cols_sq) + dot(x_low, cols_sq)
        for r in range(owned):
            column = u[:, p * owned + r : p * owned + r + 1]
            product = v * column
            weight = product[:bins] + product[bins : 2 * bins] + product[2 * bins :]
            high, low = split_two(weight)
            high_ref[p * bins : (p + 1) * bins, r * cols : (r + 1) * cols] = high
            low_ref[p * bins : (p + 1) * bins, r * cols : (r + 1) * cols] = low


def own_ridges(defocus, plane_weight, rows_table, cols_table, owned):
    poses, _, box = rows_table.shape
    cols = cols_table.shape[2]
    bins = defocus.shape[0]
    any_place = pl.BlockSpec(memory_space=pl.ANY)
    vmem = pl.BlockSpec(memory_space=pltpu.VMEM)
    planes = plane_weight.T
    table = jax.ShapeDtypeStruct((poses * bins, owned * cols), bf16)
    return pl.pallas_call(
        ridge_kernel,
        out_shape=[table, table, jax.ShapeDtypeStruct((planes.shape[0] * CLASSES, poses * bins), f32)],
        in_specs=[any_place] * 4,
        out_specs=[vmem] * 3,
        scratch_shapes=[
            pltpu.SMEM(defocus.shape, f32),
            pltpu.SMEM(planes.shape, f32),
            pltpu.VMEM((poses, owned, box), bf16),
            pltpu.VMEM(cols_table.shape, bf16),
            pltpu.SemaphoreType.DMA((4,)),
        ],
        compiler_params=pltpu.CompilerParams(vmem_limit_bytes=16 * 1024 * 1024),
        cost_estimate=pl.CostEstimate(
            flops=1000, bytes_accessed=1000, transcendentals=0
        ),
    )(defocus, planes, rows_table, cols_table)


def call_in_vmem(kernel, arrays, out_shape):
    vmem = pl.BlockSpec(memory_space=pltpu.VMEM)
    return pl.pallas_call(
        kernel,
        out_shape=out_shape,
        in_specs=[vmem] * len(arrays),
        out_specs=[vmem] * len(out_shape),
        compiler_params=pltpu.CompilerParams(vmem_limit_bytes=16 * 1024 * 1024),
        cost_estimate=pl.CostEstimate(flops=1000, bytes_accessed=1000, transcendentals=0),
    )(*arrays)


def fold_kernel(far_keep, far_came, near_send, z_keep, *refs):
    rounds = near_send.shape[0] + far_keep.shape[0]
    z_came, refs = refs[: rounds - 1], refs[rounds - 1 :]
    z_own, x_send, far_sends = refs[0], refs[1], refs[2:]
    for k, send in enumerate(far_sends):
        send[...] = (far_keep[k] + far_came[k].astype(f32)).astype(bf16)
    near, x_slots = near_send.shape[:2]
    for k in range(near):
        x_send[k * x_slots : (k + 1) * x_slots] = near_send[k]
    for side in range(2):
        value = z_keep[side]
        for came in z_came:
            value = value + came[side].astype(f32)
        if side == 0:
            z_own[...] = value
        else:
            x_send[near * x_slots :] = value.astype(bf16)


def fold_phase(far_keep, far_came, near_send, z_keep, z_came):
    far, x_slots = far_keep.shape[:2]
    z_slots = z_keep.shape[1]
    tail = far_keep.shape[2:]
    out_shape = [
        pltpu.VMEM((z_slots,) + tail, f32),
        pltpu.VMEM((near_send.shape[0] * x_slots + z_slots,) + tail, bf16),
    ]
    out_shape += [pltpu.VMEM((x_slots,) + tail, bf16)] * far
    return call_in_vmem(fold_kernel, (far_keep, far_came, near_send, z_keep, *z_came), out_shape)


def near_kernel(keep, came, own, *sends):
    near, x_slots = keep.shape[:2]
    for k, out in enumerate((own,) + sends):
        part = came[k * x_slots : (k + 1) * x_slots].astype(f32)
        out[...] = (keep[k] + part).astype(out.dtype)


def near_phase(keep, came):
    piece = keep.shape[1:]
    out_shape = [pltpu.VMEM(piece, f32)] + [pltpu.VMEM(piece, bf16)] * (keep.shape[0] - 1)
    return call_in_vmem(near_kernel, (keep, came), out_shape)


def weight_kernel(high_ref, low_ref, share_ref, z_own, z_came, out_ref, ridge_ref):
    slots, pairs = share_ref.shape
    owned, _, cols = ridge_ref.shape
    counts = z_own[0] + z_came[z_came.shape[0] - z_own.shape[0]].astype(f32)
    scaled = jnp.concatenate([counts[:CLASSES, :pairs]] * (slots // CLASSES), 0) * share_ref[...]
    c_high, c_low = split_two(scaled)
    weight = (
        dot(c_high, high_ref[...]) + dot(c_low, high_ref[...]) + dot(c_high, low_ref[...])
    )
    ridge = 1.0 / (weight + wiener_ridge)
    for r in range(owned):
        ridge_ref[r] = ridge[:, r * cols : (r + 1) * cols]
    for s in range(slots):
        out_ref[s] = ridge_ref[:, s, :]


def own_weights(tables, z_own, z_came):
    slots = tables[2].shape[0]
    _, owned, wide = z_own.shape
    cols = wide // 2
    vmem = pl.BlockSpec(memory_space=pltpu.VMEM)
    return pl.pallas_call(
        weight_kernel,
        out_shape=pltpu.VMEM((slots, owned, cols), f32),
        in_specs=[vmem] * 5,
        out_specs=vmem,
        scratch_shapes=[pltpu.VMEM((owned, slots, cols), f32)],
        compiler_params=pltpu.CompilerParams(vmem_limit_bytes=16 * 1024 * 1024),
        cost_estimate=pl.CostEstimate(flops=1000, bytes_accessed=1000, transcendentals=0),
    )(*tables, z_own, z_came)


def finish_kernel(planes, ridge_ref, x_own, z_own, z_came, *refs):
    x_came, out_ref = refs[:-1], refs[-1]
    slots, owned, cols = ridge_ref.shape
    first = z_own.shape[0]
    for s in range(slots):
        if s + 1 < first:
            value = z_own[s + 1] + z_came[z_came.shape[0] - first + s + 1].astype(f32)
        else:
            value = x_own[s + 1 - first]
            for part in x_came:
                value = value + part[s + 1 - first].astype(f32)
        factor = ridge_ref[s]
        place = (s % CLASSES) * planes + s // CLASSES
        out_ref[:, 2 * place, :] = value[:, :cols] * factor
        out_ref[:, 2 * place + 1, :] = value[:, cols:] * factor


def finish(planes, ridge, x_own, z_own, z_came, x_came):
    slots, owned, cols = ridge.shape
    vmem = pl.BlockSpec(memory_space=pltpu.VMEM)
    return pl.pallas_call(
        functools.partial(finish_kernel, planes),
        out_shape=jax.ShapeDtypeStruct((owned, 2 * slots, cols), f32),
        in_specs=[vmem] * (4 + len(x_came)),
        out_specs=vmem,
        compiler_params=pltpu.CompilerParams(vmem_limit_bytes=16 * 1024 * 1024),
        cost_estimate=pl.CostEstimate(flops=1000, bytes_accessed=1000, transcendentals=0),
    )(ridge, x_own, z_own, z_came, *x_came)


def squared_table(weight_table):
    wide_table = weight_table.astype(f32)
    return (wide_table * wide_table).astype(bf16)


def weight_totals(class_index, pose_index, defocus_bin, defocus, rows_table, cols_table, plane_weight, first_row, owned):
    box = rows_table.shape[2]
    poses = rows_table.shape[0]
    bins = defocus.shape[0]
    half = box // 2
    exact = lax.Precision.HIGHEST
    code = (class_index[:, 0] * poses + pose_index) * bins + defocus_bin
    codes = lax.all_gather(code, "img", tiled=True)
    hits = (codes[:, None] == jnp.arange(CLASSES * poses * bins, dtype=jnp.int32)).astype(f32)
    counts = jnp.sum(hits, 0).reshape(CLASSES, poses, bins)
    place = jnp.arange(box, dtype=jnp.int32)
    freq = jnp.where(place < half, place, place - box).astype(f32)
    turns = defocus[:, None] * (freq * freq)[None, :] * (1.0 / (half * half))
    turns_y = turns + ctf_phase / math.pi
    ones = jnp.ones_like(turns)
    wave_y = jnp.stack([0.5 * ones, -0.5 * turns_sine(turns_y + 0.25), 0.5 * turns_sine(turns_y)])
    wave_x = jnp.stack([ones, turns_sine(turns + 0.25), turns_sine(turns)])
    rows_own = lax.dynamic_slice_in_dim(rows_table, first_row, owned, 1)
    u = jnp.einsum("pry,mby->pmbr", squared_table(rows_own).astype(f32), wave_y, precision=exact)
    v = jnp.einsum("pxj,mbx->pmbj", squared_table(cols_table).astype(f32), wave_x, precision=exact)
    weight = counts[:, None] * plane_weight.T[None, :, :, None]
    left = weight[:, :, :, None, :, None] * u[None, None]
    return jnp.einsum("czpmbr,pmbj->rczj", left, v, precision=exact)


def by_rounds(images, class_index, pose_index, defocus_bin, defocus, rows_table, cols_table, plane_weight):
    members = lax.axis_size("img")
    rounds = members // 2
    rows = rows_table.shape[1]
    planes = plane_weight.shape[1]
    cols = cols_table.shape[2]
    owned = rows // members
    outs = own_totals(
        images, class_index, pose_index, defocus_bin, defocus, rows_table, cols_table, plane_weight, rounds
    )
    far_send, far_keep, near_send, near_keep, z_keep = outs[:5]
    z_sends = outs[5:]
    near = near_keep.shape[0]

    def along_x(value):
        return lax.ppermute(value, "img", [(i, i ^ 1) for i in range(members)])

    def along_z(value, k):
        return lax.ppermute(value, "img", [(i, i ^ (2 * k)) for i in range(members)])

    far_ks, near_ks = range(near, rounds), range(1, near)
    far_came = along_x(far_send)
    z_came = [along_z(z_sends[k - 1], k) for k in (*far_ks, *near_ks)]
    tables = own_ridges(defocus, plane_weight, rows_table, cols_table, owned)
    far_keep, tables = lax.optimization_barrier((far_keep, tables))
    z_own, x_send, *x_sends = fold_phase(far_keep, far_came, near_send, z_keep, z_came)
    z_came = along_x(x_send)
    x_came = [along_z(send, k) for send, k in zip(x_sends, far_ks)]
    x_own, *x_sends = near_phase(near_keep, z_came)
    x_came += [along_z(send, k) for send, k in zip(x_sends, near_ks)]
    ridge = own_weights(tables, z_own, z_came)
    out = finish(planes, ridge, x_own, z_own, z_came, x_came)
    return out.reshape(owned, CLASSES, planes, 2, cols)


def by_scatter(images, class_index, pose_index, defocus_bin, defocus, rows_table, cols_table, plane_weight):
    rows = rows_table.shape[1]
    cols = cols_table.shape[2]
    planes = plane_weight.shape[1]
    members = lax.axis_size("img")
    owned = rows // members
    (totals,) = own_totals(
        images, class_index, pose_index, defocus_bin, defocus, rows_table, cols_table, plane_weight, 0
    )
    slots = totals.shape[0]
    totals = totals.reshape(slots, members, owned, 2 * cols).transpose(1, 0, 2, 3)
    own = lax.psum_scatter(totals, "img", scatter_dimension=0, tiled=False)
    weight = weight_totals(
        class_index, pose_index, defocus_bin, defocus, rows_table, cols_table, plane_weight,
        lax.axis_index("img") * owned, owned,
    )
    own = own.astype(f32).reshape(planes, CLASSES, owned, 2, cols).transpose(2, 1, 0, 3, 4)
    return own / (weight[:, :, :, None, :] + wiener_ridge)


def body(*arrays):
    rows = arrays[5].shape[1]
    members = lax.axis_size("img")
    images = members * arrays[0].shape[0]
    small = members >= 4 and members & (members - 1) == 0 and images <= 256 and rows % (16 * members) == 0
    return (by_rounds if small else by_scatter)(*arrays)


def solution(mesh):
    placed = (
        P(("groups", "img"), None, None),
        P(("groups", "img"), None),
        P(("groups", "img")),
        P(("groups", "img")),
        P(),
        P(),
        P(None, None, "slab"),
        P(),
    )
    return jax.shard_map(
        body,
        mesh=mesh,
        in_specs=placed,
        out_specs=P("img", "groups", None, None, "slab"),
        check_vma=False,
    )
```

```python
import functools
import math

import jax
import jax.numpy as jnp
import numpy as np
from jax import lax
from jax.experimental import pallas as pl
from jax.experimental.pallas import tpu as pltpu
from jax.sharding import PartitionSpec as P

CLASSES = 8

wiener_ridge = 1.0
ctf_phase = 0.1
f32 = jnp.float32
bf16 = jnp.bfloat16


def packed_dft(box, sine_sign):
    half = box // 2
    k = np.concatenate([np.arange(half), [half], np.arange(1, half)])
    angle = (k[:, None] * np.arange(box)[None, :] % box) * (2.0 * math.pi / box)
    table = np.where((np.arange(box) <= half)[:, None], np.cos(angle), sine_sign * np.sin(angle))
    return (table / math.sqrt(box)).astype(np.float32)


def iota(shape, axis):
    return lax.broadcasted_iota(jnp.int32, shape, axis)


def dot(a, b, dims=((1,), (0,))):
    return lax.dot_general(a, b, (dims, ((), ())), preferred_element_type=f32)


def turns_sine(turns):
    return jnp.sin((turns - jnp.round(turns)) * (2.0 * math.pi))


def split_two(value):
    high = value.astype(bf16)
    return high, (value - high.astype(f32)).astype(bf16)


def fold_of(place, half):
    box = 2 * half
    return jnp.where(place <= half, place, box + half - place)


def slices_kernel(
    class_hbm, pose_hbm, bin_hbm, defocus_hbm, plane_hbm,
    dft_hbm, dft_t_hbm, images_hbm, rows_hbm, cols_hbm,
    *refs,
):
    outs, refs = refs[:-SCRATCH], refs[-SCRATCH:]
    (
        class_ref, pose_ref, bin_ref, defocus_ref, plane_ref,
        dft_ref, dft_t_ref, images_ref, rows_ref, cols_ref, arrived,
        rows_fold, cols_fold, wave_y, cos_x, sin_x, half_ref, spec_ref, mix_ref, totals,
    ) = refs
    count, box, _ = images_ref.shape
    half = box // 2
    poses, rows, _ = rows_ref.shape
    cols = cols_ref.shape[2]
    planes = plane_ref.shape[0]

    pairs = (
        (class_hbm, class_ref), (pose_hbm, pose_ref), (bin_hbm, bin_ref),
        (defocus_hbm, defocus_ref), (plane_hbm, plane_ref),
        (dft_hbm, dft_ref), (images_hbm.at[0:GROUP], images_ref.at[0:GROUP]),
        (dft_t_hbm, dft_t_ref), (cols_hbm, cols_ref), (rows_hbm, rows_ref),
    ) + tuple(
        (images_hbm.at[i : i + GROUP], images_ref.at[i : i + GROUP])
        for i in range(GROUP, count, GROUP)
    )
    copies = [
        pltpu.make_async_copy(source, target, arrived.at[n])
        for n, (source, target) in enumerate(pairs)
    ]
    for copy in copies:
        copy.start()

    place = iota((box, box), 0)
    other = iota((box, box), 1)
    folded = fold_of(place, half)
    near = (folded == other).astype(f32).astype(bf16)
    far = (jnp.where(folded == 0, 0, box - folded) == other).astype(f32).astype(bf16)

    for copy in copies[:5]:
        copy.wait()
    tall, lanes = wave_y.shape
    lane = iota((1, lanes), 1)
    sub = iota((count, box), 0)
    lane_defocus = jnp.zeros((1, lanes), f32)
    sub_defocus = jnp.zeros((count, box), f32)
    for i in range(count):
        value = defocus_ref[bin_ref[i]]
        lane_defocus = jnp.where(lane % count == i, value, lane_defocus)
        sub_defocus = jnp.where(sub == i, value, sub_defocus)
    scale = 1.0 / (2 * half * half)
    ky = iota((tall, lanes), 0).astype(f32)
    quarter = jnp.where(lane < count, 0.0, 0.25) + ctf_phase / (2.0 * math.pi)
    wave_y[...] = turns_sine(lane_defocus * (ky * ky * scale) + quarter)
    kx = iota((count, box), 1)
    kx = jnp.where(kx <= half, kx, kx - half).astype(f32)
    turns = sub_defocus * (kx * kx * scale)
    cos_x[...] = -turns_sine(turns + 0.25)
    sin_x[...] = -turns_sine(turns)
    totals[...] = jnp.zeros_like(totals)
    leading = 1 if len(outs) > 1 else 0
    if len(outs) > 1:
        bins = defocus_ref.shape[0]
        count_row = iota((16, 2 * cols), 0)
        count_lane = iota((16, 2 * cols), 1)
        counts = jnp.zeros((16, 2 * cols), f32)
        for i in range(count):
            hit = (count_row == class_ref[i]) & (count_lane == pose_ref[i] * bins + bin_ref[i])
            counts = counts + jnp.where(hit, 1.0, 0.0)
        totals[0] = jnp.tile(counts, (rows // 16, 1))

    tile = 8
    tile_row = iota((tile, half), 0) == 0
    tile_col = iota((tile, half), 1) == 0
    col_zero = iota((half, half), 1) == 0
    short_row = iota((16, half), 0) == 0
    short_col = iota((16, half), 1) == 0

    def without_row(value):
        return jnp.concatenate([jnp.where(tile_row, 0.0, value[:tile]), value[tile:]], 0)

    def along_rows(i):
        copies[6 if i == 0 else 9 + i // GROUP].wait()
        group = jnp.concatenate([images_ref[i + n] for n in range(GROUP)], 1)
        product = dot(dft_ref[...], group).astype(bf16)
        for n in range(GROUP):
            half_ref[i // GROUP % 2, n * box : (n + 1) * box] = product[:, n * box : (n + 1) * box]

    def along_columns(i):
        product = dot(half_ref[i // GROUP % 2], dft_t_ref[...])
        for n in range(GROUP):
            weigh(i + n, product[n * box : (n + 1) * box])

    def weigh(i, y):
        sin_col = jnp.broadcast_to(wave_y[:, i : i + 1], (tall, half))
        cos_col = jnp.broadcast_to(wave_y[:, count + i : count + i + 1], (tall, half))
        near_ctf = sin_col * cos_x[i : i + 1, :half] + cos_col * sin_x[i : i + 1, :half]
        far_ctf = sin_col * cos_x[i : i + 1, half:] + cos_col * sin_x[i : i + 1, half:]
        cc, cs = y[:half, :half], y[:half, half:]
        sc, ss = y[half:, :half], y[half:, half:]
        ss_row = without_row(ss)
        ss_in = jnp.where(col_zero, 0.0, ss_row)
        sc_in = without_row(sc)
        cs_in = jnp.where(col_zero, 0.0, cs)
        near_y, far_y = near_ctf[:half], far_ctf[:half]
        spec = spec_ref.at[i % SLOTS]
        spec[0:half, 0:half] = (near_y * (cc + ss_in)).astype(bf16)
        spec[0:half, half:] = (far_y * jnp.where(col_zero, cs, cc - ss_in)).astype(bf16)
        spec[half:box, 0:half] = (near_y * (sc_in - cs_in)).astype(bf16)
        spec[half:box, half:] = (far_y * jnp.where(col_zero, ss_row, sc_in + cs_in)).astype(bf16)
        sc_top = jnp.broadcast_to(sc[0:1], (16, half))
        ss_top = jnp.broadcast_to(ss[0:1], (16, half))
        ss_top_in = jnp.where(short_col, 0.0, ss_top)
        spec[box : box + 16, 0:half] = (
            near_ctf[half : half + 1] * jnp.where(short_row, sc_top, -ss_top_in)
        ).astype(bf16)
        spec[box : box + 16, half:] = (
            far_ctf[half : half + 1]
            * jnp.where(short_row, jnp.where(short_col, ss_top, sc_top), ss_top_in)
        ).astype(bf16)

    def mix(i):
        mixed = dot(spec_ref[i % SLOTS], cols_fold[pose_ref[i]])
        out = mix_ref.at[i % SLOTS]
        out[0:half, 0:cols] = mixed[:half, :cols].astype(bf16)
        out[0:half, cols:] = mixed[half:box, :cols].astype(bf16)
        top = iota((16, cols), 0) == 0
        real, imag = mixed[:half, cols:], -mixed[half:box, cols:]
        out[half : half + 16, 0:cols] = jnp.where(
            top, mixed[box : box + 1, :cols], real[:16]
        ).astype(bf16)
        out[half : half + 16, cols:] = jnp.where(
            top, mixed[box + 1 : box + 2, :cols], imag[:16]
        ).astype(bf16)
        out[half + 16 :, 0:cols] = real[16:].astype(bf16)
        out[half + 16 :, cols:] = imag[16:].astype(bf16)

    def insert(i):
        pose = pose_ref[i]
        pose_rows = rows_fold[pl.ds(pl.multiple_of(pose * rows, rows), rows), :]
        piece = dot(pose_rows, mix_ref[i % SLOTS])
        for z in range(planes):
            slot = leading + z * CLASSES + class_ref[i]
            totals[slot] += plane_ref[z, pose] * piece

    copies[5].wait()
    along_rows(0)
    copies[7].wait()
    copies[8].wait()
    for p in range(0, poses, 2):
        two = jnp.concatenate([cols_ref[p], cols_ref[p + 1]], 1)
        near_two = dot(near, two).astype(bf16)
        far_two = dot(far, two).astype(bf16)
        cols_fold[p] = jnp.concatenate([near_two[:, :cols], far_two[:, :cols]], 1)
        cols_fold[p + 1] = jnp.concatenate([near_two[:, cols:], far_two[:, cols:]], 1)
    along_rows(GROUP)
    along_columns(0)
    copies[9].wait()
    rows_fold[...] = dot(
        rows_ref[...].reshape(poses * rows, box), near, ((1,), (1,))
    ).astype(bf16)
    for step in range(2 * GROUP, count + 3 * GROUP, GROUP):
        for n in range(GROUP):
            if step >= 3 * GROUP:
                insert(step - 3 * GROUP + n)
            if step - 2 * GROUP < count:
                mix(step - 2 * GROUP + n)
        if step - GROUP < count:
            along_columns(step - GROUP)
        if step < count:
            along_rows(step)

    if len(outs) == 1:
        outs[0][...] = totals[...].astype(bf16)
        return
    far_send, far_keep, near_send, near_keep, z_keep = outs[:5]
    z_sends = outs[5:]
    _, x_slots, owned, _ = near_keep.shape
    rounds = len(z_sends) + 1
    me = lax.axis_index("img")
    near = near_keep.shape[0]
    for k in range(rounds):
        mine = pl.ds(pl.multiple_of((me ^ (2 * k)) * owned, owned), owned)
        theirs = pl.ds(pl.multiple_of((me ^ (2 * k + 1)) * owned, owned), owned)
        keep, send, n = (near_keep, near_send, k) if k < near else (far_keep, far_send, rounds - 1 - k)
        keep[n] = totals[-x_slots:, mine, :]
        send[n] = totals[-x_slots:, theirs, :].astype(bf16)
        z_out = z_keep if k == 0 else z_sends[k - 1]
        z_out[0] = totals[:-x_slots, mine, :].astype(z_out.dtype)
        z_out[1] = totals[:-x_slots, theirs, :].astype(z_out.dtype)


SCRATCH = 20
SLOTS = 8
GROUP = 4
Z_SLOTS = 3


def own_totals(images, class_index, pose_index, defocus_bin, defocus, rows_table, cols_table, plane_weight, turns_round):
    count, box, _ = images.shape
    poses, rows, _ = rows_table.shape
    cols = cols_table.shape[2]
    planes = plane_weight.shape[1]
    slots = CLASSES * planes
    table_y, table_x = packed_dft(box, -1.0), packed_dft(box, 1.0)
    any_place = pl.BlockSpec(memory_space=pl.ANY)
    vmem = pl.BlockSpec(memory_space=pltpu.VMEM)
    lanes = 128 * (-(-2 * count // 128))
    if turns_round == 0:
        out_shape = [jax.ShapeDtypeStruct((slots, rows, 2 * cols), bf16)]
    else:
        slots += 1
        owned = rows // (2 * turns_round)
        x_piece = (turns_round // 2, slots - Z_SLOTS, owned, 2 * cols)
        z_piece = (2, Z_SLOTS, owned, 2 * cols)
        out_shape = [pltpu.VMEM(x_piece, bf16), pltpu.VMEM(x_piece, f32)] * 2
        out_shape += [pltpu.VMEM(z_piece, f32)]
        out_shape += [pltpu.VMEM(z_piece, bf16)] * (turns_round - 1)
    operands = (
        class_index[:, 0], pose_index, defocus_bin, defocus, plane_weight.T,
        jnp.asarray(table_y, bf16), jnp.asarray(table_x.T.copy(), bf16),
        images, rows_table, cols_table,
    )
    return pl.pallas_call(
        slices_kernel,
        out_shape=out_shape,
        in_specs=[any_place] * 10,
        out_specs=[vmem] * len(out_shape),
        scratch_shapes=[pltpu.SMEM(x.shape, x.dtype) for x in operands[:5]]
        + [pltpu.VMEM(x.shape, x.dtype) for x in operands[5:]]
        + [
            pltpu.SemaphoreType.DMA((9 + count // GROUP,)),
            pltpu.VMEM((poses * rows, box), bf16),
            pltpu.VMEM((poses, box, 2 * cols), bf16),
            pltpu.VMEM((box // 2 + 8, lanes), f32),
            pltpu.VMEM((count, box), f32),
            pltpu.VMEM((count, box), f32),
            pltpu.VMEM((2, GROUP * box, box), bf16),
            pltpu.VMEM((SLOTS, box + 16, box), bf16),
            pltpu.VMEM((SLOTS, box, 2 * cols), bf16),
            pltpu.VMEM((slots, rows, 2 * cols), f32),
        ],
        compiler_params=pltpu.CompilerParams(vmem_limit_bytes=VMEM_LIMIT),
        cost_estimate=pl.CostEstimate(
            flops=2 * count * box * box * 1000, bytes_accessed=6 * 1024 * 1024, transcendentals=0
        ),
    )(*operands)


VMEM_LIMIT = 56 * 1024 * 1024


def ridge_kernel(defocus_hbm, plane_hbm, rows_hbm, cols_hbm, high_ref, low_ref, share_ref, *refs):
    defocus_ref, plane_ref, rows_ref, cols_ref, arrived = refs
    poses, owned, box = rows_ref.shape
    cols = cols_ref.shape[2]
    bins = defocus_ref.shape[0]
    planes = plane_ref.shape[0]
    half = box // 2
    first = pl.multiple_of(lax.axis_index("img") * owned, owned)
    copies = [
        pltpu.make_async_copy(defocus_hbm, defocus_ref, arrived.at[0]),
        pltpu.make_async_copy(plane_hbm, plane_ref, arrived.at[1]),
        pltpu.make_async_copy(rows_hbm.at[:, pl.ds(first, owned), :], rows_ref, arrived.at[2]),
        pltpu.make_async_copy(cols_hbm, cols_ref, arrived.at[3]),
    ]
    for copy in copies:
        copy.start()
    for copy in copies:
        copy.wait()
    share_plane = iota((planes * CLASSES, poses * bins), 0) // CLASSES
    share_pose = iota((planes * CLASSES, poses * bins), 1) // bins
    share = jnp.zeros((planes * CLASSES, poses * bins), f32)
    for p in range(poses):
        for z in range(planes):
            share = jnp.where((share_plane == z) & (share_pose == p), plane_ref[z, p], share)
    share_ref[...] = share

    bin_row = iota((bins, box), 0)
    sub_defocus = jnp.zeros((bins, box), f32)
    for b in range(bins):
        sub_defocus = jnp.where(bin_row == b, defocus_ref[b], sub_defocus)
    freq = iota((bins, box), 1)
    freq = jnp.where(freq < half, freq, box - freq).astype(f32)
    turns_x = sub_defocus * (freq * freq * (1.0 / (half * half)))
    turns_y = turns_x + ctf_phase / math.pi
    ones = jnp.ones((bins, box), f32)
    wave_y = jnp.concatenate(
        [0.5 * ones, -0.5 * turns_sine(turns_y + 0.25), 0.5 * turns_sine(turns_y)], 0
    )
    wave_x = jnp.concatenate([ones, turns_sine(turns_x + 0.25), turns_sine(turns_x)], 0)
    y_high, y_low = split_two(wave_y)
    x_high, x_low = split_two(wave_x)
    rows_sq = rows_ref[...].reshape(poses * owned, box).astype(f32)
    rows_sq = (rows_sq * rows_sq).astype(bf16)
    u = dot(y_high, rows_sq, ((1,), (1,))) + dot(y_low, rows_sq, ((1,), (1,)))
    for p in range(poses):
        cols_sq = cols_ref[p].astype(f32)
        cols_sq = (cols_sq * cols_sq).astype(bf16)
        v = dot(x_high, cols_sq) + dot(x_low, cols_sq)
        for r in range(owned):
            column = u[:, p * owned + r : p * owned + r + 1]
            product = v * column
            weight = product[:bins] + product[bins : 2 * bins] + product[2 * bins :]
            high, low = split_two(weight)
            high_ref[p * bins : (p + 1) * bins, r * cols : (r + 1) * cols] = high
            low_ref[p * bins : (p + 1) * bins, r * cols : (r + 1) * cols] = low


def own_ridges(defocus, plane_weight, rows_table, cols_table, owned):
    poses, _, box = rows_table.shape
    cols = cols_table.shape[2]
    bins = defocus.shape[0]
    any_place = pl.BlockSpec(memory_space=pl.ANY)
    vmem = pl.BlockSpec(memory_space=pltpu.VMEM)
    planes = plane_weight.T
    table = jax.ShapeDtypeStruct((poses * bins, owned * cols), bf16)
    return pl.pallas_call(
        ridge_kernel,
        out_shape=[table, table, jax.ShapeDtypeStruct((planes.shape[0] * CLASSES, poses * bins), f32)],
        in_specs=[any_place] * 4,
        out_specs=[vmem] * 3,
        scratch_shapes=[
            pltpu.SMEM(defocus.shape, f32),
            pltpu.SMEM(planes.shape, f32),
            pltpu.VMEM((poses, owned, box), bf16),
            pltpu.VMEM(cols_table.shape, bf16),
            pltpu.SemaphoreType.DMA((4,)),
        ],
        compiler_params=pltpu.CompilerParams(vmem_limit_bytes=16 * 1024 * 1024),
        cost_estimate=pl.CostEstimate(
            flops=1000, bytes_accessed=1000, transcendentals=0
        ),
    )(defocus, planes, rows_table, cols_table)


def call_in_vmem(kernel, arrays, out_shape):
    vmem = pl.BlockSpec(memory_space=pltpu.VMEM)
    return pl.pallas_call(
        kernel,
        out_shape=out_shape,
        in_specs=[vmem] * len(arrays),
        out_specs=[vmem] * len(out_shape),
        compiler_params=pltpu.CompilerParams(vmem_limit_bytes=16 * 1024 * 1024),
        cost_estimate=pl.CostEstimate(flops=1000, bytes_accessed=1000, transcendentals=0),
    )(*arrays)


def fold_kernel(far_keep, far_came, near_send, z_keep, *refs):
    rounds = near_send.shape[0] + far_keep.shape[0]
    z_came, refs = refs[: rounds - 1], refs[rounds - 1 :]
    z_own, x_send, far_sends = refs[0], refs[1], refs[2:]
    for k, send in enumerate(far_sends):
        send[...] = (far_keep[k] + far_came[k].astype(f32)).astype(bf16)
    near, x_slots = near_send.shape[:2]
    for k in range(near):
        x_send[k * x_slots : (k + 1) * x_slots] = near_send[k]
    for side in range(2):
        value = z_keep[side]
        for came in z_came:
            value = value + came[side].astype(f32)
        if side == 0:
            z_own[...] = value
        else:
            x_send[near * x_slots :] = value.astype(bf16)


def fold_phase(far_keep, far_came, near_send, z_keep, z_came):
    far, x_slots = far_keep.shape[:2]
    z_slots = z_keep.shape[1]
    tail = far_keep.shape[2:]
    out_shape = [
        pltpu.VMEM((z_slots,) + tail, f32),
        pltpu.VMEM((near_send.shape[0] * x_slots + z_slots,) + tail, bf16),
    ]
    out_shape += [pltpu.VMEM((x_slots,) + tail, bf16)] * far
    return call_in_vmem(fold_kernel, (far_keep, far_came, near_send, z_keep, *z_came), out_shape)


def near_kernel(keep, came, own, *sends):
    near, x_slots = keep.shape[:2]
    for k, out in enumerate((own,) + sends):
        part = came[k * x_slots : (k + 1) * x_slots].astype(f32)
        out[...] = (keep[k] + part).astype(out.dtype)


def near_phase(keep, came):
    piece = keep.shape[1:]
    out_shape = [pltpu.VMEM(piece, f32)] + [pltpu.VMEM(piece, bf16)] * (keep.shape[0] - 1)
    return call_in_vmem(near_kernel, (keep, came), out_shape)


def weight_kernel(high_ref, low_ref, share_ref, z_own, z_came, out_ref, ridge_ref):
    slots, pairs = share_ref.shape
    owned, _, cols = ridge_ref.shape
    counts = z_own[0] + z_came[z_came.shape[0] - z_own.shape[0]].astype(f32)
    scaled = jnp.concatenate([counts[:CLASSES, :pairs]] * (slots // CLASSES), 0) * share_ref[...]
    c_high, c_low = split_two(scaled)
    weight = (
        dot(c_high, high_ref[...]) + dot(c_low, high_ref[...]) + dot(c_high, low_ref[...])
    )
    ridge = 1.0 / (weight + wiener_ridge)
    for r in range(owned):
        ridge_ref[r] = ridge[:, r * cols : (r + 1) * cols]
    for s in range(slots):
        out_ref[s] = ridge_ref[:, s, :]


def own_weights(tables, z_own, z_came):
    slots = tables[2].shape[0]
    _, owned, wide = z_own.shape
    cols = wide // 2
    vmem = pl.BlockSpec(memory_space=pltpu.VMEM)
    return pl.pallas_call(
        weight_kernel,
        out_shape=pltpu.VMEM((slots, owned, cols), f32),
        in_specs=[vmem] * 5,
        out_specs=vmem,
        scratch_shapes=[pltpu.VMEM((owned, slots, cols), f32)],
        compiler_params=pltpu.CompilerParams(vmem_limit_bytes=16 * 1024 * 1024),
        cost_estimate=pl.CostEstimate(flops=1000, bytes_accessed=1000, transcendentals=0),
    )(*tables, z_own, z_came)


def finish_kernel(planes, ridge_ref, x_own, z_own, z_came, *refs):
    x_came, out_ref = refs[:-1], refs[-1]
    slots, owned, cols = ridge_ref.shape
    first = z_own.shape[0]
    for s in range(slots):
        if s + 1 < first:
            value = z_own[s + 1] + z_came[z_came.shape[0] - first + s + 1].astype(f32)
        else:
            value = x_own[s + 1 - first]
            for part in x_came:
                value = value + part[s + 1 - first].astype(f32)
        factor = ridge_ref[s]
        place = (s % CLASSES) * planes + s // CLASSES
        out_ref[:, 2 * place, :] = value[:, :cols] * factor
        out_ref[:, 2 * place + 1, :] = value[:, cols:] * factor


def finish(planes, ridge, x_own, z_own, z_came, x_came):
    slots, owned, cols = ridge.shape
    vmem = pl.BlockSpec(memory_space=pltpu.VMEM)
    return pl.pallas_call(
        functools.partial(finish_kernel, planes),
        out_shape=jax.ShapeDtypeStruct((owned, 2 * slots, cols), f32),
        in_specs=[vmem] * (4 + len(x_came)),
        out_specs=vmem,
        compiler_params=pltpu.CompilerParams(vmem_limit_bytes=16 * 1024 * 1024),
        cost_estimate=pl.CostEstimate(flops=1000, bytes_accessed=1000, transcendentals=0),
    )(ridge, x_own, z_own, z_came, *x_came)


def squared_table(weight_table):
    wide_table = weight_table.astype(f32)
    return (wide_table * wide_table).astype(bf16)


def weight_totals(class_index, pose_index, defocus_bin, defocus, rows_table, cols_table, plane_weight, first_row, owned):
    box = rows_table.shape[2]
    poses = rows_table.shape[0]
    bins = defocus.shape[0]
    half = box // 2
    exact = lax.Precision.HIGHEST
    code = (class_index[:, 0] * poses + pose_index) * bins + defocus_bin
    codes = lax.all_gather(code, "img", tiled=True)
    hits = (codes[:, None] == jnp.arange(CLASSES * poses * bins, dtype=jnp.int32)).astype(f32)
    counts = jnp.sum(hits, 0).reshape(CLASSES, poses, bins)
    place = jnp.arange(box, dtype=jnp.int32)
    freq = jnp.where(place < half, place, place - box).astype(f32)
    turns = defocus[:, None] * (freq * freq)[None, :] * (1.0 / (half * half))
    turns_y = turns + ctf_phase / math.pi
    ones = jnp.ones_like(turns)
    wave_y = jnp.stack([0.5 * ones, -0.5 * turns_sine(turns_y + 0.25), 0.5 * turns_sine(turns_y)])
    wave_x = jnp.stack([ones, turns_sine(turns + 0.25), turns_sine(turns)])
    rows_own = lax.dynamic_slice_in_dim(rows_table, first_row, owned, 1)
    u = jnp.einsum("pry,mby->pmbr", squared_table(rows_own).astype(f32), wave_y, precision=exact)
    v = jnp.einsum("pxj,mbx->pmbj", squared_table(cols_table).astype(f32), wave_x, precision=exact)
    weight = counts[:, None] * plane_weight.T[None, :, :, None]
    left = weight[:, :, :, None, :, None] * u[None, None]
    return jnp.einsum("czpmbr,pmbj->rczj", left, v, precision=exact)


def by_rounds(images, class_index, pose_index, defocus_bin, defocus, rows_table, cols_table, plane_weight):
    members = lax.axis_size("img")
    rounds = members // 2
    rows = rows_table.shape[1]
    planes = plane_weight.shape[1]
    cols = cols_table.shape[2]
    owned = rows // members
    outs = own_totals(
        images, class_index, pose_index, defocus_bin, defocus, rows_table, cols_table, plane_weight, rounds
    )
    far_send, far_keep, near_send, near_keep, z_keep = outs[:5]
    z_sends = outs[5:]
    near = near_keep.shape[0]

    def along_x(value):
        return lax.ppermute(value, "img", [(i, i ^ 1) for i in range(members)])

    def along_z(value, k):
        return lax.ppermute(value, "img", [(i, i ^ (2 * k)) for i in range(members)])

    far_ks, near_ks = range(near, rounds)[::-1], range(1, near)
    far_came = along_x(far_send)
    z_came = [along_z(z_sends[k - 1], k) for k in (*far_ks, *near_ks)]
    tables = own_ridges(defocus, plane_weight, rows_table, cols_table, owned)
    far_keep, tables = lax.optimization_barrier((far_keep, tables))
    z_own, x_send, *x_sends = fold_phase(far_keep, far_came, near_send, z_keep, z_came)
    z_came = along_x(x_send)
    x_came = [along_z(send, k) for send, k in zip(x_sends, far_ks)]
    x_own, *x_sends = near_phase(near_keep, z_came)
    x_came += [along_z(send, k) for send, k in zip(x_sends, near_ks)]
    ridge = own_weights(tables, z_own, z_came)
    out = finish(planes, ridge, x_own, z_own, z_came, x_came)
    return out.reshape(owned, CLASSES, planes, 2, cols)


def by_scatter(images, class_index, pose_index, defocus_bin, defocus, rows_table, cols_table, plane_weight):
    rows = rows_table.shape[1]
    cols = cols_table.shape[2]
    planes = plane_weight.shape[1]
    members = lax.axis_size("img")
    owned = rows // members
    (totals,) = own_totals(
        images, class_index, pose_index, defocus_bin, defocus, rows_table, cols_table, plane_weight, 0
    )
    slots = totals.shape[0]
    totals = totals.reshape(slots, members, owned, 2 * cols).transpose(1, 0, 2, 3)
    own = lax.psum_scatter(totals, "img", scatter_dimension=0, tiled=False)
    weight = weight_totals(
        class_index, pose_index, defocus_bin, defocus, rows_table, cols_table, plane_weight,
        lax.axis_index("img") * owned, owned,
    )
    own = own.astype(f32).reshape(planes, CLASSES, owned, 2, cols).transpose(2, 1, 0, 3, 4)
    return own / (weight[:, :, :, None, :] + wiener_ridge)


def body(*arrays):
    rows = arrays[5].shape[1]
    members = lax.axis_size("img")
    images = members * arrays[0].shape[0]
    small = members >= 4 and members & (members - 1) == 0 and images <= 256 and rows % (16 * members) == 0
    return (by_rounds if small else by_scatter)(*arrays)


def solution(mesh):
    placed = (
        P(("groups", "img"), None, None),
        P(("groups", "img"), None),
        P(("groups", "img")),
        P(("groups", "img")),
        P(),
        P(),
        P(None, None, "slab"),
        P(),
    )
    return jax.shard_map(
        body,
        mesh=mesh,
        in_specs=placed,
        out_specs=P("img", "groups", None, None, "slab"),
        check_vma=False,
    )
```

```python
import functools
import math

import jax
import jax.numpy as jnp
import numpy as np
from jax import lax
from jax.experimental import pallas as pl
from jax.experimental.pallas import tpu as pltpu
from jax.sharding import PartitionSpec as P

CLASSES = 8

wiener_ridge = 1.0
ctf_phase = 0.1
f32 = jnp.float32
bf16 = jnp.bfloat16


def packed_dft(box, sine_sign):
    half = box // 2
    k = np.concatenate([np.arange(half), [half], np.arange(1, half)])
    angle = (k[:, None] * np.arange(box)[None, :] % box) * (2.0 * math.pi / box)
    table = np.where((np.arange(box) <= half)[:, None], np.cos(angle), sine_sign * np.sin(angle))
    return (table / math.sqrt(box)).astype(np.float32)


def iota(shape, axis):
    return lax.broadcasted_iota(jnp.int32, shape, axis)


def dot(a, b, dims=((1,), (0,))):
    return lax.dot_general(a, b, (dims, ((), ())), preferred_element_type=f32)


def turns_sine(turns):
    return jnp.sin((turns - jnp.round(turns)) * (2.0 * math.pi))


def split_two(value):
    high = value.astype(bf16)
    return high, (value - high.astype(f32)).astype(bf16)


def fold_of(place, half):
    box = 2 * half
    return jnp.where(place <= half, place, box + half - place)


def slices_kernel(
    class_hbm, pose_hbm, bin_hbm, defocus_hbm, plane_hbm,
    dft_hbm, dft_t_hbm, images_hbm, rows_hbm, cols_hbm,
    *refs,
):
    outs, refs = refs[:-SCRATCH], refs[-SCRATCH:]
    (
        class_ref, pose_ref, bin_ref, defocus_ref, plane_ref,
        dft_ref, dft_t_ref, images_ref, rows_ref, cols_ref, arrived,
        rows_fold, cols_fold, wave_y, cos_x, sin_x, half_ref, spec_ref, mix_ref, totals,
    ) = refs
    count, box, _ = images_ref.shape
    half = box // 2
    poses, rows, _ = rows_ref.shape
    cols = cols_ref.shape[2]
    planes = plane_ref.shape[0]

    pairs = (
        (class_hbm, class_ref), (pose_hbm, pose_ref), (bin_hbm, bin_ref),
        (defocus_hbm, defocus_ref), (plane_hbm, plane_ref),
        (dft_hbm, dft_ref), (images_hbm.at[0:GROUP], images_ref.at[0:GROUP]),
        (dft_t_hbm, dft_t_ref), (cols_hbm, cols_ref), (rows_hbm, rows_ref),
    ) + tuple(
        (images_hbm.at[i : i + GROUP], images_ref.at[i : i + GROUP])
        for i in range(GROUP, count, GROUP)
    )
    copies = [
        pltpu.make_async_copy(source, target, arrived.at[n])
        for n, (source, target) in enumerate(pairs)
    ]
    for copy in copies:
        copy.start()

    place = iota((box, box), 0)
    other = iota((box, box), 1)
    folded = fold_of(place, half)
    near = (folded == other).astype(f32).astype(bf16)
    far = (jnp.where(folded == 0, 0, box - folded) == other).astype(f32).astype(bf16)

    for copy in copies[:5]:
        copy.wait()
    tall, lanes = wave_y.shape
    lane = iota((1, lanes), 1)
    sub = iota((count, box), 0)
    lane_defocus = jnp.zeros((1, lanes), f32)
    sub_defocus = jnp.zeros((count, box), f32)
    for i in range(count):
        value = defocus_ref[bin_ref[i]]
        lane_defocus = jnp.where(lane % count == i, value, lane_defocus)
        sub_defocus = jnp.where(sub == i, value, sub_defocus)
    scale = 1.0 / (2 * half * half)
    ky = iota((tall, lanes), 0).astype(f32)
    quarter = jnp.where(lane < count, 0.0, 0.25) + ctf_phase / (2.0 * math.pi)
    wave_y[...] = turns_sine(lane_defocus * (ky * ky * scale) + quarter)
    kx = iota((count, box), 1)
    kx = jnp.where(kx <= half, kx, kx - half).astype(f32)
    turns = sub_defocus * (kx * kx * scale)
    cos_x[...] = -turns_sine(turns + 0.25)
    sin_x[...] = -turns_sine(turns)
    totals[...] = jnp.zeros_like(totals)
    leading = 1 if len(outs) > 1 else 0
    if len(outs) > 1:
        bins = defocus_ref.shape[0]
        count_row = iota((16, 2 * cols), 0)
        count_lane = iota((16, 2 * cols), 1)
        counts = jnp.zeros((16, 2 * cols), f32)
        for i in range(count):
            hit = (count_row == class_ref[i]) & (count_lane == pose_ref[i] * bins + bin_ref[i])
            counts = counts + jnp.where(hit, 1.0, 0.0)
        totals[0] = jnp.tile(counts, (rows // 16, 1))

    tile = 8
    tile_row = iota((tile, half), 0) == 0
    tile_col = iota((tile, half), 1) == 0
    col_zero = iota((half, half), 1) == 0
    short_row = iota((16, half), 0) == 0
    short_col = iota((16, half), 1) == 0

    def without_row(value):
        return jnp.concatenate([jnp.where(tile_row, 0.0, value[:tile]), value[tile:]], 0)

    def along_rows(i):
        copies[6 if i == 0 else 9 + i // GROUP].wait()
        group = jnp.concatenate([images_ref[i + n] for n in range(GROUP)], 1)
        product = dot(dft_ref[...], group).astype(bf16)
        for n in range(GROUP):
            half_ref[i // GROUP % 2, n * box : (n + 1) * box] = product[:, n * box : (n + 1) * box]

    def along_columns(i):
        product = dot(half_ref[i // GROUP % 2], dft_t_ref[...])
        for n in range(GROUP):
            weigh(i + n, product[n * box : (n + 1) * box])

    def weigh(i, y):
        sin_col = jnp.broadcast_to(wave_y[:, i : i + 1], (tall, half))
        cos_col = jnp.broadcast_to(wave_y[:, count + i : count + i + 1], (tall, half))
        near_ctf = sin_col * cos_x[i : i + 1, :half] + cos_col * sin_x[i : i + 1, :half]
        far_ctf = sin_col * cos_x[i : i + 1, half:] + cos_col * sin_x[i : i + 1, half:]
        cc, cs = y[:half, :half], y[:half, half:]
        sc, ss = y[half:, :half], y[half:, half:]
        ss_row = without_row(ss)
        ss_in = jnp.where(col_zero, 0.0, ss_row)
        sc_in = without_row(sc)
        cs_in = jnp.where(col_zero, 0.0, cs)
        near_y, far_y = near_ctf[:half], far_ctf[:half]
        spec = spec_ref.at[i % SLOTS]
        spec[0:half, 0:half] = (near_y * (cc + ss_in)).astype(bf16)
        spec[0:half, half:] = (far_y * jnp.where(col_zero, cs, cc - ss_in)).astype(bf16)
        spec[half:box, 0:half] = (near_y * (sc_in - cs_in)).astype(bf16)
        spec[half:box, half:] = (far_y * jnp.where(col_zero, ss_row, sc_in + cs_in)).astype(bf16)
        sc_top = jnp.broadcast_to(sc[0:1], (16, half))
        ss_top = jnp.broadcast_to(ss[0:1], (16, half))
        ss_top_in = jnp.where(short_col, 0.0, ss_top)
        spec[box : box + 16, 0:half] = (
            near_ctf[half : half + 1] * jnp.where(short_row, sc_top, -ss_top_in)
        ).astype(bf16)
        spec[box : box + 16, half:] = (
            far_ctf[half : half + 1]
            * jnp.where(short_row, jnp.where(short_col, ss_top, sc_top), ss_top_in)
        ).astype(bf16)

    def mix(i):
        mixed = dot(spec_ref[i % SLOTS], cols_fold[pose_ref[i]])
        out = mix_ref.at[i % SLOTS]
        out[0:half, 0:cols] = mixed[:half, :cols].astype(bf16)
        out[0:half, cols:] = mixed[half:box, :cols].astype(bf16)
        top = iota((16, cols), 0) == 0
        real, imag = mixed[:half, cols:], -mixed[half:box, cols:]
        out[half : half + 16, 0:cols] = jnp.where(
            top, mixed[box : box + 1, :cols], real[:16]
        ).astype(bf16)
        out[half : half + 16, cols:] = jnp.where(
            top, mixed[box + 1 : box + 2, :cols], imag[:16]
        ).astype(bf16)
        out[half + 16 :, 0:cols] = real[16:].astype(bf16)
        out[half + 16 :, cols:] = imag[16:].astype(bf16)

    def insert(i):
        pose = pose_ref[i]
        pose_rows = rows_fold[pl.ds(pl.multiple_of(pose * rows, rows), rows), :]
        piece = dot(pose_rows, mix_ref[i % SLOTS])
        for z in range(planes):
            slot = leading + z * CLASSES + class_ref[i]
            totals[slot] += plane_ref[z, pose] * piece

    copies[5].wait()
    along_rows(0)
    copies[7].wait()
    copies[8].wait()
    for p in range(0, poses, 2):
        two = jnp.concatenate([cols_ref[p], cols_ref[p + 1]], 1)
        near_two = dot(near, two).astype(bf16)
        far_two = dot(far, two).astype(bf16)
        cols_fold[p] = jnp.concatenate([near_two[:, :cols], far_two[:, :cols]], 1)
        cols_fold[p + 1] = jnp.concatenate([near_two[:, cols:], far_two[:, cols:]], 1)
    along_rows(GROUP)
    along_columns(0)
    copies[9].wait()
    rows_fold[...] = dot(
        rows_ref[...].reshape(poses * rows, box), near, ((1,), (1,))
    ).astype(bf16)
    for step in range(2 * GROUP, count + 3 * GROUP, GROUP):
        for n in range(GROUP):
            if step >= 3 * GROUP:
                insert(step - 3 * GROUP + n)
            if step - 2 * GROUP < count:
                mix(step - 2 * GROUP + n)
        if step - GROUP < count:
            along_columns(step - GROUP)
        if step < count:
            along_rows(step)

    if len(outs) == 1:
        outs[0][...] = totals[...].astype(bf16)
        return
    x_send, x_keep, own_send, own_keep, z_send, z_keep = outs
    x_slots, owned, _ = own_keep.shape
    me = lax.axis_index("img")

    def rows_of(flip):
        return pl.ds(pl.multiple_of((me ^ flip) * owned, owned), owned)

    for n, k in enumerate(LINE):
        x_send[n] = totals[-x_slots:, rows_of(2 * k + 1), :].astype(bf16)
        x_keep[n] = totals[-x_slots:, rows_of(2 * k), :]
    own_send[...] = totals[-x_slots:, rows_of(1), :].astype(bf16)
    own_keep[...] = totals[-x_slots:, rows_of(0), :]
    for n in range(4):
        z_send[n] = totals[:-x_slots, rows_of(n + 4), :].astype(bf16)
        z_keep[n] = totals[:-x_slots, rows_of(n), :]


SCRATCH = 20
LINE = (2, 3, 1)
SLOTS = 8
GROUP = 4
Z_SLOTS = 4


def own_totals(images, class_index, pose_index, defocus_bin, defocus, rows_table, cols_table, plane_weight, members):
    count, box, _ = images.shape
    poses, rows, _ = rows_table.shape
    cols = cols_table.shape[2]
    planes = plane_weight.shape[1]
    slots = CLASSES * planes
    table_y, table_x = packed_dft(box, -1.0), packed_dft(box, 1.0)
    any_place = pl.BlockSpec(memory_space=pl.ANY)
    vmem = pl.BlockSpec(memory_space=pltpu.VMEM)
    lanes = 128 * (-(-2 * count // 128))
    if members == 1:
        out_shape = [jax.ShapeDtypeStruct((slots, rows, 2 * cols), bf16)]
    else:
        slots += 1
        tail = (rows // members, 2 * cols)
        x_slots = slots - Z_SLOTS
        out_shape = []
        for lead in ((len(LINE), x_slots), (x_slots,), (4, Z_SLOTS)):
            out_shape += [pltpu.VMEM(lead + tail, bf16), pltpu.VMEM(lead + tail, f32)]
    operands = (
        class_index[:, 0], pose_index, defocus_bin, defocus, plane_weight.T,
        jnp.asarray(table_y, bf16), jnp.asarray(table_x.T.copy(), bf16),
        images, rows_table, cols_table,
    )
    return pl.pallas_call(
        slices_kernel,
        out_shape=out_shape,
        in_specs=[any_place] * 10,
        out_specs=[vmem] * len(out_shape),
        scratch_shapes=[pltpu.SMEM(x.shape, x.dtype) for x in operands[:5]]
        + [pltpu.VMEM(x.shape, x.dtype) for x in operands[5:]]
        + [
            pltpu.SemaphoreType.DMA((9 + count // GROUP,)),
            pltpu.VMEM((poses * rows, box), bf16),
            pltpu.VMEM((poses, box, 2 * cols), bf16),
            pltpu.VMEM((box // 2 + 8, lanes), f32),
            pltpu.VMEM((count, box), f32),
            pltpu.VMEM((count, box), f32),
            pltpu.VMEM((2, GROUP * box, box), bf16),
            pltpu.VMEM((SLOTS, box + 16, box), bf16),
            pltpu.VMEM((SLOTS, box, 2 * cols), bf16),
            pltpu.VMEM((slots, rows, 2 * cols), f32),
        ],
        compiler_params=pltpu.CompilerParams(vmem_limit_bytes=VMEM_LIMIT),
        cost_estimate=pl.CostEstimate(
            flops=2 * count * box * box * 1000, bytes_accessed=6 * 1024 * 1024, transcendentals=0
        ),
    )(*operands)


VMEM_LIMIT = 56 * 1024 * 1024


def ridge_kernel(defocus_hbm, plane_hbm, rows_hbm, cols_hbm, high_ref, low_ref, share_ref, *refs):
    defocus_ref, plane_ref, rows_ref, cols_ref, arrived = refs
    poses, owned, box = rows_ref.shape
    cols = cols_ref.shape[2]
    bins = defocus_ref.shape[0]
    planes = plane_ref.shape[0]
    half = box // 2
    first = pl.multiple_of(lax.axis_index("img") * owned, owned)
    copies = [
        pltpu.make_async_copy(defocus_hbm, defocus_ref, arrived.at[0]),
        pltpu.make_async_copy(plane_hbm, plane_ref, arrived.at[1]),
        pltpu.make_async_copy(rows_hbm.at[:, pl.ds(first, owned), :], rows_ref, arrived.at[2]),
        pltpu.make_async_copy(cols_hbm, cols_ref, arrived.at[3]),
    ]
    for copy in copies:
        copy.start()
    for copy in copies:
        copy.wait()
    share_plane = iota((planes * CLASSES, poses * bins), 0) // CLASSES
    share_pose = iota((planes * CLASSES, poses * bins), 1) // bins
    share = jnp.zeros((planes * CLASSES, poses * bins), f32)
    for p in range(poses):
        for z in range(planes):
            share = jnp.where((share_plane == z) & (share_pose == p), plane_ref[z, p], share)
    share_ref[...] = share

    bin_row = iota((bins, box), 0)
    sub_defocus = jnp.zeros((bins, box), f32)
    for b in range(bins):
        sub_defocus = jnp.where(bin_row == b, defocus_ref[b], sub_defocus)
    freq = iota((bins, box), 1)
    freq = jnp.where(freq < half, freq, box - freq).astype(f32)
    turns_x = sub_defocus * (freq * freq * (1.0 / (half * half)))
    turns_y = turns_x + ctf_phase / math.pi
    ones = jnp.ones((bins, box), f32)
    wave_y = jnp.concatenate(
        [0.5 * ones, -0.5 * turns_sine(turns_y + 0.25), 0.5 * turns_sine(turns_y)], 0
    )
    wave_x = jnp.concatenate([ones, turns_sine(turns_x + 0.25), turns_sine(turns_x)], 0)
    y_high, y_low = split_two(wave_y)
    x_high, x_low = split_two(wave_x)
    rows_sq = rows_ref[...].reshape(poses * owned, box).astype(f32)
    rows_sq = (rows_sq * rows_sq).astype(bf16)
    u = dot(y_high, rows_sq, ((1,), (1,))) + dot(y_low, rows_sq, ((1,), (1,)))
    for p in range(poses):
        cols_sq = cols_ref[p].astype(f32)
        cols_sq = (cols_sq * cols_sq).astype(bf16)
        v = dot(x_high, cols_sq) + dot(x_low, cols_sq)
        for r in range(owned):
            column = u[:, p * owned + r : p * owned + r + 1]
            product = v * column
            weight = product[:bins] + product[bins : 2 * bins] + product[2 * bins :]
            high, low = split_two(weight)
            high_ref[p * bins : (p + 1) * bins, r * cols : (r + 1) * cols] = high
            low_ref[p * bins : (p + 1) * bins, r * cols : (r + 1) * cols] = low


def own_ridges(defocus, plane_weight, rows_table, cols_table, owned):
    poses, _, box = rows_table.shape
    cols = cols_table.shape[2]
    bins = defocus.shape[0]
    any_place = pl.BlockSpec(memory_space=pl.ANY)
    vmem = pl.BlockSpec(memory_space=pltpu.VMEM)
    planes = plane_weight.T
    table = jax.ShapeDtypeStruct((poses * bins, owned * cols), bf16)
    return pl.pallas_call(
        ridge_kernel,
        out_shape=[table, table, jax.ShapeDtypeStruct((planes.shape[0] * CLASSES, poses * bins), f32)],
        in_specs=[any_place] * 4,
        out_specs=[vmem] * 3,
        scratch_shapes=[
            pltpu.SMEM(defocus.shape, f32),
            pltpu.SMEM(planes.shape, f32),
            pltpu.VMEM((poses, owned, box), bf16),
            pltpu.VMEM(cols_table.shape, bf16),
            pltpu.SemaphoreType.DMA((4,)),
        ],
        compiler_params=pltpu.CompilerParams(vmem_limit_bytes=16 * 1024 * 1024),
        cost_estimate=pl.CostEstimate(
            flops=1000, bytes_accessed=1000, transcendentals=0
        ),
    )(defocus, planes, rows_table, cols_table)


def call_in_vmem(kernel, arrays, out_shape):
    vmem = pl.BlockSpec(memory_space=pltpu.VMEM)
    return pl.pallas_call(
        kernel,
        out_shape=out_shape,
        in_specs=[vmem] * len(arrays),
        out_specs=[vmem] * len(out_shape),
        compiler_params=pltpu.CompilerParams(vmem_limit_bytes=16 * 1024 * 1024),
        cost_estimate=pl.CostEstimate(flops=1000, bytes_accessed=1000, transcendentals=0),
    )(*arrays)


def fold_kernel(x_keep, x_came, z_keep, z_came, own_send, far_a, far_b, near, z_kept, own_out):
    own_out[...] = own_send[...]
    x_slots, z_slots = x_keep.shape[1], z_keep.shape[1]
    for n, send in enumerate((far_a, far_b, near)):
        send[:x_slots] = (x_keep[n] + x_came[n].astype(f32)).astype(bf16)
    for side in range(2):
        z_kept[side] = z_keep[side] + z_came[side].astype(f32)
        first = x_slots + side * z_slots
        near[first : first + z_slots] = (
            z_keep[2 + side] + z_came[2 + side].astype(f32)
        ).astype(bf16)


def fold_phase(x_keep, x_came, z_keep, z_came, own_send):
    x_slots, z_slots = x_keep.shape[1], z_keep.shape[1]
    tail = x_keep.shape[2:]
    out_shape = [pltpu.VMEM((x_slots,) + tail, bf16)] * 2
    out_shape += [pltpu.VMEM((x_slots + 2 * z_slots,) + tail, bf16), pltpu.VMEM((2, z_slots) + tail, f32)]
    out_shape += [pltpu.VMEM(own_send.shape, bf16)]
    return call_in_vmem(fold_kernel, (x_keep, x_came, z_keep, z_came, own_send), out_shape)


def side_kernel(z_kept, near_came, z_own, z_send):
    z_slots = z_own.shape[0]
    first = near_came.shape[0] - 2 * z_slots
    z_own[...] = z_kept[0] + near_came[first : first + z_slots].astype(f32)
    z_send[...] = (z_kept[1] + near_came[first + z_slots :].astype(f32)).astype(bf16)


def side_phase(z_kept, near_came):
    piece = z_kept.shape[1:]
    return call_in_vmem(side_kernel, (z_kept, near_came), [pltpu.VMEM(piece, f32), pltpu.VMEM(piece, bf16)])


def weight_kernel(high_ref, low_ref, share_ref, z_own, z_came, out_ref, ridge_ref):
    slots, pairs = share_ref.shape
    owned, _, cols = ridge_ref.shape
    counts = z_own[0] + z_came[0].astype(f32)
    scaled = jnp.concatenate([counts[:CLASSES, :pairs]] * (slots // CLASSES), 0) * share_ref[...]
    c_high, c_low = split_two(scaled)
    weight = (
        dot(c_high, high_ref[...]) + dot(c_low, high_ref[...]) + dot(c_high, low_ref[...])
    )
    ridge = 1.0 / (weight + wiener_ridge)
    for r in range(owned):
        ridge_ref[r] = ridge[:, r * cols : (r + 1) * cols]
    for s in range(slots):
        out_ref[s] = ridge_ref[:, s, :]


def own_weights(tables, z_own, z_came):
    slots = tables[2].shape[0]
    _, owned, wide = z_own.shape
    cols = wide // 2
    vmem = pl.BlockSpec(memory_space=pltpu.VMEM)
    return pl.pallas_call(
        weight_kernel,
        out_shape=pltpu.VMEM((slots, owned, cols), f32),
        in_specs=[vmem] * 5,
        out_specs=vmem,
        scratch_shapes=[pltpu.VMEM((owned, slots, cols), f32)],
        compiler_params=pltpu.CompilerParams(vmem_limit_bytes=16 * 1024 * 1024),
        cost_estimate=pl.CostEstimate(flops=1000, bytes_accessed=1000, transcendentals=0),
    )(*tables, z_own, z_came)


def finish_kernel(planes, ridge_ref, x_own, z_own, z_came, *refs):
    x_came, out_ref = refs[:-1], refs[-1]
    slots, owned, cols = ridge_ref.shape
    first = z_own.shape[0]
    for s in range(slots):
        if s + 1 < first:
            value = z_own[s + 1] + z_came[s + 1].astype(f32)
        else:
            value = x_own[s + 1 - first]
            for part in x_came:
                value = value + part[s + 1 - first].astype(f32)
        factor = ridge_ref[s]
        place = (s % CLASSES) * planes + s // CLASSES
        out_ref[:, 2 * place, :] = value[:, :cols] * factor
        out_ref[:, 2 * place + 1, :] = value[:, cols:] * factor


def finish(planes, ridge, x_own, z_own, z_came, x_came):
    slots, owned, cols = ridge.shape
    vmem = pl.BlockSpec(memory_space=pltpu.VMEM)
    return pl.pallas_call(
        functools.partial(finish_kernel, planes),
        out_shape=jax.ShapeDtypeStruct((owned, 2 * slots, cols), f32),
        in_specs=[vmem] * (4 + len(x_came)),
        out_specs=vmem,
        compiler_params=pltpu.CompilerParams(vmem_limit_bytes=16 * 1024 * 1024),
        cost_estimate=pl.CostEstimate(flops=1000, bytes_accessed=1000, transcendentals=0),
    )(ridge, x_own, z_own, z_came, *x_came)


def squared_table(weight_table):
    wide_table = weight_table.astype(f32)
    return (wide_table * wide_table).astype(bf16)


def weight_totals(class_index, pose_index, defocus_bin, defocus, rows_table, cols_table, plane_weight, first_row, owned):
    box = rows_table.shape[2]
    poses = rows_table.shape[0]
    bins = defocus.shape[0]
    half = box // 2
    exact = lax.Precision.HIGHEST
    code = (class_index[:, 0] * poses + pose_index) * bins + defocus_bin
    codes = lax.all_gather(code, "img", tiled=True)
    hits = (codes[:, None] == jnp.arange(CLASSES * poses * bins, dtype=jnp.int32)).astype(f32)
    counts = jnp.sum(hits, 0).reshape(CLASSES, poses, bins)
    place = jnp.arange(box, dtype=jnp.int32)
    freq = jnp.where(place < half, place, place - box).astype(f32)
    turns = defocus[:, None] * (freq * freq)[None, :] * (1.0 / (half * half))
    turns_y = turns + ctf_phase / math.pi
    ones = jnp.ones_like(turns)
    wave_y = jnp.stack([0.5 * ones, -0.5 * turns_sine(turns_y + 0.25), 0.5 * turns_sine(turns_y)])
    wave_x = jnp.stack([ones, turns_sine(turns + 0.25), turns_sine(turns)])
    rows_own = lax.dynamic_slice_in_dim(rows_table, first_row, owned, 1)
    u = jnp.einsum("pry,mby->pmbr", squared_table(rows_own).astype(f32), wave_y, precision=exact)
    v = jnp.einsum("pxj,mbx->pmbj", squared_table(cols_table).astype(f32), wave_x, precision=exact)
    weight = counts[:, None] * plane_weight.T[None, :, :, None]
    left = weight[:, :, :, None, :, None] * u[None, None]
    return jnp.einsum("czpmbr,pmbj->rczj", left, v, precision=exact)


def by_pairs(images, class_index, pose_index, defocus_bin, defocus, rows_table, cols_table, plane_weight):
    members = lax.axis_size("img")
    rows = rows_table.shape[1]
    planes = plane_weight.shape[1]
    cols = cols_table.shape[2]
    owned = rows // members

    def exchange(value, flip):
        return lax.ppermute(value, "img", [(i, i ^ flip) for i in range(members)])

    x_send, x_keep, own_send, own_keep, z_send, z_keep = own_totals(
        images, class_index, pose_index, defocus_bin, defocus, rows_table, cols_table, plane_weight, members
    )
    x_came = exchange(x_send, 1)
    z_came = exchange(z_send, 4)
    tables = own_ridges(defocus, plane_weight, rows_table, cols_table, owned)
    x_keep, tables = lax.optimization_barrier((x_keep, tables))
    far_a, far_b, near, z_kept, own_send = fold_phase(x_keep, x_came, z_keep, z_came, own_send)
    near_came = exchange(near, 2)
    far_a, far_b = exchange(far_a, 4), exchange(far_b, 6)
    own_came = exchange(own_send, 1)
    z_own, z_send = side_phase(z_kept, near_came)
    z_came = exchange(z_send, 1)
    ridge = own_weights(tables, z_own, z_came)
    out = finish(planes, ridge, own_keep, z_own, z_came, (near_came, far_a, far_b, own_came))
    return out.reshape(owned, CLASSES, planes, 2, cols)


def by_scatter(images, class_index, pose_index, defocus_bin, defocus, rows_table, cols_table, plane_weight):
    rows = rows_table.shape[1]
    cols = cols_table.shape[2]
    planes = plane_weight.shape[1]
    members = lax.axis_size("img")
    owned = rows // members
    (totals,) = own_totals(
        images, class_index, pose_index, defocus_bin, defocus, rows_table, cols_table, plane_weight, 1
    )
    slots = totals.shape[0]
    totals = totals.reshape(slots, members, owned, 2 * cols).transpose(1, 0, 2, 3)
    own = lax.psum_scatter(totals, "img", scatter_dimension=0, tiled=False)
    weight = weight_totals(
        class_index, pose_index, defocus_bin, defocus, rows_table, cols_table, plane_weight,
        lax.axis_index("img") * owned, owned,
    )
    own = own.astype(f32).reshape(planes, CLASSES, owned, 2, cols).transpose(2, 1, 0, 3, 4)
    return own / (weight[:, :, :, None, :] + wiener_ridge)


def body(*arrays):
    rows = arrays[5].shape[1]
    members = lax.axis_size("img")
    images = members * arrays[0].shape[0]
    paired = members == 8 and images <= 256 and rows % (16 * members) == 0
    return (by_pairs if paired else by_scatter)(*arrays)


def solution(mesh):
    placed = (
        P(("groups", "img"), None, None),
        P(("groups", "img"), None),
        P(("groups", "img")),
        P(("groups", "img")),
        P(),
        P(),
        P(None, None, "slab"),
        P(),
    )
    return jax.shard_map(
        body,
        mesh=mesh,
        in_specs=placed,
        out_specs=P("img", "groups", None, None, "slab"),
        check_vma=False,
    )
```

```python
import functools
import math

import jax
import jax.numpy as jnp
import numpy as np
from jax import lax
from jax.experimental import pallas as pl
from jax.experimental.pallas import tpu as pltpu
from jax.sharding import PartitionSpec as P

CLASSES = 8

wiener_ridge = 1.0
ctf_phase = 0.1
f32 = jnp.float32
bf16 = jnp.bfloat16


def packed_dft(box, sine_sign):
    half = box // 2
    k = np.concatenate([np.arange(half), [half], np.arange(1, half)])
    angle = (k[:, None] * np.arange(box)[None, :] % box) * (2.0 * math.pi / box)
    table = np.where((np.arange(box) <= half)[:, None], np.cos(angle), sine_sign * np.sin(angle))
    return (table / math.sqrt(box)).astype(np.float32)


def iota(shape, axis):
    return lax.broadcasted_iota(jnp.int32, shape, axis)


def dot(a, b, dims=((1,), (0,))):
    return lax.dot_general(a, b, (dims, ((), ())), preferred_element_type=f32)


def turns_sine(turns):
    return jnp.sin((turns - jnp.round(turns)) * (2.0 * math.pi))


def split_two(value):
    high = value.astype(bf16)
    return high, (value - high.astype(f32)).astype(bf16)


def fold_of(place, half):
    box = 2 * half
    return jnp.where(place <= half, place, box + half - place)


def slices_kernel(
    class_hbm, pose_hbm, bin_hbm, defocus_hbm, plane_hbm,
    dft_hbm, dft_t_hbm, images_hbm, rows_hbm, cols_hbm,
    *refs,
):
    outs, refs = refs[:-SCRATCH], refs[-SCRATCH:]
    (
        class_ref, pose_ref, bin_ref, defocus_ref, plane_ref,
        dft_ref, dft_t_ref, images_ref, rows_ref, cols_ref, arrived,
        rows_fold, cols_fold, wave_y, cos_x, sin_x, half_ref, spec_ref, mix_ref, totals,
    ) = refs
    count, box, _ = images_ref.shape
    half = box // 2
    poses, rows, _ = rows_ref.shape
    cols = cols_ref.shape[2]
    planes = plane_ref.shape[0]

    pairs = (
        (class_hbm, class_ref), (pose_hbm, pose_ref), (bin_hbm, bin_ref),
        (defocus_hbm, defocus_ref), (plane_hbm, plane_ref),
        (dft_hbm, dft_ref), (images_hbm.at[0:GROUP], images_ref.at[0:GROUP]),
        (dft_t_hbm, dft_t_ref), (cols_hbm, cols_ref), (rows_hbm, rows_ref),
    ) + tuple(
        (images_hbm.at[i : i + GROUP], images_ref.at[i : i + GROUP])
        for i in range(GROUP, count, GROUP)
    )
    copies = [
        pltpu.make_async_copy(source, target, arrived.at[n])
        for n, (source, target) in enumerate(pairs)
    ]
    for copy in copies:
        copy.start()

    place = iota((box, box), 0)
    other = iota((box, box), 1)
    folded = fold_of(place, half)
    near = (folded == other).astype(f32).astype(bf16)
    far = (jnp.where(folded == 0, 0, box - folded) == other).astype(f32).astype(bf16)

    for copy in copies[:5]:
        copy.wait()
    tall, lanes = wave_y.shape
    lane = iota((1, lanes), 1)
    sub = iota((count, box), 0)
    lane_defocus = jnp.zeros((1, lanes), f32)
    sub_defocus = jnp.zeros((count, box), f32)
    for i in range(count):
        value = defocus_ref[bin_ref[i]]
        lane_defocus = jnp.where(lane % count == i, value, lane_defocus)
        sub_defocus = jnp.where(sub == i, value, sub_defocus)
    scale = 1.0 / (2 * half * half)
    ky = iota((tall, lanes), 0).astype(f32)
    quarter = jnp.where(lane < count, 0.0, 0.25) + ctf_phase / (2.0 * math.pi)
    wave_y[...] = turns_sine(lane_defocus * (ky * ky * scale) + quarter)
    kx = iota((count, box), 1)
    kx = jnp.where(kx <= half, kx, kx - half).astype(f32)
    turns = sub_defocus * (kx * kx * scale)
    cos_x[...] = -turns_sine(turns + 0.25)
    sin_x[...] = -turns_sine(turns)
    totals[...] = jnp.zeros_like(totals)
    leading = 1 if len(outs) > 1 else 0
    if len(outs) > 1:
        bins = defocus_ref.shape[0]
        count_row = iota((16, 2 * cols), 0)
        count_lane = iota((16, 2 * cols), 1)
        counts = jnp.zeros((16, 2 * cols), f32)
        for i in range(count):
            hit = (count_row == class_ref[i]) & (count_lane == pose_ref[i] * bins + bin_ref[i])
            counts = counts + jnp.where(hit, 1.0, 0.0)
        totals[0] = jnp.tile(counts, (rows // 16, 1))

    tile = 8
    tile_row = iota((tile, half), 0) == 0
    tile_col = iota((tile, half), 1) == 0
    col_zero = iota((half, half), 1) == 0
    short_row = iota((16, half), 0) == 0
    short_col = iota((16, half), 1) == 0

    def without_row(value):
        return jnp.concatenate([jnp.where(tile_row, 0.0, value[:tile]), value[tile:]], 0)

    def along_rows(i):
        copies[6 if i == 0 else 9 + i // GROUP].wait()
        group = jnp.concatenate([images_ref[i + n] for n in range(GROUP)], 1)
        product = dot(dft_ref[...], group).astype(bf16)
        for n in range(GROUP):
            half_ref[i // GROUP % 2, n * box : (n + 1) * box] = product[:, n * box : (n + 1) * box]

    def along_columns(i):
        product = dot(half_ref[i // GROUP % 2], dft_t_ref[...])
        for n in range(GROUP):
            weigh(i + n, product[n * box : (n + 1) * box])

    def weigh(i, y):
        sin_col = jnp.broadcast_to(wave_y[:, i : i + 1], (tall, half))
        cos_col = jnp.broadcast_to(wave_y[:, count + i : count + i + 1], (tall, half))
        near_ctf = sin_col * cos_x[i : i + 1, :half] + cos_col * sin_x[i : i + 1, :half]
        far_ctf = sin_col * cos_x[i : i + 1, half:] + cos_col * sin_x[i : i + 1, half:]
        cc, cs = y[:half, :half], y[:half, half:]
        sc, ss = y[half:, :half], y[half:, half:]
        ss_row = without_row(ss)
        ss_in = jnp.where(col_zero, 0.0, ss_row)
        sc_in = without_row(sc)
        cs_in = jnp.where(col_zero, 0.0, cs)
        near_y, far_y = near_ctf[:half], far_ctf[:half]
        spec = spec_ref.at[i % SLOTS]
        spec[0:half, 0:half] = (near_y * (cc + ss_in)).astype(bf16)
        spec[0:half, half:] = (far_y * jnp.where(col_zero, cs, cc - ss_in)).astype(bf16)
        spec[half:box, 0:half] = (near_y * (sc_in - cs_in)).astype(bf16)
        spec[half:box, half:] = (far_y * jnp.where(col_zero, ss_row, sc_in + cs_in)).astype(bf16)
        sc_top = jnp.broadcast_to(sc[0:1], (16, half))
        ss_top = jnp.broadcast_to(ss[0:1], (16, half))
        ss_top_in = jnp.where(short_col, 0.0, ss_top)
        spec[box : box + 16, 0:half] = (
            near_ctf[half : half + 1] * jnp.where(short_row, sc_top, -ss_top_in)
        ).astype(bf16)
        spec[box : box + 16, half:] = (
            far_ctf[half : half + 1]
            * jnp.where(short_row, jnp.where(short_col, ss_top, sc_top), ss_top_in)
        ).astype(bf16)

    def mix(i):
        mixed = dot(spec_ref[i % SLOTS], cols_fold[pose_ref[i]])
        out = mix_ref.at[i % SLOTS]
        out[0:half, 0:cols] = mixed[:half, :cols].astype(bf16)
        out[0:half, cols:] = mixed[half:box, :cols].astype(bf16)
        top = iota((16, cols), 0) == 0
        real, imag = mixed[:half, cols:], -mixed[half:box, cols:]
        out[half : half + 16, 0:cols] = jnp.where(
            top, mixed[box : box + 1, :cols], real[:16]
        ).astype(bf16)
        out[half : half + 16, cols:] = jnp.where(
            top, mixed[box + 1 : box + 2, :cols], imag[:16]
        ).astype(bf16)
        out[half + 16 :, 0:cols] = real[16:].astype(bf16)
        out[half + 16 :, cols:] = imag[16:].astype(bf16)

    def insert(i):
        pose = pose_ref[i]
        pose_rows = rows_fold[pl.ds(pl.multiple_of(pose * rows, rows), rows), :]
        piece = dot(pose_rows, mix_ref[i % SLOTS])
        for z in range(planes):
            slot = leading + z * CLASSES + class_ref[i]
            totals[slot] += plane_ref[z, pose] * piece

    copies[5].wait()
    along_rows(0)
    copies[7].wait()
    copies[8].wait()
    for p in range(0, poses, 2):
        two = jnp.concatenate([cols_ref[p], cols_ref[p + 1]], 1)
        near_two = dot(near, two).astype(bf16)
        far_two = dot(far, two).astype(bf16)
        cols_fold[p] = jnp.concatenate([near_two[:, :cols], far_two[:, :cols]], 1)
        cols_fold[p + 1] = jnp.concatenate([near_two[:, cols:], far_two[:, cols:]], 1)
    along_rows(GROUP)
    along_columns(0)
    copies[9].wait()
    rows_fold[...] = dot(
        rows_ref[...].reshape(poses * rows, box), near, ((1,), (1,))
    ).astype(bf16)
    for step in range(2 * GROUP, count + 3 * GROUP, GROUP):
        for n in range(GROUP):
            if step >= 3 * GROUP:
                insert(step - 3 * GROUP + n)
            if step - 2 * GROUP < count:
                mix(step - 2 * GROUP + n)
        if step - GROUP < count:
            along_columns(step - GROUP)
        if step < count:
            along_rows(step)

    if len(outs) == 1:
        outs[0][...] = totals[...].astype(bf16)
        return
    x_send, x_keep, own_send, own_keep, z_keep = outs[:5]
    z_sends = outs[5:]
    x_slots, owned, _ = own_keep.shape
    me = lax.axis_index("img")

    def rows_of(flip):
        return pl.ds(pl.multiple_of((me ^ flip) * owned, owned), owned)

    for n, k in enumerate(LINE):
        x_send[n] = totals[-x_slots:, rows_of(2 * k + 1), :].astype(bf16)
        x_keep[n] = totals[-x_slots:, rows_of(2 * k), :]
    own_send[...] = totals[-x_slots:, rows_of(1), :].astype(bf16)
    own_keep[...] = totals[-x_slots:, rows_of(0), :]
    for side in range(2):
        z_keep[side] = totals[:-x_slots, rows_of(side), :]
        for n, k in enumerate(LINE):
            z_sends[n][side] = totals[:-x_slots, rows_of(2 * k + side), :].astype(bf16)


SCRATCH = 20
LINE = (2, 3, 1)
SLOTS = 8
GROUP = 4
Z_SLOTS = 3


def own_totals(images, class_index, pose_index, defocus_bin, defocus, rows_table, cols_table, plane_weight, members):
    count, box, _ = images.shape
    poses, rows, _ = rows_table.shape
    cols = cols_table.shape[2]
    planes = plane_weight.shape[1]
    slots = CLASSES * planes
    table_y, table_x = packed_dft(box, -1.0), packed_dft(box, 1.0)
    any_place = pl.BlockSpec(memory_space=pl.ANY)
    vmem = pl.BlockSpec(memory_space=pltpu.VMEM)
    lanes = 128 * (-(-2 * count // 128))
    if members == 1:
        out_shape = [jax.ShapeDtypeStruct((slots, rows, 2 * cols), bf16)]
    else:
        slots += 1
        tail = (rows // members, 2 * cols)
        x_slots = slots - Z_SLOTS
        out_shape = []
        for lead in ((len(LINE), x_slots), (x_slots,)):
            out_shape += [pltpu.VMEM(lead + tail, bf16), pltpu.VMEM(lead + tail, f32)]
        out_shape += [pltpu.VMEM((2, Z_SLOTS) + tail, f32)]
        out_shape += [pltpu.VMEM((2, Z_SLOTS) + tail, bf16)] * len(LINE)
    operands = (
        class_index[:, 0], pose_index, defocus_bin, defocus, plane_weight.T,
        jnp.asarray(table_y, bf16), jnp.asarray(table_x.T.copy(), bf16),
        images, rows_table, cols_table,
    )
    return pl.pallas_call(
        slices_kernel,
        out_shape=out_shape,
        in_specs=[any_place] * 10,
        out_specs=[vmem] * len(out_shape),
        scratch_shapes=[pltpu.SMEM(x.shape, x.dtype) for x in operands[:5]]
        + [pltpu.VMEM(x.shape, x.dtype) for x in operands[5:]]
        + [
            pltpu.SemaphoreType.DMA((9 + count // GROUP,)),
            pltpu.VMEM((poses * rows, box), bf16),
            pltpu.VMEM((poses, box, 2 * cols), bf16),
            pltpu.VMEM((box // 2 + 8, lanes), f32),
            pltpu.VMEM((count, box), f32),
            pltpu.VMEM((count, box), f32),
            pltpu.VMEM((2, GROUP * box, box), bf16),
            pltpu.VMEM((SLOTS, box + 16, box), bf16),
            pltpu.VMEM((SLOTS, box, 2 * cols), bf16),
            pltpu.VMEM((slots, rows, 2 * cols), f32),
        ],
        compiler_params=pltpu.CompilerParams(vmem_limit_bytes=VMEM_LIMIT),
        cost_estimate=pl.CostEstimate(
            flops=2 * count * box * box * 1000, bytes_accessed=6 * 1024 * 1024, transcendentals=0
        ),
    )(*operands)


VMEM_LIMIT = 56 * 1024 * 1024


def ridge_kernel(defocus_hbm, plane_hbm, rows_hbm, cols_hbm, high_ref, low_ref, share_ref, *refs):
    defocus_ref, plane_ref, rows_ref, cols_ref, arrived = refs
    poses, owned, box = rows_ref.shape
    cols = cols_ref.shape[2]
    bins = defocus_ref.shape[0]
    planes = plane_ref.shape[0]
    half = box // 2
    first = pl.multiple_of(lax.axis_index("img") * owned, owned)
    copies = [
        pltpu.make_async_copy(defocus_hbm, defocus_ref, arrived.at[0]),
        pltpu.make_async_copy(plane_hbm, plane_ref, arrived.at[1]),
        pltpu.make_async_copy(rows_hbm.at[:, pl.ds(first, owned), :], rows_ref, arrived.at[2]),
        pltpu.make_async_copy(cols_hbm, cols_ref, arrived.at[3]),
    ]
    for copy in copies:
        copy.start()
    for copy in copies:
        copy.wait()
    share_plane = iota((planes * CLASSES, poses * bins), 0) // CLASSES
    share_pose = iota((planes * CLASSES, poses * bins), 1) // bins
    share = jnp.zeros((planes * CLASSES, poses * bins), f32)
    for p in range(poses):
        for z in range(planes):
            share = jnp.where((share_plane == z) & (share_pose == p), plane_ref[z, p], share)
    share_ref[...] = share

    bin_row = iota((bins, box), 0)
    sub_defocus = jnp.zeros((bins, box), f32)
    for b in range(bins):
        sub_defocus = jnp.where(bin_row == b, defocus_ref[b], sub_defocus)
    freq = iota((bins, box), 1)
    freq = jnp.where(freq < half, freq, box - freq).astype(f32)
    turns_x = sub_defocus * (freq * freq * (1.0 / (half * half)))
    turns_y = turns_x + ctf_phase / math.pi
    ones = jnp.ones((bins, box), f32)
    wave_y = jnp.concatenate(
        [0.5 * ones, -0.5 * turns_sine(turns_y + 0.25), 0.5 * turns_sine(turns_y)], 0
    )
    wave_x = jnp.concatenate([ones, turns_sine(turns_x + 0.25), turns_sine(turns_x)], 0)
    y_high, y_low = split_two(wave_y)
    x_high, x_low = split_two(wave_x)
    rows_sq = rows_ref[...].reshape(poses * owned, box).astype(f32)
    rows_sq = (rows_sq * rows_sq).astype(bf16)
    u = dot(y_high, rows_sq, ((1,), (1,))) + dot(y_low, rows_sq, ((1,), (1,)))
    for p in range(poses):
        cols_sq = cols_ref[p].astype(f32)
        cols_sq = (cols_sq * cols_sq).astype(bf16)
        v = dot(x_high, cols_sq) + dot(x_low, cols_sq)
        for r in range(owned):
            column = u[:, p * owned + r : p * owned + r + 1]
            product = v * column
            weight = product[:bins] + product[bins : 2 * bins] + product[2 * bins :]
            high, low = split_two(weight)
            high_ref[p * bins : (p + 1) * bins, r * cols : (r + 1) * cols] = high
            low_ref[p * bins : (p + 1) * bins, r * cols : (r + 1) * cols] = low


def own_ridges(defocus, plane_weight, rows_table, cols_table, owned):
    poses, _, box = rows_table.shape
    cols = cols_table.shape[2]
    bins = defocus.shape[0]
    any_place = pl.BlockSpec(memory_space=pl.ANY)
    vmem = pl.BlockSpec(memory_space=pltpu.VMEM)
    planes = plane_weight.T
    table = jax.ShapeDtypeStruct((poses * bins, owned * cols), bf16)
    return pl.pallas_call(
        ridge_kernel,
        out_shape=[table, table, jax.ShapeDtypeStruct((planes.shape[0] * CLASSES, poses * bins), f32)],
        in_specs=[any_place] * 4,
        out_specs=[vmem] * 3,
        scratch_shapes=[
            pltpu.SMEM(defocus.shape, f32),
            pltpu.SMEM(planes.shape, f32),
            pltpu.VMEM((poses, owned, box), bf16),
            pltpu.VMEM(cols_table.shape, bf16),
            pltpu.SemaphoreType.DMA((4,)),
        ],
        compiler_params=pltpu.CompilerParams(vmem_limit_bytes=16 * 1024 * 1024),
        cost_estimate=pl.CostEstimate(
            flops=1000, bytes_accessed=1000, transcendentals=0
        ),
    )(defocus, planes, rows_table, cols_table)


def call_in_vmem(kernel, arrays, out_shape):
    vmem = pl.BlockSpec(memory_space=pltpu.VMEM)
    return pl.pallas_call(
        kernel,
        out_shape=out_shape,
        in_specs=[vmem] * len(arrays),
        out_specs=[vmem] * len(out_shape),
        compiler_params=pltpu.CompilerParams(vmem_limit_bytes=16 * 1024 * 1024),
        cost_estimate=pl.CostEstimate(flops=1000, bytes_accessed=1000, transcendentals=0),
    )(*arrays)


def fold_kernel(x_keep, x_came, own_send, z_keep, *refs):
    z_came, refs = refs[: len(LINE)], refs[len(LINE) :]
    x_sends, own_out, z_own, z_send = refs[: len(LINE)], *refs[len(LINE) :]
    for n, send in enumerate(x_sends):
        send[...] = (x_keep[n] + x_came[n].astype(f32)).astype(bf16)
    own_out[...] = own_send[...]
    for side, out in enumerate((z_own, z_send)):
        value = z_keep[side]
        for came in z_came:
            value = value + came[side].astype(f32)
        out[...] = value.astype(out.dtype)


def fold_phase(x_keep, x_came, own_send, z_keep, z_came):
    piece = own_send.shape
    z_piece = z_keep.shape[1:]
    out_shape = [pltpu.VMEM(piece, bf16)] * (len(LINE) + 1)
    out_shape += [pltpu.VMEM(z_piece, f32), pltpu.VMEM(z_piece, bf16)]
    return call_in_vmem(fold_kernel, (x_keep, x_came, own_send, z_keep, *z_came), out_shape)


def weight_kernel(high_ref, low_ref, share_ref, z_own, z_came, out_ref, ridge_ref):
    slots, pairs = share_ref.shape
    owned, _, cols = ridge_ref.shape
    counts = z_own[0] + z_came[0].astype(f32)
    scaled = jnp.concatenate([counts[:CLASSES, :pairs]] * (slots // CLASSES), 0) * share_ref[...]
    c_high, c_low = split_two(scaled)
    weight = (
        dot(c_high, high_ref[...]) + dot(c_low, high_ref[...]) + dot(c_high, low_ref[...])
    )
    ridge = 1.0 / (weight + wiener_ridge)
    for r in range(owned):
        ridge_ref[r] = ridge[:, r * cols : (r + 1) * cols]
    for s in range(slots):
        out_ref[s] = ridge_ref[:, s, :]


def own_weights(tables, z_own, z_came):
    slots = tables[2].shape[0]
    _, owned, wide = z_own.shape
    cols = wide // 2
    vmem = pl.BlockSpec(memory_space=pltpu.VMEM)
    return pl.pallas_call(
        weight_kernel,
        out_shape=pltpu.VMEM((slots, owned, cols), f32),
        in_specs=[vmem] * 5,
        out_specs=vmem,
        scratch_shapes=[pltpu.VMEM((owned, slots, cols), f32)],
        compiler_params=pltpu.CompilerParams(vmem_limit_bytes=16 * 1024 * 1024),
        cost_estimate=pl.CostEstimate(flops=1000, bytes_accessed=1000, transcendentals=0),
    )(*tables, z_own, z_came)


def finish_kernel(planes, ridge_ref, x_own, z_own, z_came, *refs):
    x_came, out_ref = refs[:-1], refs[-1]
    slots, owned, cols = ridge_ref.shape
    first = z_own.shape[0]
    for s in range(slots):
        if s + 1 < first:
            value = z_own[s + 1] + z_came[s + 1].astype(f32)
        else:
            value = x_own[s + 1 - first]
            for part in x_came:
                value = value + part[s + 1 - first].astype(f32)
        factor = ridge_ref[s]
        place = (s % CLASSES) * planes + s // CLASSES
        out_ref[:, 2 * place, :] = value[:, :cols] * factor
        out_ref[:, 2 * place + 1, :] = value[:, cols:] * factor


def finish(planes, ridge, x_own, z_own, z_came, x_came):
    slots, owned, cols = ridge.shape
    vmem = pl.BlockSpec(memory_space=pltpu.VMEM)
    return pl.pallas_call(
        functools.partial(finish_kernel, planes),
        out_shape=jax.ShapeDtypeStruct((owned, 2 * slots, cols), f32),
        in_specs=[vmem] * (4 + len(x_came)),
        out_specs=vmem,
        compiler_params=pltpu.CompilerParams(vmem_limit_bytes=16 * 1024 * 1024),
        cost_estimate=pl.CostEstimate(flops=1000, bytes_accessed=1000, transcendentals=0),
    )(ridge, x_own, z_own, z_came, *x_came)


def squared_table(weight_table):
    wide_table = weight_table.astype(f32)
    return (wide_table * wide_table).astype(bf16)


def weight_totals(class_index, pose_index, defocus_bin, defocus, rows_table, cols_table, plane_weight, first_row, owned):
    box = rows_table.shape[2]
    poses = rows_table.shape[0]
    bins = defocus.shape[0]
    half = box // 2
    exact = lax.Precision.HIGHEST
    code = (class_index[:, 0] * poses + pose_index) * bins + defocus_bin
    codes = lax.all_gather(code, "img", tiled=True)
    hits = (codes[:, None] == jnp.arange(CLASSES * poses * bins, dtype=jnp.int32)).astype(f32)
    counts = jnp.sum(hits, 0).reshape(CLASSES, poses, bins)
    place = jnp.arange(box, dtype=jnp.int32)
    freq = jnp.where(place < half, place, place - box).astype(f32)
    turns = defocus[:, None] * (freq * freq)[None, :] * (1.0 / (half * half))
    turns_y = turns + ctf_phase / math.pi
    ones = jnp.ones_like(turns)
    wave_y = jnp.stack([0.5 * ones, -0.5 * turns_sine(turns_y + 0.25), 0.5 * turns_sine(turns_y)])
    wave_x = jnp.stack([ones, turns_sine(turns + 0.25), turns_sine(turns)])
    rows_own = lax.dynamic_slice_in_dim(rows_table, first_row, owned, 1)
    u = jnp.einsum("pry,mby->pmbr", squared_table(rows_own).astype(f32), wave_y, precision=exact)
    v = jnp.einsum("pxj,mbx->pmbj", squared_table(cols_table).astype(f32), wave_x, precision=exact)
    weight = counts[:, None] * plane_weight.T[None, :, :, None]
    left = weight[:, :, :, None, :, None] * u[None, None]
    return jnp.einsum("czpmbr,pmbj->rczj", left, v, precision=exact)


def by_pairs(images, class_index, pose_index, defocus_bin, defocus, rows_table, cols_table, plane_weight):
    members = lax.axis_size("img")
    rows = rows_table.shape[1]
    planes = plane_weight.shape[1]
    cols = cols_table.shape[2]
    owned = rows // members

    def exchange(value, flip):
        return lax.ppermute(value, "img", [(i, i ^ flip) for i in range(members)])

    x_send, x_keep, own_send, own_keep, z_keep, *z_sends = own_totals(
        images, class_index, pose_index, defocus_bin, defocus, rows_table, cols_table, plane_weight, members
    )
    x_came = exchange(x_send, 1)
    z_came = [exchange(send, 2 * k) for send, k in zip(z_sends, LINE)]
    tables = own_ridges(defocus, plane_weight, rows_table, cols_table, owned)
    x_keep, tables = lax.optimization_barrier((x_keep, tables))
    *x_sends, own_send, z_own, z_send = fold_phase(x_keep, x_came, own_send, z_keep, z_came)
    x_came = [exchange(send, 2 * k) for send, k in zip(x_sends, LINE)]
    own_came = exchange(own_send, 1)
    z_came = exchange(z_send, 1)
    ridge = own_weights(tables, z_own, z_came)
    out = finish(planes, ridge, own_keep, z_own, z_came, (*x_came, own_came))
    return out.reshape(owned, CLASSES, planes, 2, cols)


def by_scatter(images, class_index, pose_index, defocus_bin, defocus, rows_table, cols_table, plane_weight):
    rows = rows_table.shape[1]
    cols = cols_table.shape[2]
    planes = plane_weight.shape[1]
    members = lax.axis_size("img")
    owned = rows // members
    (totals,) = own_totals(
        images, class_index, pose_index, defocus_bin, defocus, rows_table, cols_table, plane_weight, 1
    )
    slots = totals.shape[0]
    totals = totals.reshape(slots, members, owned, 2 * cols).transpose(1, 0, 2, 3)
    own = lax.psum_scatter(totals, "img", scatter_dimension=0, tiled=False)
    weight = weight_totals(
        class_index, pose_index, defocus_bin, defocus, rows_table, cols_table, plane_weight,
        lax.axis_index("img") * owned, owned,
    )
    own = own.astype(f32).reshape(planes, CLASSES, owned, 2, cols).transpose(2, 1, 0, 3, 4)
    return own / (weight[:, :, :, None, :] + wiener_ridge)


def body(*arrays):
    rows = arrays[5].shape[1]
    members = lax.axis_size("img")
    images = members * arrays[0].shape[0]
    paired = members == 8 and images <= 256 and rows % (16 * members) == 0
    return (by_pairs if paired else by_scatter)(*arrays)


def solution(mesh):
    placed = (
        P(("groups", "img"), None, None),
        P(("groups", "img"), None),
        P(("groups", "img")),
        P(("groups", "img")),
        P(),
        P(),
        P(None, None, "slab"),
        P(),
    )
    return jax.shard_map(
        body,
        mesh=mesh,
        in_specs=placed,
        out_specs=P("img", "groups", None, None, "slab"),
        check_vma=False,
    )
```

```python
import functools
import math

import jax
import jax.numpy as jnp
import numpy as np
from jax import lax
from jax.experimental import pallas as pl
from jax.experimental.pallas import tpu as pltpu
from jax.sharding import PartitionSpec as P

CLASSES = 8

wiener_ridge = 1.0
ctf_phase = 0.1
f32 = jnp.float32
bf16 = jnp.bfloat16


def packed_dft(box, sine_sign):
    half = box // 2
    k = np.concatenate([np.arange(half), [half], np.arange(1, half)])
    angle = (k[:, None] * np.arange(box)[None, :] % box) * (2.0 * math.pi / box)
    table = np.where((np.arange(box) <= half)[:, None], np.cos(angle), sine_sign * np.sin(angle))
    return (table / math.sqrt(box)).astype(np.float32)


def iota(shape, axis):
    return lax.broadcasted_iota(jnp.int32, shape, axis)


def dot(a, b, dims=((1,), (0,))):
    return lax.dot_general(a, b, (dims, ((), ())), preferred_element_type=f32)


def turns_sine(turns):
    return jnp.sin((turns - jnp.round(turns)) * (2.0 * math.pi))


def split_two(value):
    high = value.astype(bf16)
    return high, (value - high.astype(f32)).astype(bf16)


def fold_of(place, half):
    box = 2 * half
    return jnp.where(place <= half, place, box + half - place)


def slices_kernel(
    class_hbm, pose_hbm, bin_hbm, defocus_hbm, plane_hbm,
    dft_hbm, dft_t_hbm, images_hbm, rows_hbm, cols_hbm,
    *refs,
):
    outs, refs = refs[:-SCRATCH], refs[-SCRATCH:]
    (
        class_ref, pose_ref, bin_ref, defocus_ref, plane_ref,
        dft_ref, dft_t_ref, images_ref, rows_ref, cols_ref, arrived,
        rows_fold, cols_fold, wave_y, cos_x, sin_x, half_ref, spec_ref, mix_ref, totals,
    ) = refs
    count, box, _ = images_ref.shape
    half = box // 2
    poses, rows, _ = rows_ref.shape
    cols = cols_ref.shape[2]
    planes = plane_ref.shape[0]

    pairs = (
        (class_hbm, class_ref), (pose_hbm, pose_ref), (bin_hbm, bin_ref),
        (defocus_hbm, defocus_ref), (plane_hbm, plane_ref),
        (dft_hbm, dft_ref), (images_hbm.at[0:GROUP], images_ref.at[0:GROUP]),
        (dft_t_hbm, dft_t_ref), (cols_hbm, cols_ref), (rows_hbm, rows_ref),
    ) + tuple(
        (images_hbm.at[i : i + GROUP], images_ref.at[i : i + GROUP])
        for i in range(GROUP, count, GROUP)
    )
    copies = [
        pltpu.make_async_copy(source, target, arrived.at[n])
        for n, (source, target) in enumerate(pairs)
    ]
    for copy in copies:
        copy.start()

    place = iota((box, box), 0)
    other = iota((box, box), 1)
    folded = fold_of(place, half)
    near = (folded == other).astype(f32).astype(bf16)
    far = (jnp.where(folded == 0, 0, box - folded) == other).astype(f32).astype(bf16)

    for copy in copies[:5]:
        copy.wait()
    tall, lanes = wave_y.shape
    lane = iota((1, lanes), 1)
    sub = iota((count, box), 0)
    lane_defocus = jnp.zeros((1, lanes), f32)
    sub_defocus = jnp.zeros((count, box), f32)
    for i in range(count):
        value = defocus_ref[bin_ref[i]]
        lane_defocus = jnp.where(lane % count == i, value, lane_defocus)
        sub_defocus = jnp.where(sub == i, value, sub_defocus)
    scale = 1.0 / (2 * half * half)
    ky = iota((tall, lanes), 0).astype(f32)
    quarter = jnp.where(lane < count, 0.0, 0.25) + ctf_phase / (2.0 * math.pi)
    wave_y[...] = turns_sine(lane_defocus * (ky * ky * scale) + quarter)
    kx = iota((count, box), 1)
    kx = jnp.where(kx <= half, kx, kx - half).astype(f32)
    turns = sub_defocus * (kx * kx * scale)
    cos_x[...] = -turns_sine(turns + 0.25)
    sin_x[...] = -turns_sine(turns)
    totals[...] = jnp.zeros_like(totals)
    leading = 1 if len(outs) > 1 else 0
    if len(outs) > 1:
        bins = defocus_ref.shape[0]
        count_row = iota((16, 2 * cols), 0)
        count_lane = iota((16, 2 * cols), 1)
        counts = jnp.zeros((16, 2 * cols), f32)
        for i in range(count):
            hit = (count_row == class_ref[i]) & (count_lane == pose_ref[i] * bins + bin_ref[i])
            counts = counts + jnp.where(hit, 1.0, 0.0)
        totals[0] = jnp.tile(counts, (rows // 16, 1))

    tile = 8
    tile_row = iota((tile, half), 0) == 0
    tile_col = iota((tile, half), 1) == 0
    col_zero = iota((half, half), 1) == 0
    short_row = iota((16, half), 0) == 0
    short_col = iota((16, half), 1) == 0

    def without_row(value):
        return jnp.concatenate([jnp.where(tile_row, 0.0, value[:tile]), value[tile:]], 0)

    def along_rows(i):
        copies[6 if i == 0 else 9 + i // GROUP].wait()
        group = jnp.concatenate([images_ref[i + n] for n in range(GROUP)], 1)
        product = dot(dft_ref[...], group).astype(bf16)
        for n in range(GROUP):
            half_ref[i // GROUP % 2, n * box : (n + 1) * box] = product[:, n * box : (n + 1) * box]

    def along_columns(i):
        product = dot(half_ref[i // GROUP % 2], dft_t_ref[...])
        for n in range(GROUP):
            weigh(i + n, product[n * box : (n + 1) * box])

    def weigh(i, y):
        sin_col = jnp.broadcast_to(wave_y[:, i : i + 1], (tall, half))
        cos_col = jnp.broadcast_to(wave_y[:, count + i : count + i + 1], (tall, half))
        near_ctf = sin_col * cos_x[i : i + 1, :half] + cos_col * sin_x[i : i + 1, :half]
        far_ctf = sin_col * cos_x[i : i + 1, half:] + cos_col * sin_x[i : i + 1, half:]
        cc, cs = y[:half, :half], y[:half, half:]
        sc, ss = y[half:, :half], y[half:, half:]
        ss_row = without_row(ss)
        ss_in = jnp.where(col_zero, 0.0, ss_row)
        sc_in = without_row(sc)
        cs_in = jnp.where(col_zero, 0.0, cs)
        near_y, far_y = near_ctf[:half], far_ctf[:half]
        spec = spec_ref.at[i % SLOTS]
        spec[0:half, 0:half] = (near_y * (cc + ss_in)).astype(bf16)
        spec[0:half, half:] = (far_y * jnp.where(col_zero, cs, cc - ss_in)).astype(bf16)
        spec[half:box, 0:half] = (near_y * (sc_in - cs_in)).astype(bf16)
        spec[half:box, half:] = (far_y * jnp.where(col_zero, ss_row, sc_in + cs_in)).astype(bf16)
        sc_top = jnp.broadcast_to(sc[0:1], (16, half))
        ss_top = jnp.broadcast_to(ss[0:1], (16, half))
        ss_top_in = jnp.where(short_col, 0.0, ss_top)
        spec[box : box + 16, 0:half] = (
            near_ctf[half : half + 1] * jnp.where(short_row, sc_top, -ss_top_in)
        ).astype(bf16)
        spec[box : box + 16, half:] = (
            far_ctf[half : half + 1]
            * jnp.where(short_row, jnp.where(short_col, ss_top, sc_top), ss_top_in)
        ).astype(bf16)

    def mix(i):
        mixed = dot(spec_ref[i % SLOTS], cols_fold[pose_ref[i]])
        out = mix_ref.at[i % SLOTS]
        out[0:half, 0:cols] = mixed[:half, :cols].astype(bf16)
        out[0:half, cols:] = mixed[half:box, :cols].astype(bf16)
        top = iota((16, cols), 0) == 0
        real, imag = mixed[:half, cols:], -mixed[half:box, cols:]
        out[half : half + 16, 0:cols] = jnp.where(
            top, mixed[box : box + 1, :cols], real[:16]
        ).astype(bf16)
        out[half : half + 16, cols:] = jnp.where(
            top, mixed[box + 1 : box + 2, :cols], imag[:16]
        ).astype(bf16)
        out[half + 16 :, 0:cols] = real[16:].astype(bf16)
        out[half + 16 :, cols:] = imag[16:].astype(bf16)

    def insert(i):
        pose = pose_ref[i]
        pose_rows = rows_fold[pl.ds(pl.multiple_of(pose * rows, rows), rows), :]
        piece = dot(pose_rows, mix_ref[i % SLOTS])
        for z in range(planes):
            slot = leading + z * CLASSES + class_ref[i]
            totals[slot] += plane_ref[z, pose] * piece

    copies[5].wait()
    along_rows(0)
    copies[7].wait()
    copies[8].wait()
    for p in range(0, poses, 2):
        two = jnp.concatenate([cols_ref[p], cols_ref[p + 1]], 1)
        near_two = dot(near, two).astype(bf16)
        far_two = dot(far, two).astype(bf16)
        cols_fold[p] = jnp.concatenate([near_two[:, :cols], far_two[:, :cols]], 1)
        cols_fold[p + 1] = jnp.concatenate([near_two[:, cols:], far_two[:, cols:]], 1)
    along_rows(GROUP)
    along_columns(0)
    copies[9].wait()
    rows_fold[...] = dot(
        rows_ref[...].reshape(poses * rows, box), near, ((1,), (1,))
    ).astype(bf16)
    for step in range(2 * GROUP, count + 3 * GROUP, GROUP):
        for n in range(GROUP):
            if step >= 3 * GROUP:
                insert(step - 3 * GROUP + n)
            if step - 2 * GROUP < count:
                mix(step - 2 * GROUP + n)
        if step - GROUP < count:
            along_columns(step - GROUP)
        if step < count:
            along_rows(step)

    if len(outs) == 1:
        outs[0][...] = totals[...].astype(bf16)
        return
    x_send, x_keep, own_send, own_keep, z_keep = outs[:5]
    z_sends = outs[5:]
    x_slots, owned, _ = own_keep.shape
    me = lax.axis_index("img")

    def rows_of(flip):
        return pl.ds(pl.multiple_of((me ^ flip) * owned, owned), owned)

    for n, k in enumerate(LINE):
        x_send[n] = totals[-x_slots:, rows_of(2 * k + 1), :].astype(bf16)
        x_keep[n] = totals[-x_slots:, rows_of(2 * k), :]
    own_send[...] = totals[-x_slots:, rows_of(1), :].astype(bf16)
    own_keep[...] = totals[-x_slots:, rows_of(0), :]
    for k, out in zip((0,) + LINE, (z_keep, *z_sends)):
        out[:Z_SLOTS] = totals[:Z_SLOTS, rows_of(2 * k), :].astype(out.dtype)
        out[Z_SLOTS:] = totals[1:Z_SLOTS, rows_of(2 * k + 1), :].astype(out.dtype)


SCRATCH = 20
LINE = (2, 3, 1)
SLOTS = 8
GROUP = 4
Z_SLOTS = 4


def own_totals(images, class_index, pose_index, defocus_bin, defocus, rows_table, cols_table, plane_weight, members):
    count, box, _ = images.shape
    poses, rows, _ = rows_table.shape
    cols = cols_table.shape[2]
    planes = plane_weight.shape[1]
    slots = CLASSES * planes
    table_y, table_x = packed_dft(box, -1.0), packed_dft(box, 1.0)
    any_place = pl.BlockSpec(memory_space=pl.ANY)
    vmem = pl.BlockSpec(memory_space=pltpu.VMEM)
    lanes = 128 * (-(-2 * count // 128))
    if members == 1:
        out_shape = [jax.ShapeDtypeStruct((slots, rows, 2 * cols), bf16)]
    else:
        slots += 1
        tail = (rows // members, 2 * cols)
        x_slots = slots - Z_SLOTS
        out_shape = []
        for lead in ((len(LINE), x_slots), (x_slots,)):
            out_shape += [pltpu.VMEM(lead + tail, bf16), pltpu.VMEM(lead + tail, f32)]
        out_shape += [pltpu.VMEM((2 * Z_SLOTS - 1,) + tail, f32)]
        out_shape += [pltpu.VMEM((2 * Z_SLOTS - 1,) + tail, bf16)] * len(LINE)
    operands = (
        class_index[:, 0], pose_index, defocus_bin, defocus, plane_weight.T,
        jnp.asarray(table_y, bf16), jnp.asarray(table_x.T.copy(), bf16),
        images, rows_table, cols_table,
    )
    return pl.pallas_call(
        slices_kernel,
        out_shape=out_shape,
        in_specs=[any_place] * 10,
        out_specs=[vmem] * len(out_shape),
        scratch_shapes=[pltpu.SMEM(x.shape, x.dtype) for x in operands[:5]]
        + [pltpu.VMEM(x.shape, x.dtype) for x in operands[5:]]
        + [
            pltpu.SemaphoreType.DMA((9 + count // GROUP,)),
            pltpu.VMEM((poses * rows, box), bf16),
            pltpu.VMEM((poses, box, 2 * cols), bf16),
            pltpu.VMEM((box // 2 + 8, lanes), f32),
            pltpu.VMEM((count, box), f32),
            pltpu.VMEM((count, box), f32),
            pltpu.VMEM((2, GROUP * box, box), bf16),
            pltpu.VMEM((SLOTS, box + 16, box), bf16),
            pltpu.VMEM((SLOTS, box, 2 * cols), bf16),
            pltpu.VMEM((slots, rows, 2 * cols), f32),
        ],
        compiler_params=pltpu.CompilerParams(vmem_limit_bytes=VMEM_LIMIT),
        cost_estimate=pl.CostEstimate(
            flops=2 * count * box * box * 1000, bytes_accessed=6 * 1024 * 1024, transcendentals=0
        ),
    )(*operands)


VMEM_LIMIT = 56 * 1024 * 1024


def ridge_kernel(defocus_hbm, plane_hbm, rows_hbm, cols_hbm, high_ref, low_ref, share_ref, *refs):
    defocus_ref, plane_ref, rows_ref, cols_ref, arrived = refs
    poses, owned, box = rows_ref.shape
    cols = cols_ref.shape[2]
    bins = defocus_ref.shape[0]
    planes = plane_ref.shape[0]
    half = box // 2
    first = pl.multiple_of(lax.axis_index("img") * owned, owned)
    copies = [
        pltpu.make_async_copy(defocus_hbm, defocus_ref, arrived.at[0]),
        pltpu.make_async_copy(plane_hbm, plane_ref, arrived.at[1]),
        pltpu.make_async_copy(rows_hbm.at[:, pl.ds(first, owned), :], rows_ref, arrived.at[2]),
        pltpu.make_async_copy(cols_hbm, cols_ref, arrived.at[3]),
    ]
    for copy in copies:
        copy.start()
    for copy in copies:
        copy.wait()
    share_plane = iota((planes * CLASSES, poses * bins), 0) // CLASSES
    share_pose = iota((planes * CLASSES, poses * bins), 1) // bins
    share = jnp.zeros((planes * CLASSES, poses * bins), f32)
    for p in range(poses):
        for z in range(planes):
            share = jnp.where((share_plane == z) & (share_pose == p), plane_ref[z, p], share)
    share_ref[...] = share

    bin_row = iota((bins, box), 0)
    sub_defocus = jnp.zeros((bins, box), f32)
    for b in range(bins):
        sub_defocus = jnp.where(bin_row == b, defocus_ref[b], sub_defocus)
    freq = iota((bins, box), 1)
    freq = jnp.where(freq < half, freq, box - freq).astype(f32)
    turns_x = sub_defocus * (freq * freq * (1.0 / (half * half)))
    turns_y = turns_x + ctf_phase / math.pi
    ones = jnp.ones((bins, box), f32)
    wave_y = jnp.concatenate(
        [0.5 * ones, -0.5 * turns_sine(turns_y + 0.25), 0.5 * turns_sine(turns_y)], 0
    )
    wave_x = jnp.concatenate([ones, turns_sine(turns_x + 0.25), turns_sine(turns_x)], 0)
    y_high, y_low = split_two(wave_y)
    x_high, x_low = split_two(wave_x)
    rows_sq = rows_ref[...].reshape(poses * owned, box).astype(f32)
    rows_sq = (rows_sq * rows_sq).astype(bf16)
    u = dot(y_high, rows_sq, ((1,), (1,))) + dot(y_low, rows_sq, ((1,), (1,)))
    for p in range(poses):
        cols_sq = cols_ref[p].astype(f32)
        cols_sq = (cols_sq * cols_sq).astype(bf16)
        v = dot(x_high, cols_sq) + dot(x_low, cols_sq)
        for r in range(owned):
            column = u[:, p * owned + r : p * owned + r + 1]
            product = v * column
            weight = product[:bins] + product[bins : 2 * bins] + product[2 * bins :]
            high, low = split_two(weight)
            high_ref[p * bins : (p + 1) * bins, r * cols : (r + 1) * cols] = high
            low_ref[p * bins : (p + 1) * bins, r * cols : (r + 1) * cols] = low


def own_ridges(defocus, plane_weight, rows_table, cols_table, owned):
    poses, _, box = rows_table.shape
    cols = cols_table.shape[2]
    bins = defocus.shape[0]
    any_place = pl.BlockSpec(memory_space=pl.ANY)
    vmem = pl.BlockSpec(memory_space=pltpu.VMEM)
    planes = plane_weight.T
    table = pltpu.VMEM((poses * bins, owned * cols), bf16)
    return pl.pallas_call(
        ridge_kernel,
        out_shape=[table, table, pltpu.VMEM((planes.shape[0] * CLASSES, poses * bins), f32)],
        in_specs=[any_place] * 4,
        out_specs=[vmem] * 3,
        scratch_shapes=[
            pltpu.SMEM(defocus.shape, f32),
            pltpu.SMEM(planes.shape, f32),
            pltpu.VMEM((poses, owned, box), bf16),
            pltpu.VMEM(cols_table.shape, bf16),
            pltpu.SemaphoreType.DMA((4,)),
        ],
        compiler_params=pltpu.CompilerParams(vmem_limit_bytes=VMEM_LIMIT),
        cost_estimate=pl.CostEstimate(
            flops=1000, bytes_accessed=1000, transcendentals=0
        ),
    )(defocus, planes, rows_table, cols_table)


def call_in_vmem(kernel, arrays, out_shape):
    vmem = pl.BlockSpec(memory_space=pltpu.VMEM)
    return pl.pallas_call(
        kernel,
        out_shape=out_shape,
        in_specs=[vmem] * len(arrays),
        out_specs=[vmem] * len(out_shape),
        compiler_params=pltpu.CompilerParams(vmem_limit_bytes=16 * 1024 * 1024),
        cost_estimate=pl.CostEstimate(flops=1000, bytes_accessed=1000, transcendentals=0),
    )(*arrays)


def fold_kernel(x_keep, x_came, own_send, z_keep, *refs):
    z_came, refs = refs[: len(LINE)], refs[len(LINE) :]
    x_sends, own_out, z_own, z_send = refs[: len(LINE)], *refs[len(LINE) :]
    for n, send in enumerate(x_sends):
        send[...] = (x_keep[n] + x_came[n].astype(f32)).astype(bf16)
    own_out[...] = own_send[...]
    for n in range(z_keep.shape[0]):
        value = z_keep[n]
        for came in z_came:
            value = value + came[n].astype(f32)
        if n < Z_SLOTS:
            z_own[n] = value
        if n == 0:
            z_send[n] = value.astype(bf16)
        elif n >= Z_SLOTS:
            z_send[n - Z_SLOTS + 1] = value.astype(bf16)


def fold_phase(x_keep, x_came, own_send, z_keep, z_came):
    piece = own_send.shape
    z_piece = (Z_SLOTS,) + piece[1:]
    out_shape = [pltpu.VMEM(piece, bf16)] * (len(LINE) + 1)
    out_shape += [pltpu.VMEM(z_piece, f32), pltpu.VMEM(z_piece, bf16)]
    return call_in_vmem(fold_kernel, (x_keep, x_came, own_send, z_keep, *z_came), out_shape)


def weight_kernel(high_ref, low_ref, share_ref, z_own, z_came, out_ref, ridge_ref):
    slots, pairs = share_ref.shape
    owned, _, cols = ridge_ref.shape
    counts = z_own[0] + z_came[0].astype(f32)
    scaled = jnp.concatenate([counts[:CLASSES, :pairs]] * (slots // CLASSES), 0) * share_ref[...]
    c_high, c_low = split_two(scaled)
    weight = (
        dot(c_high, high_ref[...]) + dot(c_low, high_ref[...]) + dot(c_high, low_ref[...])
    )
    ridge = 1.0 / (weight + wiener_ridge)
    for r in range(owned):
        ridge_ref[r] = ridge[:, r * cols : (r + 1) * cols]
    for s in range(slots):
        out_ref[s] = ridge_ref[:, s, :]


def own_weights(tables, z_own, z_came):
    slots = tables[2].shape[0]
    _, owned, wide = z_own.shape
    cols = wide // 2
    vmem = pl.BlockSpec(memory_space=pltpu.VMEM)
    return pl.pallas_call(
        weight_kernel,
        out_shape=pltpu.VMEM((slots, owned, cols), f32),
        in_specs=[vmem] * 5,
        out_specs=vmem,
        scratch_shapes=[pltpu.VMEM((owned, slots, cols), f32)],
        compiler_params=pltpu.CompilerParams(vmem_limit_bytes=16 * 1024 * 1024),
        cost_estimate=pl.CostEstimate(flops=1000, bytes_accessed=1000, transcendentals=0),
    )(*tables, z_own, z_came)


def finish_kernel(planes, ridge_ref, x_own, z_own, z_came, *refs):
    x_came, out_ref = refs[:-1], refs[-1]
    slots, owned, cols = ridge_ref.shape
    first = z_own.shape[0]
    for s in range(slots):
        if s + 1 < first:
            value = z_own[s + 1] + z_came[s + 1].astype(f32)
        else:
            value = x_own[s + 1 - first]
            for part in x_came:
                value = value + part[s + 1 - first].astype(f32)
        factor = ridge_ref[s]
        place = (s % CLASSES) * planes + s // CLASSES
        out_ref[:, 2 * place, :] = value[:, :cols] * factor
        out_ref[:, 2 * place + 1, :] = value[:, cols:] * factor


def finish(planes, ridge, x_own, z_own, z_came, x_came):
    slots, owned, cols = ridge.shape
    vmem = pl.BlockSpec(memory_space=pltpu.VMEM)
    return pl.pallas_call(
        functools.partial(finish_kernel, planes),
        out_shape=jax.ShapeDtypeStruct((owned, 2 * slots, cols), f32),
        in_specs=[vmem] * (4 + len(x_came)),
        out_specs=vmem,
        compiler_params=pltpu.CompilerParams(vmem_limit_bytes=16 * 1024 * 1024),
        cost_estimate=pl.CostEstimate(flops=1000, bytes_accessed=1000, transcendentals=0),
    )(ridge, x_own, z_own, z_came, *x_came)


def squared_table(weight_table):
    wide_table = weight_table.astype(f32)
    return (wide_table * wide_table).astype(bf16)


def weight_totals(class_index, pose_index, defocus_bin, defocus, rows_table, cols_table, plane_weight, first_row, owned):
    box = rows_table.shape[2]
    poses = rows_table.shape[0]
    bins = defocus.shape[0]
    half = box // 2
    exact = lax.Precision.HIGHEST
    code = (class_index[:, 0] * poses + pose_index) * bins + defocus_bin
    codes = lax.all_gather(code, "img", tiled=True)
    hits = (codes[:, None] == jnp.arange(CLASSES * poses * bins, dtype=jnp.int32)).astype(f32)
    counts = jnp.sum(hits, 0).reshape(CLASSES, poses, bins)
    place = jnp.arange(box, dtype=jnp.int32)
    freq = jnp.where(place < half, place, place - box).astype(f32)
    turns = defocus[:, None] * (freq * freq)[None, :] * (1.0 / (half * half))
    turns_y = turns + ctf_phase / math.pi
    ones = jnp.ones_like(turns)
    wave_y = jnp.stack([0.5 * ones, -0.5 * turns_sine(turns_y + 0.25), 0.5 * turns_sine(turns_y)])
    wave_x = jnp.stack([ones, turns_sine(turns + 0.25), turns_sine(turns)])
    rows_own = lax.dynamic_slice_in_dim(rows_table, first_row, owned, 1)
    u = jnp.einsum("pry,mby->pmbr", squared_table(rows_own).astype(f32), wave_y, precision=exact)
    v = jnp.einsum("pxj,mbx->pmbj", squared_table(cols_table).astype(f32), wave_x, precision=exact)
    weight = counts[:, None] * plane_weight.T[None, :, :, None]
    left = weight[:, :, :, None, :, None] * u[None, None]
    return jnp.einsum("czpmbr,pmbj->rczj", left, v, precision=exact)


def by_pairs(images, class_index, pose_index, defocus_bin, defocus, rows_table, cols_table, plane_weight):
    members = lax.axis_size("img")
    rows = rows_table.shape[1]
    planes = plane_weight.shape[1]
    cols = cols_table.shape[2]
    owned = rows // members

    def exchange(value, flip):
        return lax.ppermute(value, "img", [(i, i ^ flip) for i in range(members)])

    x_send, x_keep, own_send, own_keep, z_keep, *z_sends = own_totals(
        images, class_index, pose_index, defocus_bin, defocus, rows_table, cols_table, plane_weight, members
    )
    x_came = exchange(x_send, 1)
    z_came = [exchange(send, 2 * k) for send, k in zip(z_sends, LINE)]
    tables = own_ridges(defocus, plane_weight, rows_table, cols_table, owned)
    x_keep, tables = lax.optimization_barrier((x_keep, tables))
    *x_sends, own_send, z_own, z_send = fold_phase(x_keep, x_came, own_send, z_keep, z_came)
    x_came = [exchange(send, 2 * k) for send, k in zip(x_sends, LINE)]
    own_came = exchange(own_send, 1)
    z_came = exchange(z_send, 1)
    ridge = own_weights(tables, z_own, z_came)
    out = finish(planes, ridge, own_keep, z_own, z_came, (*x_came, own_came))
    return out.reshape(owned, CLASSES, planes, 2, cols)


def by_scatter(images, class_index, pose_index, defocus_bin, defocus, rows_table, cols_table, plane_weight):
    rows = rows_table.shape[1]
    cols = cols_table.shape[2]
    planes = plane_weight.shape[1]
    members = lax.axis_size("img")
    owned = rows // members
    (totals,) = own_totals(
        images, class_index, pose_index, defocus_bin, defocus, rows_table, cols_table, plane_weight, 1
    )
    slots = totals.shape[0]
    totals = totals.reshape(slots, members, owned, 2 * cols).transpose(1, 0, 2, 3)
    own = lax.psum_scatter(totals, "img", scatter_dimension=0, tiled=False)
    weight = weight_totals(
        class_index, pose_index, defocus_bin, defocus, rows_table, cols_table, plane_weight,
        lax.axis_index("img") * owned, owned,
    )
    own = own.astype(f32).reshape(planes, CLASSES, owned, 2, cols).transpose(2, 1, 0, 3, 4)
    return own / (weight[:, :, :, None, :] + wiener_ridge)


def body(*arrays):
    rows = arrays[5].shape[1]
    members = lax.axis_size("img")
    images = members * arrays[0].shape[0]
    paired = members == 8 and images <= 256 and rows % (16 * members) == 0
    return (by_pairs if paired else by_scatter)(*arrays)


def solution(mesh):
    placed = (
        P(("groups", "img"), None, None),
        P(("groups", "img"), None),
        P(("groups", "img")),
        P(("groups", "img")),
        P(),
        P(),
        P(None, None, "slab"),
        P(),
    )
    return jax.shard_map(
        body,
        mesh=mesh,
        in_specs=placed,
        out_specs=P("img", "groups", None, None, "slab"),
        check_vma=False,
    )
```

```python
import functools
import math

import jax
import jax.numpy as jnp
import numpy as np
from jax import lax
from jax.experimental import pallas as pl
from jax.experimental.pallas import tpu as pltpu
from jax.sharding import PartitionSpec as P

CLASSES = 8

wiener_ridge = 1.0
ctf_phase = 0.1
f32 = jnp.float32
bf16 = jnp.bfloat16


def packed_dft(box, sine_sign):
    half = box // 2
    k = np.concatenate([np.arange(half), [half], np.arange(1, half)])
    angle = (k[:, None] * np.arange(box)[None, :] % box) * (2.0 * math.pi / box)
    table = np.where((np.arange(box) <= half)[:, None], np.cos(angle), sine_sign * np.sin(angle))
    return (table / math.sqrt(box)).astype(np.float32)


def iota(shape, axis):
    return lax.broadcasted_iota(jnp.int32, shape, axis)


def dot(a, b, dims=((1,), (0,))):
    return lax.dot_general(a, b, (dims, ((), ())), preferred_element_type=f32)


def turns_sine(turns):
    return jnp.sin((turns - jnp.round(turns)) * (2.0 * math.pi))


def split_two(value):
    high = value.astype(bf16)
    return high, (value - high.astype(f32)).astype(bf16)


def fold_of(place, half):
    box = 2 * half
    return jnp.where(place <= half, place, box + half - place)


def slices_kernel(
    class_hbm, pose_hbm, bin_hbm, defocus_hbm, plane_hbm,
    dft_hbm, dft_t_hbm, images_hbm, rows_hbm, cols_hbm,
    *refs,
):
    outs, refs = refs[:-SCRATCH], refs[-SCRATCH:]
    (
        class_ref, pose_ref, bin_ref, defocus_ref, plane_ref,
        dft_ref, dft_t_ref, images_ref, rows_ref, cols_ref, arrived,
        rows_fold, cols_fold, wave_y, cos_x, sin_x, half_ref, spec_ref, mix_ref, totals,
    ) = refs
    count, box, _ = images_ref.shape
    half = box // 2
    poses, rows, _ = rows_ref.shape
    cols = cols_ref.shape[2]
    planes = plane_ref.shape[0]

    pairs = (
        (class_hbm, class_ref), (pose_hbm, pose_ref), (bin_hbm, bin_ref),
        (defocus_hbm, defocus_ref), (plane_hbm, plane_ref),
        (dft_hbm, dft_ref), (images_hbm.at[0:GROUP], images_ref.at[0:GROUP]),
        (dft_t_hbm, dft_t_ref), (cols_hbm, cols_ref), (rows_hbm, rows_ref),
    ) + tuple(
        (images_hbm.at[i : i + GROUP], images_ref.at[i : i + GROUP])
        for i in range(GROUP, count, GROUP)
    )
    copies = [
        pltpu.make_async_copy(source, target, arrived.at[n])
        for n, (source, target) in enumerate(pairs)
    ]
    for copy in copies:
        copy.start()

    place = iota((box, box), 0)
    other = iota((box, box), 1)
    folded = fold_of(place, half)
    near = (folded == other).astype(f32).astype(bf16)
    far = (jnp.where(folded == 0, 0, box - folded) == other).astype(f32).astype(bf16)

    for copy in copies[:5]:
        copy.wait()
    tall, lanes = wave_y.shape
    lane = iota((1, lanes), 1)
    sub = iota((count, box), 0)
    lane_defocus = jnp.zeros((1, lanes), f32)
    sub_defocus = jnp.zeros((count, box), f32)
    for i in range(count):
        value = defocus_ref[bin_ref[i]]
        lane_defocus = jnp.where(lane % count == i, value, lane_defocus)
        sub_defocus = jnp.where(sub == i, value, sub_defocus)
    scale = 1.0 / (2 * half * half)
    ky = iota((tall, lanes), 0).astype(f32)
    quarter = jnp.where(lane < count, 0.0, 0.25) + ctf_phase / (2.0 * math.pi)
    wave_y[...] = turns_sine(lane_defocus * (ky * ky * scale) + quarter)
    kx = iota((count, box), 1)
    kx = jnp.where(kx <= half, kx, kx - half).astype(f32)
    turns = sub_defocus * (kx * kx * scale)
    cos_x[...] = -turns_sine(turns + 0.25)
    sin_x[...] = -turns_sine(turns)
    totals[...] = jnp.zeros_like(totals)
    leading = 1 if len(outs) > 1 else 0
    if len(outs) > 1:
        bins = defocus_ref.shape[0]
        count_row = iota((16, 2 * cols), 0)
        count_lane = iota((16, 2 * cols), 1)
        counts = jnp.zeros((16, 2 * cols), f32)
        for i in range(count):
            hit = (count_row == class_ref[i]) & (count_lane == pose_ref[i] * bins + bin_ref[i])
            counts = counts + jnp.where(hit, 1.0, 0.0)
        totals[0] = jnp.tile(counts, (rows // 16, 1))

    tile = 8
    tile_row = iota((tile, half), 0) == 0
    tile_col = iota((tile, half), 1) == 0
    col_zero = iota((half, half), 1) == 0
    short_row = iota((16, half), 0) == 0
    short_col = iota((16, half), 1) == 0

    def without_row(value):
        return jnp.concatenate([jnp.where(tile_row, 0.0, value[:tile]), value[tile:]], 0)

    def along_rows(i):
        copies[6 if i == 0 else 9 + i // GROUP].wait()
        group = jnp.concatenate([images_ref[i + n] for n in range(GROUP)], 1)
        product = dot(dft_ref[...], group).astype(bf16)
        for n in range(GROUP):
            half_ref[i // GROUP % 2, n * box : (n + 1) * box] = product[:, n * box : (n + 1) * box]

    def along_columns(i):
        return dot(half_ref[i // GROUP % 2], dft_t_ref[...])

    def weigh(i, y):
        sin_col = jnp.broadcast_to(wave_y[:, i : i + 1], (tall, half))
        cos_col = jnp.broadcast_to(wave_y[:, count + i : count + i + 1], (tall, half))
        near_ctf = sin_col * cos_x[i : i + 1, :half] + cos_col * sin_x[i : i + 1, :half]
        far_ctf = sin_col * cos_x[i : i + 1, half:] + cos_col * sin_x[i : i + 1, half:]
        cc, cs = y[:half, :half], y[:half, half:]
        sc, ss = y[half:, :half], y[half:, half:]
        ss_row = without_row(ss)
        ss_in = jnp.where(col_zero, 0.0, ss_row)
        sc_in = without_row(sc)
        cs_in = jnp.where(col_zero, 0.0, cs)
        near_y, far_y = near_ctf[:half], far_ctf[:half]
        spec = spec_ref.at[i % SLOTS]
        spec[0:half, 0:half] = (near_y * (cc + ss_in)).astype(bf16)
        spec[0:half, half:] = (far_y * jnp.where(col_zero, cs, cc - ss_in)).astype(bf16)
        spec[half:box, 0:half] = (near_y * (sc_in - cs_in)).astype(bf16)
        spec[half:box, half:] = (far_y * jnp.where(col_zero, ss_row, sc_in + cs_in)).astype(bf16)
        sc_top = jnp.broadcast_to(sc[0:1], (16, half))
        ss_top = jnp.broadcast_to(ss[0:1], (16, half))
        ss_top_in = jnp.where(short_col, 0.0, ss_top)
        spec[box : box + 16, 0:half] = (
            near_ctf[half : half + 1] * jnp.where(short_row, sc_top, -ss_top_in)
        ).astype(bf16)
        spec[box : box + 16, half:] = (
            far_ctf[half : half + 1]
            * jnp.where(short_row, jnp.where(short_col, ss_top, sc_top), ss_top_in)
        ).astype(bf16)

    def mix(i):
        mixed = dot(spec_ref[i % SLOTS], cols_fold[pose_ref[i]])
        out = mix_ref.at[i % SLOTS]
        out[0:half, 0:cols] = mixed[:half, :cols].astype(bf16)
        out[0:half, cols:] = mixed[half:box, :cols].astype(bf16)
        top = iota((16, cols), 0) == 0
        real, imag = mixed[:half, cols:], -mixed[half:box, cols:]
        out[half : half + 16, 0:cols] = jnp.where(
            top, mixed[box : box + 1, :cols], real[:16]
        ).astype(bf16)
        out[half : half + 16, cols:] = jnp.where(
            top, mixed[box + 1 : box + 2, :cols], imag[:16]
        ).astype(bf16)
        out[half + 16 :, 0:cols] = real[16:].astype(bf16)
        out[half + 16 :, cols:] = imag[16:].astype(bf16)

    def insert(i):
        pose = pose_ref[i]
        pose_rows = rows_fold[pl.ds(pl.multiple_of(pose * rows, rows), rows), :]
        piece = dot(pose_rows, mix_ref[i % SLOTS])
        for z in range(planes):
            slot = leading + z * CLASSES + class_ref[i]
            totals[slot] += plane_ref[z, pose] * piece

    copies[5].wait()
    along_rows(0)
    copies[7].wait()
    copies[8].wait()
    for p in range(0, poses, 2):
        two = jnp.concatenate([cols_ref[p], cols_ref[p + 1]], 1)
        near_two = dot(near, two).astype(bf16)
        far_two = dot(far, two).astype(bf16)
        cols_fold[p] = jnp.concatenate([near_two[:, :cols], far_two[:, :cols]], 1)
        cols_fold[p + 1] = jnp.concatenate([near_two[:, cols:], far_two[:, cols:]], 1)
    copies[9].wait()
    rows_fold[...] = dot(
        rows_ref[...].reshape(poses * rows, box), near, ((1,), (1,))
    ).astype(bf16)
    for first in range(0, count, GROUP):
        if first + GROUP < count:
            along_rows(first + GROUP)
        product = along_columns(first)
        for n in range(GROUP):
            weigh(first + n, product[n * box : (n + 1) * box])
            if first + n >= 1:
                mix(first + n - 1)
            if first + n >= 2:
                insert(first + n - 2)
    mix(count - 1)
    insert(count - 2)
    insert(count - 1)

    if len(outs) == 1:
        outs[0][...] = totals[...].astype(bf16)
        return
    x_send, x_keep, own_send, own_keep, z_keep = outs[:5]
    z_sends = outs[5:]
    x_slots, owned, _ = own_keep.shape
    me = lax.axis_index("img")

    def rows_of(flip):
        return pl.ds(pl.multiple_of((me ^ flip) * owned, owned), owned)

    for n, k in enumerate(LINE):
        x_send[n] = totals[-x_slots:, rows_of(2 * k + 1), :].astype(bf16)
        x_keep[n] = totals[-x_slots:, rows_of(2 * k), :]
    own_send[...] = totals[-x_slots:, rows_of(1), :].astype(bf16)
    own_keep[...] = totals[-x_slots:, rows_of(0), :]
    for k, out in zip((0,) + LINE, (z_keep, *z_sends)):
        out[:Z_SLOTS] = totals[:Z_SLOTS, rows_of(2 * k), :].astype(out.dtype)
        out[Z_SLOTS:] = totals[1:Z_SLOTS, rows_of(2 * k + 1), :].astype(out.dtype)


SCRATCH = 20
LINE = (2, 3, 1)
SLOTS = 8
GROUP = 4
Z_SLOTS = 4


def own_totals(images, class_index, pose_index, defocus_bin, defocus, rows_table, cols_table, plane_weight, members):
    count, box, _ = images.shape
    poses, rows, _ = rows_table.shape
    cols = cols_table.shape[2]
    planes = plane_weight.shape[1]
    slots = CLASSES * planes
    table_y, table_x = packed_dft(box, -1.0), packed_dft(box, 1.0)
    any_place = pl.BlockSpec(memory_space=pl.ANY)
    vmem = pl.BlockSpec(memory_space=pltpu.VMEM)
    lanes = 128 * (-(-2 * count // 128))
    if members == 1:
        out_shape = [jax.ShapeDtypeStruct((slots, rows, 2 * cols), bf16)]
    else:
        slots += 1
        tail = (rows // members, 2 * cols)
        x_slots = slots - Z_SLOTS
        out_shape = []
        for lead in ((len(LINE), x_slots), (x_slots,)):
            out_shape += [pltpu.VMEM(lead + tail, bf16), pltpu.VMEM(lead + tail, f32)]
        out_shape += [pltpu.VMEM((2 * Z_SLOTS - 1,) + tail, f32)]
        out_shape += [pltpu.VMEM((2 * Z_SLOTS - 1,) + tail, bf16)] * len(LINE)
    operands = (
        class_index[:, 0], pose_index, defocus_bin, defocus, plane_weight.T,
        jnp.asarray(table_y, bf16), jnp.asarray(table_x.T.copy(), bf16),
        images, rows_table, cols_table,
    )
    return pl.pallas_call(
        slices_kernel,
        out_shape=out_shape,
        in_specs=[any_place] * 10,
        out_specs=[vmem] * len(out_shape),
        scratch_shapes=[pltpu.SMEM(x.shape, x.dtype) for x in operands[:5]]
        + [pltpu.VMEM(x.shape, x.dtype) for x in operands[5:]]
        + [
            pltpu.SemaphoreType.DMA((9 + count // GROUP,)),
            pltpu.VMEM((poses * rows, box), bf16),
            pltpu.VMEM((poses, box, 2 * cols), bf16),
            pltpu.VMEM((box // 2 + 8, lanes), f32),
            pltpu.VMEM((count, box), f32),
            pltpu.VMEM((count, box), f32),
            pltpu.VMEM((2, GROUP * box, box), bf16),
            pltpu.VMEM((SLOTS, box + 16, box), bf16),
            pltpu.VMEM((SLOTS, box, 2 * cols), bf16),
            pltpu.VMEM((slots, rows, 2 * cols), f32),
        ],
        compiler_params=pltpu.CompilerParams(vmem_limit_bytes=VMEM_LIMIT),
        cost_estimate=pl.CostEstimate(
            flops=2 * count * box * box * 1000, bytes_accessed=6 * 1024 * 1024, transcendentals=0
        ),
    )(*operands)


VMEM_LIMIT = 56 * 1024 * 1024


def ridge_kernel(defocus_hbm, plane_hbm, rows_hbm, cols_hbm, high_ref, low_ref, share_ref, *refs):
    defocus_ref, plane_ref, rows_ref, cols_ref, arrived = refs
    poses, owned, box = rows_ref.shape
    cols = cols_ref.shape[2]
    bins = defocus_ref.shape[0]
    planes = plane_ref.shape[0]
    half = box // 2
    first = pl.multiple_of(lax.axis_index("img") * owned, owned)
    copies = [
        pltpu.make_async_copy(defocus_hbm, defocus_ref, arrived.at[0]),
        pltpu.make_async_copy(plane_hbm, plane_ref, arrived.at[1]),
        pltpu.make_async_copy(rows_hbm.at[:, pl.ds(first, owned), :], rows_ref, arrived.at[2]),
        pltpu.make_async_copy(cols_hbm, cols_ref, arrived.at[3]),
    ]
    for copy in copies:
        copy.start()
    for copy in copies:
        copy.wait()
    share_plane = iota((planes * CLASSES, poses * bins), 0) // CLASSES
    share_pose = iota((planes * CLASSES, poses * bins), 1) // bins
    share = jnp.zeros((planes * CLASSES, poses * bins), f32)
    for p in range(poses):
        for z in range(planes):
            share = jnp.where((share_plane == z) & (share_pose == p), plane_ref[z, p], share)
    share_ref[...] = share

    bin_row = iota((bins, box), 0)
    sub_defocus = jnp.zeros((bins, box), f32)
    for b in range(bins):
        sub_defocus = jnp.where(bin_row == b, defocus_ref[b], sub_defocus)
    freq = iota((bins, box), 1)
    freq = jnp.where(freq < half, freq, box - freq).astype(f32)
    turns_x = sub_defocus * (freq * freq * (1.0 / (half * half)))
    turns_y = turns_x + ctf_phase / math.pi
    ones = jnp.ones((bins, box), f32)
    wave_y = jnp.concatenate(
        [0.5 * ones, -0.5 * turns_sine(turns_y + 0.25), 0.5 * turns_sine(turns_y)], 0
    )
    wave_x = jnp.concatenate([ones, turns_sine(turns_x + 0.25), turns_sine(turns_x)], 0)
    y_high, y_low = split_two(wave_y)
    x_high, x_low = split_two(wave_x)
    rows_sq = rows_ref[...].reshape(poses * owned, box).astype(f32)
    rows_sq = (rows_sq * rows_sq).astype(bf16)
    u = dot(y_high, rows_sq, ((1,), (1,))) + dot(y_low, rows_sq, ((1,), (1,)))
    for p in range(poses):
        cols_sq = cols_ref[p].astype(f32)
        cols_sq = (cols_sq * cols_sq).astype(bf16)
        v = dot(x_high, cols_sq) + dot(x_low, cols_sq)
        for r in range(owned):
            column = u[:, p * owned + r : p * owned + r + 1]
            product = v * column
            weight = product[:bins] + product[bins : 2 * bins] + product[2 * bins :]
            high, low = split_two(weight)
            high_ref[p * bins : (p + 1) * bins, r * cols : (r + 1) * cols] = high
            low_ref[p * bins : (p + 1) * bins, r * cols : (r + 1) * cols] = low


def own_ridges(defocus, plane_weight, rows_table, cols_table, owned):
    poses, _, box = rows_table.shape
    cols = cols_table.shape[2]
    bins = defocus.shape[0]
    any_place = pl.BlockSpec(memory_space=pl.ANY)
    vmem = pl.BlockSpec(memory_space=pltpu.VMEM)
    planes = plane_weight.T
    table = pltpu.VMEM((poses * bins, owned * cols), bf16)
    return pl.pallas_call(
        ridge_kernel,
        out_shape=[table, table, pltpu.VMEM((planes.shape[0] * CLASSES, poses * bins), f32)],
        in_specs=[any_place] * 4,
        out_specs=[vmem] * 3,
        scratch_shapes=[
            pltpu.SMEM(defocus.shape, f32),
            pltpu.SMEM(planes.shape, f32),
            pltpu.VMEM((poses, owned, box), bf16),
            pltpu.VMEM(cols_table.shape, bf16),
            pltpu.SemaphoreType.DMA((4,)),
        ],
        compiler_params=pltpu.CompilerParams(vmem_limit_bytes=VMEM_LIMIT),
        cost_estimate=pl.CostEstimate(
            flops=1000, bytes_accessed=1000, transcendentals=0
        ),
    )(defocus, planes, rows_table, cols_table)


def call_in_vmem(kernel, arrays, out_shape):
    vmem = pl.BlockSpec(memory_space=pltpu.VMEM)
    return pl.pallas_call(
        kernel,
        out_shape=out_shape,
        in_specs=[vmem] * len(arrays),
        out_specs=[vmem] * len(out_shape),
        compiler_params=pltpu.CompilerParams(vmem_limit_bytes=16 * 1024 * 1024),
        cost_estimate=pl.CostEstimate(flops=1000, bytes_accessed=1000, transcendentals=0),
    )(*arrays)


def fold_kernel(x_keep, x_came, own_send, z_keep, *refs):
    z_came, refs = refs[: len(LINE)], refs[len(LINE) :]
    x_sends, own_out, z_own, z_send = refs[: len(LINE)], *refs[len(LINE) :]
    for n, send in enumerate(x_sends):
        send[...] = (x_keep[n] + x_came[n].astype(f32)).astype(bf16)
    own_out[...] = own_send[...]
    for n in range(z_keep.shape[0]):
        value = z_keep[n]
        for came in z_came:
            value = value + came[n].astype(f32)
        if n < Z_SLOTS:
            z_own[n] = value
        if n == 0:
            z_send[n] = value.astype(bf16)
        elif n >= Z_SLOTS:
            z_send[n - Z_SLOTS + 1] = value.astype(bf16)


def fold_phase(x_keep, x_came, own_send, z_keep, z_came):
    piece = own_send.shape
    z_piece = (Z_SLOTS,) + piece[1:]
    out_shape = [pltpu.VMEM(piece, bf16)] * (len(LINE) + 1)
    out_shape += [pltpu.VMEM(z_piece, f32), pltpu.VMEM(z_piece, bf16)]
    return call_in_vmem(fold_kernel, (x_keep, x_came, own_send, z_keep, *z_came), out_shape)


def weight_kernel(high_ref, low_ref, share_ref, z_own, z_came, out_ref, ridge_ref):
    slots, pairs = share_ref.shape
    owned, _, cols = ridge_ref.shape
    counts = z_own[0] + z_came[0].astype(f32)
    scaled = jnp.concatenate([counts[:CLASSES, :pairs]] * (slots // CLASSES), 0) * share_ref[...]
    c_high, c_low = split_two(scaled)
    weight = (
        dot(c_high, high_ref[...]) + dot(c_low, high_ref[...]) + dot(c_high, low_ref[...])
    )
    ridge = 1.0 / (weight + wiener_ridge)
    for r in range(owned):
        ridge_ref[r] = ridge[:, r * cols : (r + 1) * cols]
    for s in range(slots):
        out_ref[s] = ridge_ref[:, s, :]


def own_weights(tables, z_own, z_came):
    slots = tables[2].shape[0]
    _, owned, wide = z_own.shape
    cols = wide // 2
    vmem = pl.BlockSpec(memory_space=pltpu.VMEM)
    return pl.pallas_call(
        weight_kernel,
        out_shape=pltpu.VMEM((slots, owned, cols), f32),
        in_specs=[vmem] * 5,
        out_specs=vmem,
        scratch_shapes=[pltpu.VMEM((owned, slots, cols), f32)],
        compiler_params=pltpu.CompilerParams(vmem_limit_bytes=16 * 1024 * 1024),
        cost_estimate=pl.CostEstimate(flops=1000, bytes_accessed=1000, transcendentals=0),
    )(*tables, z_own, z_came)


def finish_kernel(planes, ridge_ref, x_own, z_own, z_came, *refs):
    x_came, (out_hbm, out_ref, sent) = refs[:-3], refs[-3:]
    slots, owned, cols = ridge_ref.shape
    first = z_own.shape[0]
    copies = []
    for n in range(OUT_PARTS):
        places = range(n * slots // OUT_PARTS, (n + 1) * slots // OUT_PARTS)
        for place in places:
            s = place % planes * CLASSES + place // planes
            if s + 1 < first:
                value = z_own[s + 1] + z_came[s + 1].astype(f32)
            else:
                value = x_own[s + 1 - first]
                for came in x_came:
                    value = value + came[s + 1 - first].astype(f32)
            factor = ridge_ref[s]
            out_ref[:, 2 * place, :] = value[:, :cols] * factor
            out_ref[:, 2 * place + 1, :] = value[:, cols:] * factor
        part = pl.ds(2 * places[0], 2 * len(places))
        copies.append(pltpu.make_async_copy(out_ref.at[:, part], out_hbm.at[:, part], sent.at[n]))
        copies[-1].start()
    for copy in copies:
        copy.wait()


OUT_PARTS = 2


def finish(planes, ridge, x_own, z_own, z_came, x_came):
    slots, owned, cols = ridge.shape
    vmem = pl.BlockSpec(memory_space=pltpu.VMEM)
    return pl.pallas_call(
        functools.partial(finish_kernel, planes),
        out_shape=jax.ShapeDtypeStruct((owned, 2 * slots, cols), f32),
        in_specs=[vmem] * (4 + len(x_came)),
        out_specs=pl.BlockSpec(memory_space=pl.ANY),
        scratch_shapes=[
            pltpu.VMEM((owned, 2 * slots, cols), f32),
            pltpu.SemaphoreType.DMA((OUT_PARTS,)),
        ],
        compiler_params=pltpu.CompilerParams(vmem_limit_bytes=16 * 1024 * 1024),
        cost_estimate=pl.CostEstimate(flops=1000, bytes_accessed=1000, transcendentals=0),
    )(ridge, x_own, z_own, z_came, *x_came)


def squared_table(weight_table):
    wide_table = weight_table.astype(f32)
    return (wide_table * wide_table).astype(bf16)


def weight_totals(class_index, pose_index, defocus_bin, defocus, rows_table, cols_table, plane_weight, first_row, owned):
    box = rows_table.shape[2]
    poses = rows_table.shape[0]
    bins = defocus.shape[0]
    half = box // 2
    exact = lax.Precision.HIGHEST
    code = (class_index[:, 0] * poses + pose_index) * bins + defocus_bin
    codes = lax.all_gather(code, "img", tiled=True)
    hits = (codes[:, None] == jnp.arange(CLASSES * poses * bins, dtype=jnp.int32)).astype(f32)
    counts = jnp.sum(hits, 0).reshape(CLASSES, poses, bins)
    place = jnp.arange(box, dtype=jnp.int32)
    freq = jnp.where(place < half, place, place - box).astype(f32)
    turns = defocus[:, None] * (freq * freq)[None, :] * (1.0 / (half * half))
    turns_y = turns + ctf_phase / math.pi
    ones = jnp.ones_like(turns)
    wave_y = jnp.stack([0.5 * ones, -0.5 * turns_sine(turns_y + 0.25), 0.5 * turns_sine(turns_y)])
    wave_x = jnp.stack([ones, turns_sine(turns + 0.25), turns_sine(turns)])
    rows_own = lax.dynamic_slice_in_dim(rows_table, first_row, owned, 1)
    u = jnp.einsum("pry,mby->pmbr", squared_table(rows_own).astype(f32), wave_y, precision=exact)
    v = jnp.einsum("pxj,mbx->pmbj", squared_table(cols_table).astype(f32), wave_x, precision=exact)
    weight = counts[:, None] * plane_weight.T[None, :, :, None]
    left = weight[:, :, :, None, :, None] * u[None, None]
    return jnp.einsum("czpmbr,pmbj->rczj", left, v, precision=exact)


def by_pairs(images, class_index, pose_index, defocus_bin, defocus, rows_table, cols_table, plane_weight):
    members = lax.axis_size("img")
    rows = rows_table.shape[1]
    planes = plane_weight.shape[1]
    cols = cols_table.shape[2]
    owned = rows // members

    def exchange(value, flip):
        return lax.ppermute(value, "img", [(i, i ^ flip) for i in range(members)])

    x_send, x_keep, own_send, own_keep, z_keep, *z_sends = own_totals(
        images, class_index, pose_index, defocus_bin, defocus, rows_table, cols_table, plane_weight, members
    )
    x_came = exchange(x_send, 1)
    z_came = [exchange(send, 2 * k) for send, k in zip(z_sends, LINE)]
    tables = own_ridges(defocus, plane_weight, rows_table, cols_table, owned)
    x_keep, tables = lax.optimization_barrier((x_keep, tables))
    *x_sends, own_send, z_own, z_send = fold_phase(x_keep, x_came, own_send, z_keep, z_came)
    x_came = [exchange(send, 2 * k) for send, k in zip(x_sends, LINE)]
    own_came = exchange(own_send, 1)
    z_came = exchange(z_send, 1)
    ridge = own_weights(tables, z_own, z_came)
    out = finish(planes, ridge, own_keep, z_own, z_came, (*x_came, own_came))
    return out.reshape(owned, CLASSES, planes, 2, cols)


def by_scatter(images, class_index, pose_index, defocus_bin, defocus, rows_table, cols_table, plane_weight):
    rows = rows_table.shape[1]
    cols = cols_table.shape[2]
    planes = plane_weight.shape[1]
    members = lax.axis_size("img")
    owned = rows // members
    (totals,) = own_totals(
        images, class_index, pose_index, defocus_bin, defocus, rows_table, cols_table, plane_weight, 1
    )
    slots = totals.shape[0]
    totals = totals.reshape(slots, members, owned, 2 * cols).transpose(1, 0, 2, 3)
    own = lax.psum_scatter(totals, "img", scatter_dimension=0, tiled=False)
    weight = weight_totals(
        class_index, pose_index, defocus_bin, defocus, rows_table, cols_table, plane_weight,
        lax.axis_index("img") * owned, owned,
    )
    own = own.astype(f32).reshape(planes, CLASSES, owned, 2, cols).transpose(2, 1, 0, 3, 4)
    return own / (weight[:, :, :, None, :] + wiener_ridge)


def body(*arrays):
    rows = arrays[5].shape[1]
    members = lax.axis_size("img")
    images = members * arrays[0].shape[0]
    paired = members == 8 and images <= 256 and rows % (16 * members) == 0
    return (by_pairs if paired else by_scatter)(*arrays)


def solution(mesh):
    placed = (
        P(("groups", "img"), None, None),
        P(("groups", "img"), None),
        P(("groups", "img")),
        P(("groups", "img")),
        P(),
        P(),
        P(None, None, "slab"),
        P(),
    )
    return jax.shard_map(
        body,
        mesh=mesh,
        in_specs=placed,
        out_specs=P("img", "groups", None, None, "slab"),
        check_vma=False,
    )
```

```python
import functools
import math

import jax
import jax.numpy as jnp
import numpy as np
from jax import lax
from jax.experimental import pallas as pl
from jax.experimental.pallas import tpu as pltpu
from jax.sharding import PartitionSpec as P

CLASSES = 8

wiener_ridge = 1.0
ctf_phase = 0.1
f32 = jnp.float32
bf16 = jnp.bfloat16


def packed_dft(box, sine_sign):
    half = box // 2
    k = np.concatenate([np.arange(half), [half], np.arange(1, half)])
    angle = (k[:, None] * np.arange(box)[None, :] % box) * (2.0 * math.pi / box)
    table = np.where((np.arange(box) <= half)[:, None], np.cos(angle), sine_sign * np.sin(angle))
    return (table / math.sqrt(box)).astype(np.float32)


def iota(shape, axis):
    return lax.broadcasted_iota(jnp.int32, shape, axis)


def dot(a, b, dims=((1,), (0,))):
    return lax.dot_general(a, b, (dims, ((), ())), preferred_element_type=f32)


def turns_sine(turns):
    return jnp.sin((turns - jnp.round(turns)) * (2.0 * math.pi))


def split_two(value):
    high = value.astype(bf16)
    return high, (value - high.astype(f32)).astype(bf16)


def fold_of(place, half):
    box = 2 * half
    return jnp.where(place <= half, place, box + half - place)


def slices_kernel(
    class_hbm, pose_hbm, bin_hbm, defocus_hbm, plane_hbm,
    dft_hbm, dft_t_hbm, images_hbm, rows_hbm, cols_hbm,
    *refs,
):
    outs, refs = refs[:-SCRATCH], refs[-SCRATCH:]
    (
        class_ref, pose_ref, bin_ref, defocus_ref, plane_ref,
        dft_ref, dft_t_ref, images_ref, rows_ref, cols_ref, arrived,
        rows_fold, cols_fold, wave_y, cos_x, sin_x, half_ref, spec_ref, mix_ref, totals,
    ) = refs
    count, box, _ = images_ref.shape
    half = box // 2
    poses, rows, _ = rows_ref.shape
    cols = cols_ref.shape[2]
    planes = plane_ref.shape[0]

    pairs = (
        (class_hbm, class_ref), (pose_hbm, pose_ref), (bin_hbm, bin_ref),
        (defocus_hbm, defocus_ref), (plane_hbm, plane_ref),
        (dft_hbm, dft_ref), (images_hbm.at[0:GROUP], images_ref.at[0:GROUP]),
        (dft_t_hbm, dft_t_ref), (cols_hbm, cols_ref), (rows_hbm, rows_ref),
    ) + tuple(
        (images_hbm.at[i : i + GROUP], images_ref.at[i : i + GROUP])
        for i in range(GROUP, count, GROUP)
    )
    copies = [
        pltpu.make_async_copy(source, target, arrived.at[n])
        for n, (source, target) in enumerate(pairs)
    ]
    for copy in copies:
        copy.start()

    place = iota((box, box), 0)
    other = iota((box, box), 1)
    folded = fold_of(place, half)
    near = (folded == other).astype(f32).astype(bf16)
    far = (jnp.where(folded == 0, 0, box - folded) == other).astype(f32).astype(bf16)

    for copy in copies[:5]:
        copy.wait()
    tall, lanes = wave_y.shape
    lane = iota((1, lanes), 1)
    sub = iota((count, box), 0)
    lane_defocus = jnp.zeros((1, lanes), f32)
    sub_defocus = jnp.zeros((count, box), f32)
    for i in range(count):
        value = defocus_ref[bin_ref[i]]
        lane_defocus = jnp.where(lane % count == i, value, lane_defocus)
        sub_defocus = jnp.where(sub == i, value, sub_defocus)
    scale = 1.0 / (2 * half * half)
    ky = iota((tall, lanes), 0).astype(f32)
    quarter = jnp.where(lane < count, 0.0, 0.25) + ctf_phase / (2.0 * math.pi)
    wave_y[...] = turns_sine(lane_defocus * (ky * ky * scale) + quarter)
    kx = iota((count, box), 1)
    kx = jnp.where(kx <= half, kx, kx - half).astype(f32)
    turns = sub_defocus * (kx * kx * scale)
    cos_x[...] = -turns_sine(turns + 0.25)
    sin_x[...] = -turns_sine(turns)
    totals[...] = jnp.zeros_like(totals)
    leading = 1 if len(outs) > 1 else 0
    if len(outs) > 1:
        bins = defocus_ref.shape[0]
        count_row = iota((16, 2 * cols), 0)
        count_lane = iota((16, 2 * cols), 1)
        counts = jnp.zeros((16, 2 * cols), f32)
        for i in range(count):
            hit = (count_row == class_ref[i]) & (count_lane == pose_ref[i] * bins + bin_ref[i])
            counts = counts + jnp.where(hit, 1.0, 0.0)
        totals[0] = jnp.tile(counts, (rows // 16, 1))

    tile = 8
    tile_row = iota((tile, half), 0) == 0
    tile_col = iota((tile, half), 1) == 0
    col_zero = iota((half, half), 1) == 0
    short_row = iota((16, half), 0) == 0
    short_col = iota((16, half), 1) == 0

    def without_row(value):
        return jnp.concatenate([jnp.where(tile_row, 0.0, value[:tile]), value[tile:]], 0)

    def along_rows(i):
        copies[6 if i == 0 else 9 + i // GROUP].wait()
        group = jnp.concatenate([images_ref[i + n] for n in range(GROUP)], 1)
        product = dot(dft_ref[...], group).astype(bf16)
        for n in range(GROUP):
            half_ref[i // GROUP % 2, n * box : (n + 1) * box] = product[:, n * box : (n + 1) * box]

    def along_columns(i):
        return dot(half_ref[i // GROUP % 2], dft_t_ref[...])

    def weigh(i, y):
        sin_col = jnp.broadcast_to(wave_y[:, i : i + 1], (tall, half))
        cos_col = jnp.broadcast_to(wave_y[:, count + i : count + i + 1], (tall, half))
        near_ctf = sin_col * cos_x[i : i + 1, :half] + cos_col * sin_x[i : i + 1, :half]
        far_ctf = sin_col * cos_x[i : i + 1, half:] + cos_col * sin_x[i : i + 1, half:]
        cc, cs = y[:half, :half], y[:half, half:]
        sc, ss = y[half:, :half], y[half:, half:]
        ss_row = without_row(ss)
        ss_in = jnp.where(col_zero, 0.0, ss_row)
        sc_in = without_row(sc)
        cs_in = jnp.where(col_zero, 0.0, cs)
        near_y, far_y = near_ctf[:half], far_ctf[:half]
        spec = spec_ref.at[i % SLOTS]
        spec[0:half, 0:half] = (near_y * (cc + ss_in)).astype(bf16)
        spec[0:half, half:] = (far_y * jnp.where(col_zero, cs, cc - ss_in)).astype(bf16)
        spec[half:box, 0:half] = (near_y * (sc_in - cs_in)).astype(bf16)
        spec[half:box, half:] = (far_y * jnp.where(col_zero, ss_row, sc_in + cs_in)).astype(bf16)
        sc_top = jnp.broadcast_to(sc[0:1], (16, half))
        ss_top = jnp.broadcast_to(ss[0:1], (16, half))
        ss_top_in = jnp.where(short_col, 0.0, ss_top)
        spec[box : box + 16, 0:half] = (
            near_ctf[half : half + 1] * jnp.where(short_row, sc_top, -ss_top_in)
        ).astype(bf16)
        spec[box : box + 16, half:] = (
            far_ctf[half : half + 1]
            * jnp.where(short_row, jnp.where(short_col, ss_top, sc_top), ss_top_in)
        ).astype(bf16)

    def mix(i):
        mixed = dot(spec_ref[i % SLOTS], cols_fold[pose_ref[i]])
        out = mix_ref.at[i % SLOTS]
        out[0:half, 0:cols] = mixed[:half, :cols].astype(bf16)
        out[0:half, cols:] = mixed[half:box, :cols].astype(bf16)
        top = iota((16, cols), 0) == 0
        real, imag = mixed[:half, cols:], -mixed[half:box, cols:]
        out[half : half + 16, 0:cols] = jnp.where(
            top, mixed[box : box + 1, :cols], real[:16]
        ).astype(bf16)
        out[half : half + 16, cols:] = jnp.where(
            top, mixed[box + 1 : box + 2, :cols], imag[:16]
        ).astype(bf16)
        out[half + 16 :, 0:cols] = real[16:].astype(bf16)
        out[half + 16 :, cols:] = imag[16:].astype(bf16)

    def insert(i):
        pose = pose_ref[i]
        pose_rows = rows_fold[pl.ds(pl.multiple_of(pose * rows, rows), rows), :]
        piece = dot(pose_rows, mix_ref[i % SLOTS])
        for z in range(planes):
            slot = leading + z * CLASSES + class_ref[i]
            totals[slot] += plane_ref[z, pose] * piece

    copies[5].wait()
    along_rows(0)
    copies[7].wait()
    copies[8].wait()
    for p in range(0, poses, 2):
        two = jnp.concatenate([cols_ref[p], cols_ref[p + 1]], 1)
        near_two = dot(near, two).astype(bf16)
        far_two = dot(far, two).astype(bf16)
        cols_fold[p] = jnp.concatenate([near_two[:, :cols], far_two[:, :cols]], 1)
        cols_fold[p + 1] = jnp.concatenate([near_two[:, cols:], far_two[:, cols:]], 1)
    copies[9].wait()
    rows_fold[...] = dot(
        rows_ref[...].reshape(poses * rows, box), near, ((1,), (1,))
    ).astype(bf16)
    for step in range(GROUP, count + 3 * GROUP, GROUP):
        if step < count:
            along_rows(step)
        if step - GROUP < count:
            product = along_columns(step - GROUP)
        for n in range(GROUP):
            if step - GROUP < count:
                weigh(step - GROUP + n, product[n * box : (n + 1) * box])
            if 0 <= step - 2 * GROUP < count:
                mix(step - 2 * GROUP + n)
            if step >= 3 * GROUP:
                insert(step - 3 * GROUP + n)

    if len(outs) == 1:
        outs[0][...] = totals[...].astype(bf16)
        return
    x_send, x_keep, own_send, own_keep, z_keep = outs[:5]
    z_sends = outs[5:]
    x_slots, owned, _ = own_keep.shape
    me = lax.axis_index("img")

    def rows_of(flip):
        return pl.ds(pl.multiple_of((me ^ flip) * owned, owned), owned)

    for n, k in enumerate(LINE):
        x_send[n] = totals[-x_slots:, rows_of(2 * k + 1), :].astype(bf16)
        x_keep[n] = totals[-x_slots:, rows_of(2 * k), :]
    own_send[...] = totals[-x_slots:, rows_of(1), :].astype(bf16)
    own_keep[...] = totals[-x_slots:, rows_of(0), :]
    for k, out in zip((0,) + LINE, (z_keep, *z_sends)):
        out[:Z_SLOTS] = totals[:Z_SLOTS, rows_of(2 * k), :].astype(out.dtype)
        out[Z_SLOTS:] = totals[1:Z_SLOTS, rows_of(2 * k + 1), :].astype(out.dtype)


SCRATCH = 20
LINE = (2, 3, 1)
SLOTS = 8
GROUP = 4
Z_SLOTS = 4


def own_totals(images, class_index, pose_index, defocus_bin, defocus, rows_table, cols_table, plane_weight, members):
    count, box, _ = images.shape
    poses, rows, _ = rows_table.shape
    cols = cols_table.shape[2]
    planes = plane_weight.shape[1]
    slots = CLASSES * planes
    table_y, table_x = packed_dft(box, -1.0), packed_dft(box, 1.0)
    any_place = pl.BlockSpec(memory_space=pl.ANY)
    vmem = pl.BlockSpec(memory_space=pltpu.VMEM)
    lanes = 128 * (-(-2 * count // 128))
    if members == 1:
        out_shape = [jax.ShapeDtypeStruct((slots, rows, 2 * cols), bf16)]
    else:
        slots += 1
        tail = (rows // members, 2 * cols)
        x_slots = slots - Z_SLOTS
        out_shape = []
        for lead in ((len(LINE), x_slots), (x_slots,)):
            out_shape += [pltpu.VMEM(lead + tail, bf16), pltpu.VMEM(lead + tail, f32)]
        out_shape += [pltpu.VMEM((2 * Z_SLOTS - 1,) + tail, f32)]
        out_shape += [pltpu.VMEM((2 * Z_SLOTS - 1,) + tail, bf16)] * len(LINE)
    operands = (
        class_index[:, 0], pose_index, defocus_bin, defocus, plane_weight.T,
        jnp.asarray(table_y, bf16), jnp.asarray(table_x.T.copy(), bf16),
        images, rows_table, cols_table,
    )
    return pl.pallas_call(
        slices_kernel,
        out_shape=out_shape,
        in_specs=[any_place] * 10,
        out_specs=[vmem] * len(out_shape),
        scratch_shapes=[pltpu.SMEM(x.shape, x.dtype) for x in operands[:5]]
        + [pltpu.VMEM(x.shape, x.dtype) for x in operands[5:]]
        + [
            pltpu.SemaphoreType.DMA((9 + count // GROUP,)),
            pltpu.VMEM((poses * rows, box), bf16),
            pltpu.VMEM((poses, box, 2 * cols), bf16),
            pltpu.VMEM((box // 2 + 8, lanes), f32),
            pltpu.VMEM((count, box), f32),
            pltpu.VMEM((count, box), f32),
            pltpu.VMEM((2, GROUP * box, box), bf16),
            pltpu.VMEM((SLOTS, box + 16, box), bf16),
            pltpu.VMEM((SLOTS, box, 2 * cols), bf16),
            pltpu.VMEM((slots, rows, 2 * cols), f32),
        ],
        compiler_params=pltpu.CompilerParams(vmem_limit_bytes=VMEM_LIMIT),
        cost_estimate=pl.CostEstimate(
            flops=2 * count * box * box * 1000, bytes_accessed=6 * 1024 * 1024, transcendentals=0
        ),
    )(*operands)


VMEM_LIMIT = 56 * 1024 * 1024


def ridge_kernel(defocus_hbm, plane_hbm, rows_hbm, cols_hbm, high_ref, low_ref, share_ref, *refs):
    defocus_ref, plane_ref, rows_ref, cols_ref, arrived = refs
    poses, owned, box = rows_ref.shape
    cols = cols_ref.shape[2]
    bins = defocus_ref.shape[0]
    planes = plane_ref.shape[0]
    half = box // 2
    first = pl.multiple_of(lax.axis_index("img") * owned, owned)
    copies = [
        pltpu.make_async_copy(defocus_hbm, defocus_ref, arrived.at[0]),
        pltpu.make_async_copy(plane_hbm, plane_ref, arrived.at[1]),
        pltpu.make_async_copy(rows_hbm.at[:, pl.ds(first, owned), :], rows_ref, arrived.at[2]),
        pltpu.make_async_copy(cols_hbm, cols_ref, arrived.at[3]),
    ]
    for copy in copies:
        copy.start()
    for copy in copies:
        copy.wait()
    share_plane = iota((planes * CLASSES, poses * bins), 0) // CLASSES
    share_pose = iota((planes * CLASSES, poses * bins), 1) // bins
    share = jnp.zeros((planes * CLASSES, poses * bins), f32)
    for p in range(poses):
        for z in range(planes):
            share = jnp.where((share_plane == z) & (share_pose == p), plane_ref[z, p], share)
    share_ref[...] = share

    bin_row = iota((bins, box), 0)
    sub_defocus = jnp.zeros((bins, box), f32)
    for b in range(bins):
        sub_defocus = jnp.where(bin_row == b, defocus_ref[b], sub_defocus)
    freq = iota((bins, box), 1)
    freq = jnp.where(freq < half, freq, box - freq).astype(f32)
    turns_x = sub_defocus * (freq * freq * (1.0 / (half * half)))
    turns_y = turns_x + ctf_phase / math.pi
    ones = jnp.ones((bins, box), f32)
    wave_y = jnp.concatenate(
        [0.5 * ones, -0.5 * turns_sine(turns_y + 0.25), 0.5 * turns_sine(turns_y)], 0
    )
    wave_x = jnp.concatenate([ones, turns_sine(turns_x + 0.25), turns_sine(turns_x)], 0)
    y_high, y_low = split_two(wave_y)
    x_high, x_low = split_two(wave_x)
    rows_sq = rows_ref[...].reshape(poses * owned, box).astype(f32)
    rows_sq = (rows_sq * rows_sq).astype(bf16)
    u = dot(y_high, rows_sq, ((1,), (1,))) + dot(y_low, rows_sq, ((1,), (1,)))
    for p in range(poses):
        cols_sq = cols_ref[p].astype(f32)
        cols_sq = (cols_sq * cols_sq).astype(bf16)
        v = dot(x_high, cols_sq) + dot(x_low, cols_sq)
        for r in range(owned):
            column = u[:, p * owned + r : p * owned + r + 1]
            product = v * column
            weight = product[:bins] + product[bins : 2 * bins] + product[2 * bins :]
            high, low = split_two(weight)
            high_ref[p * bins : (p + 1) * bins, r * cols : (r + 1) * cols] = high
            low_ref[p * bins : (p + 1) * bins, r * cols : (r + 1) * cols] = low


def own_ridges(defocus, plane_weight, rows_table, cols_table, owned):
    poses, _, box = rows_table.shape
    cols = cols_table.shape[2]
    bins = defocus.shape[0]
    any_place = pl.BlockSpec(memory_space=pl.ANY)
    vmem = pl.BlockSpec(memory_space=pltpu.VMEM)
    planes = plane_weight.T
    table = pltpu.VMEM((poses * bins, owned * cols), bf16)
    return pl.pallas_call(
        ridge_kernel,
        out_shape=[table, table, pltpu.VMEM((planes.shape[0] * CLASSES, poses * bins), f32)],
        in_specs=[any_place] * 4,
        out_specs=[vmem] * 3,
        scratch_shapes=[
            pltpu.SMEM(defocus.shape, f32),
            pltpu.SMEM(planes.shape, f32),
            pltpu.VMEM((poses, owned, box), bf16),
            pltpu.VMEM(cols_table.shape, bf16),
            pltpu.SemaphoreType.DMA((4,)),
        ],
        compiler_params=pltpu.CompilerParams(vmem_limit_bytes=VMEM_LIMIT),
        cost_estimate=pl.CostEstimate(
            flops=1000, bytes_accessed=1000, transcendentals=0
        ),
    )(defocus, planes, rows_table, cols_table)


def call_in_vmem(kernel, arrays, out_shape):
    vmem = pl.BlockSpec(memory_space=pltpu.VMEM)
    return pl.pallas_call(
        kernel,
        out_shape=out_shape,
        in_specs=[vmem] * len(arrays),
        out_specs=[vmem] * len(out_shape),
        compiler_params=pltpu.CompilerParams(vmem_limit_bytes=16 * 1024 * 1024),
        cost_estimate=pl.CostEstimate(flops=1000, bytes_accessed=1000, transcendentals=0),
    )(*arrays)


def fold_kernel(x_keep, x_came, own_send, z_keep, *refs):
    z_came, refs = refs[: len(LINE)], refs[len(LINE) :]
    x_sends, own_out, z_own, z_send = refs[: len(LINE)], *refs[len(LINE) :]
    for n, send in enumerate(x_sends):
        send[...] = (x_keep[n] + x_came[n].astype(f32)).astype(bf16)
    own_out[...] = own_send[...]
    for n in range(z_keep.shape[0]):
        value = z_keep[n]
        for came in z_came:
            value = value + came[n].astype(f32)
        if n < Z_SLOTS:
            z_own[n] = value
        if n == 0:
            z_send[n] = value.astype(bf16)
        elif n >= Z_SLOTS:
            z_send[n - Z_SLOTS + 1] = value.astype(bf16)


def fold_phase(x_keep, x_came, own_send, z_keep, z_came):
    piece = own_send.shape
    z_piece = (Z_SLOTS,) + piece[1:]
    out_shape = [pltpu.VMEM(piece, bf16)] * (len(LINE) + 1)
    out_shape += [pltpu.VMEM(z_piece, f32), pltpu.VMEM(z_piece, bf16)]
    return call_in_vmem(fold_kernel, (x_keep, x_came, own_send, z_keep, *z_came), out_shape)


def weight_kernel(high_ref, low_ref, share_ref, z_own, z_came, out_ref, ridge_ref):
    slots, pairs = share_ref.shape
    owned, _, cols = ridge_ref.shape
    counts = z_own[0] + z_came[0].astype(f32)
    scaled = jnp.concatenate([counts[:CLASSES, :pairs]] * (slots // CLASSES), 0) * share_ref[...]
    c_high, c_low = split_two(scaled)
    weight = (
        dot(c_high, high_ref[...]) + dot(c_low, high_ref[...]) + dot(c_high, low_ref[...])
    )
    ridge = 1.0 / (weight + wiener_ridge)
    for r in range(owned):
        ridge_ref[r] = ridge[:, r * cols : (r + 1) * cols]
    for s in range(slots):
        out_ref[s] = ridge_ref[:, s, :]


def own_weights(tables, z_own, z_came):
    slots = tables[2].shape[0]
    _, owned, wide = z_own.shape
    cols = wide // 2
    vmem = pl.BlockSpec(memory_space=pltpu.VMEM)
    return pl.pallas_call(
        weight_kernel,
        out_shape=pltpu.VMEM((slots, owned, cols), f32),
        in_specs=[vmem] * 5,
        out_specs=vmem,
        scratch_shapes=[pltpu.VMEM((owned, slots, cols), f32)],
        compiler_params=pltpu.CompilerParams(vmem_limit_bytes=16 * 1024 * 1024),
        cost_estimate=pl.CostEstimate(flops=1000, bytes_accessed=1000, transcendentals=0),
    )(*tables, z_own, z_came)


def finish_kernel(planes, ridge_ref, x_own, z_own, z_came, *refs):
    x_came, out_ref = refs[:-1], refs[-1]
    slots, owned, cols = ridge_ref.shape
    first = z_own.shape[0]
    for s in range(slots):
        if s + 1 < first:
            value = z_own[s + 1] + z_came[s + 1].astype(f32)
        else:
            value = x_own[s + 1 - first]
            for part in x_came:
                value = value + part[s + 1 - first].astype(f32)
        factor = ridge_ref[s]
        place = (s % CLASSES) * planes + s // CLASSES
        out_ref[:, 2 * place, :] = value[:, :cols] * factor
        out_ref[:, 2 * place + 1, :] = value[:, cols:] * factor


def finish(planes, ridge, x_own, z_own, z_came, x_came):
    slots, owned, cols = ridge.shape
    vmem = pl.BlockSpec(memory_space=pltpu.VMEM)
    return pl.pallas_call(
        functools.partial(finish_kernel, planes),
        out_shape=jax.ShapeDtypeStruct((owned, 2 * slots, cols), f32),
        in_specs=[vmem] * (4 + len(x_came)),
        out_specs=vmem,
        compiler_params=pltpu.CompilerParams(vmem_limit_bytes=16 * 1024 * 1024),
        cost_estimate=pl.CostEstimate(flops=1000, bytes_accessed=1000, transcendentals=0),
    )(ridge, x_own, z_own, z_came, *x_came)


def squared_table(weight_table):
    wide_table = weight_table.astype(f32)
    return (wide_table * wide_table).astype(bf16)


def weight_totals(class_index, pose_index, defocus_bin, defocus, rows_table, cols_table, plane_weight, first_row, owned):
    box = rows_table.shape[2]
    poses = rows_table.shape[0]
    bins = defocus.shape[0]
    half = box // 2
    exact = lax.Precision.HIGHEST
    code = (class_index[:, 0] * poses + pose_index) * bins + defocus_bin
    codes = lax.all_gather(code, "img", tiled=True)
    hits = (codes[:, None] == jnp.arange(CLASSES * poses * bins, dtype=jnp.int32)).astype(f32)
    counts = jnp.sum(hits, 0).reshape(CLASSES, poses, bins)
    place = jnp.arange(box, dtype=jnp.int32)
    freq = jnp.where(place < half, place, place - box).astype(f32)
    turns = defocus[:, None] * (freq * freq)[None, :] * (1.0 / (half * half))
    turns_y = turns + ctf_phase / math.pi
    ones = jnp.ones_like(turns)
    wave_y = jnp.stack([0.5 * ones, -0.5 * turns_sine(turns_y + 0.25), 0.5 * turns_sine(turns_y)])
    wave_x = jnp.stack([ones, turns_sine(turns + 0.25), turns_sine(turns)])
    rows_own = lax.dynamic_slice_in_dim(rows_table, first_row, owned, 1)
    u = jnp.einsum("pry,mby->pmbr", squared_table(rows_own).astype(f32), wave_y, precision=exact)
    v = jnp.einsum("pxj,mbx->pmbj", squared_table(cols_table).astype(f32), wave_x, precision=exact)
    weight = counts[:, None] * plane_weight.T[None, :, :, None]
    left = weight[:, :, :, None, :, None] * u[None, None]
    return jnp.einsum("czpmbr,pmbj->rczj", left, v, precision=exact)


def by_pairs(images, class_index, pose_index, defocus_bin, defocus, rows_table, cols_table, plane_weight):
    members = lax.axis_size("img")
    rows = rows_table.shape[1]
    planes = plane_weight.shape[1]
    cols = cols_table.shape[2]
    owned = rows // members

    def exchange(value, flip):
        return lax.ppermute(value, "img", [(i, i ^ flip) for i in range(members)])

    x_send, x_keep, own_send, own_keep, z_keep, *z_sends = own_totals(
        images, class_index, pose_index, defocus_bin, defocus, rows_table, cols_table, plane_weight, members
    )
    x_came = exchange(x_send, 1)
    z_came = [exchange(send, 2 * k) for send, k in zip(z_sends, LINE)]
    tables = own_ridges(defocus, plane_weight, rows_table, cols_table, owned)
    x_keep, tables = lax.optimization_barrier((x_keep, tables))
    *x_sends, own_send, z_own, z_send = fold_phase(x_keep, x_came, own_send, z_keep, z_came)
    x_came = [exchange(send, 2 * k) for send, k in zip(x_sends, LINE)]
    own_came = exchange(own_send, 1)
    z_came = exchange(z_send, 1)
    ridge = own_weights(tables, z_own, z_came)
    out = finish(planes, ridge, own_keep, z_own, z_came, (*x_came, own_came))
    return out.reshape(owned, CLASSES, planes, 2, cols)


def by_scatter(images, class_index, pose_index, defocus_bin, defocus, rows_table, cols_table, plane_weight):
    rows = rows_table.shape[1]
    cols = cols_table.shape[2]
    planes = plane_weight.shape[1]
    members = lax.axis_size("img")
    owned = rows // members
    (totals,) = own_totals(
        images, class_index, pose_index, defocus_bin, defocus, rows_table, cols_table, plane_weight, 1
    )
    slots = totals.shape[0]
    totals = totals.reshape(slots, members, owned, 2 * cols).transpose(1, 0, 2, 3)
    own = lax.psum_scatter(totals, "img", scatter_dimension=0, tiled=False)
    weight = weight_totals(
        class_index, pose_index, defocus_bin, defocus, rows_table, cols_table, plane_weight,
        lax.axis_index("img") * owned, owned,
    )
    own = own.astype(f32).reshape(planes, CLASSES, owned, 2, cols).transpose(2, 1, 0, 3, 4)
    return own / (weight[:, :, :, None, :] + wiener_ridge)


def body(*arrays):
    rows = arrays[5].shape[1]
    members = lax.axis_size("img")
    images = members * arrays[0].shape[0]
    paired = members == 8 and images <= 256 and rows % (16 * members) == 0
    return (by_pairs if paired else by_scatter)(*arrays)


def solution(mesh):
    placed = (
        P(("groups", "img"), None, None),
        P(("groups", "img"), None),
        P(("groups", "img")),
        P(("groups", "img")),
        P(),
        P(),
        P(None, None, "slab"),
        P(),
    )
    return jax.shard_map(
        body,
        mesh=mesh,
        in_specs=placed,
        out_specs=P("img", "groups", None, None, "slab"),
        check_vma=False,
    )
```

```python
import functools
import math

import jax
import jax.numpy as jnp
import numpy as np
from jax import lax
from jax.experimental import pallas as pl
from jax.experimental.pallas import tpu as pltpu
from jax.sharding import PartitionSpec as P

CLASSES = 8

wiener_ridge = 1.0
ctf_phase = 0.1
f32 = jnp.float32
bf16 = jnp.bfloat16


def packed_dft(box, sine_sign):
    half = box // 2
    k = np.concatenate([np.arange(half), [half], np.arange(1, half)])
    angle = (k[:, None] * np.arange(box)[None, :] % box) * (2.0 * math.pi / box)
    table = np.where((np.arange(box) <= half)[:, None], np.cos(angle), sine_sign * np.sin(angle))
    return (table / math.sqrt(box)).astype(np.float32)


def iota(shape, axis):
    return lax.broadcasted_iota(jnp.int32, shape, axis)


def dot(a, b, dims=((1,), (0,))):
    return lax.dot_general(a, b, (dims, ((), ())), preferred_element_type=f32)


def turns_sine(turns):
    return jnp.sin((turns - jnp.round(turns)) * (2.0 * math.pi))


def split_two(value):
    high = value.astype(bf16)
    return high, (value - high.astype(f32)).astype(bf16)


def fold_of(place, half):
    box = 2 * half
    return jnp.where(place <= half, place, box + half - place)


def slices_kernel(
    class_hbm, pose_hbm, bin_hbm, defocus_hbm, plane_hbm,
    dft_hbm, dft_t_hbm, images_hbm, rows_hbm, cols_hbm,
    *refs,
):
    outs, refs = refs[:-SCRATCH], refs[-SCRATCH:]
    (
        class_ref, pose_ref, bin_ref, defocus_ref, plane_ref,
        dft_ref, dft_t_ref, images_ref, rows_ref, cols_ref, arrived,
        rows_fold, cols_fold, wave_y, cos_x, sin_x, half_ref, spec_ref, mix_ref, totals,
    ) = refs
    count, box, _ = images_ref.shape
    half = box // 2
    poses, rows, _ = rows_ref.shape
    cols = cols_ref.shape[2]
    planes = plane_ref.shape[0]

    pairs = (
        (class_hbm, class_ref), (pose_hbm, pose_ref), (bin_hbm, bin_ref),
        (defocus_hbm, defocus_ref), (plane_hbm, plane_ref),
        (dft_hbm, dft_ref), (images_hbm.at[0:GROUP], images_ref.at[0:GROUP]),
        (dft_t_hbm, dft_t_ref), (cols_hbm, cols_ref), (rows_hbm, rows_ref),
    ) + tuple(
        (images_hbm.at[i : i + GROUP], images_ref.at[i : i + GROUP])
        for i in range(GROUP, count, GROUP)
    )
    copies = [
        pltpu.make_async_copy(source, target, arrived.at[n])
        for n, (source, target) in enumerate(pairs)
    ]
    for copy in copies:
        copy.start()

    place = iota((box, box), 0)
    other = iota((box, box), 1)
    folded = fold_of(place, half)
    near = (folded == other).astype(f32).astype(bf16)
    far = (jnp.where(folded == 0, 0, box - folded) == other).astype(f32).astype(bf16)

    for copy in copies[:5]:
        copy.wait()
    tall, lanes = wave_y.shape
    lane = iota((1, lanes), 1)
    sub = iota((count, box), 0)
    lane_defocus = jnp.zeros((1, lanes), f32)
    sub_defocus = jnp.zeros((count, box), f32)
    for i in range(count):
        value = defocus_ref[bin_ref[i]]
        lane_defocus = jnp.where(lane % count == i, value, lane_defocus)
        sub_defocus = jnp.where(sub == i, value, sub_defocus)
    scale = 1.0 / (2 * half * half)
    ky = iota((tall, lanes), 0).astype(f32)
    quarter = jnp.where(lane < count, 0.0, 0.25) + ctf_phase / (2.0 * math.pi)
    wave_y[...] = turns_sine(lane_defocus * (ky * ky * scale) + quarter)
    kx = iota((count, box), 1)
    kx = jnp.where(kx <= half, kx, kx - half).astype(f32)
    turns = sub_defocus * (kx * kx * scale)
    cos_x[...] = -turns_sine(turns + 0.25)
    sin_x[...] = -turns_sine(turns)
    totals[...] = jnp.zeros_like(totals)
    leading = 1 if len(outs) > 1 else 0
    if len(outs) > 1:
        bins = defocus_ref.shape[0]
        count_row = iota((16, 2 * cols), 0)
        count_lane = iota((16, 2 * cols), 1)
        counts = jnp.zeros((16, 2 * cols), f32)
        for i in range(count):
            hit = (count_row == class_ref[i]) & (count_lane == pose_ref[i] * bins + bin_ref[i])
            counts = counts + jnp.where(hit, 1.0, 0.0)
        totals[0] = jnp.tile(counts, (rows // 16, 1))

    tile = 8
    tile_row = iota((tile, half), 0) == 0
    tile_col = iota((tile, half), 1) == 0
    col_zero = iota((half, half), 1) == 0
    short_row = iota((16, half), 0) == 0
    short_col = iota((16, half), 1) == 0

    def without_row(value):
        return jnp.concatenate([jnp.where(tile_row, 0.0, value[:tile]), value[tile:]], 0)

    def along_rows(i):
        copies[6 if i == 0 else 9 + i // GROUP].wait()
        group = jnp.concatenate([images_ref[i + n] for n in range(GROUP)], 1)
        product = dot(dft_ref[...], group).astype(bf16)
        for n in range(GROUP):
            half_ref[i // GROUP % 2, n * box : (n + 1) * box] = product[:, n * box : (n + 1) * box]

    def along_columns(i):
        return dot(half_ref[i // GROUP % 2], dft_t_ref[...])

    def weigh(i, y):
        sin_col = jnp.broadcast_to(wave_y[:, i : i + 1], (tall, half))
        cos_col = jnp.broadcast_to(wave_y[:, count + i : count + i + 1], (tall, half))
        near_ctf = sin_col * cos_x[i : i + 1, :half] + cos_col * sin_x[i : i + 1, :half]
        far_ctf = sin_col * cos_x[i : i + 1, half:] + cos_col * sin_x[i : i + 1, half:]
        cc, cs = y[:half, :half], y[:half, half:]
        sc, ss = y[half:, :half], y[half:, half:]
        ss_row = without_row(ss)
        ss_in = jnp.where(col_zero, 0.0, ss_row)
        sc_in = without_row(sc)
        cs_in = jnp.where(col_zero, 0.0, cs)
        near_y, far_y = near_ctf[:half], far_ctf[:half]
        spec = spec_ref.at[i % SLOTS]
        spec[0:half, 0:half] = (near_y * (cc + ss_in)).astype(bf16)
        spec[0:half, half:] = (far_y * jnp.where(col_zero, cs, cc - ss_in)).astype(bf16)
        spec[half:box, 0:half] = (near_y * (sc_in - cs_in)).astype(bf16)
        spec[half:box, half:] = (far_y * jnp.where(col_zero, ss_row, sc_in + cs_in)).astype(bf16)
        sc_top = jnp.broadcast_to(sc[0:1], (16, half))
        ss_top = jnp.broadcast_to(ss[0:1], (16, half))
        ss_top_in = jnp.where(short_col, 0.0, ss_top)
        spec[box : box + 16, 0:half] = (
            near_ctf[half : half + 1] * jnp.where(short_row, sc_top, -ss_top_in)
        ).astype(bf16)
        spec[box : box + 16, half:] = (
            far_ctf[half : half + 1]
            * jnp.where(short_row, jnp.where(short_col, ss_top, sc_top), ss_top_in)
        ).astype(bf16)

    def mix(i):
        mixed = dot(spec_ref[i % SLOTS], cols_fold[pose_ref[i]])
        out = mix_ref.at[i % SLOTS]
        out[0:half, 0:cols] = mixed[:half, :cols].astype(bf16)
        out[0:half, cols:] = mixed[half:box, :cols].astype(bf16)
        top = iota((16, cols), 0) == 0
        real, imag = mixed[:half, cols:], -mixed[half:box, cols:]
        out[half : half + 16, 0:cols] = jnp.where(
            top, mixed[box : box + 1, :cols], real[:16]
        ).astype(bf16)
        out[half : half + 16, cols:] = jnp.where(
            top, mixed[box + 1 : box + 2, :cols], imag[:16]
        ).astype(bf16)
        out[half + 16 :, 0:cols] = real[16:].astype(bf16)
        out[half + 16 :, cols:] = imag[16:].astype(bf16)

    def insert(i):
        pose = pose_ref[i]
        pose_rows = rows_fold[pl.ds(pl.multiple_of(pose * rows, rows), rows), :]
        piece = dot(pose_rows, mix_ref[i % SLOTS])
        for z in range(planes):
            slot = leading + z * CLASSES + class_ref[i]
            totals[slot] += plane_ref[z, pose] * piece

    copies[5].wait()
    along_rows(0)
    copies[7].wait()
    copies[8].wait()
    for p in range(0, poses, 2):
        two = jnp.concatenate([cols_ref[p], cols_ref[p + 1]], 1)
        near_two = dot(near, two).astype(bf16)
        far_two = dot(far, two).astype(bf16)
        cols_fold[p] = jnp.concatenate([near_two[:, :cols], far_two[:, :cols]], 1)
        cols_fold[p + 1] = jnp.concatenate([near_two[:, cols:], far_two[:, cols:]], 1)
    copies[9].wait()
    rows_fold[...] = dot(
        rows_ref[...].reshape(poses * rows, box), near, ((1,), (1,))
    ).astype(bf16)
    for step in range(GROUP, count + 3 * GROUP, GROUP):
        if step < count:
            along_rows(step)
        if step - GROUP < count:
            product = along_columns(step - GROUP)
        for n in range(GROUP):
            if step - GROUP < count:
                weigh(step - GROUP + n, product[n * box : (n + 1) * box])
            if 0 <= step - 2 * GROUP < count:
                mix(step - 2 * GROUP + n)
            if step >= 3 * GROUP:
                insert(step - 3 * GROUP + n)

    if len(outs) == 1:
        outs[0][...] = totals[...].astype(bf16)
        return
    x_send, x_keep, own_send, own_keep, z_keep = outs[:5]
    z_sends = outs[5:]
    x_slots, owned, _ = own_keep.shape
    me = lax.axis_index("img")

    def rows_of(flip):
        return pl.ds(pl.multiple_of((me ^ flip) * owned, owned), owned)

    for n, k in enumerate(LINE):
        x_send[n] = totals[-x_slots:, rows_of(2 * k + 1), :].astype(bf16)
        x_keep[n] = totals[-x_slots:, rows_of(2 * k), :]
    own_send[...] = totals[-x_slots:, rows_of(1), :].astype(bf16)
    own_keep[...] = totals[-x_slots:, rows_of(0), :]
    for k, out in zip((0,) + LINE, (z_keep, *z_sends)):
        out[:Z_SLOTS] = totals[:Z_SLOTS, rows_of(2 * k), :].astype(out.dtype)
        out[Z_SLOTS:] = totals[1:Z_SLOTS, rows_of(2 * k + 1), :].astype(out.dtype)


SCRATCH = 20
LINE = (2, 3, 1)
SLOTS = 8
GROUP = 2
Z_SLOTS = 4


def own_totals(images, class_index, pose_index, defocus_bin, defocus, rows_table, cols_table, plane_weight, members):
    count, box, _ = images.shape
    poses, rows, _ = rows_table.shape
    cols = cols_table.shape[2]
    planes = plane_weight.shape[1]
    slots = CLASSES * planes
    table_y, table_x = packed_dft(box, -1.0), packed_dft(box, 1.0)
    any_place = pl.BlockSpec(memory_space=pl.ANY)
    vmem = pl.BlockSpec(memory_space=pltpu.VMEM)
    lanes = 128 * (-(-2 * count // 128))
    if members == 1:
        out_shape = [jax.ShapeDtypeStruct((slots, rows, 2 * cols), bf16)]
    else:
        slots += 1
        tail = (rows // members, 2 * cols)
        x_slots = slots - Z_SLOTS
        out_shape = []
        for lead in ((len(LINE), x_slots), (x_slots,)):
            out_shape += [pltpu.VMEM(lead + tail, bf16), pltpu.VMEM(lead + tail, f32)]
        out_shape += [pltpu.VMEM((2 * Z_SLOTS - 1,) + tail, f32)]
        out_shape += [pltpu.VMEM((2 * Z_SLOTS - 1,) + tail, bf16)] * len(LINE)
    operands = (
        class_index[:, 0], pose_index, defocus_bin, defocus, plane_weight.T,
        jnp.asarray(table_y, bf16), jnp.asarray(table_x.T.copy(), bf16),
        images, rows_table, cols_table,
    )
    return pl.pallas_call(
        slices_kernel,
        out_shape=out_shape,
        in_specs=[any_place] * 10,
        out_specs=[vmem] * len(out_shape),
        scratch_shapes=[pltpu.SMEM(x.shape, x.dtype) for x in operands[:5]]
        + [pltpu.VMEM(x.shape, x.dtype) for x in operands[5:]]
        + [
            pltpu.SemaphoreType.DMA((9 + count // GROUP,)),
            pltpu.VMEM((poses * rows, box), bf16),
            pltpu.VMEM((poses, box, 2 * cols), bf16),
            pltpu.VMEM((box // 2 + 8, lanes), f32),
            pltpu.VMEM((count, box), f32),
            pltpu.VMEM((count, box), f32),
            pltpu.VMEM((2, GROUP * box, box), bf16),
            pltpu.VMEM((SLOTS, box + 16, box), bf16),
            pltpu.VMEM((SLOTS, box, 2 * cols), bf16),
            pltpu.VMEM((slots, rows, 2 * cols), f32),
        ],
        compiler_params=pltpu.CompilerParams(vmem_limit_bytes=VMEM_LIMIT),
        cost_estimate=pl.CostEstimate(
            flops=2 * count * box * box * 1000, bytes_accessed=6 * 1024 * 1024, transcendentals=0
        ),
    )(*operands)


VMEM_LIMIT = 56 * 1024 * 1024


def ridge_kernel(defocus_hbm, plane_hbm, rows_hbm, cols_hbm, high_ref, low_ref, share_ref, *refs):
    defocus_ref, plane_ref, rows_ref, cols_ref, arrived = refs
    poses, owned, box = rows_ref.shape
    cols = cols_ref.shape[2]
    bins = defocus_ref.shape[0]
    planes = plane_ref.shape[0]
    half = box // 2
    first = pl.multiple_of(lax.axis_index("img") * owned, owned)
    copies = [
        pltpu.make_async_copy(defocus_hbm, defocus_ref, arrived.at[0]),
        pltpu.make_async_copy(plane_hbm, plane_ref, arrived.at[1]),
        pltpu.make_async_copy(rows_hbm.at[:, pl.ds(first, owned), :], rows_ref, arrived.at[2]),
        pltpu.make_async_copy(cols_hbm, cols_ref, arrived.at[3]),
    ]
    for copy in copies:
        copy.start()
    for copy in copies:
        copy.wait()
    share_plane = iota((planes * CLASSES, poses * bins), 0) // CLASSES
    share_pose = iota((planes * CLASSES, poses * bins), 1) // bins
    share = jnp.zeros((planes * CLASSES, poses * bins), f32)
    for p in range(poses):
        for z in range(planes):
            share = jnp.where((share_plane == z) & (share_pose == p), plane_ref[z, p], share)
    share_ref[...] = share

    bin_row = iota((bins, box), 0)
    sub_defocus = jnp.zeros((bins, box), f32)
    for b in range(bins):
        sub_defocus = jnp.where(bin_row == b, defocus_ref[b], sub_defocus)
    freq = iota((bins, box), 1)
    freq = jnp.where(freq < half, freq, box - freq).astype(f32)
    turns_x = sub_defocus * (freq * freq * (1.0 / (half * half)))
    turns_y = turns_x + ctf_phase / math.pi
    ones = jnp.ones((bins, box), f32)
    wave_y = jnp.concatenate(
        [0.5 * ones, -0.5 * turns_sine(turns_y + 0.25), 0.5 * turns_sine(turns_y)], 0
    )
    wave_x = jnp.concatenate([ones, turns_sine(turns_x + 0.25), turns_sine(turns_x)], 0)
    y_high, y_low = split_two(wave_y)
    x_high, x_low = split_two(wave_x)
    rows_sq = rows_ref[...].reshape(poses * owned, box).astype(f32)
    rows_sq = (rows_sq * rows_sq).astype(bf16)
    u = dot(y_high, rows_sq, ((1,), (1,))) + dot(y_low, rows_sq, ((1,), (1,)))
    for p in range(poses):
        cols_sq = cols_ref[p].astype(f32)
        cols_sq = (cols_sq * cols_sq).astype(bf16)
        v = dot(x_high, cols_sq) + dot(x_low, cols_sq)
        for r in range(owned):
            column = u[:, p * owned + r : p * owned + r + 1]
            product = v * column
            weight = product[:bins] + product[bins : 2 * bins] + product[2 * bins :]
            high, low = split_two(weight)
            high_ref[p * bins : (p + 1) * bins, r * cols : (r + 1) * cols] = high
            low_ref[p * bins : (p + 1) * bins, r * cols : (r + 1) * cols] = low


def own_ridges(defocus, plane_weight, rows_table, cols_table, owned):
    poses, _, box = rows_table.shape
    cols = cols_table.shape[2]
    bins = defocus.shape[0]
    any_place = pl.BlockSpec(memory_space=pl.ANY)
    vmem = pl.BlockSpec(memory_space=pltpu.VMEM)
    planes = plane_weight.T
    table = pltpu.VMEM((poses * bins, owned * cols), bf16)
    return pl.pallas_call(
        ridge_kernel,
        out_shape=[table, table, pltpu.VMEM((planes.shape[0] * CLASSES, poses * bins), f32)],
        in_specs=[any_place] * 4,
        out_specs=[vmem] * 3,
        scratch_shapes=[
            pltpu.SMEM(defocus.shape, f32),
            pltpu.SMEM(planes.shape, f32),
            pltpu.VMEM((poses, owned, box), bf16),
            pltpu.VMEM(cols_table.shape, bf16),
            pltpu.SemaphoreType.DMA((4,)),
        ],
        compiler_params=pltpu.CompilerParams(vmem_limit_bytes=VMEM_LIMIT),
        cost_estimate=pl.CostEstimate(
            flops=1000, bytes_accessed=1000, transcendentals=0
        ),
    )(defocus, planes, rows_table, cols_table)


def call_in_vmem(kernel, arrays, out_shape):
    vmem = pl.BlockSpec(memory_space=pltpu.VMEM)
    return pl.pallas_call(
        kernel,
        out_shape=out_shape,
        in_specs=[vmem] * len(arrays),
        out_specs=[vmem] * len(out_shape),
        compiler_params=pltpu.CompilerParams(vmem_limit_bytes=16 * 1024 * 1024),
        cost_estimate=pl.CostEstimate(flops=1000, bytes_accessed=1000, transcendentals=0),
    )(*arrays)


def fold_kernel(x_keep, x_came, own_send, z_keep, *refs):
    z_came, refs = refs[: len(LINE)], refs[len(LINE) :]
    x_sends, own_out, z_own, z_send = refs[: len(LINE)], *refs[len(LINE) :]
    for n, send in enumerate(x_sends):
        send[...] = (x_keep[n] + x_came[n].astype(f32)).astype(bf16)
    own_out[...] = own_send[...]
    for n in range(z_keep.shape[0]):
        value = z_keep[n]
        for came in z_came:
            value = value + came[n].astype(f32)
        if n < Z_SLOTS:
            z_own[n] = value
        if n == 0:
            z_send[n] = value.astype(bf16)
        elif n >= Z_SLOTS:
            z_send[n - Z_SLOTS + 1] = value.astype(bf16)


def fold_phase(x_keep, x_came, own_send, z_keep, z_came):
    piece = own_send.shape
    z_piece = (Z_SLOTS,) + piece[1:]
    out_shape = [pltpu.VMEM(piece, bf16)] * (len(LINE) + 1)
    out_shape += [pltpu.VMEM(z_piece, f32), pltpu.VMEM(z_piece, bf16)]
    return call_in_vmem(fold_kernel, (x_keep, x_came, own_send, z_keep, *z_came), out_shape)


def weight_kernel(high_ref, low_ref, share_ref, z_own, z_came, out_ref, ridge_ref):
    slots, pairs = share_ref.shape
    owned, _, cols = ridge_ref.shape
    counts = z_own[0] + z_came[0].astype(f32)
    scaled = jnp.concatenate([counts[:CLASSES, :pairs]] * (slots // CLASSES), 0) * share_ref[...]
    c_high, c_low = split_two(scaled)
    weight = (
        dot(c_high, high_ref[...]) + dot(c_low, high_ref[...]) + dot(c_high, low_ref[...])
    )
    ridge = 1.0 / (weight + wiener_ridge)
    for r in range(owned):
        ridge_ref[r] = ridge[:, r * cols : (r + 1) * cols]
    for s in range(slots):
        out_ref[s] = ridge_ref[:, s, :]


def own_weights(tables, z_own, z_came):
    slots = tables[2].shape[0]
    _, owned, wide = z_own.shape
    cols = wide // 2
    vmem = pl.BlockSpec(memory_space=pltpu.VMEM)
    return pl.pallas_call(
        weight_kernel,
        out_shape=pltpu.VMEM((slots, owned, cols), f32),
        in_specs=[vmem] * 5,
        out_specs=vmem,
        scratch_shapes=[pltpu.VMEM((owned, slots, cols), f32)],
        compiler_params=pltpu.CompilerParams(vmem_limit_bytes=16 * 1024 * 1024),
        cost_estimate=pl.CostEstimate(flops=1000, bytes_accessed=1000, transcendentals=0),
    )(*tables, z_own, z_came)


def finish_kernel(planes, ridge_ref, x_own, z_own, z_came, *refs):
    x_came, out_ref = refs[:-1], refs[-1]
    slots, owned, cols = ridge_ref.shape
    first = z_own.shape[0]
    for s in range(slots):
        if s + 1 < first:
            value = z_own[s + 1] + z_came[s + 1].astype(f32)
        else:
            value = x_own[s + 1 - first]
            for part in x_came:
                value = value + part[s + 1 - first].astype(f32)
        factor = ridge_ref[s]
        place = (s % CLASSES) * planes + s // CLASSES
        out_ref[:, 2 * place, :] = value[:, :cols] * factor
        out_ref[:, 2 * place + 1, :] = value[:, cols:] * factor


def finish(planes, ridge, x_own, z_own, z_came, x_came):
    slots, owned, cols = ridge.shape
    vmem = pl.BlockSpec(memory_space=pltpu.VMEM)
    return pl.pallas_call(
        functools.partial(finish_kernel, planes),
        out_shape=jax.ShapeDtypeStruct((owned, 2 * slots, cols), f32),
        in_specs=[vmem] * (4 + len(x_came)),
        out_specs=vmem,
        compiler_params=pltpu.CompilerParams(vmem_limit_bytes=16 * 1024 * 1024),
        cost_estimate=pl.CostEstimate(flops=1000, bytes_accessed=1000, transcendentals=0),
    )(ridge, x_own, z_own, z_came, *x_came)


def squared_table(weight_table):
    wide_table = weight_table.astype(f32)
    return (wide_table * wide_table).astype(bf16)


def weight_totals(class_index, pose_index, defocus_bin, defocus, rows_table, cols_table, plane_weight, first_row, owned):
    box = rows_table.shape[2]
    poses = rows_table.shape[0]
    bins = defocus.shape[0]
    half = box // 2
    exact = lax.Precision.HIGHEST
    code = (class_index[:, 0] * poses + pose_index) * bins + defocus_bin
    codes = lax.all_gather(code, "img", tiled=True)
    hits = (codes[:, None] == jnp.arange(CLASSES * poses * bins, dtype=jnp.int32)).astype(f32)
    counts = jnp.sum(hits, 0).reshape(CLASSES, poses, bins)
    place = jnp.arange(box, dtype=jnp.int32)
    freq = jnp.where(place < half, place, place - box).astype(f32)
    turns = defocus[:, None] * (freq * freq)[None, :] * (1.0 / (half * half))
    turns_y = turns + ctf_phase / math.pi
    ones = jnp.ones_like(turns)
    wave_y = jnp.stack([0.5 * ones, -0.5 * turns_sine(turns_y + 0.25), 0.5 * turns_sine(turns_y)])
    wave_x = jnp.stack([ones, turns_sine(turns + 0.25), turns_sine(turns)])
    rows_own = lax.dynamic_slice_in_dim(rows_table, first_row, owned, 1)
    u = jnp.einsum("pry,mby->pmbr", squared_table(rows_own).astype(f32), wave_y, precision=exact)
    v = jnp.einsum("pxj,mbx->pmbj", squared_table(cols_table).astype(f32), wave_x, precision=exact)
    weight = counts[:, None] * plane_weight.T[None, :, :, None]
    left = weight[:, :, :, None, :, None] * u[None, None]
    return jnp.einsum("czpmbr,pmbj->rczj", left, v, precision=exact)


def by_pairs(images, class_index, pose_index, defocus_bin, defocus, rows_table, cols_table, plane_weight):
    members = lax.axis_size("img")
    rows = rows_table.shape[1]
    planes = plane_weight.shape[1]
    cols = cols_table.shape[2]
    owned = rows // members

    def exchange(value, flip):
        return lax.ppermute(value, "img", [(i, i ^ flip) for i in range(members)])

    x_send, x_keep, own_send, own_keep, z_keep, *z_sends = own_totals(
        images, class_index, pose_index, defocus_bin, defocus, rows_table, cols_table, plane_weight, members
    )
    x_came = exchange(x_send, 1)
    z_came = [exchange(send, 2 * k) for send, k in zip(z_sends, LINE)]
    tables = own_ridges(defocus, plane_weight, rows_table, cols_table, owned)
    x_keep, tables = lax.optimization_barrier((x_keep, tables))
    *x_sends, own_send, z_own, z_send = fold_phase(x_keep, x_came, own_send, z_keep, z_came)
    x_came = [exchange(send, 2 * k) for send, k in zip(x_sends, LINE)]
    own_came = exchange(own_send, 1)
    z_came = exchange(z_send, 1)
    ridge = own_weights(tables, z_own, z_came)
    out = finish(planes, ridge, own_keep, z_own, z_came, (*x_came, own_came))
    return out.reshape(owned, CLASSES, planes, 2, cols)


def by_scatter(images, class_index, pose_index, defocus_bin, defocus, rows_table, cols_table, plane_weight):
    rows = rows_table.shape[1]
    cols = cols_table.shape[2]
    planes = plane_weight.shape[1]
    members = lax.axis_size("img")
    owned = rows // members
    (totals,) = own_totals(
        images, class_index, pose_index, defocus_bin, defocus, rows_table, cols_table, plane_weight, 1
    )
    slots = totals.shape[0]
    totals = totals.reshape(slots, members, owned, 2 * cols).transpose(1, 0, 2, 3)
    own = lax.psum_scatter(totals, "img", scatter_dimension=0, tiled=False)
    weight = weight_totals(
        class_index, pose_index, defocus_bin, defocus, rows_table, cols_table, plane_weight,
        lax.axis_index("img") * owned, owned,
    )
    own = own.astype(f32).reshape(planes, CLASSES, owned, 2, cols).transpose(2, 1, 0, 3, 4)
    return own / (weight[:, :, :, None, :] + wiener_ridge)


def body(*arrays):
    rows = arrays[5].shape[1]
    members = lax.axis_size("img")
    images = members * arrays[0].shape[0]
    paired = members == 8 and images <= 256 and rows % (16 * members) == 0
    return (by_pairs if paired else by_scatter)(*arrays)


def solution(mesh):
    placed = (
        P(("groups", "img"), None, None),
        P(("groups", "img"), None),
        P(("groups", "img")),
        P(("groups", "img")),
        P(),
        P(),
        P(None, None, "slab"),
        P(),
    )
    return jax.shard_map(
        body,
        mesh=mesh,
        in_specs=placed,
        out_specs=P("img", "groups", None, None, "slab"),
        check_vma=False,
    )
```

```python
import functools
import math

import jax
import jax.numpy as jnp
import numpy as np
from jax import lax
from jax.experimental import pallas as pl
from jax.experimental.pallas import tpu as pltpu
from jax.sharding import PartitionSpec as P

CLASSES = 8

wiener_ridge = 1.0
ctf_phase = 0.1
f32 = jnp.float32
bf16 = jnp.bfloat16


def packed_dft(box, sine_sign):
    half = box // 2
    k = np.concatenate([np.arange(half), [half], np.arange(1, half)])
    angle = (k[:, None] * np.arange(box)[None, :] % box) * (2.0 * math.pi / box)
    table = np.where((np.arange(box) <= half)[:, None], np.cos(angle), sine_sign * np.sin(angle))
    return (table / math.sqrt(box)).astype(np.float32)


def iota(shape, axis):
    return lax.broadcasted_iota(jnp.int32, shape, axis)


def dot(a, b, dims=((1,), (0,))):
    return lax.dot_general(a, b, (dims, ((), ())), preferred_element_type=f32)


def turns_sine(turns):
    return jnp.sin((turns - jnp.round(turns)) * (2.0 * math.pi))


def split_two(value):
    high = value.astype(bf16)
    return high, (value - high.astype(f32)).astype(bf16)


def fold_of(place, half):
    box = 2 * half
    return jnp.where(place <= half, place, box + half - place)


def slices_kernel(
    class_hbm, pose_hbm, bin_hbm, defocus_hbm, plane_hbm,
    dft_hbm, dft_t_hbm, images_hbm, rows_hbm, cols_hbm,
    *refs,
):
    outs, refs = refs[:-SCRATCH], refs[-SCRATCH:]
    (
        class_ref, pose_ref, bin_ref, defocus_ref, plane_ref,
        dft_ref, dft_t_ref, images_ref, rows_ref, cols_ref, arrived,
        rows_fold, cols_fold, wave_y, cos_x, sin_x, half_ref, spec_ref, mix_ref, totals,
    ) = refs
    count, box, _ = images_ref.shape
    half = box // 2
    poses, rows, _ = rows_ref.shape
    cols = cols_ref.shape[2]
    planes = plane_ref.shape[0]

    pairs = (
        (class_hbm, class_ref), (pose_hbm, pose_ref), (bin_hbm, bin_ref),
        (defocus_hbm, defocus_ref), (plane_hbm, plane_ref),
        (dft_hbm, dft_ref), (images_hbm.at[0:GROUP], images_ref.at[0:GROUP]),
        (dft_t_hbm, dft_t_ref), (cols_hbm, cols_ref), (rows_hbm, rows_ref),
    ) + tuple(
        (images_hbm.at[i : i + GROUP], images_ref.at[i : i + GROUP])
        for i in range(GROUP, count, GROUP)
    )
    copies = [
        pltpu.make_async_copy(source, target, arrived.at[n])
        for n, (source, target) in enumerate(pairs)
    ]
    for copy in copies:
        copy.start()

    place = iota((box, box), 0)
    other = iota((box, box), 1)
    folded = fold_of(place, half)
    near = (folded == other).astype(f32).astype(bf16)
    far = (jnp.where(folded == 0, 0, box - folded) == other).astype(f32).astype(bf16)

    for copy in copies[:5]:
        copy.wait()
    tall, lanes = wave_y.shape
    lane = iota((1, lanes), 1)
    sub = iota((count, box), 0)
    lane_defocus = jnp.zeros((1, lanes), f32)
    sub_defocus = jnp.zeros((count, box), f32)
    for i in range(count):
        value = defocus_ref[bin_ref[i]]
        lane_defocus = jnp.where(lane % count == i, value, lane_defocus)
        sub_defocus = jnp.where(sub == i, value, sub_defocus)
    scale = 1.0 / (2 * half * half)
    ky = iota((tall, lanes), 0).astype(f32)
    quarter = jnp.where(lane < count, 0.0, 0.25) + ctf_phase / (2.0 * math.pi)
    wave_y[...] = turns_sine(lane_defocus * (ky * ky * scale) + quarter)
    kx = iota((count, box), 1)
    kx = jnp.where(kx <= half, kx, kx - half).astype(f32)
    turns = sub_defocus * (kx * kx * scale)
    cos_x[...] = -turns_sine(turns + 0.25)
    sin_x[...] = -turns_sine(turns)
    totals[...] = jnp.zeros_like(totals)
    leading = 1 if len(outs) > 1 else 0
    if len(outs) > 1:
        bins = defocus_ref.shape[0]
        count_row = iota((16, 2 * cols), 0)
        count_lane = iota((16, 2 * cols), 1)
        counts = jnp.zeros((16, 2 * cols), f32)
        for i in range(count):
            hit = (count_row == class_ref[i]) & (count_lane == pose_ref[i] * bins + bin_ref[i])
            counts = counts + jnp.where(hit, 1.0, 0.0)
        totals[0] = jnp.tile(counts, (rows // 16, 1))

    tile = 8
    tile_row = iota((tile, half), 0) == 0
    tile_col = iota((tile, half), 1) == 0
    col_zero = iota((half, half), 1) == 0
    short_row = iota((16, half), 0) == 0
    short_col = iota((16, half), 1) == 0

    def without_row(value):
        return jnp.concatenate([jnp.where(tile_row, 0.0, value[:tile]), value[tile:]], 0)

    def along_rows(i, wide):
        if i % GROUP == 0:
            copies[6 if i == 0 else 9 + i // GROUP].wait()
        group = jnp.concatenate([images_ref[i + n] for n in range(wide)], 1)
        product = dot(dft_ref[...], group).astype(bf16)
        for n in range(wide):
            place = (i + n) % GROUP * box
            half_ref[i // GROUP % 2, place : place + box] = product[:, n * box : (n + 1) * box]

    def along_columns(i):
        return dot(half_ref[i // GROUP % 2], dft_t_ref[...])

    def weigh(i, y):
        sin_col = jnp.broadcast_to(wave_y[:, i : i + 1], (tall, half))
        cos_col = jnp.broadcast_to(wave_y[:, count + i : count + i + 1], (tall, half))
        near_ctf = sin_col * cos_x[i : i + 1, :half] + cos_col * sin_x[i : i + 1, :half]
        far_ctf = sin_col * cos_x[i : i + 1, half:] + cos_col * sin_x[i : i + 1, half:]
        cc, cs = y[:half, :half], y[:half, half:]
        sc, ss = y[half:, :half], y[half:, half:]
        ss_row = without_row(ss)
        ss_in = jnp.where(col_zero, 0.0, ss_row)
        sc_in = without_row(sc)
        cs_in = jnp.where(col_zero, 0.0, cs)
        near_y, far_y = near_ctf[:half], far_ctf[:half]
        spec = spec_ref.at[i % SLOTS]
        spec[0:half, 0:half] = (near_y * (cc + ss_in)).astype(bf16)
        spec[0:half, half:] = (far_y * jnp.where(col_zero, cs, cc - ss_in)).astype(bf16)
        yield
        spec[half:box, 0:half] = (near_y * (sc_in - cs_in)).astype(bf16)
        spec[half:box, half:] = (far_y * jnp.where(col_zero, ss_row, sc_in + cs_in)).astype(bf16)
        sc_top = jnp.broadcast_to(sc[0:1], (16, half))
        ss_top = jnp.broadcast_to(ss[0:1], (16, half))
        ss_top_in = jnp.where(short_col, 0.0, ss_top)
        spec[box : box + 16, 0:half] = (
            near_ctf[half : half + 1] * jnp.where(short_row, sc_top, -ss_top_in)
        ).astype(bf16)
        spec[box : box + 16, half:] = (
            far_ctf[half : half + 1]
            * jnp.where(short_row, jnp.where(short_col, ss_top, sc_top), ss_top_in)
        ).astype(bf16)

    def mix(i):
        mixed = dot(spec_ref[i % SLOTS], cols_fold[pose_ref[i]])
        out = mix_ref.at[i % SLOTS]
        out[0:half, 0:cols] = mixed[:half, :cols].astype(bf16)
        out[0:half, cols:] = mixed[half:box, :cols].astype(bf16)
        top = iota((16, cols), 0) == 0
        real, imag = mixed[:half, cols:], -mixed[half:box, cols:]
        out[half : half + 16, 0:cols] = jnp.where(
            top, mixed[box : box + 1, :cols], real[:16]
        ).astype(bf16)
        out[half : half + 16, cols:] = jnp.where(
            top, mixed[box + 1 : box + 2, :cols], imag[:16]
        ).astype(bf16)
        out[half + 16 :, 0:cols] = real[16:].astype(bf16)
        out[half + 16 :, cols:] = imag[16:].astype(bf16)

    def insert(i):
        pose = pose_ref[i]
        pose_rows = rows_fold[pl.ds(pl.multiple_of(pose * rows, rows), rows), :]
        piece = dot(pose_rows, mix_ref[i % SLOTS])
        for z in range(planes):
            slot = leading + z * CLASSES + class_ref[i]
            totals[slot] += plane_ref[z, pose] * piece

    copies[5].wait()
    along_rows(0, GROUP)
    copies[7].wait()
    copies[8].wait()
    for p in range(0, poses, 2):
        two = jnp.concatenate([cols_ref[p], cols_ref[p + 1]], 1)
        near_two = dot(near, two).astype(bf16)
        far_two = dot(far, two).astype(bf16)
        cols_fold[p] = jnp.concatenate([near_two[:, :cols], far_two[:, :cols]], 1)
        cols_fold[p + 1] = jnp.concatenate([near_two[:, cols:], far_two[:, cols:]], 1)
    copies[9].wait()
    rows_fold[...] = dot(
        rows_ref[...].reshape(poses * rows, box), near, ((1,), (1,))
    ).astype(bf16)
    for step in range(GROUP, count + 3 * GROUP, GROUP):
        if step - GROUP < count:
            product = along_columns(step - GROUP)
        for n in range(GROUP):
            parts = iter(())
            if step - GROUP < count:
                parts = weigh(step - GROUP + n, product[n * box : (n + 1) * box])
            next(parts, None)
            if 0 <= step - 2 * GROUP < count:
                mix(step - 2 * GROUP + n)
            next(parts, None)
            if step >= 3 * GROUP:
                insert(step - 3 * GROUP + n)
            if step < count and n % 2 == 0:
                along_rows(step + n, 2)

    if len(outs) == 1:
        outs[0][...] = totals[...].astype(bf16)
        return
    x_send, x_keep, own_send, own_keep, z_keep = outs[:5]
    z_sends = outs[5:]
    x_slots, owned, _ = own_keep.shape
    me = lax.axis_index("img")

    def rows_of(flip):
        return pl.ds(pl.multiple_of((me ^ flip) * owned, owned), owned)

    for n, k in enumerate(LINE):
        x_send[n] = totals[-x_slots:, rows_of(2 * k + 1), :].astype(bf16)
        x_keep[n] = totals[-x_slots:, rows_of(2 * k), :]
    own_send[...] = totals[-x_slots:, rows_of(1), :].astype(bf16)
    own_keep[...] = totals[-x_slots:, rows_of(0), :]
    for k, out in zip((0,) + LINE, (z_keep, *z_sends)):
        out[:Z_SLOTS] = totals[:Z_SLOTS, rows_of(2 * k), :].astype(out.dtype)
        out[Z_SLOTS:] = totals[1:Z_SLOTS, rows_of(2 * k + 1), :].astype(out.dtype)


SCRATCH = 20
LINE = (2, 3, 1)
SLOTS = 8
GROUP = 4
Z_SLOTS = 4


def own_totals(images, class_index, pose_index, defocus_bin, defocus, rows_table, cols_table, plane_weight, members):
    count, box, _ = images.shape
    poses, rows, _ = rows_table.shape
    cols = cols_table.shape[2]
    planes = plane_weight.shape[1]
    slots = CLASSES * planes
    table_y, table_x = packed_dft(box, -1.0), packed_dft(box, 1.0)
    any_place = pl.BlockSpec(memory_space=pl.ANY)
    vmem = pl.BlockSpec(memory_space=pltpu.VMEM)
    lanes = 128 * (-(-2 * count // 128))
    if members == 1:
        out_shape = [jax.ShapeDtypeStruct((slots, rows, 2 * cols), bf16)]
    else:
        slots += 1
        tail = (rows // members, 2 * cols)
        x_slots = slots - Z_SLOTS
        out_shape = []
        for lead in ((len(LINE), x_slots), (x_slots,)):
            out_shape += [pltpu.VMEM(lead + tail, bf16), pltpu.VMEM(lead + tail, f32)]
        out_shape += [pltpu.VMEM((2 * Z_SLOTS - 1,) + tail, f32)]
        out_shape += [pltpu.VMEM((2 * Z_SLOTS - 1,) + tail, bf16)] * len(LINE)
    operands = (
        class_index[:, 0], pose_index, defocus_bin, defocus, plane_weight.T,
        jnp.asarray(table_y, bf16), jnp.asarray(table_x.T.copy(), bf16),
        images, rows_table, cols_table,
    )
    return pl.pallas_call(
        slices_kernel,
        out_shape=out_shape,
        in_specs=[any_place] * 10,
        out_specs=[vmem] * len(out_shape),
        scratch_shapes=[pltpu.SMEM(x.shape, x.dtype) for x in operands[:5]]
        + [pltpu.VMEM(x.shape, x.dtype) for x in operands[5:]]
        + [
            pltpu.SemaphoreType.DMA((9 + count // GROUP,)),
            pltpu.VMEM((poses * rows, box), bf16),
            pltpu.VMEM((poses, box, 2 * cols), bf16),
            pltpu.VMEM((box // 2 + 8, lanes), f32),
            pltpu.VMEM((count, box), f32),
            pltpu.VMEM((count, box), f32),
            pltpu.VMEM((2, GROUP * box, box), bf16),
            pltpu.VMEM((SLOTS, box + 16, box), bf16),
            pltpu.VMEM((SLOTS, box, 2 * cols), bf16),
            pltpu.VMEM((slots, rows, 2 * cols), f32),
        ],
        compiler_params=pltpu.CompilerParams(vmem_limit_bytes=VMEM_LIMIT),
        cost_estimate=pl.CostEstimate(
            flops=2 * count * box * box * 1000, bytes_accessed=6 * 1024 * 1024, transcendentals=0
        ),
    )(*operands)


VMEM_LIMIT = 56 * 1024 * 1024


def ridge_kernel(defocus_hbm, plane_hbm, rows_hbm, cols_hbm, high_ref, low_ref, share_ref, *refs):
    defocus_ref, plane_ref, rows_ref, cols_ref, arrived = refs
    poses, owned, box = rows_ref.shape
    cols = cols_ref.shape[2]
    bins = defocus_ref.shape[0]
    planes = plane_ref.shape[0]
    half = box // 2
    first = pl.multiple_of(lax.axis_index("img") * owned, owned)
    copies = [
        pltpu.make_async_copy(defocus_hbm, defocus_ref, arrived.at[0]),
        pltpu.make_async_copy(plane_hbm, plane_ref, arrived.at[1]),
        pltpu.make_async_copy(rows_hbm.at[:, pl.ds(first, owned), :], rows_ref, arrived.at[2]),
        pltpu.make_async_copy(cols_hbm, cols_ref, arrived.at[3]),
    ]
    for copy in copies:
        copy.start()
    for copy in copies:
        copy.wait()
    share_plane = iota((planes * CLASSES, poses * bins), 0) // CLASSES
    share_pose = iota((planes * CLASSES, poses * bins), 1) // bins
    share = jnp.zeros((planes * CLASSES, poses * bins), f32)
    for p in range(poses):
        for z in range(planes):
            share = jnp.where((share_plane == z) & (share_pose == p), plane_ref[z, p], share)
    share_ref[...] = share

    bin_row = iota((bins, box), 0)
    sub_defocus = jnp.zeros((bins, box), f32)
    for b in range(bins):
        sub_defocus = jnp.where(bin_row == b, defocus_ref[b], sub_defocus)
    freq = iota((bins, box), 1)
    freq = jnp.where(freq < half, freq, box - freq).astype(f32)
    turns_x = sub_defocus * (freq * freq * (1.0 / (half * half)))
    turns_y = turns_x + ctf_phase / math.pi
    ones = jnp.ones((bins, box), f32)
    wave_y = jnp.concatenate(
        [0.5 * ones, -0.5 * turns_sine(turns_y + 0.25), 0.5 * turns_sine(turns_y)], 0
    )
    wave_x = jnp.concatenate([ones, turns_sine(turns_x + 0.25), turns_sine(turns_x)], 0)
    y_high, y_low = split_two(wave_y)
    x_high, x_low = split_two(wave_x)
    rows_sq = rows_ref[...].reshape(poses * owned, box).astype(f32)
    rows_sq = (rows_sq * rows_sq).astype(bf16)
    u = dot(y_high, rows_sq, ((1,), (1,))) + dot(y_low, rows_sq, ((1,), (1,)))
    for p in range(poses):
        cols_sq = cols_ref[p].astype(f32)
        cols_sq = (cols_sq * cols_sq).astype(bf16)
        v = dot(x_high, cols_sq) + dot(x_low, cols_sq)
        for r in range(owned):
            column = u[:, p * owned + r : p * owned + r + 1]
            product = v * column
            weight = product[:bins] + product[bins : 2 * bins] + product[2 * bins :]
            high, low = split_two(weight)
            high_ref[p * bins : (p + 1) * bins, r * cols : (r + 1) * cols] = high
            low_ref[p * bins : (p + 1) * bins, r * cols : (r + 1) * cols] = low


def own_ridges(defocus, plane_weight, rows_table, cols_table, owned):
    poses, _, box = rows_table.shape
    cols = cols_table.shape[2]
    bins = defocus.shape[0]
    any_place = pl.BlockSpec(memory_space=pl.ANY)
    vmem = pl.BlockSpec(memory_space=pltpu.VMEM)
    planes = plane_weight.T
    table = pltpu.VMEM((poses * bins, owned * cols), bf16)
    return pl.pallas_call(
        ridge_kernel,
        out_shape=[table, table, pltpu.VMEM((planes.shape[0] * CLASSES, poses * bins), f32)],
        in_specs=[any_place] * 4,
        out_specs=[vmem] * 3,
        scratch_shapes=[
            pltpu.SMEM(defocus.shape, f32),
            pltpu.SMEM(planes.shape, f32),
            pltpu.VMEM((poses, owned, box), bf16),
            pltpu.VMEM(cols_table.shape, bf16),
            pltpu.SemaphoreType.DMA((4,)),
        ],
        compiler_params=pltpu.CompilerParams(vmem_limit_bytes=VMEM_LIMIT),
        cost_estimate=pl.CostEstimate(
            flops=1000, bytes_accessed=1000, transcendentals=0
        ),
    )(defocus, planes, rows_table, cols_table)


def call_in_vmem(kernel, arrays, out_shape):
    vmem = pl.BlockSpec(memory_space=pltpu.VMEM)
    return pl.pallas_call(
        kernel,
        out_shape=out_shape,
        in_specs=[vmem] * len(arrays),
        out_specs=[vmem] * len(out_shape),
        compiler_params=pltpu.CompilerParams(vmem_limit_bytes=16 * 1024 * 1024),
        cost_estimate=pl.CostEstimate(flops=1000, bytes_accessed=1000, transcendentals=0),
    )(*arrays)


def fold_kernel(x_keep, x_came, own_send, z_keep, *refs):
    z_came, refs = refs[: len(LINE)], refs[len(LINE) :]
    x_sends, own_out, z_own, z_send = refs[: len(LINE)], *refs[len(LINE) :]
    for n, send in enumerate(x_sends):
        send[...] = (x_keep[n] + x_came[n].astype(f32)).astype(bf16)
    own_out[...] = own_send[...]
    for n in range(z_keep.shape[0]):
        value = z_keep[n]
        for came in z_came:
            value = value + came[n].astype(f32)
        if n < Z_SLOTS:
            z_own[n] = value
        if n == 0:
            z_send[n] = value.astype(bf16)
        elif n >= Z_SLOTS:
            z_send[n - Z_SLOTS + 1] = value.astype(bf16)


def fold_phase(x_keep, x_came, own_send, z_keep, z_came):
    piece = own_send.shape
    z_piece = (Z_SLOTS,) + piece[1:]
    out_shape = [pltpu.VMEM(piece, bf16)] * (len(LINE) + 1)
    out_shape += [pltpu.VMEM(z_piece, f32), pltpu.VMEM(z_piece, bf16)]
    return call_in_vmem(fold_kernel, (x_keep, x_came, own_send, z_keep, *z_came), out_shape)


def weight_kernel(high_ref, low_ref, share_ref, z_own, z_came, out_ref, ridge_ref):
    slots, pairs = share_ref.shape
    owned, _, cols = ridge_ref.shape
    counts = z_own[0] + z_came[0].astype(f32)
    scaled = jnp.concatenate([counts[:CLASSES, :pairs]] * (slots // CLASSES), 0) * share_ref[...]
    c_high, c_low = split_two(scaled)
    weight = (
        dot(c_high, high_ref[...]) + dot(c_low, high_ref[...]) + dot(c_high, low_ref[...])
    )
    ridge = 1.0 / (weight + wiener_ridge)
    for r in range(owned):
        ridge_ref[r] = ridge[:, r * cols : (r + 1) * cols]
    for s in range(slots):
        out_ref[s] = ridge_ref[:, s, :]


def own_weights(tables, z_own, z_came):
    slots = tables[2].shape[0]
    _, owned, wide = z_own.shape
    cols = wide // 2
    vmem = pl.BlockSpec(memory_space=pltpu.VMEM)
    return pl.pallas_call(
        weight_kernel,
        out_shape=pltpu.VMEM((slots, owned, cols), f32),
        in_specs=[vmem] * 5,
        out_specs=vmem,
        scratch_shapes=[pltpu.VMEM((owned, slots, cols), f32)],
        compiler_params=pltpu.CompilerParams(vmem_limit_bytes=16 * 1024 * 1024),
        cost_estimate=pl.CostEstimate(flops=1000, bytes_accessed=1000, transcendentals=0),
    )(*tables, z_own, z_came)


def finish_kernel(planes, ridge_ref, x_own, z_own, z_came, *refs):
    x_came, out_ref = refs[:-1], refs[-1]
    slots, owned, cols = ridge_ref.shape
    first = z_own.shape[0]
    for s in range(slots):
        if s + 1 < first:
            value = z_own[s + 1] + z_came[s + 1].astype(f32)
        else:
            value = x_own[s + 1 - first]
            for part in x_came:
                value = value + part[s + 1 - first].astype(f32)
        factor = ridge_ref[s]
        place = (s % CLASSES) * planes + s // CLASSES
        out_ref[:, 2 * place, :] = value[:, :cols] * factor
        out_ref[:, 2 * place + 1, :] = value[:, cols:] * factor


def finish(planes, ridge, x_own, z_own, z_came, x_came):
    slots, owned, cols = ridge.shape
    vmem = pl.BlockSpec(memory_space=pltpu.VMEM)
    return pl.pallas_call(
        functools.partial(finish_kernel, planes),
        out_shape=jax.ShapeDtypeStruct((owned, 2 * slots, cols), f32),
        in_specs=[vmem] * (4 + len(x_came)),
        out_specs=vmem,
        compiler_params=pltpu.CompilerParams(vmem_limit_bytes=16 * 1024 * 1024),
        cost_estimate=pl.CostEstimate(flops=1000, bytes_accessed=1000, transcendentals=0),
    )(ridge, x_own, z_own, z_came, *x_came)


def squared_table(weight_table):
    wide_table = weight_table.astype(f32)
    return (wide_table * wide_table).astype(bf16)


def weight_totals(class_index, pose_index, defocus_bin, defocus, rows_table, cols_table, plane_weight, first_row, owned):
    box = rows_table.shape[2]
    poses = rows_table.shape[0]
    bins = defocus.shape[0]
    half = box // 2
    exact = lax.Precision.HIGHEST
    code = (class_index[:, 0] * poses + pose_index) * bins + defocus_bin
    codes = lax.all_gather(code, "img", tiled=True)
    hits = (codes[:, None] == jnp.arange(CLASSES * poses * bins, dtype=jnp.int32)).astype(f32)
    counts = jnp.sum(hits, 0).reshape(CLASSES, poses, bins)
    place = jnp.arange(box, dtype=jnp.int32)
    freq = jnp.where(place < half, place, place - box).astype(f32)
    turns = defocus[:, None] * (freq * freq)[None, :] * (1.0 / (half * half))
    turns_y = turns + ctf_phase / math.pi
    ones = jnp.ones_like(turns)
    wave_y = jnp.stack([0.5 * ones, -0.5 * turns_sine(turns_y + 0.25), 0.5 * turns_sine(turns_y)])
    wave_x = jnp.stack([ones, turns_sine(turns + 0.25), turns_sine(turns)])
    rows_own = lax.dynamic_slice_in_dim(rows_table, first_row, owned, 1)
    u = jnp.einsum("pry,mby->pmbr", squared_table(rows_own).astype(f32), wave_y, precision=exact)
    v = jnp.einsum("pxj,mbx->pmbj", squared_table(cols_table).astype(f32), wave_x, precision=exact)
    weight = counts[:, None] * plane_weight.T[None, :, :, None]
    left = weight[:, :, :, None, :, None] * u[None, None]
    return jnp.einsum("czpmbr,pmbj->rczj", left, v, precision=exact)


def by_pairs(images, class_index, pose_index, defocus_bin, defocus, rows_table, cols_table, plane_weight):
    members = lax.axis_size("img")
    rows = rows_table.shape[1]
    planes = plane_weight.shape[1]
    cols = cols_table.shape[2]
    owned = rows // members

    def exchange(value, flip):
        return lax.ppermute(value, "img", [(i, i ^ flip) for i in range(members)])

    x_send, x_keep, own_send, own_keep, z_keep, *z_sends = own_totals(
        images, class_index, pose_index, defocus_bin, defocus, rows_table, cols_table, plane_weight, members
    )
    x_came = exchange(x_send, 1)
    z_came = [exchange(send, 2 * k) for send, k in zip(z_sends, LINE)]
    tables = own_ridges(defocus, plane_weight, rows_table, cols_table, owned)
    x_keep, tables = lax.optimization_barrier((x_keep, tables))
    *x_sends, own_send, z_own, z_send = fold_phase(x_keep, x_came, own_send, z_keep, z_came)
    x_came = [exchange(send, 2 * k) for send, k in zip(x_sends, LINE)]
    own_came = exchange(own_send, 1)
    z_came = exchange(z_send, 1)
    ridge = own_weights(tables, z_own, z_came)
    out = finish(planes, ridge, own_keep, z_own, z_came, (*x_came, own_came))
    return out.reshape(owned, CLASSES, planes, 2, cols)


def by_scatter(images, class_index, pose_index, defocus_bin, defocus, rows_table, cols_table, plane_weight):
    rows = rows_table.shape[1]
    cols = cols_table.shape[2]
    planes = plane_weight.shape[1]
    members = lax.axis_size("img")
    owned = rows // members
    (totals,) = own_totals(
        images, class_index, pose_index, defocus_bin, defocus, rows_table, cols_table, plane_weight, 1
    )
    slots = totals.shape[0]
    totals = totals.reshape(slots, members, owned, 2 * cols).transpose(1, 0, 2, 3)
    own = lax.psum_scatter(totals, "img", scatter_dimension=0, tiled=False)
    weight = weight_totals(
        class_index, pose_index, defocus_bin, defocus, rows_table, cols_table, plane_weight,
        lax.axis_index("img") * owned, owned,
    )
    own = own.astype(f32).reshape(planes, CLASSES, owned, 2, cols).transpose(2, 1, 0, 3, 4)
    return own / (weight[:, :, :, None, :] + wiener_ridge)


def body(*arrays):
    rows = arrays[5].shape[1]
    members = lax.axis_size("img")
    images = members * arrays[0].shape[0]
    paired = members == 8 and images <= 256 and rows % (16 * members) == 0
    return (by_pairs if paired else by_scatter)(*arrays)


def solution(mesh):
    placed = (
        P(("groups", "img"), None, None),
        P(("groups", "img"), None),
        P(("groups", "img")),
        P(("groups", "img")),
        P(),
        P(),
        P(None, None, "slab"),
        P(),
    )
    return jax.shard_map(
        body,
        mesh=mesh,
        in_specs=placed,
        out_specs=P("img", "groups", None, None, "slab"),
        check_vma=False,
    )
```

```python
import functools
import math

import jax
import jax.numpy as jnp
import numpy as np
from jax import lax
from jax.experimental import pallas as pl
from jax.experimental.pallas import tpu as pltpu
from jax.sharding import PartitionSpec as P

CLASSES = 8

wiener_ridge = 1.0
ctf_phase = 0.1
f32 = jnp.float32
bf16 = jnp.bfloat16


def packed_dft(box, sine_sign):
    half = box // 2
    k = np.concatenate([np.arange(half), [half], np.arange(1, half)])
    angle = (k[:, None] * np.arange(box)[None, :] % box) * (2.0 * math.pi / box)
    table = np.where((np.arange(box) <= half)[:, None], np.cos(angle), sine_sign * np.sin(angle))
    return (table / math.sqrt(box)).astype(np.float32)


def iota(shape, axis):
    return lax.broadcasted_iota(jnp.int32, shape, axis)


def dot(a, b, dims=((1,), (0,))):
    return lax.dot_general(a, b, (dims, ((), ())), preferred_element_type=f32)


def turns_sine(turns):
    return jnp.sin((turns - jnp.round(turns)) * (2.0 * math.pi))


def split_two(value):
    high = value.astype(bf16)
    return high, (value - high.astype(f32)).astype(bf16)


def fold_of(place, half):
    box = 2 * half
    return jnp.where(place <= half, place, box + half - place)


def slices_kernel(
    class_hbm, pose_hbm, bin_hbm, defocus_hbm, plane_hbm,
    dft_hbm, dft_t_hbm, images_hbm, rows_hbm, cols_hbm,
    *refs,
):
    outs, refs = refs[:-SCRATCH], refs[-SCRATCH:]
    (
        class_ref, pose_ref, bin_ref, defocus_ref, plane_ref,
        dft_ref, dft_t_ref, images_ref, rows_ref, cols_ref, arrived,
        rows_fold, cols_fold, wave_y, cos_x, sin_x, half_ref, spec_ref, mix_ref, totals,
    ) = refs
    count, box, _ = images_ref.shape
    half = box // 2
    poses, rows, _ = rows_ref.shape
    cols = cols_ref.shape[2]
    planes = plane_ref.shape[0]

    pairs = (
        (class_hbm, class_ref), (pose_hbm, pose_ref), (bin_hbm, bin_ref),
        (defocus_hbm, defocus_ref), (plane_hbm, plane_ref),
        (dft_hbm, dft_ref), (images_hbm.at[0:GROUP], images_ref.at[0:GROUP]),
        (dft_t_hbm, dft_t_ref), (cols_hbm, cols_ref), (rows_hbm, rows_ref),
    ) + tuple(
        (images_hbm.at[i : i + GROUP], images_ref.at[i : i + GROUP])
        for i in range(GROUP, count, GROUP)
    )
    copies = [
        pltpu.make_async_copy(source, target, arrived.at[n])
        for n, (source, target) in enumerate(pairs)
    ]
    for copy in copies:
        copy.start()

    place = iota((box, box), 0)
    other = iota((box, box), 1)
    folded = fold_of(place, half)
    near = (folded == other).astype(f32).astype(bf16)
    far = (jnp.where(folded == 0, 0, box - folded) == other).astype(f32).astype(bf16)

    for copy in copies[:5]:
        copy.wait()
    tall, lanes = wave_y.shape
    lane = iota((1, lanes), 1)
    sub = iota((count, box), 0)
    lane_defocus = jnp.zeros((1, lanes), f32)
    sub_defocus = jnp.zeros((count, box), f32)
    for i in range(count):
        value = defocus_ref[bin_ref[i]]
        lane_defocus = jnp.where(lane % count == i, value, lane_defocus)
        sub_defocus = jnp.where(sub == i, value, sub_defocus)
    scale = 1.0 / (2 * half * half)
    ky = iota((tall, lanes), 0).astype(f32)
    quarter = jnp.where(lane < count, 0.0, 0.25) + ctf_phase / (2.0 * math.pi)
    wave_y[...] = turns_sine(lane_defocus * (ky * ky * scale) + quarter)
    kx = iota((count, box), 1)
    kx = jnp.where(kx <= half, kx, kx - half).astype(f32)
    turns = sub_defocus * (kx * kx * scale)
    cos_x[...] = -turns_sine(turns + 0.25)
    sin_x[...] = -turns_sine(turns)
    totals[...] = jnp.zeros_like(totals)
    leading = 1 if len(outs) > 1 else 0
    if len(outs) > 1:
        bins = defocus_ref.shape[0]
        count_row = iota((16, 2 * cols), 0)
        count_lane = iota((16, 2 * cols), 1)
        counts = jnp.zeros((16, 2 * cols), f32)
        for i in range(count):
            hit = (count_row == class_ref[i]) & (count_lane == pose_ref[i] * bins + bin_ref[i])
            counts = counts + jnp.where(hit, 1.0, 0.0)
        totals[0] = jnp.tile(counts, (rows // 16, 1))

    tile = 8
    tile_row = iota((tile, half), 0) == 0
    tile_col = iota((tile, half), 1) == 0
    col_zero = iota((half, half), 1) == 0
    short_row = iota((16, half), 0) == 0
    short_col = iota((16, half), 1) == 0

    def without_row(value):
        return jnp.concatenate([jnp.where(tile_row, 0.0, value[:tile]), value[tile:]], 0)

    def along_rows(i, wide):
        if i % GROUP == 0:
            copies[6 if i == 0 else 9 + i // GROUP].wait()
        group = jnp.concatenate([images_ref[i + n] for n in range(wide)], 1)
        product = dot(dft_ref[...], group).astype(bf16)
        for n in range(wide):
            place = (i + n) % GROUP * box
            half_ref[i // GROUP % 2, place : place + box] = product[:, n * box : (n + 1) * box]

    def along_columns(i):
        return dot(half_ref[i // GROUP % 2], dft_t_ref[...])

    def weigh(i, y):
        sin_col = jnp.broadcast_to(wave_y[:, i : i + 1], (tall, half))
        cos_col = jnp.broadcast_to(wave_y[:, count + i : count + i + 1], (tall, half))
        near_ctf = sin_col * cos_x[i : i + 1, :half] + cos_col * sin_x[i : i + 1, :half]
        far_ctf = sin_col * cos_x[i : i + 1, half:] + cos_col * sin_x[i : i + 1, half:]
        cc, cs = y[:half, :half], y[:half, half:]
        sc, ss = y[half:, :half], y[half:, half:]
        ss_row = without_row(ss)
        ss_in = jnp.where(col_zero, 0.0, ss_row)
        sc_in = without_row(sc)
        cs_in = jnp.where(col_zero, 0.0, cs)
        near_y, far_y = near_ctf[:half], far_ctf[:half]
        spec = spec_ref.at[i % SLOTS]
        spec[0:half, 0:half] = (near_y * (cc + ss_in)).astype(bf16)
        spec[0:half, half:] = (far_y * jnp.where(col_zero, cs, cc - ss_in)).astype(bf16)
        yield
        spec[half:box, 0:half] = (near_y * (sc_in - cs_in)).astype(bf16)
        spec[half:box, half:] = (far_y * jnp.where(col_zero, ss_row, sc_in + cs_in)).astype(bf16)
        sc_top = jnp.broadcast_to(sc[0:1], (16, half))
        ss_top = jnp.broadcast_to(ss[0:1], (16, half))
        ss_top_in = jnp.where(short_col, 0.0, ss_top)
        spec[box : box + 16, 0:half] = (
            near_ctf[half : half + 1] * jnp.where(short_row, sc_top, -ss_top_in)
        ).astype(bf16)
        spec[box : box + 16, half:] = (
            far_ctf[half : half + 1]
            * jnp.where(short_row, jnp.where(short_col, ss_top, sc_top), ss_top_in)
        ).astype(bf16)

    def mix(i):
        mixed = dot(spec_ref[i % SLOTS], cols_fold[pose_ref[i]])
        out = mix_ref.at[i % SLOTS]
        out[0:half, 0:cols] = mixed[:half, :cols].astype(bf16)
        out[0:half, cols:] = mixed[half:box, :cols].astype(bf16)
        top = iota((16, cols), 0) == 0
        real, imag = mixed[:half, cols:], -mixed[half:box, cols:]
        out[half : half + 16, 0:cols] = jnp.where(
            top, mixed[box : box + 1, :cols], real[:16]
        ).astype(bf16)
        out[half : half + 16, cols:] = jnp.where(
            top, mixed[box + 1 : box + 2, :cols], imag[:16]
        ).astype(bf16)
        out[half + 16 :, 0:cols] = real[16:].astype(bf16)
        out[half + 16 :, cols:] = imag[16:].astype(bf16)

    def insert(i):
        pose = pose_ref[i]
        pose_rows = rows_fold[pl.ds(pl.multiple_of(pose * rows, rows), rows), :]
        piece = dot(pose_rows, mix_ref[i % SLOTS])
        for z in range(planes):
            slot = leading + z * CLASSES + class_ref[i]
            totals[slot] += plane_ref[z, pose] * piece

    copies[5].wait()
    along_rows(0, GROUP)
    copies[7].wait()
    copies[8].wait()
    for p in range(0, poses, 2):
        two = jnp.concatenate([cols_ref[p], cols_ref[p + 1]], 1)
        near_two = dot(near, two).astype(bf16)
        far_two = dot(far, two).astype(bf16)
        cols_fold[p] = jnp.concatenate([near_two[:, :cols], far_two[:, :cols]], 1)
        cols_fold[p + 1] = jnp.concatenate([near_two[:, cols:], far_two[:, cols:]], 1)
    copies[9].wait()
    rows_fold[...] = dot(
        rows_ref[...].reshape(poses * rows, box), near, ((1,), (1,))
    ).astype(bf16)
    for step in range(GROUP, count + 3 * GROUP, GROUP):
        if step - GROUP < count:
            product = along_columns(step - GROUP)
        for n in range(GROUP):
            parts = iter(())
            if step - GROUP < count:
                parts = weigh(step - GROUP + n, product[n * box : (n + 1) * box])
            next(parts, None)
            if 0 <= step - 2 * GROUP < count:
                mix(step - 2 * GROUP + n)
            next(parts, None)
            if step >= 3 * GROUP:
                insert(step - 3 * GROUP + n)
            if step < count and n % 2 == 0:
                along_rows(step + n, 2)

    if len(outs) == 1:
        outs[0][...] = totals[...].astype(bf16)
        return
    x_send, x_keep, own_send, own_keep, z_keep = outs[:5]
    z_sends = outs[5:]
    x_slots, owned, _ = own_keep.shape
    me = lax.axis_index("img")

    def rows_of(flip):
        return pl.ds(pl.multiple_of((me ^ flip) * owned, owned), owned)

    for n, k in enumerate(LINE):
        x_send[n] = totals[-x_slots:, rows_of(2 * k + 1), :].astype(bf16)
        x_keep[n] = totals[-x_slots:, rows_of(2 * k), :]
    own_send[...] = totals[-x_slots:, rows_of(1), :].astype(bf16)
    own_keep[...] = totals[-x_slots:, rows_of(0), :]
    for k, out in zip((0,) + LINE, (z_keep, *z_sends)):
        out[:Z_SLOTS] = totals[:Z_SLOTS, rows_of(2 * k), :].astype(out.dtype)
        out[Z_SLOTS:] = totals[1:Z_SLOTS, rows_of(2 * k + 1), :].astype(out.dtype)


SCRATCH = 20
LINE = (2, 3, 1)
SLOTS = 16
GROUP = 8
Z_SLOTS = 4


def own_totals(images, class_index, pose_index, defocus_bin, defocus, rows_table, cols_table, plane_weight, members):
    count, box, _ = images.shape
    poses, rows, _ = rows_table.shape
    cols = cols_table.shape[2]
    planes = plane_weight.shape[1]
    slots = CLASSES * planes
    table_y, table_x = packed_dft(box, -1.0), packed_dft(box, 1.0)
    any_place = pl.BlockSpec(memory_space=pl.ANY)
    vmem = pl.BlockSpec(memory_space=pltpu.VMEM)
    lanes = 128 * (-(-2 * count // 128))
    if members == 1:
        out_shape = [jax.ShapeDtypeStruct((slots, rows, 2 * cols), bf16)]
    else:
        slots += 1
        tail = (rows // members, 2 * cols)
        x_slots = slots - Z_SLOTS
        out_shape = []
        for lead in ((len(LINE), x_slots), (x_slots,)):
            out_shape += [pltpu.VMEM(lead + tail, bf16), pltpu.VMEM(lead + tail, f32)]
        out_shape += [pltpu.VMEM((2 * Z_SLOTS - 1,) + tail, f32)]
        out_shape += [pltpu.VMEM((2 * Z_SLOTS - 1,) + tail, bf16)] * len(LINE)
    operands = (
        class_index[:, 0], pose_index, defocus_bin, defocus, plane_weight.T,
        jnp.asarray(table_y, bf16), jnp.asarray(table_x.T.copy(), bf16),
        images, rows_table, cols_table,
    )
    return pl.pallas_call(
        slices_kernel,
        out_shape=out_shape,
        in_specs=[any_place] * 10,
        out_specs=[vmem] * len(out_shape),
        scratch_shapes=[pltpu.SMEM(x.shape, x.dtype) for x in operands[:5]]
        + [pltpu.VMEM(x.shape, x.dtype) for x in operands[5:]]
        + [
            pltpu.SemaphoreType.DMA((9 + count // GROUP,)),
            pltpu.VMEM((poses * rows, box), bf16),
            pltpu.VMEM((poses, box, 2 * cols), bf16),
            pltpu.VMEM((box // 2 + 8, lanes), f32),
            pltpu.VMEM((count, box), f32),
            pltpu.VMEM((count, box), f32),
            pltpu.VMEM((2, GROUP * box, box), bf16),
            pltpu.VMEM((SLOTS, box + 16, box), bf16),
            pltpu.VMEM((SLOTS, box, 2 * cols), bf16),
            pltpu.VMEM((slots, rows, 2 * cols), f32),
        ],
        compiler_params=pltpu.CompilerParams(vmem_limit_bytes=VMEM_LIMIT),
        cost_estimate=pl.CostEstimate(
            flops=2 * count * box * box * 1000, bytes_accessed=6 * 1024 * 1024, transcendentals=0
        ),
    )(*operands)


VMEM_LIMIT = 56 * 1024 * 1024


def ridge_kernel(defocus_hbm, plane_hbm, rows_hbm, cols_hbm, high_ref, low_ref, share_ref, *refs):
    defocus_ref, plane_ref, rows_ref, cols_ref, arrived = refs
    poses, owned, box = rows_ref.shape
    cols = cols_ref.shape[2]
    bins = defocus_ref.shape[0]
    planes = plane_ref.shape[0]
    half = box // 2
    first = pl.multiple_of(lax.axis_index("img") * owned, owned)
    copies = [
        pltpu.make_async_copy(defocus_hbm, defocus_ref, arrived.at[0]),
        pltpu.make_async_copy(plane_hbm, plane_ref, arrived.at[1]),
        pltpu.make_async_copy(rows_hbm.at[:, pl.ds(first, owned), :], rows_ref, arrived.at[2]),
        pltpu.make_async_copy(cols_hbm, cols_ref, arrived.at[3]),
    ]
    for copy in copies:
        copy.start()
    for copy in copies:
        copy.wait()
    share_plane = iota((planes * CLASSES, poses * bins), 0) // CLASSES
    share_pose = iota((planes * CLASSES, poses * bins), 1) // bins
    share = jnp.zeros((planes * CLASSES, poses * bins), f32)
    for p in range(poses):
        for z in range(planes):
            share = jnp.where((share_plane == z) & (share_pose == p), plane_ref[z, p], share)
    share_ref[...] = share

    bin_row = iota((bins, box), 0)
    sub_defocus = jnp.zeros((bins, box), f32)
    for b in range(bins):
        sub_defocus = jnp.where(bin_row == b, defocus_ref[b], sub_defocus)
    freq = iota((bins, box), 1)
    freq = jnp.where(freq < half, freq, box - freq).astype(f32)
    turns_x = sub_defocus * (freq * freq * (1.0 / (half * half)))
    turns_y = turns_x + ctf_phase / math.pi
    ones = jnp.ones((bins, box), f32)
    wave_y = jnp.concatenate(
        [0.5 * ones, -0.5 * turns_sine(turns_y + 0.25), 0.5 * turns_sine(turns_y)], 0
    )
    wave_x = jnp.concatenate([ones, turns_sine(turns_x + 0.25), turns_sine(turns_x)], 0)
    y_high, y_low = split_two(wave_y)
    x_high, x_low = split_two(wave_x)
    rows_sq = rows_ref[...].reshape(poses * owned, box).astype(f32)
    rows_sq = (rows_sq * rows_sq).astype(bf16)
    u = dot(y_high, rows_sq, ((1,), (1,))) + dot(y_low, rows_sq, ((1,), (1,)))
    for p in range(poses):
        cols_sq = cols_ref[p].astype(f32)
        cols_sq = (cols_sq * cols_sq).astype(bf16)
        v = dot(x_high, cols_sq) + dot(x_low, cols_sq)
        for r in range(owned):
            column = u[:, p * owned + r : p * owned + r + 1]
            product = v * column
            weight = product[:bins] + product[bins : 2 * bins] + product[2 * bins :]
            high, low = split_two(weight)
            high_ref[p * bins : (p + 1) * bins, r * cols : (r + 1) * cols] = high
            low_ref[p * bins : (p + 1) * bins, r * cols : (r + 1) * cols] = low


def own_ridges(defocus, plane_weight, rows_table, cols_table, owned):
    poses, _, box = rows_table.shape
    cols = cols_table.shape[2]
    bins = defocus.shape[0]
    any_place = pl.BlockSpec(memory_space=pl.ANY)
    vmem = pl.BlockSpec(memory_space=pltpu.VMEM)
    planes = plane_weight.T
    table = pltpu.VMEM((poses * bins, owned * cols), bf16)
    return pl.pallas_call(
        ridge_kernel,
        out_shape=[table, table, pltpu.VMEM((planes.shape[0] * CLASSES, poses * bins), f32)],
        in_specs=[any_place] * 4,
        out_specs=[vmem] * 3,
        scratch_shapes=[
            pltpu.SMEM(defocus.shape, f32),
            pltpu.SMEM(planes.shape, f32),
            pltpu.VMEM((poses, owned, box), bf16),
            pltpu.VMEM(cols_table.shape, bf16),
            pltpu.SemaphoreType.DMA((4,)),
        ],
        compiler_params=pltpu.CompilerParams(vmem_limit_bytes=VMEM_LIMIT),
        cost_estimate=pl.CostEstimate(
            flops=1000, bytes_accessed=1000, transcendentals=0
        ),
    )(defocus, planes, rows_table, cols_table)


def call_in_vmem(kernel, arrays, out_shape):
    vmem = pl.BlockSpec(memory_space=pltpu.VMEM)
    return pl.pallas_call(
        kernel,
        out_shape=out_shape,
        in_specs=[vmem] * len(arrays),
        out_specs=[vmem] * len(out_shape),
        compiler_params=pltpu.CompilerParams(vmem_limit_bytes=16 * 1024 * 1024),
        cost_estimate=pl.CostEstimate(flops=1000, bytes_accessed=1000, transcendentals=0),
    )(*arrays)


def fold_kernel(x_keep, x_came, own_send, z_keep, *refs):
    z_came, refs = refs[: len(LINE)], refs[len(LINE) :]
    x_sends, own_out, z_own, z_send = refs[: len(LINE)], *refs[len(LINE) :]
    for n, send in enumerate(x_sends):
        send[...] = (x_keep[n] + x_came[n].astype(f32)).astype(bf16)
    own_out[...] = own_send[...]
    for n in range(z_keep.shape[0]):
        value = z_keep[n]
        for came in z_came:
            value = value + came[n].astype(f32)
        if n < Z_SLOTS:
            z_own[n] = value
        if n == 0:
            z_send[n] = value.astype(bf16)
        elif n >= Z_SLOTS:
            z_send[n - Z_SLOTS + 1] = value.astype(bf16)


def fold_phase(x_keep, x_came, own_send, z_keep, z_came):
    piece = own_send.shape
    z_piece = (Z_SLOTS,) + piece[1:]
    out_shape = [pltpu.VMEM(piece, bf16)] * (len(LINE) + 1)
    out_shape += [pltpu.VMEM(z_piece, f32), pltpu.VMEM(z_piece, bf16)]
    return call_in_vmem(fold_kernel, (x_keep, x_came, own_send, z_keep, *z_came), out_shape)


def weight_kernel(high_ref, low_ref, share_ref, z_own, z_came, out_ref, ridge_ref):
    slots, pairs = share_ref.shape
    owned, _, cols = ridge_ref.shape
    counts = z_own[0] + z_came[0].astype(f32)
    scaled = jnp.concatenate([counts[:CLASSES, :pairs]] * (slots // CLASSES), 0) * share_ref[...]
    c_high, c_low = split_two(scaled)
    weight = (
        dot(c_high, high_ref[...]) + dot(c_low, high_ref[...]) + dot(c_high, low_ref[...])
    )
    ridge = 1.0 / (weight + wiener_ridge)
    for r in range(owned):
        ridge_ref[r] = ridge[:, r * cols : (r + 1) * cols]
    for s in range(slots):
        out_ref[s] = ridge_ref[:, s, :]


def own_weights(tables, z_own, z_came):
    slots = tables[2].shape[0]
    _, owned, wide = z_own.shape
    cols = wide // 2
    vmem = pl.BlockSpec(memory_space=pltpu.VMEM)
    return pl.pallas_call(
        weight_kernel,
        out_shape=pltpu.VMEM((slots, owned, cols), f32),
        in_specs=[vmem] * 5,
        out_specs=vmem,
        scratch_shapes=[pltpu.VMEM((owned, slots, cols), f32)],
        compiler_params=pltpu.CompilerParams(vmem_limit_bytes=16 * 1024 * 1024),
        cost_estimate=pl.CostEstimate(flops=1000, bytes_accessed=1000, transcendentals=0),
    )(*tables, z_own, z_came)


def finish_kernel(planes, ridge_ref, x_own, z_own, z_came, *refs):
    x_came, out_ref = refs[:-1], refs[-1]
    slots, owned, cols = ridge_ref.shape
    first = z_own.shape[0]
    for s in range(slots):
        if s + 1 < first:
            value = z_own[s + 1] + z_came[s + 1].astype(f32)
        else:
            value = x_own[s + 1 - first]
            for part in x_came:
                value = value + part[s + 1 - first].astype(f32)
        factor = ridge_ref[s]
        place = (s % CLASSES) * planes + s // CLASSES
        out_ref[:, 2 * place, :] = value[:, :cols] * factor
        out_ref[:, 2 * place + 1, :] = value[:, cols:] * factor


def finish(planes, ridge, x_own, z_own, z_came, x_came):
    slots, owned, cols = ridge.shape
    vmem = pl.BlockSpec(memory_space=pltpu.VMEM)
    return pl.pallas_call(
        functools.partial(finish_kernel, planes),
        out_shape=jax.ShapeDtypeStruct((owned, 2 * slots, cols), f32),
        in_specs=[vmem] * (4 + len(x_came)),
        out_specs=vmem,
        compiler_params=pltpu.CompilerParams(vmem_limit_bytes=16 * 1024 * 1024),
        cost_estimate=pl.CostEstimate(flops=1000, bytes_accessed=1000, transcendentals=0),
    )(ridge, x_own, z_own, z_came, *x_came)


def squared_table(weight_table):
    wide_table = weight_table.astype(f32)
    return (wide_table * wide_table).astype(bf16)


def weight_totals(class_index, pose_index, defocus_bin, defocus, rows_table, cols_table, plane_weight, first_row, owned):
    box = rows_table.shape[2]
    poses = rows_table.shape[0]
    bins = defocus.shape[0]
    half = box // 2
    exact = lax.Precision.HIGHEST
    code = (class_index[:, 0] * poses + pose_index) * bins + defocus_bin
    codes = lax.all_gather(code, "img", tiled=True)
    hits = (codes[:, None] == jnp.arange(CLASSES * poses * bins, dtype=jnp.int32)).astype(f32)
    counts = jnp.sum(hits, 0).reshape(CLASSES, poses, bins)
    place = jnp.arange(box, dtype=jnp.int32)
    freq = jnp.where(place < half, place, place - box).astype(f32)
    turns = defocus[:, None] * (freq * freq)[None, :] * (1.0 / (half * half))
    turns_y = turns + ctf_phase / math.pi
    ones = jnp.ones_like(turns)
    wave_y = jnp.stack([0.5 * ones, -0.5 * turns_sine(turns_y + 0.25), 0.5 * turns_sine(turns_y)])
    wave_x = jnp.stack([ones, turns_sine(turns + 0.25), turns_sine(turns)])
    rows_own = lax.dynamic_slice_in_dim(rows_table, first_row, owned, 1)
    u = jnp.einsum("pry,mby->pmbr", squared_table(rows_own).astype(f32), wave_y, precision=exact)
    v = jnp.einsum("pxj,mbx->pmbj", squared_table(cols_table).astype(f32), wave_x, precision=exact)
    weight = counts[:, None] * plane_weight.T[None, :, :, None]
    left = weight[:, :, :, None, :, None] * u[None, None]
    return jnp.einsum("czpmbr,pmbj->rczj", left, v, precision=exact)


def by_pairs(images, class_index, pose_index, defocus_bin, defocus, rows_table, cols_table, plane_weight):
    members = lax.axis_size("img")
    rows = rows_table.shape[1]
    planes = plane_weight.shape[1]
    cols = cols_table.shape[2]
    owned = rows // members

    def exchange(value, flip):
        return lax.ppermute(value, "img", [(i, i ^ flip) for i in range(members)])

    x_send, x_keep, own_send, own_keep, z_keep, *z_sends = own_totals(
        images, class_index, pose_index, defocus_bin, defocus, rows_table, cols_table, plane_weight, members
    )
    x_came = exchange(x_send, 1)
    z_came = [exchange(send, 2 * k) for send, k in zip(z_sends, LINE)]
    tables = own_ridges(defocus, plane_weight, rows_table, cols_table, owned)
    x_keep, tables = lax.optimization_barrier((x_keep, tables))
    *x_sends, own_send, z_own, z_send = fold_phase(x_keep, x_came, own_send, z_keep, z_came)
    x_came = [exchange(send, 2 * k) for send, k in zip(x_sends, LINE)]
    own_came = exchange(own_send, 1)
    z_came = exchange(z_send, 1)
    ridge = own_weights(tables, z_own, z_came)
    out = finish(planes, ridge, own_keep, z_own, z_came, (*x_came, own_came))
    return out.reshape(owned, CLASSES, planes, 2, cols)


def by_scatter(images, class_index, pose_index, defocus_bin, defocus, rows_table, cols_table, plane_weight):
    rows = rows_table.shape[1]
    cols = cols_table.shape[2]
    planes = plane_weight.shape[1]
    members = lax.axis_size("img")
    owned = rows // members
    (totals,) = own_totals(
        images, class_index, pose_index, defocus_bin, defocus, rows_table, cols_table, plane_weight, 1
    )
    slots = totals.shape[0]
    totals = totals.reshape(slots, members, owned, 2 * cols).transpose(1, 0, 2, 3)
    own = lax.psum_scatter(totals, "img", scatter_dimension=0, tiled=False)
    weight = weight_totals(
        class_index, pose_index, defocus_bin, defocus, rows_table, cols_table, plane_weight,
        lax.axis_index("img") * owned, owned,
    )
    own = own.astype(f32).reshape(planes, CLASSES, owned, 2, cols).transpose(2, 1, 0, 3, 4)
    return own / (weight[:, :, :, None, :] + wiener_ridge)


def body(*arrays):
    rows = arrays[5].shape[1]
    members = lax.axis_size("img")
    images = members * arrays[0].shape[0]
    paired = members == 8 and images <= 256 and rows % (16 * members) == 0
    return (by_pairs if paired else by_scatter)(*arrays)


def solution(mesh):
    placed = (
        P(("groups", "img"), None, None),
        P(("groups", "img"), None),
        P(("groups", "img")),
        P(("groups", "img")),
        P(),
        P(),
        P(None, None, "slab"),
        P(),
    )
    return jax.shard_map(
        body,
        mesh=mesh,
        in_specs=placed,
        out_specs=P("img", "groups", None, None, "slab"),
        check_vma=False,
    )
```

```python
import functools
import math

import jax
import jax.numpy as jnp
import numpy as np
from jax import lax
from jax.experimental import pallas as pl
from jax.experimental.pallas import tpu as pltpu
from jax.sharding import PartitionSpec as P

CLASSES = 8

wiener_ridge = 1.0
ctf_phase = 0.1
f32 = jnp.float32
bf16 = jnp.bfloat16


def packed_dft(box, sine_sign):
    half = box // 2
    k = np.concatenate([np.arange(half), [half], np.arange(1, half)])
    angle = (k[:, None] * np.arange(box)[None, :] % box) * (2.0 * math.pi / box)
    table = np.where((np.arange(box) <= half)[:, None], np.cos(angle), sine_sign * np.sin(angle))
    return (table / math.sqrt(box)).astype(np.float32)


def iota(shape, axis):
    return lax.broadcasted_iota(jnp.int32, shape, axis)


def dot(a, b, dims=((1,), (0,))):
    return lax.dot_general(a, b, (dims, ((), ())), preferred_element_type=f32)


def turns_sine(turns):
    return jnp.sin((turns - jnp.round(turns)) * (2.0 * math.pi))


def split_two(value):
    high = value.astype(bf16)
    return high, (value - high.astype(f32)).astype(bf16)


def fold_of(place, half):
    box = 2 * half
    return jnp.where(place <= half, place, box + half - place)


def slices_kernel(
    class_hbm, pose_hbm, bin_hbm, defocus_hbm, plane_hbm,
    dft_hbm, dft_t_hbm, images_hbm, rows_hbm, cols_hbm,
    *refs,
):
    outs, refs = refs[:-SCRATCH], refs[-SCRATCH:]
    (
        class_ref, pose_ref, bin_ref, defocus_ref, plane_ref,
        dft_ref, dft_t_ref, images_ref, rows_ref, cols_ref, arrived,
        rows_fold, cols_fold, wave_y, cos_x, sin_x, half_ref, spec_ref, mix_ref, totals,
    ) = refs
    count, box, _ = images_ref.shape
    half = box // 2
    poses, rows, _ = rows_ref.shape
    cols = cols_ref.shape[2]
    planes = plane_ref.shape[0]

    pairs = (
        (class_hbm, class_ref), (pose_hbm, pose_ref), (bin_hbm, bin_ref),
        (defocus_hbm, defocus_ref), (plane_hbm, plane_ref),
        (dft_hbm, dft_ref), (images_hbm.at[0:LOAD], images_ref.at[0:LOAD]),
        (dft_t_hbm, dft_t_ref), (cols_hbm, cols_ref), (rows_hbm, rows_ref),
    ) + tuple(
        (images_hbm.at[i : i + LOAD], images_ref.at[i : i + LOAD])
        for i in range(LOAD, count, LOAD)
    )
    copies = [
        pltpu.make_async_copy(source, target, arrived.at[n])
        for n, (source, target) in enumerate(pairs)
    ]
    for copy in copies:
        copy.start()

    place = iota((box, box), 0)
    other = iota((box, box), 1)
    folded = fold_of(place, half)
    near = (folded == other).astype(f32).astype(bf16)
    far = (jnp.where(folded == 0, 0, box - folded) == other).astype(f32).astype(bf16)

    for copy in copies[:5]:
        copy.wait()
    tall, lanes = wave_y.shape
    lane = iota((1, lanes), 1)
    sub = iota((count, box), 0)
    lane_defocus = jnp.zeros((1, lanes), f32)
    sub_defocus = jnp.zeros((count, box), f32)
    for i in range(count):
        value = defocus_ref[bin_ref[i]]
        lane_defocus = jnp.where(lane % count == i, value, lane_defocus)
        sub_defocus = jnp.where(sub == i, value, sub_defocus)
    scale = 1.0 / (2 * half * half)
    ky = iota((tall, lanes), 0).astype(f32)
    quarter = jnp.where(lane < count, 0.0, 0.25) + ctf_phase / (2.0 * math.pi)
    wave_y[...] = turns_sine(lane_defocus * (ky * ky * scale) + quarter)
    kx = iota((count, box), 1)
    kx = jnp.where(kx <= half, kx, kx - half).astype(f32)
    turns = sub_defocus * (kx * kx * scale)
    cos_x[...] = -turns_sine(turns + 0.25)
    sin_x[...] = -turns_sine(turns)
    totals[...] = jnp.zeros_like(totals)
    leading = 1 if len(outs) > 1 else 0
    if len(outs) > 1:
        bins = defocus_ref.shape[0]
        count_row = iota((16, 2 * cols), 0)
        count_lane = iota((16, 2 * cols), 1)
        counts = jnp.zeros((16, 2 * cols), f32)
        for i in range(count):
            hit = (count_row == class_ref[i]) & (count_lane == pose_ref[i] * bins + bin_ref[i])
            counts = counts + jnp.where(hit, 1.0, 0.0)
        totals[0] = jnp.tile(counts, (rows // 16, 1))

    tile = 8
    tile_row = iota((tile, half), 0) == 0
    tile_col = iota((tile, half), 1) == 0
    col_zero = iota((half, half), 1) == 0
    short_row = iota((16, half), 0) == 0
    short_col = iota((16, half), 1) == 0

    def without_row(value):
        return jnp.concatenate([jnp.where(tile_row, 0.0, value[:tile]), value[tile:]], 0)

    def along_rows(i, wide):
        if i % LOAD == 0:
            copies[6 if i == 0 else 9 + i // LOAD].wait()
        group = jnp.concatenate([images_ref[i + n] for n in range(wide)], 1)
        product = dot(dft_ref[...], group).astype(bf16)
        for n in range(wide):
            place = (i + n) % GROUP * box
            half_ref[i // GROUP % 2, place : place + box] = product[:, n * box : (n + 1) * box]

    def along_columns(i):
        return dot(half_ref[i // GROUP % 2], dft_t_ref[...])

    def weigh(i, y):
        sin_col = jnp.broadcast_to(wave_y[:, i : i + 1], (tall, half))
        cos_col = jnp.broadcast_to(wave_y[:, count + i : count + i + 1], (tall, half))
        near_ctf = sin_col * cos_x[i : i + 1, :half] + cos_col * sin_x[i : i + 1, :half]
        far_ctf = sin_col * cos_x[i : i + 1, half:] + cos_col * sin_x[i : i + 1, half:]
        cc, cs = y[:half, :half], y[:half, half:]
        sc, ss = y[half:, :half], y[half:, half:]
        ss_row = without_row(ss)
        ss_in = jnp.where(col_zero, 0.0, ss_row)
        sc_in = without_row(sc)
        cs_in = jnp.where(col_zero, 0.0, cs)
        near_y, far_y = near_ctf[:half], far_ctf[:half]
        spec = spec_ref.at[i % SLOTS]
        spec[0:half, 0:half] = (near_y * (cc + ss_in)).astype(bf16)
        spec[0:half, half:] = (far_y * jnp.where(col_zero, cs, cc - ss_in)).astype(bf16)
        yield
        spec[half:box, 0:half] = (near_y * (sc_in - cs_in)).astype(bf16)
        spec[half:box, half:] = (far_y * jnp.where(col_zero, ss_row, sc_in + cs_in)).astype(bf16)
        sc_top = jnp.broadcast_to(sc[0:1], (16, half))
        ss_top = jnp.broadcast_to(ss[0:1], (16, half))
        ss_top_in = jnp.where(short_col, 0.0, ss_top)
        spec[box : box + 16, 0:half] = (
            near_ctf[half : half + 1] * jnp.where(short_row, sc_top, -ss_top_in)
        ).astype(bf16)
        spec[box : box + 16, half:] = (
            far_ctf[half : half + 1]
            * jnp.where(short_row, jnp.where(short_col, ss_top, sc_top), ss_top_in)
        ).astype(bf16)

    def mix(i):
        mixed = dot(spec_ref[i % SLOTS], cols_fold[pose_ref[i]])
        out = mix_ref.at[i % SLOTS]
        out[0:half, 0:cols] = mixed[:half, :cols].astype(bf16)
        out[0:half, cols:] = mixed[half:box, :cols].astype(bf16)
        top = iota((16, cols), 0) == 0
        real, imag = mixed[:half, cols:], -mixed[half:box, cols:]
        out[half : half + 16, 0:cols] = jnp.where(
            top, mixed[box : box + 1, :cols], real[:16]
        ).astype(bf16)
        out[half : half + 16, cols:] = jnp.where(
            top, mixed[box + 1 : box + 2, :cols], imag[:16]
        ).astype(bf16)
        out[half + 16 :, 0:cols] = real[16:].astype(bf16)
        out[half + 16 :, cols:] = imag[16:].astype(bf16)

    def insert(i):
        pose = pose_ref[i]
        pose_rows = rows_fold[pl.ds(pl.multiple_of(pose * rows, rows), rows), :]
        piece = dot(pose_rows, mix_ref[i % SLOTS])
        for z in range(planes):
            slot = leading + z * CLASSES + class_ref[i]
            totals[slot] += plane_ref[z, pose] * piece

    copies[5].wait()
    along_rows(0, LOAD)
    copies[7].wait()
    copies[8].wait()
    for p in range(0, poses, 2):
        two = jnp.concatenate([cols_ref[p], cols_ref[p + 1]], 1)
        near_two = dot(near, two).astype(bf16)
        far_two = dot(far, two).astype(bf16)
        cols_fold[p] = jnp.concatenate([near_two[:, :cols], far_two[:, :cols]], 1)
        cols_fold[p + 1] = jnp.concatenate([near_two[:, cols:], far_two[:, cols:]], 1)
    for i in range(LOAD, GROUP, LOAD):
        along_rows(i, LOAD)
    copies[9].wait()
    rows_fold[...] = dot(
        rows_ref[...].reshape(poses * rows, box), near, ((1,), (1,))
    ).astype(bf16)
    for i in range(count + 2 * LAG):
        parts = iter(())
        if i < count:
            if i % GROUP == 0:
                product = along_columns(i)
            n = i % GROUP
            parts = weigh(i, product[n * box : (n + 1) * box])
        next(parts, None)
        if 0 <= i - LAG < count:
            mix(i - LAG)
        next(parts, None)
        if i >= 2 * LAG:
            insert(i - 2 * LAG)
        if i + GROUP < count and i % 2 == 0:
            along_rows(i + GROUP, 2)

    if len(outs) == 1:
        outs[0][...] = totals[...].astype(bf16)
        return
    x_send, x_keep, own_send, own_keep, z_keep = outs[:5]
    z_sends = outs[5:]
    x_slots, owned, _ = own_keep.shape
    me = lax.axis_index("img")

    def rows_of(flip):
        return pl.ds(pl.multiple_of((me ^ flip) * owned, owned), owned)

    for n, k in enumerate(LINE):
        x_send[n] = totals[-x_slots:, rows_of(2 * k + 1), :].astype(bf16)
        x_keep[n] = totals[-x_slots:, rows_of(2 * k), :]
    own_send[...] = totals[-x_slots:, rows_of(1), :].astype(bf16)
    own_keep[...] = totals[-x_slots:, rows_of(0), :]
    for k, out in zip((0,) + LINE, (z_keep, *z_sends)):
        out[:Z_SLOTS] = totals[:Z_SLOTS, rows_of(2 * k), :].astype(out.dtype)
        out[Z_SLOTS:] = totals[1:Z_SLOTS, rows_of(2 * k + 1), :].astype(out.dtype)


SCRATCH = 20
LINE = (2, 3, 1)
SLOTS = 16
GROUP = 8
LOAD = 4
LAG = 6
Z_SLOTS = 4


def own_totals(images, class_index, pose_index, defocus_bin, defocus, rows_table, cols_table, plane_weight, members):
    count, box, _ = images.shape
    poses, rows, _ = rows_table.shape
    cols = cols_table.shape[2]
    planes = plane_weight.shape[1]
    slots = CLASSES * planes
    table_y, table_x = packed_dft(box, -1.0), packed_dft(box, 1.0)
    any_place = pl.BlockSpec(memory_space=pl.ANY)
    vmem = pl.BlockSpec(memory_space=pltpu.VMEM)
    lanes = 128 * (-(-2 * count // 128))
    if members == 1:
        out_shape = [jax.ShapeDtypeStruct((slots, rows, 2 * cols), bf16)]
    else:
        slots += 1
        tail = (rows // members, 2 * cols)
        x_slots = slots - Z_SLOTS
        out_shape = []
        for lead in ((len(LINE), x_slots), (x_slots,)):
            out_shape += [pltpu.VMEM(lead + tail, bf16), pltpu.VMEM(lead + tail, f32)]
        out_shape += [pltpu.VMEM((2 * Z_SLOTS - 1,) + tail, f32)]
        out_shape += [pltpu.VMEM((2 * Z_SLOTS - 1,) + tail, bf16)] * len(LINE)
    operands = (
        class_index[:, 0], pose_index, defocus_bin, defocus, plane_weight.T,
        jnp.asarray(table_y, bf16), jnp.asarray(table_x.T.copy(), bf16),
        images, rows_table, cols_table,
    )
    return pl.pallas_call(
        slices_kernel,
        out_shape=out_shape,
        in_specs=[any_place] * 10,
        out_specs=[vmem] * len(out_shape),
        scratch_shapes=[pltpu.SMEM(x.shape, x.dtype) for x in operands[:5]]
        + [pltpu.VMEM(x.shape, x.dtype) for x in operands[5:]]
        + [
            pltpu.SemaphoreType.DMA((9 + count // LOAD,)),
            pltpu.VMEM((poses * rows, box), bf16),
            pltpu.VMEM((poses, box, 2 * cols), bf16),
            pltpu.VMEM((box // 2 + 8, lanes), f32),
            pltpu.VMEM((count, box), f32),
            pltpu.VMEM((count, box), f32),
            pltpu.VMEM((2, GROUP * box, box), bf16),
            pltpu.VMEM((SLOTS, box + 16, box), bf16),
            pltpu.VMEM((SLOTS, box, 2 * cols), bf16),
            pltpu.VMEM((slots, rows, 2 * cols), f32),
        ],
        compiler_params=pltpu.CompilerParams(vmem_limit_bytes=VMEM_LIMIT),
        cost_estimate=pl.CostEstimate(
            flops=2 * count * box * box * 1000, bytes_accessed=6 * 1024 * 1024, transcendentals=0
        ),
    )(*operands)


VMEM_LIMIT = 56 * 1024 * 1024


def ridge_kernel(defocus_hbm, plane_hbm, rows_hbm, cols_hbm, high_ref, low_ref, share_ref, *refs):
    defocus_ref, plane_ref, rows_ref, cols_ref, arrived = refs
    poses, owned, box = rows_ref.shape
    cols = cols_ref.shape[2]
    bins = defocus_ref.shape[0]
    planes = plane_ref.shape[0]
    half = box // 2
    first = pl.multiple_of(lax.axis_index("img") * owned, owned)
    copies = [
        pltpu.make_async_copy(defocus_hbm, defocus_ref, arrived.at[0]),
        pltpu.make_async_copy(plane_hbm, plane_ref, arrived.at[1]),
        pltpu.make_async_copy(rows_hbm.at[:, pl.ds(first, owned), :], rows_ref, arrived.at[2]),
        pltpu.make_async_copy(cols_hbm, cols_ref, arrived.at[3]),
    ]
    for copy in copies:
        copy.start()
    for copy in copies:
        copy.wait()
    share_plane = iota((planes * CLASSES, poses * bins), 0) // CLASSES
    share_pose = iota((planes * CLASSES, poses * bins), 1) // bins
    share = jnp.zeros((planes * CLASSES, poses * bins), f32)
    for p in range(poses):
        for z in range(planes):
            share = jnp.where((share_plane == z) & (share_pose == p), plane_ref[z, p], share)
    share_ref[...] = share

    bin_row = iota((bins, box), 0)
    sub_defocus = jnp.zeros((bins, box), f32)
    for b in range(bins):
        sub_defocus = jnp.where(bin_row == b, defocus_ref[b], sub_defocus)
    freq = iota((bins, box), 1)
    freq = jnp.where(freq < half, freq, box - freq).astype(f32)
    turns_x = sub_defocus * (freq * freq * (1.0 / (half * half)))
    turns_y = turns_x + ctf_phase / math.pi
    ones = jnp.ones((bins, box), f32)
    wave_y = jnp.concatenate(
        [0.5 * ones, -0.5 * turns_sine(turns_y + 0.25), 0.5 * turns_sine(turns_y)], 0
    )
    wave_x = jnp.concatenate([ones, turns_sine(turns_x + 0.25), turns_sine(turns_x)], 0)
    y_high, y_low = split_two(wave_y)
    x_high, x_low = split_two(wave_x)
    rows_sq = rows_ref[...].reshape(poses * owned, box).astype(f32)
    rows_sq = (rows_sq * rows_sq).astype(bf16)
    u = dot(y_high, rows_sq, ((1,), (1,))) + dot(y_low, rows_sq, ((1,), (1,)))
    for p in range(poses):
        cols_sq = cols_ref[p].astype(f32)
        cols_sq = (cols_sq * cols_sq).astype(bf16)
        v = dot(x_high, cols_sq) + dot(x_low, cols_sq)
        for r in range(owned):
            column = u[:, p * owned + r : p * owned + r + 1]
            product = v * column
            weight = product[:bins] + product[bins : 2 * bins] + product[2 * bins :]
            high, low = split_two(weight)
            high_ref[p * bins : (p + 1) * bins, r * cols : (r + 1) * cols] = high
            low_ref[p * bins : (p + 1) * bins, r * cols : (r + 1) * cols] = low


def own_ridges(defocus, plane_weight, rows_table, cols_table, owned):
    poses, _, box = rows_table.shape
    cols = cols_table.shape[2]
    bins = defocus.shape[0]
    any_place = pl.BlockSpec(memory_space=pl.ANY)
    vmem = pl.BlockSpec(memory_space=pltpu.VMEM)
    planes = plane_weight.T
    table = pltpu.VMEM((poses * bins, owned * cols), bf16)
    return pl.pallas_call(
        ridge_kernel,
        out_shape=[table, table, pltpu.VMEM((planes.shape[0] * CLASSES, poses * bins), f32)],
        in_specs=[any_place] * 4,
        out_specs=[vmem] * 3,
        scratch_shapes=[
            pltpu.SMEM(defocus.shape, f32),
            pltpu.SMEM(planes.shape, f32),
            pltpu.VMEM((poses, owned, box), bf16),
            pltpu.VMEM(cols_table.shape, bf16),
            pltpu.SemaphoreType.DMA((4,)),
        ],
        compiler_params=pltpu.CompilerParams(vmem_limit_bytes=VMEM_LIMIT),
        cost_estimate=pl.CostEstimate(
            flops=1000, bytes_accessed=1000, transcendentals=0
        ),
    )(defocus, planes, rows_table, cols_table)


def call_in_vmem(kernel, arrays, out_shape):
    vmem = pl.BlockSpec(memory_space=pltpu.VMEM)
    return pl.pallas_call(
        kernel,
        out_shape=out_shape,
        in_specs=[vmem] * len(arrays),
        out_specs=[vmem] * len(out_shape),
        compiler_params=pltpu.CompilerParams(vmem_limit_bytes=16 * 1024 * 1024),
        cost_estimate=pl.CostEstimate(flops=1000, bytes_accessed=1000, transcendentals=0),
    )(*arrays)


def fold_kernel(x_keep, x_came, own_send, z_keep, *refs):
    z_came, refs = refs[: len(LINE)], refs[len(LINE) :]
    x_sends, own_out, z_own, z_send = refs[: len(LINE)], *refs[len(LINE) :]
    for n, send in enumerate(x_sends):
        send[...] = (x_keep[n] + x_came[n].astype(f32)).astype(bf16)
    own_out[...] = own_send[...]
    for n in range(z_keep.shape[0]):
        value = z_keep[n]
        for came in z_came:
            value = value + came[n].astype(f32)
        if n < Z_SLOTS:
            z_own[n] = value
        if n == 0:
            z_send[n] = value.astype(bf16)
        elif n >= Z_SLOTS:
            z_send[n - Z_SLOTS + 1] = value.astype(bf16)


def fold_phase(x_keep, x_came, own_send, z_keep, z_came):
    piece = own_send.shape
    z_piece = (Z_SLOTS,) + piece[1:]
    out_shape = [pltpu.VMEM(piece, bf16)] * (len(LINE) + 1)
    out_shape += [pltpu.VMEM(z_piece, f32), pltpu.VMEM(z_piece, bf16)]
    return call_in_vmem(fold_kernel, (x_keep, x_came, own_send, z_keep, *z_came), out_shape)


def weight_kernel(high_ref, low_ref, share_ref, z_own, z_came, out_ref, ridge_ref):
    slots, pairs = share_ref.shape
    owned, _, cols = ridge_ref.shape
    counts = z_own[0] + z_came[0].astype(f32)
    scaled = jnp.concatenate([counts[:CLASSES, :pairs]] * (slots // CLASSES), 0) * share_ref[...]
    c_high, c_low = split_two(scaled)
    weight = (
        dot(c_high, high_ref[...]) + dot(c_low, high_ref[...]) + dot(c_high, low_ref[...])
    )
    ridge = 1.0 / (weight + wiener_ridge)
    for r in range(owned):
        ridge_ref[r] = ridge[:, r * cols : (r + 1) * cols]
    for s in range(slots):
        out_ref[s] = ridge_ref[:, s, :]


def own_weights(tables, z_own, z_came):
    slots = tables[2].shape[0]
    _, owned, wide = z_own.shape
    cols = wide // 2
    vmem = pl.BlockSpec(memory_space=pltpu.VMEM)
    return pl.pallas_call(
        weight_kernel,
        out_shape=pltpu.VMEM((slots, owned, cols), f32),
        in_specs=[vmem] * 5,
        out_specs=vmem,
        scratch_shapes=[pltpu.VMEM((owned, slots, cols), f32)],
        compiler_params=pltpu.CompilerParams(vmem_limit_bytes=16 * 1024 * 1024),
        cost_estimate=pl.CostEstimate(flops=1000, bytes_accessed=1000, transcendentals=0),
    )(*tables, z_own, z_came)


def finish_kernel(planes, ridge_ref, x_own, z_own, z_came, *refs):
    x_came, out_ref = refs[:-1], refs[-1]
    slots, owned, cols = ridge_ref.shape
    first = z_own.shape[0]
    for s in range(slots):
        if s + 1 < first:
            value = z_own[s + 1] + z_came[s + 1].astype(f32)
        else:
            value = x_own[s + 1 - first]
            for part in x_came:
                value = value + part[s + 1 - first].astype(f32)
        factor = ridge_ref[s]
        place = (s % CLASSES) * planes + s // CLASSES
        out_ref[:, 2 * place, :] = value[:, :cols] * factor
        out_ref[:, 2 * place + 1, :] = value[:, cols:] * factor


def finish(planes, ridge, x_own, z_own, z_came, x_came):
    slots, owned, cols = ridge.shape
    vmem = pl.BlockSpec(memory_space=pltpu.VMEM)
    return pl.pallas_call(
        functools.partial(finish_kernel, planes),
        out_shape=jax.ShapeDtypeStruct((owned, 2 * slots, cols), f32),
        in_specs=[vmem] * (4 + len(x_came)),
        out_specs=vmem,
        compiler_params=pltpu.CompilerParams(vmem_limit_bytes=16 * 1024 * 1024),
        cost_estimate=pl.CostEstimate(flops=1000, bytes_accessed=1000, transcendentals=0),
    )(ridge, x_own, z_own, z_came, *x_came)


def squared_table(weight_table):
    wide_table = weight_table.astype(f32)
    return (wide_table * wide_table).astype(bf16)


def weight_totals(class_index, pose_index, defocus_bin, defocus, rows_table, cols_table, plane_weight, first_row, owned):
    box = rows_table.shape[2]
    poses = rows_table.shape[0]
    bins = defocus.shape[0]
    half = box // 2
    exact = lax.Precision.HIGHEST
    code = (class_index[:, 0] * poses + pose_index) * bins + defocus_bin
    codes = lax.all_gather(code, "img", tiled=True)
    hits = (codes[:, None] == jnp.arange(CLASSES * poses * bins, dtype=jnp.int32)).astype(f32)
    counts = jnp.sum(hits, 0).reshape(CLASSES, poses, bins)
    place = jnp.arange(box, dtype=jnp.int32)
    freq = jnp.where(place < half, place, place - box).astype(f32)
    turns = defocus[:, None] * (freq * freq)[None, :] * (1.0 / (half * half))
    turns_y = turns + ctf_phase / math.pi
    ones = jnp.ones_like(turns)
    wave_y = jnp.stack([0.5 * ones, -0.5 * turns_sine(turns_y + 0.25), 0.5 * turns_sine(turns_y)])
    wave_x = jnp.stack([ones, turns_sine(turns + 0.25), turns_sine(turns)])
    rows_own = lax.dynamic_slice_in_dim(rows_table, first_row, owned, 1)
    u = jnp.einsum("pry,mby->pmbr", squared_table(rows_own).astype(f32), wave_y, precision=exact)
    v = jnp.einsum("pxj,mbx->pmbj", squared_table(cols_table).astype(f32), wave_x, precision=exact)
    weight = counts[:, None] * plane_weight.T[None, :, :, None]
    left = weight[:, :, :, None, :, None] * u[None, None]
    return jnp.einsum("czpmbr,pmbj->rczj", left, v, precision=exact)


def by_pairs(images, class_index, pose_index, defocus_bin, defocus, rows_table, cols_table, plane_weight):
    members = lax.axis_size("img")
    rows = rows_table.shape[1]
    planes = plane_weight.shape[1]
    cols = cols_table.shape[2]
    owned = rows // members

    def exchange(value, flip):
        return lax.ppermute(value, "img", [(i, i ^ flip) for i in range(members)])

    x_send, x_keep, own_send, own_keep, z_keep, *z_sends = own_totals(
        images, class_index, pose_index, defocus_bin, defocus, rows_table, cols_table, plane_weight, members
    )
    x_came = exchange(x_send, 1)
    z_came = [exchange(send, 2 * k) for send, k in zip(z_sends, LINE)]
    tables = own_ridges(defocus, plane_weight, rows_table, cols_table, owned)
    x_keep, tables = lax.optimization_barrier((x_keep, tables))
    *x_sends, own_send, z_own, z_send = fold_phase(x_keep, x_came, own_send, z_keep, z_came)
    x_came = [exchange(send, 2 * k) for send, k in zip(x_sends, LINE)]
    own_came = exchange(own_send, 1)
    z_came = exchange(z_send, 1)
    ridge = own_weights(tables, z_own, z_came)
    out = finish(planes, ridge, own_keep, z_own, z_came, (*x_came, own_came))
    return out.reshape(owned, CLASSES, planes, 2, cols)


def by_scatter(images, class_index, pose_index, defocus_bin, defocus, rows_table, cols_table, plane_weight):
    rows = rows_table.shape[1]
    cols = cols_table.shape[2]
    planes = plane_weight.shape[1]
    members = lax.axis_size("img")
    owned = rows // members
    (totals,) = own_totals(
        images, class_index, pose_index, defocus_bin, defocus, rows_table, cols_table, plane_weight, 1
    )
    slots = totals.shape[0]
    totals = totals.reshape(slots, members, owned, 2 * cols).transpose(1, 0, 2, 3)
    own = lax.psum_scatter(totals, "img", scatter_dimension=0, tiled=False)
    weight = weight_totals(
        class_index, pose_index, defocus_bin, defocus, rows_table, cols_table, plane_weight,
        lax.axis_index("img") * owned, owned,
    )
    own = own.astype(f32).reshape(planes, CLASSES, owned, 2, cols).transpose(2, 1, 0, 3, 4)
    return own / (weight[:, :, :, None, :] + wiener_ridge)


def body(*arrays):
    rows = arrays[5].shape[1]
    members = lax.axis_size("img")
    images = members * arrays[0].shape[0]
    paired = members == 8 and images <= 256 and rows % (16 * members) == 0
    return (by_pairs if paired else by_scatter)(*arrays)


def solution(mesh):
    placed = (
        P(("groups", "img"), None, None),
        P(("groups", "img"), None),
        P(("groups", "img")),
        P(("groups", "img")),
        P(),
        P(),
        P(None, None, "slab"),
        P(),
    )
    return jax.shard_map(
        body,
        mesh=mesh,
        in_specs=placed,
        out_specs=P("img", "groups", None, None, "slab"),
        check_vma=False,
    )
```

```python
import functools
import math

import jax
import jax.numpy as jnp
import numpy as np
from jax import lax
from jax.experimental import pallas as pl
from jax.experimental.pallas import tpu as pltpu
from jax.sharding import PartitionSpec as P

CLASSES = 8

wiener_ridge = 1.0
ctf_phase = 0.1
f32 = jnp.float32
bf16 = jnp.bfloat16


def packed_dft(box, sine_sign):
    half = box // 2
    k = np.concatenate([np.arange(half), [half], np.arange(1, half)])
    angle = (k[:, None] * np.arange(box)[None, :] % box) * (2.0 * math.pi / box)
    table = np.where((np.arange(box) <= half)[:, None], np.cos(angle), sine_sign * np.sin(angle))
    return (table / math.sqrt(box)).astype(np.float32)


def iota(shape, axis):
    return lax.broadcasted_iota(jnp.int32, shape, axis)


def dot(a, b, dims=((1,), (0,))):
    return lax.dot_general(a, b, (dims, ((), ())), preferred_element_type=f32)


def turns_sine(turns):
    return jnp.sin((turns - jnp.round(turns)) * (2.0 * math.pi))


def split_two(value):
    high = value.astype(bf16)
    return high, (value - high.astype(f32)).astype(bf16)


def fold_of(place, half):
    box = 2 * half
    return jnp.where(place <= half, place, box + half - place)


def slices_kernel(
    class_hbm, pose_hbm, bin_hbm, defocus_hbm, plane_hbm,
    dft_hbm, dft_t_hbm, images_hbm, rows_hbm, cols_hbm,
    *refs,
):
    outs, refs = refs[:-SCRATCH], refs[-SCRATCH:]
    (
        class_ref, pose_ref, bin_ref, defocus_ref, plane_ref,
        dft_ref, dft_t_ref, images_ref, rows_ref, cols_ref, arrived,
        rows_fold, cols_fold, wave_y, cos_x, sin_x, half_ref, spec_ref, mix_ref, totals,
    ) = refs
    count, box, _ = images_ref.shape
    half = box // 2
    poses, rows, _ = rows_ref.shape
    cols = cols_ref.shape[2]
    planes = plane_ref.shape[0]

    pairs = (
        (class_hbm, class_ref), (pose_hbm, pose_ref), (bin_hbm, bin_ref),
        (defocus_hbm, defocus_ref), (plane_hbm, plane_ref),
        (dft_hbm, dft_ref), (images_hbm.at[0:LOAD], images_ref.at[0:LOAD]),
        (dft_t_hbm, dft_t_ref), (cols_hbm, cols_ref), (rows_hbm, rows_ref),
    ) + tuple(
        (images_hbm.at[i : i + LOAD], images_ref.at[i : i + LOAD])
        for i in range(LOAD, count, LOAD)
    )
    copies = [
        pltpu.make_async_copy(source, target, arrived.at[n])
        for n, (source, target) in enumerate(pairs)
    ]
    for copy in copies:
        copy.start()

    place = iota((box, box), 0)
    other = iota((box, box), 1)
    folded = fold_of(place, half)
    near = (folded == other).astype(f32).astype(bf16)
    far = (jnp.where(folded == 0, 0, box - folded) == other).astype(f32).astype(bf16)

    for copy in copies[:5]:
        copy.wait()
    tall, lanes = wave_y.shape
    lane = iota((1, lanes), 1)
    sub = iota((count, box), 0)
    lane_defocus = jnp.zeros((1, lanes), f32)
    sub_defocus = jnp.zeros((count, box), f32)
    for i in range(count):
        value = defocus_ref[bin_ref[i]]
        lane_defocus = jnp.where(lane % count == i, value, lane_defocus)
        sub_defocus = jnp.where(sub == i, value, sub_defocus)
    scale = 1.0 / (2 * half * half)
    ky = iota((tall, lanes), 0).astype(f32)
    quarter = jnp.where(lane < count, 0.0, 0.25) + ctf_phase / (2.0 * math.pi)
    wave_y[...] = turns_sine(lane_defocus * (ky * ky * scale) + quarter)
    kx = iota((count, box), 1)
    kx = jnp.where(kx <= half, kx, kx - half).astype(f32)
    turns = sub_defocus * (kx * kx * scale)
    cos_x[...] = -turns_sine(turns + 0.25)
    sin_x[...] = -turns_sine(turns)
    totals[...] = jnp.zeros_like(totals)
    leading = 1 if len(outs) > 1 else 0
    if len(outs) > 1:
        bins = defocus_ref.shape[0]
        count_row = iota((16, 2 * cols), 0)
        count_lane = iota((16, 2 * cols), 1)
        counts = jnp.zeros((16, 2 * cols), f32)
        for i in range(count):
            hit = (count_row == class_ref[i]) & (count_lane == pose_ref[i] * bins + bin_ref[i])
            counts = counts + jnp.where(hit, 1.0, 0.0)
        totals[0] = jnp.tile(counts, (rows // 16, 1))

    tile = 8
    tile_row = iota((tile, half), 0) == 0
    tile_col = iota((tile, half), 1) == 0
    col_zero = iota((half, half), 1) == 0
    short_row = iota((16, half), 0) == 0
    short_col = iota((16, half), 1) == 0

    def without_row(value):
        return jnp.concatenate([jnp.where(tile_row, 0.0, value[:tile]), value[tile:]], 0)

    def along_rows(i, wide):
        if i % LOAD == 0:
            copies[6 if i == 0 else 9 + i // LOAD].wait()
        group = jnp.concatenate([images_ref[i + n] for n in range(wide)], 1)
        product = dot(dft_ref[...], group).astype(bf16)
        for n in range(wide):
            place = (i + n) % GROUP * box
            half_ref[i // GROUP % 2, place : place + box] = product[:, n * box : (n + 1) * box]

    def along_columns(i):
        return dot(half_ref[i // GROUP % 2], dft_t_ref[...])

    def weigh(i, y):
        sin_col = jnp.broadcast_to(wave_y[:, i : i + 1], (tall, half))
        cos_col = jnp.broadcast_to(wave_y[:, count + i : count + i + 1], (tall, half))
        near_ctf = sin_col * cos_x[i : i + 1, :half] + cos_col * sin_x[i : i + 1, :half]
        far_ctf = sin_col * cos_x[i : i + 1, half:] + cos_col * sin_x[i : i + 1, half:]
        cc, cs = y[:half, :half], y[:half, half:]
        sc, ss = y[half:, :half], y[half:, half:]
        ss_row = without_row(ss)
        ss_in = jnp.where(col_zero, 0.0, ss_row)
        sc_in = without_row(sc)
        cs_in = jnp.where(col_zero, 0.0, cs)
        near_y, far_y = near_ctf[:half], far_ctf[:half]
        spec = spec_ref.at[i % SLOTS]
        spec[0:half, 0:half] = (near_y * (cc + ss_in)).astype(bf16)
        spec[0:half, half:] = (far_y * jnp.where(col_zero, cs, cc - ss_in)).astype(bf16)
        yield
        spec[half:box, 0:half] = (near_y * (sc_in - cs_in)).astype(bf16)
        spec[half:box, half:] = (far_y * jnp.where(col_zero, ss_row, sc_in + cs_in)).astype(bf16)
        sc_top = jnp.broadcast_to(sc[0:1], (16, half))
        ss_top = jnp.broadcast_to(ss[0:1], (16, half))
        ss_top_in = jnp.where(short_col, 0.0, ss_top)
        spec[box : box + 16, 0:half] = (
            near_ctf[half : half + 1] * jnp.where(short_row, sc_top, -ss_top_in)
        ).astype(bf16)
        spec[box : box + 16, half:] = (
            far_ctf[half : half + 1]
            * jnp.where(short_row, jnp.where(short_col, ss_top, sc_top), ss_top_in)
        ).astype(bf16)

    def mix(i):
        mixed = dot(spec_ref[i % SLOTS], cols_fold[pose_ref[i]])
        out = mix_ref.at[i % SLOTS]
        out[0:half, 0:cols] = mixed[:half, :cols].astype(bf16)
        out[0:half, cols:] = mixed[half:box, :cols].astype(bf16)
        top = iota((16, cols), 0) == 0
        real, imag = mixed[:half, cols:], -mixed[half:box, cols:]
        out[half : half + 16, 0:cols] = jnp.where(
            top, mixed[box : box + 1, :cols], real[:16]
        ).astype(bf16)
        out[half : half + 16, cols:] = jnp.where(
            top, mixed[box + 1 : box + 2, :cols], imag[:16]
        ).astype(bf16)
        out[half + 16 :, 0:cols] = real[16:].astype(bf16)
        out[half + 16 :, cols:] = imag[16:].astype(bf16)

    def insert(i):
        pose = pose_ref[i]
        pose_rows = rows_fold[pl.ds(pl.multiple_of(pose * rows, rows), rows), :]
        piece = dot(pose_rows, mix_ref[i % SLOTS])
        for z in range(planes):
            slot = leading + z * CLASSES + class_ref[i]
            totals[slot] += plane_ref[z, pose] * piece

    copies[5].wait()
    along_rows(0, LOAD)
    copies[7].wait()
    copies[8].wait()
    for p in range(0, poses, 2):
        two = jnp.concatenate([cols_ref[p], cols_ref[p + 1]], 1)
        near_two = dot(near, two).astype(bf16)
        far_two = dot(far, two).astype(bf16)
        cols_fold[p] = jnp.concatenate([near_two[:, :cols], far_two[:, :cols]], 1)
        cols_fold[p + 1] = jnp.concatenate([near_two[:, cols:], far_two[:, cols:]], 1)
    for i in range(LOAD, GROUP, LOAD):
        along_rows(i, LOAD)
    copies[9].wait()
    rows_fold[...] = dot(
        rows_ref[...].reshape(poses * rows, box), near, ((1,), (1,))
    ).astype(bf16)
    for i in range(count + 2 * LAG):
        parts = iter(())
        if i < count:
            if i % GROUP == 0:
                product = along_columns(i)
            n = i % GROUP
            parts = weigh(i, product[n * box : (n + 1) * box])
        next(parts, None)
        if 0 <= i - LAG < count:
            mix(i - LAG)
        next(parts, None)
        if i >= 2 * LAG:
            insert(i - 2 * LAG)
        if i + GROUP < count and i % 2 == 0:
            along_rows(i + GROUP, 2)

    if len(outs) == 1:
        outs[0][...] = totals[...].astype(bf16)
        return
    x_send, x_keep, own_send, own_keep, z_keep = outs[:5]
    z_sends = outs[5:]
    x_slots, owned, _ = own_keep.shape
    me = lax.axis_index("img")

    def rows_of(flip):
        return pl.ds(pl.multiple_of((me ^ flip) * owned, owned), owned)

    for n, k in enumerate(LINE):
        x_send[n] = totals[-x_slots:, rows_of(2 * k + 1), :].astype(bf16)
        x_keep[n] = totals[-x_slots:, rows_of(2 * k), :]
    own_send[...] = totals[-x_slots:, rows_of(1), :].astype(bf16)
    own_keep[...] = totals[-x_slots:, rows_of(0), :]
    for k, out in zip((0,) + LINE, (z_keep, *z_sends)):
        out[:Z_SLOTS] = totals[:Z_SLOTS, rows_of(2 * k), :].astype(out.dtype)
        out[Z_SLOTS:] = totals[1:Z_SLOTS, rows_of(2 * k + 1), :].astype(out.dtype)


SCRATCH = 20
LINE = (2, 3, 1)
SLOTS = 16
GROUP = 8
LOAD = 4
LAG = 8
Z_SLOTS = 4


def own_totals(images, class_index, pose_index, defocus_bin, defocus, rows_table, cols_table, plane_weight, members):
    count, box, _ = images.shape
    poses, rows, _ = rows_table.shape
    cols = cols_table.shape[2]
    planes = plane_weight.shape[1]
    slots = CLASSES * planes
    table_y, table_x = packed_dft(box, -1.0), packed_dft(box, 1.0)
    any_place = pl.BlockSpec(memory_space=pl.ANY)
    vmem = pl.BlockSpec(memory_space=pltpu.VMEM)
    lanes = 128 * (-(-2 * count // 128))
    if members == 1:
        out_shape = [jax.ShapeDtypeStruct((slots, rows, 2 * cols), bf16)]
    else:
        slots += 1
        tail = (rows // members, 2 * cols)
        x_slots = slots - Z_SLOTS
        out_shape = []
        for lead in ((len(LINE), x_slots), (x_slots,)):
            out_shape += [pltpu.VMEM(lead + tail, bf16), pltpu.VMEM(lead + tail, f32)]
        out_shape += [pltpu.VMEM((2 * Z_SLOTS - 1,) + tail, f32)]
        out_shape += [pltpu.VMEM((2 * Z_SLOTS - 1,) + tail, bf16)] * len(LINE)
    operands = (
        class_index[:, 0], pose_index, defocus_bin, defocus, plane_weight.T,
        jnp.asarray(table_y, bf16), jnp.asarray(table_x.T.copy(), bf16),
        images, rows_table, cols_table,
    )
    return pl.pallas_call(
        slices_kernel,
        out_shape=out_shape,
        in_specs=[any_place] * 10,
        out_specs=[vmem] * len(out_shape),
        scratch_shapes=[pltpu.SMEM(x.shape, x.dtype) for x in operands[:5]]
        + [pltpu.VMEM(x.shape, x.dtype) for x in operands[5:]]
        + [
            pltpu.SemaphoreType.DMA((9 + count // LOAD,)),
            pltpu.VMEM((poses * rows, box), bf16),
            pltpu.VMEM((poses, box, 2 * cols), bf16),
            pltpu.VMEM((box // 2 + 8, lanes), f32),
            pltpu.VMEM((count, box), f32),
            pltpu.VMEM((count, box), f32),
            pltpu.VMEM((2, GROUP * box, box), bf16),
            pltpu.VMEM((SLOTS, box + 16, box), bf16),
            pltpu.VMEM((SLOTS, box, 2 * cols), bf16),
            pltpu.VMEM((slots, rows, 2 * cols), f32),
        ],
        compiler_params=pltpu.CompilerParams(vmem_limit_bytes=VMEM_LIMIT),
        cost_estimate=pl.CostEstimate(
            flops=2 * count * box * box * 1000, bytes_accessed=6 * 1024 * 1024, transcendentals=0
        ),
    )(*operands)


VMEM_LIMIT = 56 * 1024 * 1024


def ridge_kernel(defocus_hbm, plane_hbm, rows_hbm, cols_hbm, high_ref, low_ref, share_ref, *refs):
    defocus_ref, plane_ref, rows_ref, cols_ref, arrived = refs
    poses, owned, box = rows_ref.shape
    cols = cols_ref.shape[2]
    bins = defocus_ref.shape[0]
    planes = plane_ref.shape[0]
    half = box // 2
    first = pl.multiple_of(lax.axis_index("img") * owned, owned)
    copies = [
        pltpu.make_async_copy(defocus_hbm, defocus_ref, arrived.at[0]),
        pltpu.make_async_copy(plane_hbm, plane_ref, arrived.at[1]),
        pltpu.make_async_copy(rows_hbm.at[:, pl.ds(first, owned), :], rows_ref, arrived.at[2]),
        pltpu.make_async_copy(cols_hbm, cols_ref, arrived.at[3]),
    ]
    for copy in copies:
        copy.start()
    for copy in copies:
        copy.wait()
    share_plane = iota((planes * CLASSES, poses * bins), 0) // CLASSES
    share_pose = iota((planes * CLASSES, poses * bins), 1) // bins
    share = jnp.zeros((planes * CLASSES, poses * bins), f32)
    for p in range(poses):
        for z in range(planes):
            share = jnp.where((share_plane == z) & (share_pose == p), plane_ref[z, p], share)
    share_ref[...] = share

    bin_row = iota((bins, box), 0)
    sub_defocus = jnp.zeros((bins, box), f32)
    for b in range(bins):
        sub_defocus = jnp.where(bin_row == b, defocus_ref[b], sub_defocus)
    freq = iota((bins, box), 1)
    freq = jnp.where(freq < half, freq, box - freq).astype(f32)
    turns_x = sub_defocus * (freq * freq * (1.0 / (half * half)))
    turns_y = turns_x + ctf_phase / math.pi
    ones = jnp.ones((bins, box), f32)
    wave_y = jnp.concatenate(
        [0.5 * ones, -0.5 * turns_sine(turns_y + 0.25), 0.5 * turns_sine(turns_y)], 0
    )
    wave_x = jnp.concatenate([ones, turns_sine(turns_x + 0.25), turns_sine(turns_x)], 0)
    y_high, y_low = split_two(wave_y)
    x_high, x_low = split_two(wave_x)
    rows_sq = rows_ref[...].reshape(poses * owned, box).astype(f32)
    rows_sq = (rows_sq * rows_sq).astype(bf16)
    u = dot(y_high, rows_sq, ((1,), (1,))) + dot(y_low, rows_sq, ((1,), (1,)))
    for p in range(poses):
        cols_sq = cols_ref[p].astype(f32)
        cols_sq = (cols_sq * cols_sq).astype(bf16)
        v = dot(x_high, cols_sq) + dot(x_low, cols_sq)
        for r in range(owned):
            column = u[:, p * owned + r : p * owned + r + 1]
            product = v * column
            weight = product[:bins] + product[bins : 2 * bins] + product[2 * bins :]
            high, low = split_two(weight)
            high_ref[p * bins : (p + 1) * bins, r * cols : (r + 1) * cols] = high
            low_ref[p * bins : (p + 1) * bins, r * cols : (r + 1) * cols] = low


def own_ridges(defocus, plane_weight, rows_table, cols_table, owned):
    poses, _, box = rows_table.shape
    cols = cols_table.shape[2]
    bins = defocus.shape[0]
    any_place = pl.BlockSpec(memory_space=pl.ANY)
    vmem = pl.BlockSpec(memory_space=pltpu.VMEM)
    planes = plane_weight.T
    table = pltpu.VMEM((poses * bins, owned * cols), bf16)
    return pl.pallas_call(
        ridge_kernel,
        out_shape=[table, table, pltpu.VMEM((planes.shape[0] * CLASSES, poses * bins), f32)],
        in_specs=[any_place] * 4,
        out_specs=[vmem] * 3,
        scratch_shapes=[
            pltpu.SMEM(defocus.shape, f32),
            pltpu.SMEM(planes.shape, f32),
            pltpu.VMEM((poses, owned, box), bf16),
            pltpu.VMEM(cols_table.shape, bf16),
            pltpu.SemaphoreType.DMA((4,)),
        ],
        compiler_params=pltpu.CompilerParams(vmem_limit_bytes=VMEM_LIMIT),
        cost_estimate=pl.CostEstimate(
            flops=1000, bytes_accessed=1000, transcendentals=0
        ),
    )(defocus, planes, rows_table, cols_table)


def call_in_vmem(kernel, arrays, out_shape):
    vmem = pl.BlockSpec(memory_space=pltpu.VMEM)
    return pl.pallas_call(
        kernel,
        out_shape=out_shape,
        in_specs=[vmem] * len(arrays),
        out_specs=[vmem] * len(out_shape),
        compiler_params=pltpu.CompilerParams(vmem_limit_bytes=16 * 1024 * 1024),
        cost_estimate=pl.CostEstimate(flops=1000, bytes_accessed=1000, transcendentals=0),
    )(*arrays)


def fold_kernel(x_keep, x_came, own_send, z_keep, *refs):
    z_came, refs = refs[: len(LINE)], refs[len(LINE) :]
    x_sends, own_out, z_own, z_send = refs[: len(LINE)], *refs[len(LINE) :]
    for n, send in enumerate(x_sends):
        send[...] = (x_keep[n] + x_came[n].astype(f32)).astype(bf16)
    own_out[...] = own_send[...]
    for n in range(z_keep.shape[0]):
        value = z_keep[n]
        for came in z_came:
            value = value + came[n].astype(f32)
        if n < Z_SLOTS:
            z_own[n] = value
        if n == 0:
            z_send[n] = value.astype(bf16)
        elif n >= Z_SLOTS:
            z_send[n - Z_SLOTS + 1] = value.astype(bf16)


def fold_phase(x_keep, x_came, own_send, z_keep, z_came):
    piece = own_send.shape
    z_piece = (Z_SLOTS,) + piece[1:]
    out_shape = [pltpu.VMEM(piece, bf16)] * (len(LINE) + 1)
    out_shape += [pltpu.VMEM(z_piece, f32), pltpu.VMEM(z_piece, bf16)]
    return call_in_vmem(fold_kernel, (x_keep, x_came, own_send, z_keep, *z_came), out_shape)


def weight_kernel(high_ref, low_ref, share_ref, z_own, z_came, out_ref, ridge_ref):
    slots, pairs = share_ref.shape
    owned, _, cols = ridge_ref.shape
    counts = z_own[0] + z_came[0].astype(f32)
    scaled = jnp.concatenate([counts[:CLASSES, :pairs]] * (slots // CLASSES), 0) * share_ref[...]
    c_high, c_low = split_two(scaled)
    weight = (
        dot(c_high, high_ref[...]) + dot(c_low, high_ref[...]) + dot(c_high, low_ref[...])
    )
    ridge = 1.0 / (weight + wiener_ridge)
    for r in range(owned):
        ridge_ref[r] = ridge[:, r * cols : (r + 1) * cols]
    for s in range(slots):
        out_ref[s] = ridge_ref[:, s, :]


def own_weights(tables, z_own, z_came):
    slots = tables[2].shape[0]
    _, owned, wide = z_own.shape
    cols = wide // 2
    vmem = pl.BlockSpec(memory_space=pltpu.VMEM)
    return pl.pallas_call(
        weight_kernel,
        out_shape=pltpu.VMEM((slots, owned, cols), f32),
        in_specs=[vmem] * 5,
        out_specs=vmem,
        scratch_shapes=[pltpu.VMEM((owned, slots, cols), f32)],
        compiler_params=pltpu.CompilerParams(vmem_limit_bytes=16 * 1024 * 1024),
        cost_estimate=pl.CostEstimate(flops=1000, bytes_accessed=1000, transcendentals=0),
    )(*tables, z_own, z_came)


def finish_kernel(planes, ridge_ref, x_own, z_own, z_came, *refs):
    x_came, out_ref = refs[:-1], refs[-1]
    slots, owned, cols = ridge_ref.shape
    first = z_own.shape[0]
    for s in range(slots):
        if s + 1 < first:
            value = z_own[s + 1] + z_came[s + 1].astype(f32)
        else:
            value = x_own[s + 1 - first]
            for part in x_came:
                value = value + part[s + 1 - first].astype(f32)
        factor = ridge_ref[s]
        place = (s % CLASSES) * planes + s // CLASSES
        out_ref[:, 2 * place, :] = value[:, :cols] * factor
        out_ref[:, 2 * place + 1, :] = value[:, cols:] * factor


def finish(planes, ridge, x_own, z_own, z_came, x_came):
    slots, owned, cols = ridge.shape
    vmem = pl.BlockSpec(memory_space=pltpu.VMEM)
    return pl.pallas_call(
        functools.partial(finish_kernel, planes),
        out_shape=jax.ShapeDtypeStruct((owned, 2 * slots, cols), f32),
        in_specs=[vmem] * (4 + len(x_came)),
        out_specs=vmem,
        compiler_params=pltpu.CompilerParams(vmem_limit_bytes=16 * 1024 * 1024),
        cost_estimate=pl.CostEstimate(flops=1000, bytes_accessed=1000, transcendentals=0),
    )(ridge, x_own, z_own, z_came, *x_came)


def squared_table(weight_table):
    wide_table = weight_table.astype(f32)
    return (wide_table * wide_table).astype(bf16)


def weight_totals(class_index, pose_index, defocus_bin, defocus, rows_table, cols_table, plane_weight, first_row, owned):
    box = rows_table.shape[2]
    poses = rows_table.shape[0]
    bins = defocus.shape[0]
    half = box // 2
    exact = lax.Precision.HIGHEST
    code = (class_index[:, 0] * poses + pose_index) * bins + defocus_bin
    codes = lax.all_gather(code, "img", tiled=True)
    hits = (codes[:, None] == jnp.arange(CLASSES * poses * bins, dtype=jnp.int32)).astype(f32)
    counts = jnp.sum(hits, 0).reshape(CLASSES, poses, bins)
    place = jnp.arange(box, dtype=jnp.int32)
    freq = jnp.where(place < half, place, place - box).astype(f32)
    turns = defocus[:, None] * (freq * freq)[None, :] * (1.0 / (half * half))
    turns_y = turns + ctf_phase / math.pi
    ones = jnp.ones_like(turns)
    wave_y = jnp.stack([0.5 * ones, -0.5 * turns_sine(turns_y + 0.25), 0.5 * turns_sine(turns_y)])
    wave_x = jnp.stack([ones, turns_sine(turns + 0.25), turns_sine(turns)])
    rows_own = lax.dynamic_slice_in_dim(rows_table, first_row, owned, 1)
    u = jnp.einsum("pry,mby->pmbr", squared_table(rows_own).astype(f32), wave_y, precision=exact)
    v = jnp.einsum("pxj,mbx->pmbj", squared_table(cols_table).astype(f32), wave_x, precision=exact)
    weight = counts[:, None] * plane_weight.T[None, :, :, None]
    left = weight[:, :, :, None, :, None] * u[None, None]
    return jnp.einsum("czpmbr,pmbj->rczj", left, v, precision=exact)


def by_pairs(images, class_index, pose_index, defocus_bin, defocus, rows_table, cols_table, plane_weight):
    members = lax.axis_size("img")
    rows = rows_table.shape[1]
    planes = plane_weight.shape[1]
    cols = cols_table.shape[2]
    owned = rows // members

    def exchange(value, flip):
        return lax.ppermute(value, "img", [(i, i ^ flip) for i in range(members)])

    x_send, x_keep, own_send, own_keep, z_keep, *z_sends = own_totals(
        images, class_index, pose_index, defocus_bin, defocus, rows_table, cols_table, plane_weight, members
    )
    x_came = exchange(x_send, 1)
    z_came = [exchange(send, 2 * k) for send, k in zip(z_sends, LINE)]
    tables = own_ridges(defocus, plane_weight, rows_table, cols_table, owned)
    x_keep, tables = lax.optimization_barrier((x_keep, tables))
    *x_sends, own_send, z_own, z_send = fold_phase(x_keep, x_came, own_send, z_keep, z_came)
    x_came = [exchange(send, 2 * k) for send, k in zip(x_sends, LINE)]
    own_came = exchange(own_send, 1)
    z_came = exchange(z_send, 1)
    ridge = own_weights(tables, z_own, z_came)
    out = finish(planes, ridge, own_keep, z_own, z_came, (*x_came, own_came))
    return out.reshape(owned, CLASSES, planes, 2, cols)


def by_scatter(images, class_index, pose_index, defocus_bin, defocus, rows_table, cols_table, plane_weight):
    rows = rows_table.shape[1]
    cols = cols_table.shape[2]
    planes = plane_weight.shape[1]
    members = lax.axis_size("img")
    owned = rows // members
    (totals,) = own_totals(
        images, class_index, pose_index, defocus_bin, defocus, rows_table, cols_table, plane_weight, 1
    )
    slots = totals.shape[0]
    totals = totals.reshape(slots, members, owned, 2 * cols).transpose(1, 0, 2, 3)
    own = lax.psum_scatter(totals, "img", scatter_dimension=0, tiled=False)
    weight = weight_totals(
        class_index, pose_index, defocus_bin, defocus, rows_table, cols_table, plane_weight,
        lax.axis_index("img") * owned, owned,
    )
    own = own.astype(f32).reshape(planes, CLASSES, owned, 2, cols).transpose(2, 1, 0, 3, 4)
    return own / (weight[:, :, :, None, :] + wiener_ridge)


def body(*arrays):
    rows = arrays[5].shape[1]
    members = lax.axis_size("img")
    images = members * arrays[0].shape[0]
    paired = members == 8 and images <= 256 and rows % (16 * members) == 0
    return (by_pairs if paired else by_scatter)(*arrays)


def solution(mesh):
    placed = (
        P(("groups", "img"), None, None),
        P(("groups", "img"), None),
        P(("groups", "img")),
        P(("groups", "img")),
        P(),
        P(),
        P(None, None, "slab"),
        P(),
    )
    return jax.shard_map(
        body,
        mesh=mesh,
        in_specs=placed,
        out_specs=P("img", "groups", None, None, "slab"),
        check_vma=False,
    )
```

```python
import functools
import math

import jax
import jax.numpy as jnp
import numpy as np
from jax import lax
from jax.experimental import pallas as pl
from jax.experimental.pallas import tpu as pltpu
from jax.sharding import PartitionSpec as P

CLASSES = 8

wiener_ridge = 1.0
ctf_phase = 0.1
f32 = jnp.float32
bf16 = jnp.bfloat16


def packed_dft(box, sine_sign):
    half = box // 2
    k = np.concatenate([np.arange(half), [half], np.arange(1, half)])
    angle = (k[:, None] * np.arange(box)[None, :] % box) * (2.0 * math.pi / box)
    table = np.where((np.arange(box) <= half)[:, None], np.cos(angle), sine_sign * np.sin(angle))
    return (table / math.sqrt(box)).astype(np.float32)


def iota(shape, axis):
    return lax.broadcasted_iota(jnp.int32, shape, axis)


def dot(a, b, dims=((1,), (0,))):
    return lax.dot_general(a, b, (dims, ((), ())), preferred_element_type=f32)


def turns_sine(turns):
    return jnp.sin((turns - jnp.round(turns)) * (2.0 * math.pi))


def split_two(value):
    high = value.astype(bf16)
    return high, (value - high.astype(f32)).astype(bf16)


def fold_of(place, half):
    box = 2 * half
    return jnp.where(place <= half, place, box + half - place)


def slices_kernel(
    class_hbm, pose_hbm, bin_hbm, defocus_hbm, plane_hbm,
    dft_hbm, dft_t_hbm, images_hbm, rows_hbm, cols_hbm,
    *refs,
):
    outs, refs = refs[:-SCRATCH], refs[-SCRATCH:]
    (
        class_ref, pose_ref, bin_ref, defocus_ref, plane_ref,
        dft_ref, dft_t_ref, images_ref, rows_ref, cols_ref, arrived,
        rows_fold, cols_fold, wave_y, cos_x, sin_x, half_ref, spec_ref, mix_ref, totals,
    ) = refs
    count, box, _ = images_ref.shape
    half = box // 2
    poses, rows, _ = rows_ref.shape
    cols = cols_ref.shape[2]
    planes = plane_ref.shape[0]

    pairs = (
        (class_hbm, class_ref), (pose_hbm, pose_ref), (bin_hbm, bin_ref),
        (defocus_hbm, defocus_ref), (plane_hbm, plane_ref),
        (dft_hbm, dft_ref), (images_hbm.at[0:GROUP], images_ref.at[0:GROUP]),
        (dft_t_hbm, dft_t_ref), (cols_hbm, cols_ref), (rows_hbm, rows_ref),
    ) + tuple(
        (images_hbm.at[i : i + GROUP], images_ref.at[i : i + GROUP])
        for i in range(GROUP, count, GROUP)
    )
    copies = [
        pltpu.make_async_copy(source, target, arrived.at[n])
        for n, (source, target) in enumerate(pairs)
    ]
    for copy in copies:
        copy.start()

    place = iota((box, box), 0)
    other = iota((box, box), 1)
    folded = fold_of(place, half)
    near = (folded == other).astype(f32).astype(bf16)
    far = (jnp.where(folded == 0, 0, box - folded) == other).astype(f32).astype(bf16)

    for copy in copies[:5]:
        copy.wait()
    tall, lanes = wave_y.shape
    lane = iota((1, lanes), 1)
    sub = iota((count, box), 0)
    lane_defocus = jnp.zeros((1, lanes), f32)
    sub_defocus = jnp.zeros((count, box), f32)
    for i in range(count):
        value = defocus_ref[bin_ref[i]]
        lane_defocus = jnp.where(lane % count == i, value, lane_defocus)
        sub_defocus = jnp.where(sub == i, value, sub_defocus)
    scale = 1.0 / (2 * half * half)
    ky = iota((tall, lanes), 0).astype(f32)
    quarter = jnp.where(lane < count, 0.0, 0.25) + ctf_phase / (2.0 * math.pi)
    wave_y[...] = turns_sine(lane_defocus * (ky * ky * scale) + quarter)
    kx = iota((count, box), 1)
    kx = jnp.where(kx <= half, kx, kx - half).astype(f32)
    turns = sub_defocus * (kx * kx * scale)
    cos_x[...] = -turns_sine(turns + 0.25)
    sin_x[...] = -turns_sine(turns)
    totals[...] = jnp.zeros_like(totals)
    leading = 1 if len(outs) > 1 else 0
    if len(outs) > 1:
        bins = defocus_ref.shape[0]
        count_row = iota((16, 2 * cols), 0)
        count_lane = iota((16, 2 * cols), 1)
        counts = jnp.zeros((16, 2 * cols), f32)
        for i in range(count):
            hit = (count_row == class_ref[i]) & (count_lane == pose_ref[i] * bins + bin_ref[i])
            counts = counts + jnp.where(hit, 1.0, 0.0)
        totals[0] = jnp.tile(counts, (rows // 16, 1))

    tile = 8
    tile_row = iota((tile, half), 0) == 0
    tile_col = iota((tile, half), 1) == 0
    col_zero = iota((half, half), 1) == 0
    short_row = iota((16, half), 0) == 0
    short_col = iota((16, half), 1) == 0

    def without_row(value):
        return jnp.concatenate([jnp.where(tile_row, 0.0, value[:tile]), value[tile:]], 0)

    def along_rows(i, wide):
        if i % GROUP == 0:
            copies[6 if i == 0 else 9 + i // GROUP].wait()
        group = jnp.concatenate([images_ref[i + n] for n in range(wide)], 1)
        product = dot(dft_ref[...], group).astype(bf16)
        for n in range(wide):
            place = (i + n) % GROUP * box
            half_ref[i // GROUP % 2, place : place + box] = product[:, n * box : (n + 1) * box]

    def along_columns(i):
        return dot(half_ref[i // GROUP % 2], dft_t_ref[...])

    def weigh(i, y):
        sin_col = jnp.broadcast_to(wave_y[:, i : i + 1], (tall, half))
        cos_col = jnp.broadcast_to(wave_y[:, count + i : count + i + 1], (tall, half))
        near_ctf = sin_col * cos_x[i : i + 1, :half] + cos_col * sin_x[i : i + 1, :half]
        far_ctf = sin_col * cos_x[i : i + 1, half:] + cos_col * sin_x[i : i + 1, half:]
        cc, cs = y[:half, :half], y[:half, half:]
        sc, ss = y[half:, :half], y[half:, half:]
        ss_row = without_row(ss)
        ss_in = jnp.where(col_zero, 0.0, ss_row)
        sc_in = without_row(sc)
        cs_in = jnp.where(col_zero, 0.0, cs)
        near_y, far_y = near_ctf[:half], far_ctf[:half]
        spec = spec_ref.at[i % SLOTS]
        spec[0:half, 0:half] = (near_y * (cc + ss_in)).astype(bf16)
        spec[0:half, half:] = (far_y * jnp.where(col_zero, cs, cc - ss_in)).astype(bf16)
        yield
        spec[half:box, 0:half] = (near_y * (sc_in - cs_in)).astype(bf16)
        spec[half:box, half:] = (far_y * jnp.where(col_zero, ss_row, sc_in + cs_in)).astype(bf16)
        sc_top = jnp.broadcast_to(sc[0:1], (16, half))
        ss_top = jnp.broadcast_to(ss[0:1], (16, half))
        ss_top_in = jnp.where(short_col, 0.0, ss_top)
        spec[box : box + 16, 0:half] = (
            near_ctf[half : half + 1] * jnp.where(short_row, sc_top, -ss_top_in)
        ).astype(bf16)
        spec[box : box + 16, half:] = (
            far_ctf[half : half + 1]
            * jnp.where(short_row, jnp.where(short_col, ss_top, sc_top), ss_top_in)
        ).astype(bf16)

    def mix(i):
        mixed = dot(spec_ref[i % SLOTS], cols_fold[pose_ref[i]])
        out = mix_ref.at[i % SLOTS]
        out[0:half, 0:cols] = mixed[:half, :cols].astype(bf16)
        out[0:half, cols:] = mixed[half:box, :cols].astype(bf16)
        top = iota((16, cols), 0) == 0
        real, imag = mixed[:half, cols:], -mixed[half:box, cols:]
        out[half : half + 16, 0:cols] = jnp.where(
            top, mixed[box : box + 1, :cols], real[:16]
        ).astype(bf16)
        out[half : half + 16, cols:] = jnp.where(
            top, mixed[box + 1 : box + 2, :cols], imag[:16]
        ).astype(bf16)
        out[half + 16 :, 0:cols] = real[16:].astype(bf16)
        out[half + 16 :, cols:] = imag[16:].astype(bf16)

    def insert(i):
        pose = pose_ref[i]
        pose_rows = rows_fold[pl.ds(pl.multiple_of(pose * rows, rows), rows), :]
        piece = dot(pose_rows, mix_ref[i % SLOTS])
        for z in range(planes):
            slot = leading + z * CLASSES + class_ref[i]
            totals[slot] += plane_ref[z, pose] * piece

    copies[5].wait()
    along_rows(0, GROUP)
    copies[7].wait()
    copies[8].wait()
    for p in range(0, poses, 2):
        two = jnp.concatenate([cols_ref[p], cols_ref[p + 1]], 1)
        near_two = dot(near, two).astype(bf16)
        far_two = dot(far, two).astype(bf16)
        cols_fold[p] = jnp.concatenate([near_two[:, :cols], far_two[:, :cols]], 1)
        cols_fold[p + 1] = jnp.concatenate([near_two[:, cols:], far_two[:, cols:]], 1)
    copies[9].wait()
    rows_fold[...] = dot(
        rows_ref[...].reshape(poses * rows, box), near, ((1,), (1,))
    ).astype(bf16)
    for step in range(GROUP, count + 3 * GROUP, GROUP):
        if step - GROUP < count:
            product = along_columns(step - GROUP)
        for n in range(GROUP):
            parts = iter(())
            if step - GROUP < count:
                parts = weigh(step - GROUP + n, product[n * box : (n + 1) * box])
            next(parts, None)
            if 0 <= step - 2 * GROUP < count:
                mix(step - 2 * GROUP + n)
            next(parts, None)
            if step >= 3 * GROUP:
                insert(step - 3 * GROUP + n)
            if step < count and n % 2 == 0:
                along_rows(step + n, 2)

    if len(outs) == 1:
        outs[0][...] = totals[...].astype(bf16)
        return
    x_send, x_keep, own_send, own_keep, z_keep = outs[:5]
    z_sends = outs[5:]
    x_slots, owned, _ = own_keep.shape
    me = lax.axis_index("img")

    def rows_of(flip):
        return pl.ds(pl.multiple_of((me ^ flip) * owned, owned), owned)

    for n, k in enumerate(LINE):
        x_send[n] = totals[-x_slots:, rows_of(2 * k + 1), :].astype(bf16)
        x_keep[n] = totals[-x_slots:, rows_of(2 * k), :]
    own_send[...] = totals[-x_slots:, rows_of(1), :].astype(bf16)
    own_keep[...] = totals[-x_slots:, rows_of(0), :]
    for k, out in zip((0,) + LINE, (z_keep, *z_sends)):
        out[:Z_SLOTS] = totals[:Z_SLOTS, rows_of(2 * k), :].astype(out.dtype)
        out[Z_SLOTS:] = totals[1:Z_SLOTS, rows_of(2 * k + 1), :].astype(out.dtype)


SCRATCH = 20
LINE = (2, 3, 1)
SLOTS = 16
GROUP = 16
Z_SLOTS = 4


def own_totals(images, class_index, pose_index, defocus_bin, defocus, rows_table, cols_table, plane_weight, members):
    count, box, _ = images.shape
    poses, rows, _ = rows_table.shape
    cols = cols_table.shape[2]
    planes = plane_weight.shape[1]
    slots = CLASSES * planes
    table_y, table_x = packed_dft(box, -1.0), packed_dft(box, 1.0)
    any_place = pl.BlockSpec(memory_space=pl.ANY)
    vmem = pl.BlockSpec(memory_space=pltpu.VMEM)
    lanes = 128 * (-(-2 * count // 128))
    if members == 1:
        out_shape = [jax.ShapeDtypeStruct((slots, rows, 2 * cols), bf16)]
    else:
        slots += 1
        tail = (rows // members, 2 * cols)
        x_slots = slots - Z_SLOTS
        out_shape = []
        for lead in ((len(LINE), x_slots), (x_slots,)):
            out_shape += [pltpu.VMEM(lead + tail, bf16), pltpu.VMEM(lead + tail, f32)]
        out_shape += [pltpu.VMEM((2 * Z_SLOTS - 1,) + tail, f32)]
        out_shape += [pltpu.VMEM((2 * Z_SLOTS - 1,) + tail, bf16)] * len(LINE)
    operands = (
        class_index[:, 0], pose_index, defocus_bin, defocus, plane_weight.T,
        jnp.asarray(table_y, bf16), jnp.asarray(table_x.T.copy(), bf16),
        images, rows_table, cols_table,
    )
    return pl.pallas_call(
        slices_kernel,
        out_shape=out_shape,
        in_specs=[any_place] * 10,
        out_specs=[vmem] * len(out_shape),
        scratch_shapes=[pltpu.SMEM(x.shape, x.dtype) for x in operands[:5]]
        + [pltpu.VMEM(x.shape, x.dtype) for x in operands[5:]]
        + [
            pltpu.SemaphoreType.DMA((9 + count // GROUP,)),
            pltpu.VMEM((poses * rows, box), bf16),
            pltpu.VMEM((poses, box, 2 * cols), bf16),
            pltpu.VMEM((box // 2 + 8, lanes), f32),
            pltpu.VMEM((count, box), f32),
            pltpu.VMEM((count, box), f32),
            pltpu.VMEM((2, GROUP * box, box), bf16),
            pltpu.VMEM((SLOTS, box + 16, box), bf16),
            pltpu.VMEM((SLOTS, box, 2 * cols), bf16),
            pltpu.VMEM((slots, rows, 2 * cols), f32),
        ],
        compiler_params=pltpu.CompilerParams(vmem_limit_bytes=VMEM_LIMIT),
        cost_estimate=pl.CostEstimate(
            flops=2 * count * box * box * 1000, bytes_accessed=6 * 1024 * 1024, transcendentals=0
        ),
    )(*operands)


VMEM_LIMIT = 56 * 1024 * 1024


def ridge_kernel(defocus_hbm, plane_hbm, rows_hbm, cols_hbm, high_ref, low_ref, share_ref, *refs):
    defocus_ref, plane_ref, rows_ref, cols_ref, arrived = refs
    poses, owned, box = rows_ref.shape
    cols = cols_ref.shape[2]
    bins = defocus_ref.shape[0]
    planes = plane_ref.shape[0]
    half = box // 2
    first = pl.multiple_of(lax.axis_index("img") * owned, owned)
    copies = [
        pltpu.make_async_copy(defocus_hbm, defocus_ref, arrived.at[0]),
        pltpu.make_async_copy(plane_hbm, plane_ref, arrived.at[1]),
        pltpu.make_async_copy(rows_hbm.at[:, pl.ds(first, owned), :], rows_ref, arrived.at[2]),
        pltpu.make_async_copy(cols_hbm, cols_ref, arrived.at[3]),
    ]
    for copy in copies:
        copy.start()
    for copy in copies:
        copy.wait()
    share_plane = iota((planes * CLASSES, poses * bins), 0) // CLASSES
    share_pose = iota((planes * CLASSES, poses * bins), 1) // bins
    share = jnp.zeros((planes * CLASSES, poses * bins), f32)
    for p in range(poses):
        for z in range(planes):
            share = jnp.where((share_plane == z) & (share_pose == p), plane_ref[z, p], share)
    share_ref[...] = share

    bin_row = iota((bins, box), 0)
    sub_defocus = jnp.zeros((bins, box), f32)
    for b in range(bins):
        sub_defocus = jnp.where(bin_row == b, defocus_ref[b], sub_defocus)
    freq = iota((bins, box), 1)
    freq = jnp.where(freq < half, freq, box - freq).astype(f32)
    turns_x = sub_defocus * (freq * freq * (1.0 / (half * half)))
    turns_y = turns_x + ctf_phase / math.pi
    ones = jnp.ones((bins, box), f32)
    wave_y = jnp.concatenate(
        [0.5 * ones, -0.5 * turns_sine(turns_y + 0.25), 0.5 * turns_sine(turns_y)], 0
    )
    wave_x = jnp.concatenate([ones, turns_sine(turns_x + 0.25), turns_sine(turns_x)], 0)
    y_high, y_low = split_two(wave_y)
    x_high, x_low = split_two(wave_x)
    rows_sq = rows_ref[...].reshape(poses * owned, box).astype(f32)
    rows_sq = (rows_sq * rows_sq).astype(bf16)
    u = dot(y_high, rows_sq, ((1,), (1,))) + dot(y_low, rows_sq, ((1,), (1,)))
    for p in range(poses):
        cols_sq = cols_ref[p].astype(f32)
        cols_sq = (cols_sq * cols_sq).astype(bf16)
        v = dot(x_high, cols_sq) + dot(x_low, cols_sq)
        for r in range(owned):
            column = u[:, p * owned + r : p * owned + r + 1]
            product = v * column
            weight = product[:bins] + product[bins : 2 * bins] + product[2 * bins :]
            high, low = split_two(weight)
            high_ref[p * bins : (p + 1) * bins, r * cols : (r + 1) * cols] = high
            low_ref[p * bins : (p + 1) * bins, r * cols : (r + 1) * cols] = low


def own_ridges(defocus, plane_weight, rows_table, cols_table, owned):
    poses, _, box = rows_table.shape
    cols = cols_table.shape[2]
    bins = defocus.shape[0]
    any_place = pl.BlockSpec(memory_space=pl.ANY)
    vmem = pl.BlockSpec(memory_space=pltpu.VMEM)
    planes = plane_weight.T
    table = pltpu.VMEM((poses * bins, owned * cols), bf16)
    return pl.pallas_call(
        ridge_kernel,
        out_shape=[table, table, pltpu.VMEM((planes.shape[0] * CLASSES, poses * bins), f32)],
        in_specs=[any_place] * 4,
        out_specs=[vmem] * 3,
        scratch_shapes=[
            pltpu.SMEM(defocus.shape, f32),
            pltpu.SMEM(planes.shape, f32),
            pltpu.VMEM((poses, owned, box), bf16),
            pltpu.VMEM(cols_table.shape, bf16),
            pltpu.SemaphoreType.DMA((4,)),
        ],
        compiler_params=pltpu.CompilerParams(vmem_limit_bytes=VMEM_LIMIT),
        cost_estimate=pl.CostEstimate(
            flops=1000, bytes_accessed=1000, transcendentals=0
        ),
    )(defocus, planes, rows_table, cols_table)


def call_in_vmem(kernel, arrays, out_shape):
    vmem = pl.BlockSpec(memory_space=pltpu.VMEM)
    return pl.pallas_call(
        kernel,
        out_shape=out_shape,
        in_specs=[vmem] * len(arrays),
        out_specs=[vmem] * len(out_shape),
        compiler_params=pltpu.CompilerParams(vmem_limit_bytes=16 * 1024 * 1024),
        cost_estimate=pl.CostEstimate(flops=1000, bytes_accessed=1000, transcendentals=0),
    )(*arrays)


def fold_kernel(x_keep, x_came, own_send, z_keep, *refs):
    z_came, refs = refs[: len(LINE)], refs[len(LINE) :]
    x_sends, own_out, z_own, z_send = refs[: len(LINE)], *refs[len(LINE) :]
    for n, send in enumerate(x_sends):
        send[...] = (x_keep[n] + x_came[n].astype(f32)).astype(bf16)
    own_out[...] = own_send[...]
    for n in range(z_keep.shape[0]):
        value = z_keep[n]
        for came in z_came:
            value = value + came[n].astype(f32)
        if n < Z_SLOTS:
            z_own[n] = value
        if n == 0:
            z_send[n] = value.astype(bf16)
        elif n >= Z_SLOTS:
            z_send[n - Z_SLOTS + 1] = value.astype(bf16)


def fold_phase(x_keep, x_came, own_send, z_keep, z_came):
    piece = own_send.shape
    z_piece = (Z_SLOTS,) + piece[1:]
    out_shape = [pltpu.VMEM(piece, bf16)] * (len(LINE) + 1)
    out_shape += [pltpu.VMEM(z_piece, f32), pltpu.VMEM(z_piece, bf16)]
    return call_in_vmem(fold_kernel, (x_keep, x_came, own_send, z_keep, *z_came), out_shape)


def weight_kernel(high_ref, low_ref, share_ref, z_own, z_came, out_ref, ridge_ref):
    slots, pairs = share_ref.shape
    owned, _, cols = ridge_ref.shape
    counts = z_own[0] + z_came[0].astype(f32)
    scaled = jnp.concatenate([counts[:CLASSES, :pairs]] * (slots // CLASSES), 0) * share_ref[...]
    c_high, c_low = split_two(scaled)
    weight = (
        dot(c_high, high_ref[...]) + dot(c_low, high_ref[...]) + dot(c_high, low_ref[...])
    )
    ridge = 1.0 / (weight + wiener_ridge)
    for r in range(owned):
        ridge_ref[r] = ridge[:, r * cols : (r + 1) * cols]
    for s in range(slots):
        out_ref[s] = ridge_ref[:, s, :]


def own_weights(tables, z_own, z_came):
    slots = tables[2].shape[0]
    _, owned, wide = z_own.shape
    cols = wide // 2
    vmem = pl.BlockSpec(memory_space=pltpu.VMEM)
    return pl.pallas_call(
        weight_kernel,
        out_shape=pltpu.VMEM((slots, owned, cols), f32),
        in_specs=[vmem] * 5,
        out_specs=vmem,
        scratch_shapes=[pltpu.VMEM((owned, slots, cols), f32)],
        compiler_params=pltpu.CompilerParams(vmem_limit_bytes=16 * 1024 * 1024),
        cost_estimate=pl.CostEstimate(flops=1000, bytes_accessed=1000, transcendentals=0),
    )(*tables, z_own, z_came)


def finish_kernel(planes, ridge_ref, x_own, z_own, z_came, *refs):
    x_came, out_ref = refs[:-1], refs[-1]
    slots, owned, cols = ridge_ref.shape
    first = z_own.shape[0]
    for s in range(slots):
        if s + 1 < first:
            value = z_own[s + 1] + z_came[s + 1].astype(f32)
        else:
            value = x_own[s + 1 - first]
            for part in x_came:
                value = value + part[s + 1 - first].astype(f32)
        factor = ridge_ref[s]
        place = (s % CLASSES) * planes + s // CLASSES
        out_ref[:, 2 * place, :] = value[:, :cols] * factor
        out_ref[:, 2 * place + 1, :] = value[:, cols:] * factor


def finish(planes, ridge, x_own, z_own, z_came, x_came):
    slots, owned, cols = ridge.shape
    vmem = pl.BlockSpec(memory_space=pltpu.VMEM)
    return pl.pallas_call(
        functools.partial(finish_kernel, planes),
        out_shape=jax.ShapeDtypeStruct((owned, 2 * slots, cols), f32),
        in_specs=[vmem] * (4 + len(x_came)),
        out_specs=vmem,
        compiler_params=pltpu.CompilerParams(vmem_limit_bytes=16 * 1024 * 1024),
        cost_estimate=pl.CostEstimate(flops=1000, bytes_accessed=1000, transcendentals=0),
    )(ridge, x_own, z_own, z_came, *x_came)


def squared_table(weight_table):
    wide_table = weight_table.astype(f32)
    return (wide_table * wide_table).astype(bf16)


def weight_totals(class_index, pose_index, defocus_bin, defocus, rows_table, cols_table, plane_weight, first_row, owned):
    box = rows_table.shape[2]
    poses = rows_table.shape[0]
    bins = defocus.shape[0]
    half = box // 2
    exact = lax.Precision.HIGHEST
    code = (class_index[:, 0] * poses + pose_index) * bins + defocus_bin
    codes = lax.all_gather(code, "img", tiled=True)
    hits = (codes[:, None] == jnp.arange(CLASSES * poses * bins, dtype=jnp.int32)).astype(f32)
    counts = jnp.sum(hits, 0).reshape(CLASSES, poses, bins)
    place = jnp.arange(box, dtype=jnp.int32)
    freq = jnp.where(place < half, place, place - box).astype(f32)
    turns = defocus[:, None] * (freq * freq)[None, :] * (1.0 / (half * half))
    turns_y = turns + ctf_phase / math.pi
    ones = jnp.ones_like(turns)
    wave_y = jnp.stack([0.5 * ones, -0.5 * turns_sine(turns_y + 0.25), 0.5 * turns_sine(turns_y)])
    wave_x = jnp.stack([ones, turns_sine(turns + 0.25), turns_sine(turns)])
    rows_own = lax.dynamic_slice_in_dim(rows_table, first_row, owned, 1)
    u = jnp.einsum("pry,mby->pmbr", squared_table(rows_own).astype(f32), wave_y, precision=exact)
    v = jnp.einsum("pxj,mbx->pmbj", squared_table(cols_table).astype(f32), wave_x, precision=exact)
    weight = counts[:, None] * plane_weight.T[None, :, :, None]
    left = weight[:, :, :, None, :, None] * u[None, None]
    return jnp.einsum("czpmbr,pmbj->rczj", left, v, precision=exact)


def by_pairs(images, class_index, pose_index, defocus_bin, defocus, rows_table, cols_table, plane_weight):
    members = lax.axis_size("img")
    rows = rows_table.shape[1]
    planes = plane_weight.shape[1]
    cols = cols_table.shape[2]
    owned = rows // members

    def exchange(value, flip):
        return lax.ppermute(value, "img", [(i, i ^ flip) for i in range(members)])

    x_send, x_keep, own_send, own_keep, z_keep, *z_sends = own_totals(
        images, class_index, pose_index, defocus_bin, defocus, rows_table, cols_table, plane_weight, members
    )
    x_came = exchange(x_send, 1)
    z_came = [exchange(send, 2 * k) for send, k in zip(z_sends, LINE)]
    tables = own_ridges(defocus, plane_weight, rows_table, cols_table, owned)
    x_keep, tables = lax.optimization_barrier((x_keep, tables))
    *x_sends, own_send, z_own, z_send = fold_phase(x_keep, x_came, own_send, z_keep, z_came)
    x_came = [exchange(send, 2 * k) for send, k in zip(x_sends, LINE)]
    own_came = exchange(own_send, 1)
    z_came = exchange(z_send, 1)
    ridge = own_weights(tables, z_own, z_came)
    out = finish(planes, ridge, own_keep, z_own, z_came, (*x_came, own_came))
    return out.reshape(owned, CLASSES, planes, 2, cols)


def by_scatter(images, class_index, pose_index, defocus_bin, defocus, rows_table, cols_table, plane_weight):
    rows = rows_table.shape[1]
    cols = cols_table.shape[2]
    planes = plane_weight.shape[1]
    members = lax.axis_size("img")
    owned = rows // members
    (totals,) = own_totals(
        images, class_index, pose_index, defocus_bin, defocus, rows_table, cols_table, plane_weight, 1
    )
    slots = totals.shape[0]
    totals = totals.reshape(slots, members, owned, 2 * cols).transpose(1, 0, 2, 3)
    own = lax.psum_scatter(totals, "img", scatter_dimension=0, tiled=False)
    weight = weight_totals(
        class_index, pose_index, defocus_bin, defocus, rows_table, cols_table, plane_weight,
        lax.axis_index("img") * owned, owned,
    )
    own = own.astype(f32).reshape(planes, CLASSES, owned, 2, cols).transpose(2, 1, 0, 3, 4)
    return own / (weight[:, :, :, None, :] + wiener_ridge)


def body(*arrays):
    rows = arrays[5].shape[1]
    members = lax.axis_size("img")
    images = members * arrays[0].shape[0]
    paired = members == 8 and images <= 256 and rows % (16 * members) == 0
    return (by_pairs if paired else by_scatter)(*arrays)


def solution(mesh):
    placed = (
        P(("groups", "img"), None, None),
        P(("groups", "img"), None),
        P(("groups", "img")),
        P(("groups", "img")),
        P(),
        P(),
        P(None, None, "slab"),
        P(),
    )
    return jax.shard_map(
        body,
        mesh=mesh,
        in_specs=placed,
        out_specs=P("img", "groups", None, None, "slab"),
        check_vma=False,
    )
```

```python
import functools
import math

import jax
import jax.numpy as jnp
import numpy as np
from jax import lax
from jax.experimental import pallas as pl
from jax.experimental.pallas import tpu as pltpu
from jax.sharding import PartitionSpec as P

CLASSES = 8

wiener_ridge = 1.0
ctf_phase = 0.1
f32 = jnp.float32
bf16 = jnp.bfloat16


def packed_dft(box, sine_sign):
    half = box // 2
    k = np.concatenate([np.arange(half), [half], np.arange(1, half)])
    angle = (k[:, None] * np.arange(box)[None, :] % box) * (2.0 * math.pi / box)
    table = np.where((np.arange(box) <= half)[:, None], np.cos(angle), sine_sign * np.sin(angle))
    return (table / math.sqrt(box)).astype(np.float32)


def iota(shape, axis):
    return lax.broadcasted_iota(jnp.int32, shape, axis)


def dot(a, b, dims=((1,), (0,))):
    return lax.dot_general(a, b, (dims, ((), ())), preferred_element_type=f32)


def turns_sine(turns):
    return jnp.sin((turns - jnp.round(turns)) * (2.0 * math.pi))


def split_two(value):
    high = value.astype(bf16)
    return high, (value - high.astype(f32)).astype(bf16)


def fold_of(place, half):
    box = 2 * half
    return jnp.where(place <= half, place, box + half - place)


def slices_kernel(
    class_hbm, pose_hbm, bin_hbm, defocus_hbm, plane_hbm,
    dft_hbm, dft_t_hbm, images_hbm, rows_hbm, cols_hbm,
    *refs,
):
    outs, refs = refs[:-SCRATCH], refs[-SCRATCH:]
    (
        class_ref, pose_ref, bin_ref, defocus_ref, plane_ref,
        dft_ref, dft_t_ref, images_ref, rows_ref, cols_ref, arrived,
        rows_fold, cols_fold, wave_y, cos_x, sin_x, half_ref, spec_ref, mix_ref, totals,
    ) = refs
    count, box, _ = images_ref.shape
    half = box // 2
    poses, rows, _ = rows_ref.shape
    cols = cols_ref.shape[2]
    planes = plane_ref.shape[0]

    pairs = (
        (class_hbm, class_ref), (pose_hbm, pose_ref), (bin_hbm, bin_ref),
        (defocus_hbm, defocus_ref), (plane_hbm, plane_ref),
        (dft_hbm, dft_ref), (images_hbm.at[0:GROUP], images_ref.at[0:GROUP]),
        (dft_t_hbm, dft_t_ref), (cols_hbm, cols_ref), (rows_hbm, rows_ref),
    ) + tuple(
        (images_hbm.at[i : i + GROUP], images_ref.at[i : i + GROUP])
        for i in range(GROUP, count, GROUP)
    )
    copies = [
        pltpu.make_async_copy(source, target, arrived.at[n])
        for n, (source, target) in enumerate(pairs)
    ]
    for copy in copies:
        copy.start()

    place = iota((box, box), 0)
    other = iota((box, box), 1)
    folded = fold_of(place, half)
    near = (folded == other).astype(f32).astype(bf16)
    far = (jnp.where(folded == 0, 0, box - folded) == other).astype(f32).astype(bf16)

    for copy in copies[:5]:
        copy.wait()
    tall, lanes = wave_y.shape
    lane = iota((1, lanes), 1)
    sub = iota((count, box), 0)
    lane_defocus = jnp.zeros((1, lanes), f32)
    sub_defocus = jnp.zeros((count, box), f32)
    for i in range(count):
        value = defocus_ref[bin_ref[i]]
        lane_defocus = jnp.where(lane % count == i, value, lane_defocus)
        sub_defocus = jnp.where(sub == i, value, sub_defocus)
    scale = 1.0 / (2 * half * half)
    ky = iota((tall, lanes), 0).astype(f32)
    quarter = jnp.where(lane < count, 0.0, 0.25) + ctf_phase / (2.0 * math.pi)
    wave_y[...] = turns_sine(lane_defocus * (ky * ky * scale) + quarter)
    kx = iota((count, box), 1)
    kx = jnp.where(kx <= half, kx, kx - half).astype(f32)
    turns = sub_defocus * (kx * kx * scale)
    cos_x[...] = -turns_sine(turns + 0.25)
    sin_x[...] = -turns_sine(turns)
    totals[...] = jnp.zeros_like(totals)
    leading = 1 if len(outs) > 1 else 0
    if len(outs) > 1:
        bins = defocus_ref.shape[0]
        count_row = iota((16, 2 * cols), 0)
        count_lane = iota((16, 2 * cols), 1)
        counts = jnp.zeros((16, 2 * cols), f32)
        for i in range(count):
            hit = (count_row == class_ref[i]) & (count_lane == pose_ref[i] * bins + bin_ref[i])
            counts = counts + jnp.where(hit, 1.0, 0.0)
        totals[0] = jnp.tile(counts, (rows // 16, 1))

    tile = 8
    tile_row = iota((tile, half), 0) == 0
    tile_col = iota((tile, half), 1) == 0
    col_zero = iota((half, half), 1) == 0
    short_row = iota((16, half), 0) == 0
    short_col = iota((16, half), 1) == 0

    def without_row(value):
        return jnp.concatenate([jnp.where(tile_row, 0.0, value[:tile]), value[tile:]], 0)

    def along_rows(i, wide):
        if i % GROUP == 0:
            copies[6 if i == 0 else 9 + i // GROUP].wait()
        group = jnp.concatenate([images_ref[i + n] for n in range(wide)], 1)
        product = dot(dft_ref[...], group).astype(bf16)
        for n in range(wide):
            place = (i + n) % GROUP * box
            half_ref[i // GROUP % 2, place : place + box] = product[:, n * box : (n + 1) * box]

    def along_columns(i):
        return dot(half_ref[i // GROUP % 2], dft_t_ref[...])

    def weigh(i, y):
        sin_col = jnp.broadcast_to(wave_y[:, i : i + 1], (tall, half))
        cos_col = jnp.broadcast_to(wave_y[:, count + i : count + i + 1], (tall, half))
        near_ctf = sin_col * cos_x[i : i + 1, :half] + cos_col * sin_x[i : i + 1, :half]
        far_ctf = sin_col * cos_x[i : i + 1, half:] + cos_col * sin_x[i : i + 1, half:]
        cc, cs = y[:half, :half], y[:half, half:]
        sc, ss = y[half:, :half], y[half:, half:]
        ss_row = without_row(ss)
        ss_in = jnp.where(col_zero, 0.0, ss_row)
        sc_in = without_row(sc)
        cs_in = jnp.where(col_zero, 0.0, cs)
        near_y, far_y = near_ctf[:half], far_ctf[:half]
        spec = spec_ref.at[i % SLOTS]
        spec[0:half, 0:half] = (near_y * (cc + ss_in)).astype(bf16)
        spec[0:half, half:] = (far_y * jnp.where(col_zero, cs, cc - ss_in)).astype(bf16)
        yield
        spec[half:box, 0:half] = (near_y * (sc_in - cs_in)).astype(bf16)
        spec[half:box, half:] = (far_y * jnp.where(col_zero, ss_row, sc_in + cs_in)).astype(bf16)
        sc_top = jnp.broadcast_to(sc[0:1], (16, half))
        ss_top = jnp.broadcast_to(ss[0:1], (16, half))
        ss_top_in = jnp.where(short_col, 0.0, ss_top)
        spec[box : box + 16, 0:half] = (
            near_ctf[half : half + 1] * jnp.where(short_row, sc_top, -ss_top_in)
        ).astype(bf16)
        spec[box : box + 16, half:] = (
            far_ctf[half : half + 1]
            * jnp.where(short_row, jnp.where(short_col, ss_top, sc_top), ss_top_in)
        ).astype(bf16)

    def mix(i):
        mixed = dot(spec_ref[i % SLOTS], cols_fold[pose_ref[i]])
        out = mix_ref.at[i % SLOTS]
        out[0:half, 0:cols] = mixed[:half, :cols].astype(bf16)
        out[0:half, cols:] = mixed[half:box, :cols].astype(bf16)
        top = iota((16, cols), 0) == 0
        real, imag = mixed[:half, cols:], -mixed[half:box, cols:]
        out[half : half + 16, 0:cols] = jnp.where(
            top, mixed[box : box + 1, :cols], real[:16]
        ).astype(bf16)
        out[half : half + 16, cols:] = jnp.where(
            top, mixed[box + 1 : box + 2, :cols], imag[:16]
        ).astype(bf16)
        out[half + 16 :, 0:cols] = real[16:].astype(bf16)
        out[half + 16 :, cols:] = imag[16:].astype(bf16)

    def insert(i):
        pose = pose_ref[i]
        pose_rows = rows_fold[pl.ds(pl.multiple_of(pose * rows, rows), rows), :]
        piece = dot(pose_rows, mix_ref[i % SLOTS])
        for z in range(planes):
            slot = leading + z * CLASSES + class_ref[i]
            totals[slot] += plane_ref[z, pose] * piece

    copies[5].wait()
    along_rows(0, GROUP)
    copies[7].wait()
    copies[8].wait()
    for p in range(0, poses, 2):
        two = jnp.concatenate([cols_ref[p], cols_ref[p + 1]], 1)
        near_two = dot(near, two).astype(bf16)
        far_two = dot(far, two).astype(bf16)
        cols_fold[p] = jnp.concatenate([near_two[:, :cols], far_two[:, :cols]], 1)
        cols_fold[p + 1] = jnp.concatenate([near_two[:, cols:], far_two[:, cols:]], 1)
    copies[9].wait()
    rows_fold[...] = dot(
        rows_ref[...].reshape(poses * rows, box), near, ((1,), (1,))
    ).astype(bf16)
    for step in range(GROUP, count + 3 * GROUP, GROUP):
        if step - GROUP < count:
            product = along_columns(step - GROUP)
        for n in range(GROUP):
            parts = iter(())
            if step - GROUP < count:
                parts = weigh(step - GROUP + n, product[n * box : (n + 1) * box])
            next(parts, None)
            if 0 <= step - 2 * GROUP < count:
                mix(step - 2 * GROUP + n)
            next(parts, None)
            late = step - 2 * GROUP + n - GROUP // 2
            if step >= 2 * GROUP and 0 <= late < count:
                insert(late)
            if step < count and n % 2 == 0:
                along_rows(step + n, 2)

    if len(outs) == 1:
        outs[0][...] = totals[...].astype(bf16)
        return
    x_send, x_keep, own_send, own_keep, z_keep = outs[:5]
    z_sends = outs[5:]
    x_slots, owned, _ = own_keep.shape
    me = lax.axis_index("img")

    def rows_of(flip):
        return pl.ds(pl.multiple_of((me ^ flip) * owned, owned), owned)

    for n, k in enumerate(LINE):
        x_send[n] = totals[-x_slots:, rows_of(2 * k + 1), :].astype(bf16)
        x_keep[n] = totals[-x_slots:, rows_of(2 * k), :]
    own_send[...] = totals[-x_slots:, rows_of(1), :].astype(bf16)
    own_keep[...] = totals[-x_slots:, rows_of(0), :]
    for k, out in zip((0,) + LINE, (z_keep, *z_sends)):
        out[:Z_SLOTS] = totals[:Z_SLOTS, rows_of(2 * k), :].astype(out.dtype)
        out[Z_SLOTS:] = totals[1:Z_SLOTS, rows_of(2 * k + 1), :].astype(out.dtype)


SCRATCH = 20
LINE = (2, 3, 1)
SLOTS = 16
GROUP = 16
Z_SLOTS = 4


def own_totals(images, class_index, pose_index, defocus_bin, defocus, rows_table, cols_table, plane_weight, members):
    count, box, _ = images.shape
    poses, rows, _ = rows_table.shape
    cols = cols_table.shape[2]
    planes = plane_weight.shape[1]
    slots = CLASSES * planes
    table_y, table_x = packed_dft(box, -1.0), packed_dft(box, 1.0)
    any_place = pl.BlockSpec(memory_space=pl.ANY)
    vmem = pl.BlockSpec(memory_space=pltpu.VMEM)
    lanes = 128 * (-(-2 * count // 128))
    if members == 1:
        out_shape = [jax.ShapeDtypeStruct((slots, rows, 2 * cols), bf16)]
    else:
        slots += 1
        tail = (rows // members, 2 * cols)
        x_slots = slots - Z_SLOTS
        out_shape = []
        for lead in ((len(LINE), x_slots), (x_slots,)):
            out_shape += [pltpu.VMEM(lead + tail, bf16), pltpu.VMEM(lead + tail, f32)]
        out_shape += [pltpu.VMEM((2 * Z_SLOTS - 1,) + tail, f32)]
        out_shape += [pltpu.VMEM((2 * Z_SLOTS - 1,) + tail, bf16)] * len(LINE)
    operands = (
        class_index[:, 0], pose_index, defocus_bin, defocus, plane_weight.T,
        jnp.asarray(table_y, bf16), jnp.asarray(table_x.T.copy(), bf16),
        images, rows_table, cols_table,
    )
    return pl.pallas_call(
        slices_kernel,
        out_shape=out_shape,
        in_specs=[any_place] * 10,
        out_specs=[vmem] * len(out_shape),
        scratch_shapes=[pltpu.SMEM(x.shape, x.dtype) for x in operands[:5]]
        + [pltpu.VMEM(x.shape, x.dtype) for x in operands[5:]]
        + [
            pltpu.SemaphoreType.DMA((9 + count // GROUP,)),
            pltpu.VMEM((poses * rows, box), bf16),
            pltpu.VMEM((poses, box, 2 * cols), bf16),
            pltpu.VMEM((box // 2 + 8, lanes), f32),
            pltpu.VMEM((count, box), f32),
            pltpu.VMEM((count, box), f32),
            pltpu.VMEM((2, GROUP * box, box), bf16),
            pltpu.VMEM((SLOTS, box + 16, box), bf16),
            pltpu.VMEM((SLOTS, box, 2 * cols), bf16),
            pltpu.VMEM((slots, rows, 2 * cols), f32),
        ],
        compiler_params=pltpu.CompilerParams(vmem_limit_bytes=VMEM_LIMIT),
        cost_estimate=pl.CostEstimate(
            flops=2 * count * box * box * 1000, bytes_accessed=6 * 1024 * 1024, transcendentals=0
        ),
    )(*operands)


VMEM_LIMIT = 56 * 1024 * 1024


def ridge_kernel(defocus_hbm, plane_hbm, rows_hbm, cols_hbm, high_ref, low_ref, share_ref, *refs):
    defocus_ref, plane_ref, rows_ref, cols_ref, arrived = refs
    poses, owned, box = rows_ref.shape
    cols = cols_ref.shape[2]
    bins = defocus_ref.shape[0]
    planes = plane_ref.shape[0]
    half = box // 2
    first = pl.multiple_of(lax.axis_index("img") * owned, owned)
    copies = [
        pltpu.make_async_copy(defocus_hbm, defocus_ref, arrived.at[0]),
        pltpu.make_async_copy(plane_hbm, plane_ref, arrived.at[1]),
        pltpu.make_async_copy(rows_hbm.at[:, pl.ds(first, owned), :], rows_ref, arrived.at[2]),
        pltpu.make_async_copy(cols_hbm, cols_ref, arrived.at[3]),
    ]
    for copy in copies:
        copy.start()
    for copy in copies:
        copy.wait()
    share_plane = iota((planes * CLASSES, poses * bins), 0) // CLASSES
    share_pose = iota((planes * CLASSES, poses * bins), 1) // bins
    share = jnp.zeros((planes * CLASSES, poses * bins), f32)
    for p in range(poses):
        for z in range(planes):
            share = jnp.where((share_plane == z) & (share_pose == p), plane_ref[z, p], share)
    share_ref[...] = share

    bin_row = iota((bins, box), 0)
    sub_defocus = jnp.zeros((bins, box), f32)
    for b in range(bins):
        sub_defocus = jnp.where(bin_row == b, defocus_ref[b], sub_defocus)
    freq = iota((bins, box), 1)
    freq = jnp.where(freq < half, freq, box - freq).astype(f32)
    turns_x = sub_defocus * (freq * freq * (1.0 / (half * half)))
    turns_y = turns_x + ctf_phase / math.pi
    ones = jnp.ones((bins, box), f32)
    wave_y = jnp.concatenate(
        [0.5 * ones, -0.5 * turns_sine(turns_y + 0.25), 0.5 * turns_sine(turns_y)], 0
    )
    wave_x = jnp.concatenate([ones, turns_sine(turns_x + 0.25), turns_sine(turns_x)], 0)
    y_high, y_low = split_two(wave_y)
    x_high, x_low = split_two(wave_x)
    rows_sq = rows_ref[...].reshape(poses * owned, box).astype(f32)
    rows_sq = (rows_sq * rows_sq).astype(bf16)
    u = dot(y_high, rows_sq, ((1,), (1,))) + dot(y_low, rows_sq, ((1,), (1,)))
    for p in range(poses):
        cols_sq = cols_ref[p].astype(f32)
        cols_sq = (cols_sq * cols_sq).astype(bf16)
        v = dot(x_high, cols_sq) + dot(x_low, cols_sq)
        for r in range(owned):
            column = u[:, p * owned + r : p * owned + r + 1]
            product = v * column
            weight = product[:bins] + product[bins : 2 * bins] + product[2 * bins :]
            high, low = split_two(weight)
            high_ref[p * bins : (p + 1) * bins, r * cols : (r + 1) * cols] = high
            low_ref[p * bins : (p + 1) * bins, r * cols : (r + 1) * cols] = low


def own_ridges(defocus, plane_weight, rows_table, cols_table, owned):
    poses, _, box = rows_table.shape
    cols = cols_table.shape[2]
    bins = defocus.shape[0]
    any_place = pl.BlockSpec(memory_space=pl.ANY)
    vmem = pl.BlockSpec(memory_space=pltpu.VMEM)
    planes = plane_weight.T
    table = pltpu.VMEM((poses * bins, owned * cols), bf16)
    return pl.pallas_call(
        ridge_kernel,
        out_shape=[table, table, pltpu.VMEM((planes.shape[0] * CLASSES, poses * bins), f32)],
        in_specs=[any_place] * 4,
        out_specs=[vmem] * 3,
        scratch_shapes=[
            pltpu.SMEM(defocus.shape, f32),
            pltpu.SMEM(planes.shape, f32),
            pltpu.VMEM((poses, owned, box), bf16),
            pltpu.VMEM(cols_table.shape, bf16),
            pltpu.SemaphoreType.DMA((4,)),
        ],
        compiler_params=pltpu.CompilerParams(vmem_limit_bytes=VMEM_LIMIT),
        cost_estimate=pl.CostEstimate(
            flops=1000, bytes_accessed=1000, transcendentals=0
        ),
    )(defocus, planes, rows_table, cols_table)


def call_in_vmem(kernel, arrays, out_shape):
    vmem = pl.BlockSpec(memory_space=pltpu.VMEM)
    return pl.pallas_call(
        kernel,
        out_shape=out_shape,
        in_specs=[vmem] * len(arrays),
        out_specs=[vmem] * len(out_shape),
        compiler_params=pltpu.CompilerParams(vmem_limit_bytes=16 * 1024 * 1024),
        cost_estimate=pl.CostEstimate(flops=1000, bytes_accessed=1000, transcendentals=0),
    )(*arrays)


def fold_kernel(x_keep, x_came, own_send, z_keep, *refs):
    z_came, refs = refs[: len(LINE)], refs[len(LINE) :]
    x_sends, own_out, z_own, z_send = refs[: len(LINE)], *refs[len(LINE) :]
    for n, send in enumerate(x_sends):
        send[...] = (x_keep[n] + x_came[n].astype(f32)).astype(bf16)
    own_out[...] = own_send[...]
    for n in range(z_keep.shape[0]):
        value = z_keep[n]
        for came in z_came:
            value = value + came[n].astype(f32)
        if n < Z_SLOTS:
            z_own[n] = value
        if n == 0:
            z_send[n] = value.astype(bf16)
        elif n >= Z_SLOTS:
            z_send[n - Z_SLOTS + 1] = value.astype(bf16)


def fold_phase(x_keep, x_came, own_send, z_keep, z_came):
    piece = own_send.shape
    z_piece = (Z_SLOTS,) + piece[1:]
    out_shape = [pltpu.VMEM(piece, bf16)] * (len(LINE) + 1)
    out_shape += [pltpu.VMEM(z_piece, f32), pltpu.VMEM(z_piece, bf16)]
    return call_in_vmem(fold_kernel, (x_keep, x_came, own_send, z_keep, *z_came), out_shape)


def weight_kernel(high_ref, low_ref, share_ref, z_own, z_came, out_ref, ridge_ref):
    slots, pairs = share_ref.shape
    owned, _, cols = ridge_ref.shape
    counts = z_own[0] + z_came[0].astype(f32)
    scaled = jnp.concatenate([counts[:CLASSES, :pairs]] * (slots // CLASSES), 0) * share_ref[...]
    c_high, c_low = split_two(scaled)
    weight = (
        dot(c_high, high_ref[...]) + dot(c_low, high_ref[...]) + dot(c_high, low_ref[...])
    )
    ridge = 1.0 / (weight + wiener_ridge)
    for r in range(owned):
        ridge_ref[r] = ridge[:, r * cols : (r + 1) * cols]
    for s in range(slots):
        out_ref[s] = ridge_ref[:, s, :]


def own_weights(tables, z_own, z_came):
    slots = tables[2].shape[0]
    _, owned, wide = z_own.shape
    cols = wide // 2
    vmem = pl.BlockSpec(memory_space=pltpu.VMEM)
    return pl.pallas_call(
        weight_kernel,
        out_shape=pltpu.VMEM((slots, owned, cols), f32),
        in_specs=[vmem] * 5,
        out_specs=vmem,
        scratch_shapes=[pltpu.VMEM((owned, slots, cols), f32)],
        compiler_params=pltpu.CompilerParams(vmem_limit_bytes=16 * 1024 * 1024),
        cost_estimate=pl.CostEstimate(flops=1000, bytes_accessed=1000, transcendentals=0),
    )(*tables, z_own, z_came)


def finish_kernel(planes, ridge_ref, x_own, z_own, z_came, *refs):
    x_came, out_ref = refs[:-1], refs[-1]
    slots, owned, cols = ridge_ref.shape
    first = z_own.shape[0]
    for s in range(slots):
        if s + 1 < first:
            value = z_own[s + 1] + z_came[s + 1].astype(f32)
        else:
            value = x_own[s + 1 - first]
            for part in x_came:
                value = value + part[s + 1 - first].astype(f32)
        factor = ridge_ref[s]
        place = (s % CLASSES) * planes + s // CLASSES
        out_ref[:, 2 * place, :] = value[:, :cols] * factor
        out_ref[:, 2 * place + 1, :] = value[:, cols:] * factor


def finish(planes, ridge, x_own, z_own, z_came, x_came):
    slots, owned, cols = ridge.shape
    vmem = pl.BlockSpec(memory_space=pltpu.VMEM)
    return pl.pallas_call(
        functools.partial(finish_kernel, planes),
        out_shape=jax.ShapeDtypeStruct((owned, 2 * slots, cols), f32),
        in_specs=[vmem] * (4 + len(x_came)),
        out_specs=vmem,
        compiler_params=pltpu.CompilerParams(vmem_limit_bytes=16 * 1024 * 1024),
        cost_estimate=pl.CostEstimate(flops=1000, bytes_accessed=1000, transcendentals=0),
    )(ridge, x_own, z_own, z_came, *x_came)


def squared_table(weight_table):
    wide_table = weight_table.astype(f32)
    return (wide_table * wide_table).astype(bf16)


def weight_totals(class_index, pose_index, defocus_bin, defocus, rows_table, cols_table, plane_weight, first_row, owned):
    box = rows_table.shape[2]
    poses = rows_table.shape[0]
    bins = defocus.shape[0]
    half = box // 2
    exact = lax.Precision.HIGHEST
    code = (class_index[:, 0] * poses + pose_index) * bins + defocus_bin
    codes = lax.all_gather(code, "img", tiled=True)
    hits = (codes[:, None] == jnp.arange(CLASSES * poses * bins, dtype=jnp.int32)).astype(f32)
    counts = jnp.sum(hits, 0).reshape(CLASSES, poses, bins)
    place = jnp.arange(box, dtype=jnp.int32)
    freq = jnp.where(place < half, place, place - box).astype(f32)
    turns = defocus[:, None] * (freq * freq)[None, :] * (1.0 / (half * half))
    turns_y = turns + ctf_phase / math.pi
    ones = jnp.ones_like(turns)
    wave_y = jnp.stack([0.5 * ones, -0.5 * turns_sine(turns_y + 0.25), 0.5 * turns_sine(turns_y)])
    wave_x = jnp.stack([ones, turns_sine(turns + 0.25), turns_sine(turns)])
    rows_own = lax.dynamic_slice_in_dim(rows_table, first_row, owned, 1)
    u = jnp.einsum("pry,mby->pmbr", squared_table(rows_own).astype(f32), wave_y, precision=exact)
    v = jnp.einsum("pxj,mbx->pmbj", squared_table(cols_table).astype(f32), wave_x, precision=exact)
    weight = counts[:, None] * plane_weight.T[None, :, :, None]
    left = weight[:, :, :, None, :, None] * u[None, None]
    return jnp.einsum("czpmbr,pmbj->rczj", left, v, precision=exact)


def by_pairs(images, class_index, pose_index, defocus_bin, defocus, rows_table, cols_table, plane_weight):
    members = lax.axis_size("img")
    rows = rows_table.shape[1]
    planes = plane_weight.shape[1]
    cols = cols_table.shape[2]
    owned = rows // members

    def exchange(value, flip):
        return lax.ppermute(value, "img", [(i, i ^ flip) for i in range(members)])

    x_send, x_keep, own_send, own_keep, z_keep, *z_sends = own_totals(
        images, class_index, pose_index, defocus_bin, defocus, rows_table, cols_table, plane_weight, members
    )
    x_came = exchange(x_send, 1)
    z_came = [exchange(send, 2 * k) for send, k in zip(z_sends, LINE)]
    tables = own_ridges(defocus, plane_weight, rows_table, cols_table, owned)
    x_keep, tables = lax.optimization_barrier((x_keep, tables))
    *x_sends, own_send, z_own, z_send = fold_phase(x_keep, x_came, own_send, z_keep, z_came)
    x_came = [exchange(send, 2 * k) for send, k in zip(x_sends, LINE)]
    own_came = exchange(own_send, 1)
    z_came = exchange(z_send, 1)
    ridge = own_weights(tables, z_own, z_came)
    out = finish(planes, ridge, own_keep, z_own, z_came, (*x_came, own_came))
    return out.reshape(owned, CLASSES, planes, 2, cols)


def by_scatter(images, class_index, pose_index, defocus_bin, defocus, rows_table, cols_table, plane_weight):
    rows = rows_table.shape[1]
    cols = cols_table.shape[2]
    planes = plane_weight.shape[1]
    members = lax.axis_size("img")
    owned = rows // members
    (totals,) = own_totals(
        images, class_index, pose_index, defocus_bin, defocus, rows_table, cols_table, plane_weight, 1
    )
    slots = totals.shape[0]
    totals = totals.reshape(slots, members, owned, 2 * cols).transpose(1, 0, 2, 3)
    own = lax.psum_scatter(totals, "img", scatter_dimension=0, tiled=False)
    weight = weight_totals(
        class_index, pose_index, defocus_bin, defocus, rows_table, cols_table, plane_weight,
        lax.axis_index("img") * owned, owned,
    )
    own = own.astype(f32).reshape(planes, CLASSES, owned, 2, cols).transpose(2, 1, 0, 3, 4)
    return own / (weight[:, :, :, None, :] + wiener_ridge)


def body(*arrays):
    rows = arrays[5].shape[1]
    members = lax.axis_size("img")
    images = members * arrays[0].shape[0]
    paired = members == 8 and images <= 256 and rows % (16 * members) == 0
    return (by_pairs if paired else by_scatter)(*arrays)


def solution(mesh):
    placed = (
        P(("groups", "img"), None, None),
        P(("groups", "img"), None),
        P(("groups", "img")),
        P(("groups", "img")),
        P(),
        P(),
        P(None, None, "slab"),
        P(),
    )
    return jax.shard_map(
        body,
        mesh=mesh,
        in_specs=placed,
        out_specs=P("img", "groups", None, None, "slab"),
        check_vma=False,
    )
```
